32 devices in a mesh: dp: 8 (over y, x, core), group: 4 (over z).
Axes of the slice: x: 2, y: 2, z: 4, core: 2. Of those that a mesh axis runs over, the one named last changes fastest.
Arguments:
- queries: bfloat16 [8, 4, 192, 2048], P('dp', 'group'), may hold values from -6 to 6
- resp_keys: bfloat16 [8, 4, 192, 512], P('dp', 'group'), may hold values from -6 to 6
- resp_values: bfloat16 [8, 4, 192, 512], P('dp', 'group'), may hold values from -6 to 6
- prompt_cache: bfloat16 [8, 4, 2, 256, 512], P('dp', 'group'), may hold values from -1.6953125 to 1.6953125
- owners: int32 [8], P('dp'), may hold values from 0 to 3
- lengths: int32 [8, 4], P('dp', 'group'), may hold values from 1 to 192, 384 in all within a row
- q_gain: float32 [128], replicated, may hold values from 0.5 to 1.5
- k_gain: float32 [128], replicated, may hold values from 0.5 to 1.5
- grad_out: bfloat16 [8, 4, 192, 2048], P('dp', 'group'), may hold values from -6 to 6
Outputs:
- attended: bfloat16 [8, 4, 192, 2048], P('dp', 'group')
- d_queries: bfloat16 [8, 4, 192, 2048], P('dp', 'group')
- d_resp_keys: bfloat16 [8, 4, 192, 512], P('dp', 'group')
- d_resp_values: bfloat16 [8, 4, 192, 512], P('dp', 'group')
- d_prompt_cache: bfloat16 [8, 4, 2, 256, 512], P('dp', 'group')
- gain_grads: float32 [2, 128], replicated
The draws below stay inside these ranges and needn't reach their ends.
Inputs may be any that keep to these rules, and one draw needn't show every extreme that they name: In each group the lengths sum to 384 and the longest is 192.
All inputs are finite; a program needn't handle non-finite values.
Results may differ from the reference program's by a relative error of at most 0.0095.
Values may be sent and summed in bfloat16 or wider, within the bound.
No kernel may reach another device: no remote copies, remote signals or barrier semaphores. Data moves between devices by JAX's collectives and lax.ppermute only.
A program may use at most 64 MiB of HBM per device.

```python
import math
import jax
import jax.numpy as jnp
import numpy as np
from jax import lax

HEADS = 16
KV_HEADS = 4
HD = 128
PROMPT = 256
RESP = 192
GROUPS = 8
N_GROUP = 4


def with_ends(values, stream_key, least, high):
    longest = values.shape.index(max(values.shape))
    spots = []
    for shift in (0, 1):
        where = [jax.random.randint(jax.random.fold_in(stream_key, axis), (), 0, length) for axis, length in enumerate(values.shape)]
        where[longest] = (where[longest] + shift) % values.shape[longest]
        spots.append(tuple(where))
    return values.at[spots[0]].set(least).at[spots[1]].set(high)


def shard_levels(key, shape, pieces, low, high):
    def one(position, blocks):
        draws = jax.random.uniform(jax.random.fold_in(jax.random.fold_in(key, 6), position), (blocks,), jnp.float32, low / len(pieces), high / len(pieces))
        return jnp.repeat(jnp.exp(draws), shape[position] // blocks).reshape((-1,) + (1,) * (len(shape) - position - 1))

    factor_of = one(*pieces[0])
    for cut in pieces[1:]:
        factor_of = factor_of * one(*cut)
    return factor_of


def length_profile(number_of, total, bound, skew):
    loads = [(1 << 20) // math.isqrt(standing ** skew) + 1 for standing in range(2, number_of + 1)]
    spare, counts = total - bound - (number_of - 1), [1] * (number_of - 1)
    while spare > 0:
        movable = [i for i in range(number_of - 1) if counts[i] < bound]
        pool, left = sum([loads[i] for i in movable]), spare
        for i in movable:
            addition = min(bound - counts[i], max(1, left * loads[i] // pool), spare)
            counts[i] = counts[i] + addition
            spare = spare - addition
    return np.array([bound] + counts)


def uneven(key, count, total, limit, slope):
    if count == 2:
        one = jax.random.randint(key, (), max(1, total - limit), min(limit, total - 1) + 1)
        return jnp.stack([one, total - one])
    sizes = jnp.asarray(length_profile(count, total, limit, slope), jnp.int32)
    couples = (count - 1) // 2
    source_of, sink = sizes[1:1 + 2 * couples:2], sizes[2:2 + 2 * couples:2]
    room = jnp.minimum(source_of - 1, limit - sink)
    passed = jax.random.randint(jax.random.fold_in(key, 1), (couples,), 0, 1 << 20) % (room + 1)
    sizes = sizes.at[1:1 + 2 * couples:2].set(source_of - passed).at[2:2 + 2 * couples:2].set(sink + passed)
    return sizes[jax.random.permutation(jax.random.fold_in(key, 2), count)]


def normal_values(stream_key, dims, deviation, reach, cuts=(), kind=jnp.bfloat16):
    entries = jax.random.normal(stream_key, dims, jnp.float32) * deviation
    if len(cuts) > 0:
        entries = shard_levels(stream_key, dims, cuts, -0.22, 0.18) * entries
    return jnp.clip(entries, min=-reach, max=reach).astype(kind)


def setup_inputs(seed: int = 0) -> dict:
    keys = jax.random.split(jax.random.key(seed), 10)
    queries = normal_values(keys[0], (GROUPS, N_GROUP, RESP, HEADS * HD), 1.0, 6.0, ((0, 8), (1, 4)))
    resp_keys = normal_values(keys[1], (GROUPS, N_GROUP, RESP, KV_HEADS * HD), 1.0, 6.0, ((0, 8), (1, 4)))
    resp_values = normal_values(keys[2], (GROUPS, N_GROUP, RESP, KV_HEADS * HD), 1.0, 6.0, ((0, 8), (1, 4)))
    prompt_cache = jnp.clip(jax.random.uniform(keys[3], (GROUPS, N_GROUP, 2, PROMPT, KV_HEADS * HD), jnp.float32, -1.6953125, 1.6953125) * shard_levels(keys[3], (GROUPS, N_GROUP, 2, PROMPT, KV_HEADS * HD), ((0, 8), (1, 4)), -0.4, 0.0), -1.6953125, 1.6953125).astype(jnp.bfloat16)
    owners = with_ends(jax.random.randint(keys[4], (GROUPS,), 0, N_GROUP), jax.random.fold_in(keys[4], 1), 0, N_GROUP - 1).astype(jnp.int32)
    lengths = jax.vmap(lambda own: uneven(own, N_GROUP, N_GROUP * RESP // 2, RESP, 1))(jax.random.split(keys[5], GROUPS)).reshape((GROUPS, N_GROUP)).astype(jnp.int32)
    q_gain = jnp.clip(1.0 + 0.1 * jax.random.normal(keys[6], (HD,), jnp.float32), 0.5, 1.5)
    k_gain = jnp.clip(1.0 + 0.1 * jax.random.normal(keys[7], (HD,), jnp.float32), 0.5, 1.5)
    grad_out = normal_values(keys[8], (GROUPS, N_GROUP, RESP, HEADS * HD), 1.0, 6.0, ((0, 8), (1, 4)))
    return dict(queries=queries, resp_keys=resp_keys, resp_values=resp_values, prompt_cache=prompt_cache, owners=owners, lengths=lengths, q_gain=q_gain, k_gain=k_gain, grad_out=grad_out)


def normalize(raw_vals, gain_vec):
    widened = raw_vals.astype(jnp.float32)
    inverse = lax.rsqrt(lax.optimization_barrier(jnp.mean(widened * widened, axis=-1, keepdims=True)) + 1e-06)
    unit_vals = widened * inverse
    return (unit_vals * gain_vec, unit_vals, inverse)

def norm_back(unit_vals, inverse, gain_vec, upstream):
    scaled_up = upstream * gain_vec
    d_input = inverse * (scaled_up - unit_vals * lax.optimization_barrier(jnp.mean(scaled_up * unit_vals, axis=-1, keepdims=True)))
    gain_term = lax.optimization_barrier(jnp.sum(upstream * unit_vals, axis=tuple(range(upstream.ndim - 1))))
    return (d_input, gain_term)

def attend_local(queries, resp_keys, resp_values, cache, q_gain, k_gain, live_len, grad_out, head_size):
    resp_rows = queries.shape[0]
    prompt_rows = cache.shape[1]
    kv_heads = resp_keys.shape[1] // head_size
    share = queries.shape[1] // head_size // kv_heads
    q_scaled, q_unit, q_inv = normalize(queries.reshape(resp_rows, kv_heads, share, head_size), q_gain)
    k_scaled, k_unit, k_inv = normalize(resp_keys.reshape(resp_rows, kv_heads, head_size), k_gain)
    q_hat = q_scaled.astype(jnp.bfloat16)
    k_hat = k_scaled.astype(jnp.bfloat16)
    keys_all = jnp.concatenate([cache[0].reshape(prompt_rows, kv_heads, head_size), k_hat], axis=0)
    vals_all = jnp.concatenate([cache[1].reshape(prompt_rows, kv_heads, head_size), resp_values.reshape(resp_rows, kv_heads, head_size)], axis=0)
    score_scale = head_size ** (-0.5)
    scores = jnp.einsum('rkgd,skd->kgrs', q_hat, keys_all, preferred_element_type=jnp.float32) * score_scale
    row_index = jnp.arange(resp_rows, dtype=jnp.int32)[:, None]
    col_index = jnp.arange(prompt_rows + resp_rows, dtype=jnp.int32)[None, :]
    self_col = col_index - prompt_rows
    allowed = (col_index < prompt_rows) | (self_col <= row_index) & (self_col < live_len)
    expo = jnp.where(allowed, jnp.exp(scores), jnp.float32(0.0))
    probs = expo / lax.optimization_barrier(jnp.sum(expo, axis=-1, keepdims=True))
    probs_low = probs.astype(jnp.bfloat16)
    live = (jnp.arange(resp_rows, dtype=jnp.int32) < live_len)[:, None, None, None]
    attended_full = jnp.einsum('kgrs,skd->rkgd', probs_low, vals_all, preferred_element_type=jnp.float32)
    attended = jnp.where(live, attended_full, jnp.float32(0.0)).astype(jnp.bfloat16)
    d_out = jnp.where(live, grad_out.reshape(resp_rows, kv_heads, share, head_size), jnp.zeros((), jnp.bfloat16))
    d_probs = jnp.einsum('rkgd,skd->kgrs', d_out, vals_all, preferred_element_type=jnp.float32)
    delta = lax.optimization_barrier(jnp.sum(probs * d_probs, axis=-1, keepdims=True))
    d_scores = (probs * (d_probs - delta) * score_scale).astype(jnp.bfloat16)
    d_qhat = jnp.einsum('kgrs,skd->rkgd', d_scores, keys_all, preferred_element_type=jnp.float32)
    d_keys = jnp.einsum('kgrs,rkgd->skd', d_scores, q_hat, preferred_element_type=jnp.float32)
    d_vals = jnp.einsum('kgrs,rkgd->skd', probs_low, d_out, preferred_element_type=jnp.float32)
    d_query_in, q_term = norm_back(q_unit, q_inv, q_gain, d_qhat)
    d_key_in, k_term = norm_back(k_unit, k_inv, k_gain, d_keys[prompt_rows:])
    width_q = queries.shape[1]
    width_k = resp_keys.shape[1]
    prompt_part = jnp.stack([d_keys[:prompt_rows].reshape(prompt_rows, width_k), d_vals[:prompt_rows].reshape(prompt_rows, width_k)])
    return (attended.reshape(resp_rows, width_q), d_query_in.astype(jnp.bfloat16).reshape(resp_rows, width_q), d_key_in.astype(jnp.bfloat16).reshape(resp_rows, width_k), d_vals[prompt_rows:].astype(jnp.bfloat16).reshape(resp_rows, width_k), prompt_part, jnp.stack([q_term, k_term]))

def reference(queries, resp_keys, resp_values, prompt_cache, owners, lengths, q_gain, k_gain, grad_out):

    def one_group(index):
        owner = owners[index]
        cache = prompt_cache[index, owner]

        def one_member(member):
            return attend_local(queries[index, member], resp_keys[index, member], resp_values[index, member], cache, q_gain, k_gain, lengths[index, member], grad_out[index, member], HD)
        attended, d_query, d_key, d_value, parts, gains = lax.map(one_member, jnp.arange(N_GROUP, dtype=jnp.int32))
        summed = lax.optimization_barrier(jnp.sum(parts, axis=0)).astype(jnp.bfloat16)
        mine = (jnp.arange(N_GROUP, dtype=jnp.int32) == owner)[:, None, None, None]
        placed = jnp.where(mine, summed[None], jnp.zeros((), jnp.bfloat16))
        return (attended, d_query, d_key, d_value, placed, lax.optimization_barrier(jnp.sum(gains, axis=0)))
    attended, d_query, d_key, d_value, placed, gains = lax.map(one_group, jnp.arange(GROUPS, dtype=jnp.int32))
    return (attended, d_query, d_key, d_value, placed, lax.optimization_barrier(jnp.sum(gains, axis=0)))
```

```python
import functools

import jax
import jax.numpy as jnp
from jax import lax
from jax.experimental import pallas as pl
from jax.experimental.pallas import tpu as pltpu
from jax.sharding import PartitionSpec as P

HD = 128
EPS = 1e-06
LOG2E = 1.4426950408889634
BF = jnp.bfloat16
F32 = jnp.float32


def dot_nn(a, b):
    return lax.dot_general(a, b, (((1,), (0,)), ((), ())), preferred_element_type=F32)


def dot_nt(a, b):
    return lax.dot_general(a, b, (((1,), (1,)), ((), ())), preferred_element_type=F32)


def head_kernel(
    share, rows, width, meta, q_ref, g_ref, k_ref, v_ref, pr_ref, gain_ref, acc_ref, *rest
):
    att_ref, dq_ref, dk_ref, dv_ref, part_ref, gacc_ref = rest[-6:]
    live_len = meta[1]
    scale = HD ** (-0.5)

    def stacked(ref):
        return jnp.concatenate([ref[:, i * HD : (i + 1) * HD] for i in range(share)], axis=0)

    q_gain = gain_ref[:, 0:1]
    q_t = stacked(q_ref).T
    g_t = stacked(g_ref).T

    raw_k = k_ref[...].astype(F32)
    k_inv = lax.rsqrt(jnp.mean(raw_k * raw_k, axis=-1, keepdims=True) + EPS)
    k_unit = raw_k * k_inv
    kg_row = acc_ref[2:3, :]
    k_hat = (k_unit * kg_row).astype(BF)
    p_key = pr_ref[0]
    p_val = pr_ref[1]
    r_val = v_ref[...]
    p_key_t = p_key.T
    p_val_t = p_val.T
    k_hat_t = k_hat.T
    r_val_t = r_val.T

    total = share * rows
    d_kp = d_kr = d_vp = d_vr = q_term = None
    att_parts, dq_parts = [], []
    for start in range(0, total, width):
        cols = slice(start, start + width)
        token = (lax.broadcasted_iota(jnp.int32, (1, width), 1) + start) % rows
        live = token < live_len
        raw_q = q_t[:, cols].astype(F32)
        q_inv = lax.rsqrt(jnp.mean(raw_q * raw_q, axis=0, keepdims=True) + EPS)
        q_unit = raw_q * q_inv
        q_hat = (q_unit * q_gain).astype(BF)
        d_o = jnp.where(live, g_t[:, cols].astype(F32), 0.0)
        d_ob = d_o.astype(BF)

        e_p = jnp.exp2(dot_nn(p_key, q_hat) * (scale * LOG2E))
        causal = lax.broadcasted_iota(jnp.int32, (rows, width), 0) <= token
        e_r = jnp.where(causal, jnp.exp2(dot_nn(k_hat, q_hat) * (scale * LOG2E)), 0.0)
        inv_sum = 1.0 / (
            jnp.sum(e_p, axis=0, keepdims=True) + jnp.sum(e_r, axis=0, keepdims=True)
        )
        eb_p = e_p.astype(BF)
        eb_r = e_r.astype(BF)
        out = (dot_nn(p_val_t, eb_p) + dot_nn(r_val_t, eb_r)) * inv_sum
        att_parts.append(jnp.where(live, out, 0.0).astype(BF))
        delta = jnp.sum(d_o * out, axis=0, keepdims=True)
        ds_p = (e_p * (dot_nn(p_val, d_ob) - delta)).astype(BF)
        ds_r = (e_r * (dot_nn(r_val, d_ob) - delta)).astype(BF)
        weight = inv_sum * scale
        d_qhat = (dot_nn(p_key_t, ds_p) + dot_nn(k_hat_t, ds_r)) * weight
        q_w = (q_hat.astype(F32) * weight).astype(BF)
        d_ow = (d_o * inv_sum).astype(BF)
        terms = (
            dot_nt(ds_p, q_w),
            dot_nt(ds_r, q_w),
            dot_nt(eb_p, d_ow),
            dot_nt(eb_r, d_ow),
            d_qhat * q_unit,
        )
        if d_kp is None:
            d_kp, d_kr, d_vp, d_vr, q_term = terms
        else:
            d_kp, d_kr, d_vp, d_vr, q_term = [
                a + b for a, b in zip((d_kp, d_kr, d_vp, d_vr, q_term), terms)
            ]
        up = d_qhat * q_gain
        mean = jnp.mean(up * q_unit, axis=0, keepdims=True)
        dq_parts.append((q_inv * (up - q_unit * mean)).astype(BF))

    att = jnp.concatenate(att_parts, axis=1).T
    d_q = jnp.concatenate(dq_parts, axis=1).T
    for i in range(share):
        att_ref[:, i * HD : (i + 1) * HD] = att[i * rows : (i + 1) * rows, :]
        dq_ref[:, i * HD : (i + 1) * HD] = d_q[i * rows : (i + 1) * rows, :]
    part_ref[0] = d_kp.astype(BF)
    part_ref[1] = d_vp.astype(BF)
    dv_ref[...] = d_vr.astype(BF)
    up_k = d_kr * kg_row
    mean_k = jnp.mean(up_k * k_unit, axis=-1, keepdims=True)
    dk_ref[...] = (k_inv * (up_k - k_unit * mean_k)).astype(BF)
    folded = q_term[:, :HD]
    for start in range(HD, width, HD):
        folded = folded + q_term[:, start : start + HD]
    gacc_ref[0:1, :] = acc_ref[0:1, :] + jnp.sum(folded.T, axis=0, keepdims=True)
    gacc_ref[1:2, :] = acc_ref[1:2, :] + jnp.sum(d_kr * k_unit, axis=0, keepdims=True)
    gacc_ref[2:3, :] = kg_row


def one_head(meta, q, g, k, v, prompt, gain_cols, acc, buffers, kv_heads):
    rows, q_width = q.shape
    share = q_width // HD // kv_heads
    wide = share * HD
    by_head_q = pl.BlockSpec((rows, wide), lambda i, m: (0, m[0]))
    by_head_k = pl.BlockSpec((rows, HD), lambda i, m: (0, m[0]))
    whole = lambda a: pl.BlockSpec(a.shape, lambda i, m: (0,) * a.ndim)
    any_spec = pl.BlockSpec(memory_space=pl.ANY)
    in_specs = [by_head_q, by_head_q, by_head_k, by_head_k, whole(prompt), whole(gain_cols), whole(acc)]
    in_specs += [any_spec] * len(buffers)
    part = jax.ShapeDtypeStruct(prompt.shape, BF)
    out_shape = [
        jax.ShapeDtypeStruct((rows, q_width), BF),
        jax.ShapeDtypeStruct((rows, q_width), BF),
        jax.ShapeDtypeStruct((rows, kv_heads * HD), BF),
        jax.ShapeDtypeStruct((rows, kv_heads * HD), BF),
        part,
        jax.ShapeDtypeStruct(acc.shape, F32),
    ]
    outs = pl.pallas_call(
        functools.partial(head_kernel, share, rows, 2 * HD),
        out_shape=out_shape,
        grid_spec=pltpu.PrefetchScalarGridSpec(
            num_scalar_prefetch=1,
            grid=(1,),
            in_specs=in_specs,
            out_specs=[by_head_q, by_head_q, by_head_k, by_head_k, whole(part), whole(acc)],
        ),
        input_output_aliases={8 + i: i for i in range(len(buffers))},
        compiler_params=pltpu.CompilerParams(vmem_limit_bytes=40 * 2**20),
        cost_estimate=pl.CostEstimate(
            flops=12 * share * rows * (rows + prompt.shape[1]) * HD,
            bytes_accessed=5 * rows * wide * 2,
            transcendentals=share * rows * (rows + prompt.shape[1]),
        ),
        name="attend_head",
    )(meta, q, g, k, v, prompt, gain_cols, acc, *buffers)
    return outs[:4], outs[4], outs[5]


def place_kernel(meta, *refs):
    out_ref = refs[-1]
    mine = meta[0] > 0
    for i, ref in enumerate(refs[:-1]):
        at = pl.multiple_of(meta[1 + i] * HD, HD)
        out_ref[:, :, pl.ds(at, HD)] = jnp.where(mine, ref[...], jnp.zeros((), BF))


def place(meta, heads):
    depth, rows, _ = heads[0].shape
    return pl.pallas_call(
        place_kernel,
        out_shape=jax.ShapeDtypeStruct((depth, rows, HD * len(heads)), BF),
        in_specs=[pl.BlockSpec(memory_space=pltpu.SMEM)]
        + [pl.BlockSpec(memory_space=pltpu.VMEM)] * len(heads),
        out_specs=pl.BlockSpec(memory_space=pltpu.VMEM),
        name="place_prompt_grad",
    )(meta, *heads)


def pair_sum(value, axis, size):
    step = 1
    while step < size:
        value = value + lax.ppermute(value, axis, [(i, i ^ step) for i in range(size)])
        step *= 2
    return value


def local(
    n_dp, n_group, queries, resp_keys, resp_values, prompt_cache, owners, lengths, q_gain, k_gain, grad_out
):
    q, g = queries[0, 0], grad_out[0, 0]
    k, v = resp_keys[0, 0], resp_values[0, 0]
    cache = prompt_cache[0, 0]
    owner = owners[0]
    live_len = lengths[0, 0]
    me = lax.axis_index("group")
    kv_heads = k.shape[1] // HD
    depth, p_rows, _ = cache.shape
    direct = n_group == kv_heads

    def shift(x, s):
        return lax.ppermute(x, "group", [(i, (i + s) % n_group) for i in range(n_group)])

    def head_of(array, index):
        return lax.dynamic_slice(array, (0, 0, index * HD), (depth, p_rows, HD))

    if direct:
        got = [head_of(cache, me)]
        for s in range(1, n_group):
            got.append(shift(head_of(cache, (me + s) % n_group), s))
        mine = got[0]
        for s in range(1, n_group):
            mine = jnp.where(owner == (me - s) % n_group, got[s], mine)
        order = [(me - s) % n_group for s in range(n_group)]
        prompts = [mine] + [shift(mine, s) for s in range(1, n_group)]
    else:
        cache = lax.psum(jnp.where(me == owner, cache, jnp.zeros_like(cache)), "group")
        order = [jnp.int32(h) for h in range(kv_heads)]
        prompts = [head_of(cache, h) for h in order]

    gain_cols = jnp.stack([q_gain, k_gain], axis=1)
    acc = jnp.zeros((8, HD), F32).at[2].set(k_gain)
    buffers, parts = (), []
    for head, prompt in zip(order, prompts):
        meta = jnp.stack([head, live_len]).astype(jnp.int32)
        buffers, part, acc = one_head(meta, q, g, k, v, prompt, gain_cols, acc, buffers, kv_heads)
        parts.append(part)

    if direct:
        back = [shift(parts[s], -s).astype(F32) for s in range(1, n_group)]
        total = parts[0].astype(F32)
        for b in back:
            total = total + b
        total = total.astype(BF)
        heads = [total] + [shift(total, s) for s in range(1, n_group)]
    else:
        total = lax.psum(jnp.concatenate(parts, axis=-1).astype(F32), "group").astype(BF)
        heads = [head_of(total, h) for h in order]
    flag = (me == owner).astype(jnp.int32)
    placed = place(jnp.stack([flag] + order).astype(jnp.int32), heads)

    gains = pair_sum(pair_sum(acc[:2], "group", n_group), "dp", n_dp)
    attended, d_query, d_key, d_value = buffers
    return (
        attended[None, None],
        d_query[None, None],
        d_key[None, None],
        d_value[None, None],
        placed[None, None],
        gains,
    )


def solution(mesh):
    in_specs = (
        P("dp", "group", None, None),
        P("dp", "group", None, None),
        P("dp", "group", None, None),
        P("dp", "group", None, None, None),
        P("dp"),
        P("dp", "group"),
        P(),
        P(),
        P("dp", "group", None, None),
    )
    out_specs = (
        P("dp", "group", None, None),
        P("dp", "group", None, None),
        P("dp", "group", None, None),
        P("dp", "group", None, None),
        P("dp", "group", None, None, None),
        P(),
    )
    body = functools.partial(local, mesh.shape["dp"], mesh.shape["group"])
    return jax.shard_map(body, mesh=mesh, in_specs=in_specs, out_specs=out_specs, check_vma=False)
```

```python
import functools

import jax
import jax.numpy as jnp
from jax import lax
from jax.experimental import pallas as pl
from jax.experimental.pallas import tpu as pltpu
from jax.sharding import PartitionSpec as P

HD = 128
EPS = 1e-06
LOG2E = 1.4426950408889634
BF = jnp.bfloat16
F32 = jnp.float32


def dot_nn(a, b):
    return lax.dot_general(a, b, (((1,), (0,)), ((), ())), preferred_element_type=F32)


def dot_nt(a, b):
    return lax.dot_general(a, b, (((1,), (1,)), ((), ())), preferred_element_type=F32)


def head_kernel(
    share, rows, width, meta, q_ref, g_ref, k_ref, v_ref, pr_ref, gain_ref, acc_ref, *rest
):
    att_ref, dq_ref, dk_ref, dv_ref, part_ref, gacc_ref = rest[-6:]
    live_len = meta[1]
    scale = HD ** (-0.5)

    def stacked(ref):
        return jnp.concatenate([ref[:, i * HD : (i + 1) * HD] for i in range(share)], axis=0)

    q_gain = gain_ref[:, 0:1]
    q_t = stacked(q_ref).T
    g_t = stacked(g_ref).T

    raw_k = k_ref[...].astype(F32)
    k_inv = lax.rsqrt(jnp.mean(raw_k * raw_k, axis=-1, keepdims=True) + EPS)
    k_unit = raw_k * k_inv
    kg_row = acc_ref[2:3, :]
    k_hat = (k_unit * kg_row).astype(BF)
    p_key = pr_ref[0]
    p_val = pr_ref[1]
    r_val = v_ref[...]
    p_key_t = p_key.T
    p_val_t = p_val.T
    k_hat_t = k_hat.T
    r_val_t = r_val.T

    total = share * rows
    d_kp = d_kr = d_vp = d_vr = q_term = None
    att_parts, dq_parts = [], []
    for start in range(0, total, width):
        cols = slice(start, start + width)
        token = (lax.broadcasted_iota(jnp.int32, (1, width), 1) + start) % rows
        live = token < live_len
        raw_q = q_t[:, cols].astype(F32)
        q_inv = lax.rsqrt(jnp.mean(raw_q * raw_q, axis=0, keepdims=True) + EPS)
        q_unit = raw_q * q_inv
        q_hat = (q_unit * q_gain).astype(BF)
        d_o = jnp.where(live, g_t[:, cols].astype(F32), 0.0)
        d_ob = d_o.astype(BF)

        e_p = jnp.exp2(dot_nn(p_key, q_hat) * (scale * LOG2E))
        causal = lax.broadcasted_iota(jnp.int32, (rows, width), 0) <= token
        e_r = jnp.where(causal, jnp.exp2(dot_nn(k_hat, q_hat) * (scale * LOG2E)), 0.0)
        inv_sum = 1.0 / (
            jnp.sum(e_p, axis=0, keepdims=True) + jnp.sum(e_r, axis=0, keepdims=True)
        )
        eb_p = e_p.astype(BF)
        eb_r = e_r.astype(BF)
        out = (dot_nn(p_val_t, eb_p) + dot_nn(r_val_t, eb_r)) * inv_sum
        att_parts.append(jnp.where(live, out, 0.0).astype(BF))
        delta = jnp.sum(d_o * out, axis=0, keepdims=True)
        ds_p = (e_p * (dot_nn(p_val, d_ob) - delta)).astype(BF)
        ds_r = (e_r * (dot_nn(r_val, d_ob) - delta)).astype(BF)
        weight = inv_sum * scale
        d_qhat = (dot_nn(p_key_t, ds_p) + dot_nn(k_hat_t, ds_r)) * weight
        q_w = (q_hat.astype(F32) * weight).astype(BF)
        d_ow = (d_o * inv_sum).astype(BF)
        terms = (
            dot_nt(ds_p, q_w),
            dot_nt(ds_r, q_w),
            dot_nt(eb_p, d_ow),
            dot_nt(eb_r, d_ow),
            d_qhat * q_unit,
        )
        if d_kp is None:
            d_kp, d_kr, d_vp, d_vr, q_term = terms
        else:
            d_kp, d_kr, d_vp, d_vr, q_term = [
                a + b for a, b in zip((d_kp, d_kr, d_vp, d_vr, q_term), terms)
            ]
        up = d_qhat * q_gain
        mean = jnp.mean(up * q_unit, axis=0, keepdims=True)
        dq_parts.append((q_inv * (up - q_unit * mean)).astype(BF))

    att = jnp.concatenate(att_parts, axis=1).T
    d_q = jnp.concatenate(dq_parts, axis=1).T
    for i in range(share):
        att_ref[:, i * HD : (i + 1) * HD] = att[i * rows : (i + 1) * rows, :]
        dq_ref[:, i * HD : (i + 1) * HD] = d_q[i * rows : (i + 1) * rows, :]
    part_ref[0] = d_kp.astype(BF)
    part_ref[1] = d_vp.astype(BF)
    dv_ref[...] = d_vr.astype(BF)
    up_k = d_kr * kg_row
    mean_k = jnp.mean(up_k * k_unit, axis=-1, keepdims=True)
    dk_ref[...] = (k_inv * (up_k - k_unit * mean_k)).astype(BF)
    folded = q_term[:, :HD]
    for start in range(HD, width, HD):
        folded = folded + q_term[:, start : start + HD]
    gacc_ref[0:1, :] = acc_ref[0:1, :] + jnp.sum(folded.T, axis=0, keepdims=True)
    gacc_ref[1:2, :] = acc_ref[1:2, :] + jnp.sum(d_kr * k_unit, axis=0, keepdims=True)
    gacc_ref[2:3, :] = kg_row


def one_head(meta, q, g, k, v, prompt, gain_cols, acc, buffers, kv_heads):
    rows, q_width = q.shape
    share = q_width // HD // kv_heads
    wide = share * HD
    by_head_q = pl.BlockSpec((rows, wide), lambda i, m: (0, m[0]))
    by_head_k = pl.BlockSpec((rows, HD), lambda i, m: (0, m[0]))
    whole = lambda a: pl.BlockSpec(a.shape, lambda i, m: (0,) * a.ndim)
    any_spec = pl.BlockSpec(memory_space=pl.ANY)
    in_specs = [by_head_q, by_head_q, by_head_k, by_head_k, whole(prompt), whole(gain_cols), whole(acc)]
    in_specs += [any_spec] * len(buffers)
    part = jax.ShapeDtypeStruct(prompt.shape, BF)
    out_shape = [
        jax.ShapeDtypeStruct((rows, q_width), BF),
        jax.ShapeDtypeStruct((rows, q_width), BF),
        jax.ShapeDtypeStruct((rows, kv_heads * HD), BF),
        jax.ShapeDtypeStruct((rows, kv_heads * HD), BF),
        part,
        jax.ShapeDtypeStruct(acc.shape, F32),
    ]
    outs = pl.pallas_call(
        functools.partial(head_kernel, share, rows, 2 * HD),
        out_shape=out_shape,
        grid_spec=pltpu.PrefetchScalarGridSpec(
            num_scalar_prefetch=1,
            grid=(1,),
            in_specs=in_specs,
            out_specs=[by_head_q, by_head_q, by_head_k, by_head_k, whole(part), whole(acc)],
        ),
        input_output_aliases={8 + i: i for i in range(len(buffers))},
        compiler_params=pltpu.CompilerParams(vmem_limit_bytes=40 * 2**20),
        cost_estimate=pl.CostEstimate(
            flops=12 * share * rows * (rows + prompt.shape[1]) * HD,
            bytes_accessed=5 * rows * wide * 2,
            transcendentals=share * rows * (rows + prompt.shape[1]),
        ),
        name="attend_head",
    )(meta, q, g, k, v, prompt, gain_cols, acc, *buffers)
    return outs[:4], outs[4], outs[5]


TAIL = 16


def join_kernel(own_ref, *rest):
    backs, gains_ref, out_ref = rest[:-2], rest[-2], rest[-1]
    depth, rows, _ = own_ref.shape
    for d in range(depth):
        total = own_ref[d].astype(F32)
        for back in backs:
            total = total + back[d].astype(F32)
        out_ref[d * rows : (d + 1) * rows, :] = total.astype(BF)
    gains = gains_ref[...]
    high = gains.astype(BF)
    gains = gains - high.astype(F32)
    middle = gains.astype(BF)
    low = (gains - middle.astype(F32)).astype(BF)
    pieces = jnp.concatenate([p[0:2].astype(F32) for p in (high, middle, low)], axis=0)
    pad = jnp.zeros((TAIL - pieces.shape[0], HD), F32)
    out_ref[depth * rows :, :] = jnp.concatenate([pieces, pad], axis=0).astype(BF)


def join(own, backs, gains):
    depth, rows, _ = own.shape
    vmem = pl.BlockSpec(memory_space=pltpu.VMEM)
    return pl.pallas_call(
        join_kernel,
        out_shape=jax.ShapeDtypeStruct((depth * rows + TAIL, HD), BF),
        in_specs=[vmem] * (2 + len(backs)),
        out_specs=vmem,
        compiler_params=pltpu.CompilerParams(vmem_limit_bytes=8 * 2**20),
        name="join_parts",
    )(own, *backs, gains)


def place_kernel(meta, *refs):
    payloads, out_ref, gain_ref, stage = refs[:-3], refs[-3], refs[-2], refs[-1]
    mine = meta[0] > 0
    depth, rows, _ = out_ref.shape
    for i, ref in enumerate(payloads):
        at = pl.multiple_of(meta[1 + i] * HD, HD)
        for d in range(depth):
            block = ref[d * rows : (d + 1) * rows, :]
            out_ref[d, :, pl.ds(at, HD)] = jnp.where(mine, block, jnp.zeros_like(block))
        tail = ref[depth * rows :, :].astype(F32)
        stage[meta[1 + i]] = tail[0:2] + tail[2:4] + tail[4:6]
    total = stage[0]
    for i in range(1, len(payloads)):
        total = total + stage[i]
    gain_ref[...] = total


def place(meta, payloads, depth, rows):
    count = len(payloads)
    vmem = pl.BlockSpec(memory_space=pltpu.VMEM)
    return pl.pallas_call(
        place_kernel,
        out_shape=[
            jax.ShapeDtypeStruct((depth, rows, HD * count), BF),
            jax.ShapeDtypeStruct((2, HD), F32),
        ],
        in_specs=[pl.BlockSpec(memory_space=pltpu.SMEM)] + [vmem] * count,
        out_specs=[vmem, vmem],
        scratch_shapes=[pltpu.VMEM((count, 2, HD), F32)],
        compiler_params=pltpu.CompilerParams(vmem_limit_bytes=8 * 2**20),
        name="place_prompt_grad",
    )(meta, *payloads)


def pair_sum(value, axis, size):
    step = 1
    while step < size:
        value = value + lax.ppermute(value, axis, [(i, i ^ step) for i in range(size)])
        step *= 2
    return value


def local(
    n_dp, n_group, queries, resp_keys, resp_values, prompt_cache, owners, lengths, q_gain, k_gain, grad_out
):
    q, g = queries[0, 0], grad_out[0, 0]
    k, v = resp_keys[0, 0], resp_values[0, 0]
    cache = prompt_cache[0, 0]
    owner = owners[0]
    live_len = lengths[0, 0]
    me = lax.axis_index("group")
    kv_heads = k.shape[1] // HD
    depth, p_rows, _ = cache.shape
    direct = n_group == kv_heads

    def shift(x, s):
        return lax.ppermute(x, "group", [(i, (i + s) % n_group) for i in range(n_group)])

    def head_of(array, index):
        return lax.dynamic_slice(array, (0, 0, index * HD), (depth, p_rows, HD))

    if direct:
        got = [head_of(cache, me)]
        for s in range(1, n_group):
            got.append(shift(head_of(cache, (me + s) % n_group), s))
        mine = got[0]
        for s in range(1, n_group):
            mine = jnp.where(owner == (me - s) % n_group, got[s], mine)
        order = [(me - s) % n_group for s in range(n_group)]
        prompts = [mine] + [shift(mine, s) for s in range(1, n_group)]
    else:
        cache = lax.psum(jnp.where(me == owner, cache, jnp.zeros_like(cache)), "group")
        order = [jnp.int32(h) for h in range(kv_heads)]
        prompts = [head_of(cache, h) for h in order]

    gain_cols = jnp.stack([q_gain, k_gain], axis=1)
    acc = jnp.zeros((8, HD), F32).at[2].set(k_gain)
    buffers, parts, backs = (), [], []
    for s, (head, prompt) in enumerate(zip(order, prompts)):
        if direct and s == n_group - 1:
            prompt, backs[0] = lax.optimization_barrier((prompt, backs[0]))
        meta = jnp.stack([head, live_len]).astype(jnp.int32)
        buffers, part, acc = one_head(meta, q, g, k, v, prompt, gain_cols, acc, buffers, kv_heads)
        parts.append(part)
        if direct and s > 0:
            backs.append(shift(part, -s))

    mine_flag = (me == owner).astype(jnp.int32)
    if direct:
        payload = join(parts[0], backs, pair_sum(acc, "dp", n_dp))
        payloads = [payload] + [shift(payload, s) for s in range(1, n_group)]
        meta = jnp.stack([mine_flag] + order).astype(jnp.int32)
        placed, gains = place(meta, payloads, depth, p_rows)
    else:
        total = lax.psum(jnp.concatenate(parts, axis=-1).astype(F32), "group").astype(BF)
        placed = jnp.where(mine_flag > 0, total, jnp.zeros((), BF))
        gains = pair_sum(pair_sum(acc[:2], "dp", n_dp), "group", n_group)
    attended, d_query, d_key, d_value = buffers
    return (
        attended[None, None],
        d_query[None, None],
        d_key[None, None],
        d_value[None, None],
        placed[None, None],
        gains,
    )


def solution(mesh):
    in_specs = (
        P("dp", "group", None, None),
        P("dp", "group", None, None),
        P("dp", "group", None, None),
        P("dp", "group", None, None, None),
        P("dp"),
        P("dp", "group"),
        P(),
        P(),
        P("dp", "group", None, None),
    )
    out_specs = (
        P("dp", "group", None, None),
        P("dp", "group", None, None),
        P("dp", "group", None, None),
        P("dp", "group", None, None),
        P("dp", "group", None, None, None),
        P(),
    )
    body = functools.partial(local, mesh.shape["dp"], mesh.shape["group"])
    return jax.shard_map(body, mesh=mesh, in_specs=in_specs, out_specs=out_specs, check_vma=False)
```

```python
import functools

import jax
import jax.numpy as jnp
from jax import lax
from jax.experimental import pallas as pl
from jax.experimental.pallas import tpu as pltpu
from jax.sharding import PartitionSpec as P

HD = 128
EPS = 1e-06
LOG2E = 1.4426950408889634
BF = jnp.bfloat16
F32 = jnp.float32


def dot_nn(a, b):
    return lax.dot_general(a, b, (((1,), (0,)), ((), ())), preferred_element_type=F32)


def dot_nt(a, b):
    return lax.dot_general(a, b, (((1,), (1,)), ((), ())), preferred_element_type=F32)


VMEM = pl.BlockSpec(memory_space=pltpu.VMEM)
SMEM = pl.BlockSpec(memory_space=pltpu.SMEM)
ANY = pl.BlockSpec(memory_space=pl.ANY)


def params(mib):
    return pltpu.CompilerParams(vmem_limit_bytes=mib * 2**20)


def cut_kernel(order, cache_ref, *rest):
    outs, sems = rest[:-1], rest[-1]
    copies = []
    for i, out in enumerate(outs):
        at = pl.multiple_of(order[i] * HD, HD)
        copy = pltpu.make_async_copy(cache_ref.at[:, :, pl.ds(at, HD)], out, sems.at[i])
        copy.start()
        copies.append(copy)
    for copy in copies:
        copy.wait()


def cut(order, cache, count):
    depth, rows, _ = cache.shape
    return pl.pallas_call(
        cut_kernel,
        out_shape=[jax.ShapeDtypeStruct((depth, rows, HD), BF)] * count,
        in_specs=[SMEM, ANY],
        out_specs=[VMEM] * count,
        scratch_shapes=[pltpu.SemaphoreType.DMA((count,))],
        compiler_params=params(4),
        name="cut_prompt",
    )(order, cache)


def pick_kernel(which, *refs):
    picked = refs[0][...]
    for i in range(1, len(refs) - 1):
        picked = jnp.where(which[0] == i, refs[i][...], picked)
    refs[-1][...] = picked


def pick(which, blocks):
    return pl.pallas_call(
        pick_kernel,
        out_shape=jax.ShapeDtypeStruct(blocks[0].shape, BF),
        in_specs=[SMEM] + [VMEM] * len(blocks),
        out_specs=VMEM,
        compiler_params=params(4),
        name="pick_owner",
    )(which, *blocks)


KEPT = 8


def prepare_kernel(count, share, rows, width, meta, q_ref, g_ref, k_ref, v_ref, gain_ref, kg_ref, *outs):
    live_len = meta[count]
    scale = HD ** (-0.5)
    q_gain = gain_ref[...]
    k_gain = kg_ref[...]
    for s in range(count):
        qt_ref, gt_ref, row_ref, er_ref, ot_ref, dp_ref, kh_ref, ku_ref = outs[s * KEPT : (s + 1) * KEPT]
        base = meta[s]

        def stacked(ref):
            at = [pl.multiple_of((base * share + i) * HD, HD) for i in range(share)]
            return jnp.concatenate([ref[:, pl.ds(x, HD)] for x in at], axis=0)

        q_t = stacked(q_ref).T
        g_t = stacked(g_ref).T
        qt_ref[...] = q_t
        k_at = pl.ds(pl.multiple_of(base * HD, HD), HD)
        raw_k = k_ref[:, k_at].astype(F32)
        k_unit = raw_k * lax.rsqrt(jnp.mean(raw_k * raw_k, axis=-1, keepdims=True) + EPS)
        k_hat = (k_unit * k_gain).astype(BF)
        kh_ref[...] = k_hat
        ku_ref[...] = k_unit
        r_val = v_ref[:, k_at]
        r_val_t = r_val.T
        for start in range(0, share * rows, width):
            cols = slice(start, start + width)
            token = (lax.broadcasted_iota(jnp.int32, (1, width), 1) + start) % rows
            raw_q = q_t[:, cols].astype(F32)
            q_inv = lax.rsqrt(jnp.mean(raw_q * raw_q, axis=0, keepdims=True) + EPS)
            q_hat = (raw_q * q_inv * q_gain).astype(BF)
            d_o = jnp.where(token < live_len, g_t[:, cols].astype(F32), 0.0).astype(BF)
            gt_ref[:, cols] = d_o
            causal = lax.broadcasted_iota(jnp.int32, (rows, width), 0) <= token
            e_r = jnp.where(causal, jnp.exp2(dot_nn(k_hat, q_hat) * (scale * LOG2E)), 0.0)
            eb_r = e_r.astype(BF)
            er_ref[:, cols] = eb_r
            ot_ref[:, cols] = dot_nn(r_val_t, eb_r)
            dp_ref[:, cols] = dot_nn(r_val, d_o)
            row_ref[0:1, cols] = q_inv
            row_ref[1:2, cols] = jnp.sum(e_r, axis=0, keepdims=True)


def prepare(meta, q, g, k, v, q_gain, k_gain, count):
    rows, q_width = q.shape
    share = q_width // k.shape[1]
    total = share * rows
    each = [
        jax.ShapeDtypeStruct((HD, total), BF),
        jax.ShapeDtypeStruct((HD, total), BF),
        jax.ShapeDtypeStruct((8, total), F32),
        jax.ShapeDtypeStruct((rows, total), BF),
        jax.ShapeDtypeStruct((HD, total), F32),
        jax.ShapeDtypeStruct((rows, total), F32),
        jax.ShapeDtypeStruct((rows, HD), BF),
        jax.ShapeDtypeStruct((rows, HD), F32),
    ]
    outs = pl.pallas_call(
        functools.partial(prepare_kernel, count, share, rows, 2 * HD),
        out_shape=each * count,
        in_specs=[SMEM] + [VMEM] * 6,
        out_specs=[VMEM] * (KEPT * count),
        compiler_params=params(24),
        cost_estimate=pl.CostEstimate(
            flops=6 * count * total * rows * HD,
            bytes_accessed=5 * rows * q_width * 2,
            transcendentals=count * total * rows,
        ),
        name="prepare_response",
    )(meta, q, g, k, v, q_gain, k_gain)
    return [list(outs[s * KEPT : (s + 1) * KEPT]) for s in range(count)]


def head_kernel(
    width, pr_ref, qt_ref, gt_ref, row_ref, er_ref, ot_ref, dp_ref, kh_ref, ku_ref, gain_ref, acc_ref,
    part_ref, at_ref, dq_ref, dkr_ref, dvr_ref, gacc_ref,
):
    scale = HD ** (-0.5)
    q_gain = gain_ref[...]
    p_key = pr_ref[0]
    p_val = pr_ref[1]
    k_hat_t = kh_ref[...].T
    p_key_t = p_key.T
    p_val_t = p_val.T
    sums = None
    for start in range(0, qt_ref.shape[1], width):
        cols = slice(start, start + width)
        q_unit = qt_ref[:, cols].astype(F32) * row_ref[0:1, cols]
        q_hat = (q_unit * q_gain).astype(BF)
        d_ob = gt_ref[:, cols]
        d_o = d_ob.astype(F32)
        e_p = jnp.exp2(dot_nn(p_key, q_hat) * (scale * LOG2E))
        inv_sum = 1.0 / (jnp.sum(e_p, axis=0, keepdims=True) + row_ref[1:2, cols])
        eb_p = e_p.astype(BF)
        eb_r = er_ref[:, cols]
        out = (dot_nn(p_val_t, eb_p) + ot_ref[:, cols]) * inv_sum
        at_ref[:, cols] = out.astype(BF)
        delta = jnp.sum(d_o * out, axis=0, keepdims=True)
        ds_p = (e_p * (dot_nn(p_val, d_ob) - delta)).astype(BF)
        ds_r = (eb_r.astype(F32) * (dp_ref[:, cols] - delta)).astype(BF)
        weight = inv_sum * scale
        q_w = (q_hat.astype(F32) * weight).astype(BF)
        d_ow = (d_o * inv_sum).astype(BF)
        d_qhat = (dot_nn(p_key_t, ds_p) + dot_nn(k_hat_t, ds_r)) * weight
        dq_ref[:, cols] = d_qhat
        terms = (
            dot_nt(ds_p, q_w),
            dot_nt(eb_p, d_ow),
            dot_nt(ds_r, q_w),
            dot_nt(eb_r, d_ow),
            d_qhat * q_unit,
        )
        sums = terms if sums is None else [a + b for a, b in zip(sums, terms)]
    d_kp, d_vp, d_kr, d_vr, q_term = sums
    part_ref[0] = d_kp.astype(BF)
    part_ref[1] = d_vp.astype(BF)
    dkr_ref[...] = d_kr
    dvr_ref[...] = d_vr.astype(BF)
    folded = q_term[:, :HD]
    for start in range(HD, width, HD):
        folded = folded + q_term[:, start : start + HD]
    gacc_ref[0:1, :] = acc_ref[0:1, :] + jnp.sum(folded.T, axis=0, keepdims=True)
    gacc_ref[1:2, :] = acc_ref[1:2, :] + jnp.sum(d_kr * ku_ref[...], axis=0, keepdims=True)
    gacc_ref[2:8, :] = jnp.zeros((6, HD), F32)


def one_head(prompt, kept, q_gain, acc):
    total = kept[0].shape[1]
    rows = kept[3].shape[0]
    return pl.pallas_call(
        functools.partial(head_kernel, 2 * HD),
        out_shape=[
            jax.ShapeDtypeStruct(prompt.shape, BF),
            jax.ShapeDtypeStruct((HD, total), BF),
            jax.ShapeDtypeStruct((HD, total), F32),
            jax.ShapeDtypeStruct((rows, HD), F32),
            jax.ShapeDtypeStruct((rows, HD), BF),
            jax.ShapeDtypeStruct(acc.shape, F32),
        ],
        in_specs=[VMEM] * 11,
        out_specs=[VMEM] * 6,
        compiler_params=params(16),
        cost_estimate=pl.CostEstimate(
            flops=(8 * prompt.shape[1] + 4 * rows) * total * HD,
            bytes_accessed=2**20,
            transcendentals=total * prompt.shape[1],
        ),
        name="attend_head",
    )(prompt, *kept, q_gain, acc)


def finish_kernel(count, share, rows, width, meta, k_ref, gain_ref, kg_ref, *refs):
    ins, (att_ref, dq_ref, dk_ref, dv_ref) = refs[:-4], refs[-4:]
    live_len = meta[count]
    q_gain = gain_ref[...]
    k_gain = kg_ref[...]
    for s in range(count):
        qt_ref, row_ref, ku_ref, at_in, dq_in, dkr_ref, dvr_ref = ins[s * 7 : (s + 1) * 7]
        base = meta[s]
        k_at = pl.ds(pl.multiple_of(base * HD, HD), HD)
        dv_ref[:, k_at] = dvr_ref[...]
        raw_k = k_ref[:, k_at].astype(F32)
        k_inv = lax.rsqrt(jnp.mean(raw_k * raw_k, axis=-1, keepdims=True) + EPS)
        k_unit = ku_ref[...]
        up_k = dkr_ref[...] * k_gain
        mean_k = jnp.mean(up_k * k_unit, axis=-1, keepdims=True)
        dk_ref[:, k_at] = (k_inv * (up_k - k_unit * mean_k)).astype(BF)
        parts = []
        for start in range(0, share * rows, width):
            cols = slice(start, start + width)
            q_inv = row_ref[0:1, cols]
            q_unit = qt_ref[:, cols].astype(F32) * q_inv
            up = dq_in[:, cols] * q_gain
            mean = jnp.mean(up * q_unit, axis=0, keepdims=True)
            parts.append((q_inv * (up - q_unit * mean)).astype(BF))
        d_q = jnp.concatenate(parts, axis=1).T
        att = at_in[...].T
        live = lax.broadcasted_iota(jnp.int32, (rows, HD), 0) < live_len
        for i in range(share):
            at = pl.ds(pl.multiple_of((base * share + i) * HD, HD), HD)
            block = att[i * rows : (i + 1) * rows, :].astype(F32)
            att_ref[:, at] = jnp.where(live, block, 0.0).astype(BF)
            dq_ref[:, at] = d_q[i * rows : (i + 1) * rows, :]


def finish(meta, k, q_gain, k_gain, per_head, q_width):
    rows, k_width = k.shape
    flat = [x for group in per_head for x in group]
    return pl.pallas_call(
        functools.partial(finish_kernel, len(per_head), q_width // k_width, rows, 2 * HD),
        out_shape=[
            jax.ShapeDtypeStruct((rows, q_width), BF),
            jax.ShapeDtypeStruct((rows, q_width), BF),
            jax.ShapeDtypeStruct((rows, k_width), BF),
            jax.ShapeDtypeStruct((rows, k_width), BF),
        ],
        in_specs=[SMEM] + [VMEM] * (3 + len(flat)),
        out_specs=[VMEM] * 4,
        compiler_params=params(16),
        cost_estimate=pl.CostEstimate(
            flops=40 * rows * q_width, bytes_accessed=10 * rows * q_width, transcendentals=0
        ),
        name="finish_response",
    )(meta, k, q_gain, k_gain, *flat)


def join_kernel(*refs):
    total = refs[0][...].astype(F32)
    for ref in refs[1:-1]:
        total = total + ref[...].astype(F32)
    refs[-1][...] = total.astype(BF)


def join(parts):
    return pl.pallas_call(
        join_kernel,
        out_shape=jax.ShapeDtypeStruct(parts[0].shape, BF),
        in_specs=[VMEM] * len(parts),
        out_specs=VMEM,
        compiler_params=params(4),
        name="join_parts",
    )(*parts)


def ordered_sum_kernel(count, order, *refs):
    stage = refs[-1]
    for i in range(count):
        stage[order[i]] = refs[i][...]
    total = stage[0]
    for i in range(1, count):
        total = total + stage[i]
    refs[count][...] = total


def ordered_sum(order, terms):
    count = len(terms)
    return pl.pallas_call(
        functools.partial(ordered_sum_kernel, count),
        out_shape=jax.ShapeDtypeStruct(terms[0].shape, F32),
        in_specs=[SMEM] + [VMEM] * count,
        out_specs=VMEM,
        scratch_shapes=[pltpu.VMEM((count,) + terms[0].shape, F32)],
        compiler_params=params(4),
        name="sum_gains",
    )(order, *terms)


def place_kernel(meta, *refs):
    heads, out_ref = refs[:-1], refs[-1]
    mine = meta[0] > 0
    for i, ref in enumerate(heads):
        at = pl.multiple_of(meta[1 + i] * HD, HD)
        out_ref[:, :, pl.ds(at, HD)] = jnp.where(mine, ref[...], jnp.zeros_like(ref[...]))


def place(meta, heads):
    depth, rows, _ = heads[0].shape
    return pl.pallas_call(
        place_kernel,
        out_shape=jax.ShapeDtypeStruct((depth, rows, HD * len(heads)), BF),
        in_specs=[SMEM] + [VMEM] * len(heads),
        out_specs=VMEM,
        compiler_params=params(8),
        name="place_prompt_grad",
    )(meta, *heads)


def pair_sum(value, axis, size):
    step = 1
    while step < size:
        value = value + lax.ppermute(value, axis, [(i, i ^ step) for i in range(size)])
        step *= 2
    return value


def local(
    n_dp, n_group, queries, resp_keys, resp_values, prompt_cache, owners, lengths, q_gain, k_gain, grad_out
):
    q, g = queries[0, 0], grad_out[0, 0]
    k, v = resp_keys[0, 0], resp_values[0, 0]
    cache = prompt_cache[0, 0]
    owner = owners[0]
    live_len = lengths[0, 0]
    me = lax.axis_index("group")
    kv_heads = k.shape[1] // HD
    depth, p_rows, _ = cache.shape
    direct = n_group == kv_heads

    def shift(x, s):
        return lax.ppermute(x, "group", [(i, (i + s) % n_group) for i in range(n_group)])

    gain_col = q_gain[:, None]
    gain_row = k_gain[None, :]
    if direct:
        order = jnp.stack([(me - s) % n_group for s in range(n_group)]).astype(jnp.int32)
    else:
        order = jnp.arange(kv_heads, dtype=jnp.int32)
    meta = jnp.concatenate([order, live_len[None]])
    kept = prepare(meta, q, g, k, v, gain_col, gain_row, kv_heads)
    if direct:
        blocks = cut(order, cache, kv_heads)
        got = [blocks[0]] + [shift(blocks[s], -s) for s in range(1, n_group)]
        got[1], kept[0][2] = lax.optimization_barrier((got[1], kept[0][2]))
        mine = pick(jnp.reshape((owner - me) % n_group, (1,)).astype(jnp.int32), got)
        prompts = [mine] + [shift(mine, s) for s in range(1, n_group)]
    else:
        cache = lax.psum(jnp.where(me == owner, cache, jnp.zeros_like(cache)), "group")
        prompts = cut(order, cache, kv_heads)

    acc = jnp.zeros((8, HD), F32)
    parts, backs, per_head = [], [], []
    for s, prompt in enumerate(prompts):
        if direct and s == n_group - 1:
            prompt, backs[0] = lax.optimization_barrier((prompt, backs[0]))
        part, out_t, d_q, d_kr, d_vr, acc = one_head(prompt, kept[s], gain_col, acc)
        per_head.append((kept[s][0], kept[s][2], kept[s][7], out_t, d_q, d_kr, d_vr))
        parts.append(part)
        if direct and s > 0:
            backs.append(shift(part, -s))

    mine_flag = (me == owner).astype(jnp.int32)
    if direct:
        total = join([parts[0]] + backs)
        gains = ordered_sum(order, [acc] + [shift(acc, s) for s in range(1, n_group)])
        total, gains = lax.optimization_barrier((total, gains))
        heads = [total] + [shift(total, s) for s in range(1, n_group)]
        placed = place(jnp.concatenate([mine_flag[None], order]), heads)
    else:
        total = lax.psum(jnp.concatenate(parts, axis=-1).astype(F32), "group").astype(BF)
        placed = jnp.where(mine_flag > 0, total, jnp.zeros((), BF))
        gains = pair_sum(acc, "group", n_group)
    gains = pair_sum(gains, "dp", n_dp)[:2]
    attended, d_query, d_key, d_value = finish(meta, k, gain_col, gain_row, per_head, q.shape[1])
    return (
        attended[None, None],
        d_query[None, None],
        d_key[None, None],
        d_value[None, None],
        placed[None, None],
        gains,
    )


def solution(mesh):
    in_specs = (
        P("dp", "group", None, None),
        P("dp", "group", None, None),
        P("dp", "group", None, None),
        P("dp", "group", None, None, None),
        P("dp"),
        P("dp", "group"),
        P(),
        P(),
        P("dp", "group", None, None),
    )
    out_specs = (
        P("dp", "group", None, None),
        P("dp", "group", None, None),
        P("dp", "group", None, None),
        P("dp", "group", None, None),
        P("dp", "group", None, None, None),
        P(),
    )
    body = functools.partial(local, mesh.shape["dp"], mesh.shape["group"])
    return jax.shard_map(body, mesh=mesh, in_specs=in_specs, out_specs=out_specs, check_vma=False)
```

```python
import functools

import jax
import jax.numpy as jnp
from jax import lax
from jax.experimental import pallas as pl
from jax.experimental.pallas import tpu as pltpu
from jax.sharding import PartitionSpec as P

HD = 128
EPS = 1e-06
LOG2E = 1.4426950408889634
BF = jnp.bfloat16
F32 = jnp.float32


def dot_nn(a, b):
    return lax.dot_general(a, b, (((1,), (0,)), ((), ())), preferred_element_type=F32)


def dot_nt(a, b):
    return lax.dot_general(a, b, (((1,), (1,)), ((), ())), preferred_element_type=F32)


VMEM = pl.BlockSpec(memory_space=pltpu.VMEM)
SMEM = pl.BlockSpec(memory_space=pltpu.SMEM)
HBM = pl.BlockSpec(memory_space=pltpu.HBM)


def params(mib):
    return pltpu.CompilerParams(vmem_limit_bytes=mib * 2**20)


def cut_kernel(order, cache_ref, *rest):
    outs, sems = rest[:-1], rest[-1]
    copies = []
    for i, out in enumerate(outs):
        at = pl.multiple_of(order[i] * HD, HD)
        copy = pltpu.make_async_copy(cache_ref.at[:, :, pl.ds(at, HD)], out, sems.at[i])
        copy.start()
        copies.append(copy)
    for copy in copies:
        copy.wait()


def cut(order, cache, count):
    depth, rows, _ = cache.shape
    return pl.pallas_call(
        cut_kernel,
        out_shape=[jax.ShapeDtypeStruct((depth, rows, HD), BF)] * count,
        in_specs=[SMEM, HBM],
        out_specs=[VMEM] * count,
        scratch_shapes=[pltpu.SemaphoreType.DMA((count,))],
        compiler_params=params(4),
        name="cut_prompt",
    )(order, cache)


def pick_kernel(which, *refs):
    picked = refs[0][...]
    for i in range(1, len(refs) - 1):
        picked = jnp.where(which[0] == i, refs[i][...], picked)
    refs[-1][...] = picked


def pick(which, blocks):
    return pl.pallas_call(
        pick_kernel,
        out_shape=jax.ShapeDtypeStruct(blocks[0].shape, BF),
        in_specs=[SMEM] + [VMEM] * len(blocks),
        out_specs=VMEM,
        compiler_params=params(4),
        name="pick_owner",
    )(which, *blocks)


KEPT = 8


def prepare_kernel(count, share, rows, width, meta, q_in, g_in, k_in, v_in, gain_ref, kg_ref, *rest):
    outs, (q_buf, g_buf, k_buf, v_buf, sems) = rest[:-5], rest[-5:]
    live_len = meta[count]
    scale = HD ** (-0.5)
    wide = share * HD
    copies = []
    for s in range(count):
        group = []
        for j, (src, buf, size) in enumerate(
            ((q_in, q_buf, wide), (k_in, k_buf, HD), (g_in, g_buf, wide), (v_in, v_buf, HD))
        ):
            at = pl.multiple_of(meta[s] * size, size)
            copy = pltpu.make_async_copy(src.at[:, pl.ds(at, size)], buf.at[s], sems.at[s, j])
            copy.start()
            group.append(copy)
        copies.append(group)
    q_gain = gain_ref[...]
    k_gain = kg_ref[...]
    for s in range(count):
        qt_ref, gt_ref, row_ref, er_ref, ot_ref, dp_ref, kh_ref, ku_ref = outs[s * KEPT : (s + 1) * KEPT]
        for copy in copies[s]:
            copy.wait()
        q_t = jnp.concatenate([q_buf[s, :, i * HD : (i + 1) * HD] for i in range(share)], axis=0).T
        g_t = jnp.concatenate([g_buf[s, :, i * HD : (i + 1) * HD] for i in range(share)], axis=0).T
        qt_ref[...] = q_t
        raw_k = k_buf[s].astype(F32)
        k_inv = lax.rsqrt(jnp.mean(raw_k * raw_k, axis=-1, keepdims=True) + EPS)
        k_unit = raw_k * k_inv
        k_hat = (k_unit * k_gain).astype(BF)
        kh_ref[...] = k_hat
        ku_ref[:, :HD] = k_unit
        ku_ref[:, HD:] = jnp.broadcast_to(k_inv, (rows, HD))
        r_val = v_buf[s]
        r_val_t = r_val.T
        for start in range(0, share * rows, width):
            cols = slice(start, start + width)
            token = (lax.broadcasted_iota(jnp.int32, (1, width), 1) + start) % rows
            raw_q = q_t[:, cols].astype(F32)
            q_inv = lax.rsqrt(jnp.mean(raw_q * raw_q, axis=0, keepdims=True) + EPS)
            q_hat = (raw_q * q_inv * q_gain).astype(BF)
            d_o = jnp.where(token < live_len, g_t[:, cols].astype(F32), 0.0).astype(BF)
            gt_ref[:, cols] = d_o
            causal = lax.broadcasted_iota(jnp.int32, (rows, width), 0) <= token
            e_r = jnp.where(causal, jnp.exp2(dot_nn(k_hat, q_hat) * (scale * LOG2E)), 0.0)
            eb_r = e_r.astype(BF)
            er_ref[:, cols] = eb_r
            ot_ref[:, cols] = dot_nn(r_val_t, eb_r)
            dp_ref[:, cols] = dot_nn(r_val, d_o)
            row_ref[0:1, cols] = q_inv
            row_ref[1:2, cols] = jnp.sum(e_r, axis=0, keepdims=True)


def prepare(meta, q, g, k, v, q_gain, k_gain, count):
    rows, q_width = q.shape
    share = q_width // k.shape[1]
    total = share * rows
    each = [
        jax.ShapeDtypeStruct((HD, total), BF),
        jax.ShapeDtypeStruct((HD, total), BF),
        jax.ShapeDtypeStruct((8, total), F32),
        jax.ShapeDtypeStruct((rows, total), BF),
        jax.ShapeDtypeStruct((HD, total), F32),
        jax.ShapeDtypeStruct((rows, total), F32),
        jax.ShapeDtypeStruct((rows, HD), BF),
        jax.ShapeDtypeStruct((rows, 2 * HD), F32),
    ]
    outs = pl.pallas_call(
        functools.partial(prepare_kernel, count, share, rows, 2 * HD),
        out_shape=each * count,
        in_specs=[SMEM] + [HBM] * 4 + [VMEM] * 2,
        out_specs=[VMEM] * (KEPT * count),
        scratch_shapes=[
            pltpu.VMEM((count, rows, share * HD), BF),
            pltpu.VMEM((count, rows, share * HD), BF),
            pltpu.VMEM((count, rows, HD), BF),
            pltpu.VMEM((count, rows, HD), BF),
            pltpu.SemaphoreType.DMA((count, 4)),
        ],
        compiler_params=params(16),
        cost_estimate=pl.CostEstimate(
            flops=6 * count * total * rows * HD,
            bytes_accessed=5 * rows * q_width * 2,
            transcendentals=count * total * rows,
        ),
        name="prepare_response",
    )(meta, q, g, k, v, q_gain, k_gain)
    return [list(outs[s * KEPT : (s + 1) * KEPT]) for s in range(count)]


def attend(width, pr_ref, kept, q_gain, acc_ref, part_ref, at_ref, dq_ref, gacc_ref):
    qt_ref, gt_ref, row_ref, er_ref, ot_ref, dp_ref, kh_ref, ku_ref = kept
    scale = HD ** (-0.5)
    p_key = pr_ref[0]
    p_val = pr_ref[1]
    k_hat_t = kh_ref[...].T
    p_key_t = p_key.T
    p_val_t = p_val.T
    sums = None
    for start in range(0, qt_ref.shape[1], width):
        cols = slice(start, start + width)
        q_unit = qt_ref[:, cols].astype(F32) * row_ref[0:1, cols]
        q_hat = (q_unit * q_gain).astype(BF)
        d_ob = gt_ref[:, cols]
        d_o = d_ob.astype(F32)
        e_p = jnp.exp2(dot_nn(p_key, q_hat) * (scale * LOG2E))
        inv_sum = 1.0 / (jnp.sum(e_p, axis=0, keepdims=True) + row_ref[1:2, cols])
        eb_p = e_p.astype(BF)
        eb_r = er_ref[:, cols]
        out = (dot_nn(p_val_t, eb_p) + ot_ref[:, cols]) * inv_sum
        at_ref[:, cols] = out.astype(BF)
        delta = jnp.sum(d_o * out, axis=0, keepdims=True)
        ds_p = (e_p * (dot_nn(p_val, d_ob) - delta)).astype(BF)
        ds_r = (eb_r.astype(F32) * (dp_ref[:, cols] - delta)).astype(BF)
        weight = inv_sum * scale
        q_w = (q_hat.astype(F32) * weight).astype(BF)
        d_ow = (d_o * inv_sum).astype(BF)
        d_qhat = (dot_nn(p_key_t, ds_p) + dot_nn(k_hat_t, ds_r)) * weight
        dq_ref[:, cols] = d_qhat
        terms = (
            dot_nt(ds_p, q_w),
            dot_nt(eb_p, d_ow),
            dot_nt(ds_r, q_w),
            dot_nt(eb_r, d_ow),
            d_qhat * q_unit,
        )
        sums = terms if sums is None else [a + b for a, b in zip(sums, terms)]
    d_kp, d_vp, d_kr, d_vr, q_term = sums
    part_ref[0] = d_kp.astype(BF)
    part_ref[1] = d_vp.astype(BF)
    folded = q_term[:, :HD]
    for start in range(HD, width, HD):
        folded = folded + q_term[:, start : start + HD]
    gacc_ref[0:1, :] = acc_ref[0:1, :] + jnp.sum(folded.T, axis=0, keepdims=True)
    gacc_ref[1:2, :] = acc_ref[1:2, :] + jnp.sum(d_kr * ku_ref[:, :HD], axis=0, keepdims=True)
    return d_kr, d_vr


def settle(width, head, live_len, kept, q_gain, k_gain, at_ref, dq_ref, d_kr, d_vr, outs, bufs, sems):
    qt_ref, row_ref, ku_ref = kept[0], kept[2], kept[7]
    a_buf, q_buf, k_buf, v_buf = bufs
    rows, wide = a_buf.shape
    share = wide // HD
    copies = []

    def send(j, buf):
        size = buf.shape[1]
        at = pl.multiple_of(head * size, size)
        copy = pltpu.make_async_copy(buf, outs[j].at[:, pl.ds(at, size)], sems.at[j])
        copy.start()
        copies.append(copy)

    att = at_ref[...].T
    live = lax.broadcasted_iota(jnp.int32, (rows, HD), 0) < live_len
    for i in range(share):
        block = att[i * rows : (i + 1) * rows, :].astype(F32)
        a_buf[:, i * HD : (i + 1) * HD] = jnp.where(live, block, 0.0).astype(BF)
    send(0, a_buf)
    v_buf[...] = d_vr.astype(BF)
    send(3, v_buf)
    k_unit = ku_ref[:, :HD]
    up_k = d_kr * k_gain
    mean_k = jnp.mean(up_k * k_unit, axis=-1, keepdims=True)
    k_buf[...] = (ku_ref[:, HD:] * (up_k - k_unit * mean_k)).astype(BF)
    send(2, k_buf)
    parts = []
    for start in range(0, share * rows, width):
        cols = slice(start, start + width)
        q_inv = row_ref[0:1, cols]
        q_unit = qt_ref[:, cols].astype(F32) * q_inv
        up = dq_ref[:, cols] * q_gain
        mean = jnp.mean(up * q_unit, axis=0, keepdims=True)
        parts.append((q_inv * (up - q_unit * mean)).astype(BF))
    d_q = jnp.concatenate(parts, axis=1).T
    for i in range(share):
        q_buf[:, i * HD : (i + 1) * HD] = d_q[i * rows : (i + 1) * rows, :]
    send(1, q_buf)
    for copy in copies:
        copy.wait()


def whole_kernel(s, width, meta, pr_ref, *rest):
    kept, (gain_ref, kg_ref, acc_ref) = rest[:KEPT], rest[KEPT : KEPT + 3]
    part_ref, gacc_ref, *rest = rest[-13:]
    outs, (at_ref, dq_ref), bufs, sems = rest[:4], rest[4:6], rest[6:10], rest[10]
    q_gain = gain_ref[...]
    d_kr, d_vr = attend(width, pr_ref, kept, q_gain, acc_ref, part_ref, at_ref, dq_ref, gacc_ref)
    live_len = meta[meta.shape[0] - 1]
    settle(width, meta[s], live_len, kept, q_gain, kg_ref[...], at_ref, dq_ref, d_kr, d_vr, outs, bufs, sems)


def first_kernel(width, pr_ref, *rest):
    kept, (gain_ref, acc_ref) = rest[:KEPT], rest[KEPT : KEPT + 2]
    part_ref, gacc_ref, at_ref, dq_ref, dkr_ref, dvr_ref = rest[-6:]
    d_kr, d_vr = attend(width, pr_ref, kept, gain_ref[...], acc_ref, part_ref, at_ref, dq_ref, gacc_ref)
    dkr_ref[...] = d_kr
    dvr_ref[...] = d_vr


def second_kernel(s, width, meta, *rest):
    kept, (gain_ref, kg_ref, at_ref, dq_ref, dkr_ref, dvr_ref) = rest[:KEPT], rest[KEPT : KEPT + 6]
    outs, bufs, sems = rest[-9:-5], rest[-5:-1], rest[-1]
    live_len = meta[meta.shape[0] - 1]
    settle(
        width, meta[s], live_len, kept, gain_ref[...], kg_ref[...], at_ref, dq_ref,
        dkr_ref[...], dvr_ref[...], outs, bufs, sems,
    )


def out_shapes(rows, q_width, k_width):
    widths = (q_width, q_width, k_width, k_width)
    return [jax.ShapeDtypeStruct((rows, w), BF) for w in widths]


def out_scratch(rows, share):
    widths = (share * HD, share * HD, HD, HD)
    return [pltpu.VMEM((rows, w), BF) for w in widths] + [pltpu.SemaphoreType.DMA((4,))]


def cost(prompt_rows, rows, total):
    return pl.CostEstimate(
        flops=(8 * prompt_rows + 4 * rows) * total * HD,
        bytes_accessed=2**20,
        transcendentals=total * prompt_rows,
    )


def whole_head(s, meta, prompt, kept, q_gain, k_gain, acc, buffers, q_width, k_width):
    total = kept[0].shape[1]
    rows = kept[3].shape[0]
    outs = pl.pallas_call(
        functools.partial(whole_kernel, s, 2 * HD),
        out_shape=[
            jax.ShapeDtypeStruct(prompt.shape, BF),
            jax.ShapeDtypeStruct(acc.shape, F32),
        ]
        + out_shapes(rows, q_width, k_width),
        in_specs=[SMEM] + [VMEM] * (4 + KEPT) + [HBM] * len(buffers),
        out_specs=[VMEM] * 2 + [HBM] * 4,
        scratch_shapes=[pltpu.VMEM((HD, total), BF), pltpu.VMEM((HD, total), F32)]
        + out_scratch(rows, total // rows),
        input_output_aliases={5 + KEPT + i: 2 + i for i in range(len(buffers))},
        compiler_params=params(16),
        cost_estimate=cost(prompt.shape[1], rows, total),
        name="attend_head",
    )(meta, prompt, *kept, q_gain, k_gain, acc, *buffers)
    return outs[0], outs[1], outs[2:]


def first_half(prompt, kept, q_gain, acc):
    total = kept[0].shape[1]
    rows = kept[3].shape[0]
    return pl.pallas_call(
        functools.partial(first_kernel, 2 * HD),
        out_shape=[
            jax.ShapeDtypeStruct(prompt.shape, BF),
            jax.ShapeDtypeStruct(acc.shape, F32),
            jax.ShapeDtypeStruct((HD, total), BF),
            jax.ShapeDtypeStruct((HD, total), F32),
            jax.ShapeDtypeStruct((rows, HD), F32),
            jax.ShapeDtypeStruct((rows, HD), F32),
        ],
        in_specs=[VMEM] * (3 + KEPT),
        out_specs=[VMEM] * 6,
        compiler_params=params(16),
        cost_estimate=cost(prompt.shape[1], rows, total),
        name="attend_last_head",
    )(prompt, *kept, q_gain, acc)


def second_half(s, meta, kept, q_gain, k_gain, results, buffers):
    total = kept[0].shape[1]
    rows = kept[3].shape[0]
    return pl.pallas_call(
        functools.partial(second_kernel, s, 2 * HD),
        out_shape=out_shapes(rows, buffers[0].shape[1], buffers[2].shape[1]),
        in_specs=[SMEM] + [VMEM] * (KEPT + 6) + [HBM] * 4,
        out_specs=[HBM] * 4,
        scratch_shapes=out_scratch(rows, total // rows),
        input_output_aliases={7 + KEPT + i: i for i in range(4)},
        compiler_params=params(16),
        cost_estimate=pl.CostEstimate(flops=0, bytes_accessed=2**20, transcendentals=0),
        name="settle_last_head",
    )(meta, *kept, q_gain, k_gain, *results, *buffers)


def join_kernel(*refs):
    total = refs[0][...].astype(F32)
    for ref in refs[1:-1]:
        total = total + ref[...].astype(F32)
    refs[-1][...] = total.astype(BF)


def join(parts):
    return pl.pallas_call(
        join_kernel,
        out_shape=jax.ShapeDtypeStruct(parts[0].shape, BF),
        in_specs=[VMEM] * len(parts),
        out_specs=VMEM,
        compiler_params=params(4),
        name="join_parts",
    )(*parts)


def ordered_sum_kernel(count, order, *refs):
    stage = refs[-1]
    for i in range(count):
        stage[order[i]] = refs[i][...]
    total = stage[0]
    for i in range(1, count):
        total = total + stage[i]
    refs[count][...] = total


def ordered_sum(order, terms):
    count = len(terms)
    return pl.pallas_call(
        functools.partial(ordered_sum_kernel, count),
        out_shape=jax.ShapeDtypeStruct(terms[0].shape, F32),
        in_specs=[SMEM] + [VMEM] * count,
        out_specs=VMEM,
        scratch_shapes=[pltpu.VMEM((count,) + terms[0].shape, F32)],
        compiler_params=params(4),
        name="sum_gains",
    )(order, *terms)


def place_kernel(meta, *refs):
    heads, out_ref = refs[:-1], refs[-1]
    mine = meta[0] > 0
    for i, ref in enumerate(heads):
        at = pl.multiple_of(meta[1 + i] * HD, HD)
        out_ref[:, :, pl.ds(at, HD)] = jnp.where(mine, ref[...], jnp.zeros_like(ref[...]))


def place(meta, heads):
    depth, rows, _ = heads[0].shape
    return pl.pallas_call(
        place_kernel,
        out_shape=jax.ShapeDtypeStruct((depth, rows, HD * len(heads)), BF),
        in_specs=[SMEM] + [VMEM] * len(heads),
        out_specs=VMEM,
        compiler_params=params(8),
        name="place_prompt_grad",
    )(meta, *heads)


def pair_sum(value, axis, size):
    step = 1
    while step < size:
        value = value + lax.ppermute(value, axis, [(i, i ^ step) for i in range(size)])
        step *= 2
    return value


def local(
    n_dp, n_group, queries, resp_keys, resp_values, prompt_cache, owners, lengths, q_gain, k_gain, grad_out
):
    q, g = queries[0, 0], grad_out[0, 0]
    k, v = resp_keys[0, 0], resp_values[0, 0]
    cache = prompt_cache[0, 0]
    owner = owners[0]
    live_len = lengths[0, 0]
    me = lax.axis_index("group")
    kv_heads = k.shape[1] // HD
    depth, p_rows, _ = cache.shape
    direct = n_group == kv_heads

    def shift(x, s):
        return lax.ppermute(x, "group", [(i, (i + s) % n_group) for i in range(n_group)])

    gain_col = q_gain[:, None]
    gain_row = k_gain[None, :]
    if direct:
        order = jnp.stack([(me - s) % n_group for s in range(n_group)]).astype(jnp.int32)
    else:
        order = jnp.arange(kv_heads, dtype=jnp.int32)
    meta = jnp.concatenate([order, live_len[None]])
    q, g, k, v = [pltpu.with_memory_space_constraint(x, pltpu.HBM) for x in (q, g, k, v)]
    kept = prepare(meta, q, g, k, v, gain_col, gain_row, kv_heads)
    if direct:
        blocks = cut(order, pltpu.with_memory_space_constraint(cache, pltpu.HBM), kv_heads)
        got = [blocks[0]] + [shift(blocks[s], -s) for s in range(1, n_group)]
        got[1], kept[0][2] = lax.optimization_barrier((got[1], kept[0][2]))
        mine = pick(jnp.reshape((owner - me) % n_group, (1,)).astype(jnp.int32), got)
        prompts = [mine] + [shift(mine, s) for s in range(1, n_group)]
    else:
        cache = lax.psum(jnp.where(me == owner, cache, jnp.zeros_like(cache)), "group")
        prompts = cut(order, cache, kv_heads)

    acc = jnp.zeros((2, HD), F32)
    parts, backs, buffers = [], [], ()
    for s, prompt in enumerate(prompts):
        last = s == kv_heads - 1
        if last and direct:
            prompt, backs[0] = lax.optimization_barrier((prompt, backs[0]))
        if last:
            part, acc, *results = first_half(prompt, kept[s], gain_col, acc)
        else:
            part, acc, buffers = whole_head(
                s, meta, prompt, kept[s], gain_col, gain_row, acc, buffers, q.shape[1], k.shape[1]
            )
        parts.append(part)
        if direct and s > 0:
            backs.append(shift(part, -s))
    buffers = list(second_half(kv_heads - 1, meta, kept[-1], gain_col, gain_row, results, buffers))

    mine_flag = (me == owner).astype(jnp.int32)
    if direct:
        backs[-1], buffers[2] = lax.optimization_barrier((backs[-1], buffers[2]))
        total = join([parts[0]] + backs)
        gains = ordered_sum(order, [acc] + [shift(acc, s) for s in range(1, n_group)])
        total, gains = lax.optimization_barrier((total, gains))
        heads = [total] + [shift(total, s) for s in range(1, n_group)]
        placed = place(jnp.concatenate([mine_flag[None], order]), heads)
    else:
        total = lax.psum(jnp.concatenate(parts, axis=-1).astype(F32), "group").astype(BF)
        placed = jnp.where(mine_flag > 0, total, jnp.zeros((), BF))
        gains = pair_sum(acc, "group", n_group)
    gains = pair_sum(gains, "dp", n_dp)
    attended, d_query, d_key, d_value = buffers
    return (
        attended[None, None],
        d_query[None, None],
        d_key[None, None],
        d_value[None, None],
        placed[None, None],
        gains,
    )


def solution(mesh):
    in_specs = (
        P("dp", "group", None, None),
        P("dp", "group", None, None),
        P("dp", "group", None, None),
        P("dp", "group", None, None, None),
        P("dp"),
        P("dp", "group"),
        P(),
        P(),
        P("dp", "group", None, None),
    )
    out_specs = (
        P("dp", "group", None, None),
        P("dp", "group", None, None),
        P("dp", "group", None, None),
        P("dp", "group", None, None),
        P("dp", "group", None, None, None),
        P(),
    )
    body = functools.partial(local, mesh.shape["dp"], mesh.shape["group"])
    return jax.shard_map(body, mesh=mesh, in_specs=in_specs, out_specs=out_specs, check_vma=False)
```

```python
import functools

import jax
import jax.numpy as jnp
from jax import lax
from jax.experimental import pallas as pl
from jax.experimental.pallas import tpu as pltpu
from jax.sharding import PartitionSpec as P

HD = 128
EPS = 1e-06
LOG2E = 1.4426950408889634
BF = jnp.bfloat16
F32 = jnp.float32


def dot_nn(a, b):
    return lax.dot_general(a, b, (((1,), (0,)), ((), ())), preferred_element_type=F32)


def dot_nt(a, b):
    return lax.dot_general(a, b, (((1,), (1,)), ((), ())), preferred_element_type=F32)


VMEM = pl.BlockSpec(memory_space=pltpu.VMEM)
SMEM = pl.BlockSpec(memory_space=pltpu.SMEM)
HBM = pl.BlockSpec(memory_space=pltpu.HBM)


SHORT = pl.CostEstimate(flops=0, bytes_accessed=0, transcendentals=0)


def params(mib):
    return pltpu.CompilerParams(vmem_limit_bytes=mib * 2**20)


def cut_kernel(cache_ref, *rest):
    outs, sems = rest[:-1], rest[-1]
    copies = []
    for i, out in enumerate(outs):
        copy = pltpu.make_async_copy(cache_ref.at[:, :, i * HD : (i + 1) * HD], out, sems.at[i])
        copy.start()
        copies.append(copy)
    for copy in copies:
        copy.wait()


def cut(cache, count):
    depth, rows, _ = cache.shape
    return pl.pallas_call(
        cut_kernel,
        out_shape=[jax.ShapeDtypeStruct((depth, rows, HD), BF)] * count,
        in_specs=[HBM],
        out_specs=[VMEM] * count,
        scratch_shapes=[pltpu.SemaphoreType.DMA((count,))],
        compiler_params=params(4),
        cost_estimate=SHORT,
        name="cut_prompt",
    )(cache)


def prepare_kernel(heads, share, rows, width, meta, q_in, g_in, k_in, v_in, gain_ref, kg_ref, *rest):
    outs, (q_buf, g_buf, k_buf, v_buf, sems) = rest[:-5], rest[-5:]
    live_len = meta[0]
    scale = HD ** (-0.5)
    wide = share * HD
    copies = []
    for s, head in enumerate(heads):
        group = []
        for j, (src, buf, size) in enumerate(
            ((q_in, q_buf, wide), (k_in, k_buf, HD), (g_in, g_buf, wide), (v_in, v_buf, HD))
        ):
            src = src.at[:, head * size : (head + 1) * size]
            copy = pltpu.make_async_copy(src, buf.at[s], sems.at[s, j])
            copy.start()
            group.append(copy)
        copies.append(group)
    q_gain = gain_ref[...]
    k_gain = kg_ref[...]
    for s in range(len(heads)):
        low_ref, high_ref, key_ref = outs[s * 3 : (s + 1) * 3]
        for copy in copies[s]:
            copy.wait()
        q_t = jnp.concatenate([q_buf[s, :, i * HD : (i + 1) * HD] for i in range(share)], axis=0).T
        g_t = jnp.concatenate([g_buf[s, :, i * HD : (i + 1) * HD] for i in range(share)], axis=0).T
        low_ref[:HD, :] = q_t
        raw_k = k_buf[s].astype(F32)
        k_inv = lax.rsqrt(jnp.mean(raw_k * raw_k, axis=-1, keepdims=True) + EPS)
        k_unit = raw_k * k_inv
        k_hat = (k_unit * k_gain).astype(BF)
        key_ref[:, :HD] = k_unit
        key_ref[:, HD : 2 * HD] = jnp.broadcast_to(k_inv, (rows, HD))
        key_ref[:, 2 * HD :] = k_hat.astype(F32)
        r_val = v_buf[s]
        r_val_t = r_val.T
        for start in range(0, share * rows, width):
            cols = slice(start, start + width)
            token = (lax.broadcasted_iota(jnp.int32, (1, width), 1) + start) % rows
            raw_q = q_t[:, cols].astype(F32)
            q_inv = lax.rsqrt(jnp.mean(raw_q * raw_q, axis=0, keepdims=True) + EPS)
            q_hat = (raw_q * q_inv * q_gain).astype(BF)
            d_o = jnp.where(token < live_len, g_t[:, cols].astype(F32), 0.0).astype(BF)
            low_ref[HD : 2 * HD, cols] = d_o
            causal = lax.broadcasted_iota(jnp.int32, (rows, width), 0) <= token
            e_r = jnp.where(causal, jnp.exp2(dot_nn(k_hat, q_hat) * (scale * LOG2E)), 0.0)
            eb_r = e_r.astype(BF)
            low_ref[2 * HD :, cols] = eb_r
            high_ref[:HD, cols] = dot_nn(r_val_t, eb_r)
            high_ref[HD : HD + rows, cols] = dot_nn(r_val, d_o)
            high_ref[HD + rows : HD + rows + 1, cols] = q_inv
            high_ref[HD + rows + 1 : HD + rows + 2, cols] = jnp.sum(e_r, axis=0, keepdims=True)


def prepare(heads, meta, q, g, k, v, q_gain, k_gain):
    count = len(heads)
    rows, q_width = q.shape
    share = q_width // k.shape[1]
    total = share * rows
    each = [
        jax.ShapeDtypeStruct((2 * HD + rows, total), BF),
        jax.ShapeDtypeStruct((HD + rows + 8, total), F32),
        jax.ShapeDtypeStruct((rows, 3 * HD), F32),
    ]
    outs = pl.pallas_call(
        functools.partial(prepare_kernel, heads, share, rows, 2 * HD),
        out_shape=each * count,
        in_specs=[SMEM] + [HBM] * 4 + [VMEM] * 2,
        out_specs=[VMEM] * (3 * count),
        scratch_shapes=[
            pltpu.VMEM((count, rows, share * HD), BF),
            pltpu.VMEM((count, rows, share * HD), BF),
            pltpu.VMEM((count, rows, HD), BF),
            pltpu.VMEM((count, rows, HD), BF),
            pltpu.SemaphoreType.DMA((count, 4)),
        ],
        compiler_params=params(16),
        cost_estimate=SHORT,
        name="prepare_response",
    )(meta, q, g, k, v, q_gain, k_gain)
    return [list(outs[s * 3 : (s + 1) * 3]) for s in range(count)]


def head_kernel(
    width, meta, near_ref, far_ref, low_ref, high_ref, key_ref, gain_ref, acc_ref, part_ref, gacc_ref, store_ref
):
    rows = key_ref.shape[0]
    scale = HD ** (-0.5)
    flag = meta[1] > 0
    q_gain = gain_ref[...]
    p_key = jnp.where(flag, far_ref[0], near_ref[0])
    p_val = jnp.where(flag, far_ref[1], near_ref[1])
    k_hat_t = key_ref[:, 2 * HD :].astype(BF).T
    p_key_t = p_key.T
    p_val_t = p_val.T
    sums = None
    for start in range(0, low_ref.shape[1], width):
        cols = slice(start, start + width)
        q_inv = high_ref[HD + rows : HD + rows + 1, cols]
        q_unit = low_ref[:HD, cols].astype(F32) * q_inv
        q_hat = (q_unit * q_gain).astype(BF)
        d_ob = low_ref[HD : 2 * HD, cols]
        d_o = d_ob.astype(F32)
        e_p = jnp.exp2(dot_nn(p_key, q_hat) * (scale * LOG2E))
        row_sum = jnp.sum(e_p, axis=0, keepdims=True) + high_ref[HD + rows + 1 : HD + rows + 2, cols]
        inv_sum = 1.0 / row_sum
        eb_p = e_p.astype(BF)
        eb_r = low_ref[2 * HD :, cols]
        out = (dot_nn(p_val_t, eb_p) + high_ref[:HD, cols]) * inv_sum
        delta = jnp.sum(d_o * out, axis=0, keepdims=True)
        ds_p = (e_p * (dot_nn(p_val, d_ob) - delta)).astype(BF)
        ds_r = (eb_r.astype(F32) * (high_ref[HD : HD + rows, cols] - delta)).astype(BF)
        weight = inv_sum * scale
        q_w = (q_hat.astype(F32) * weight).astype(BF)
        d_ow = (d_o * inv_sum).astype(BF)
        d_qhat = (dot_nn(p_key_t, ds_p) + dot_nn(k_hat_t, ds_r)) * weight
        store_ref[:HD, cols] = d_qhat
        store_ref[HD : 2 * HD, cols] = out
        store_ref[2 * HD : 3 * HD, cols] = q_unit
        store_ref[3 * HD : 3 * HD + 1, cols] = q_inv
        terms = (
            dot_nt(ds_p, q_w),
            dot_nt(eb_p, d_ow),
            dot_nt(ds_r, q_w),
            dot_nt(eb_r, d_ow),
            d_qhat * q_unit,
        )
        sums = terms if sums is None else [a + b for a, b in zip(sums, terms)]
    d_kp, d_vp, d_kr, d_vr, q_term = sums
    part_ref[0] = d_kp.astype(BF)
    part_ref[1] = d_vp.astype(BF)
    base = 3 * HD + 8
    store_ref[base:, :HD] = d_kr
    store_ref[base:, HD : 2 * HD] = d_vr
    store_ref[base:, 2 * HD : 4 * HD] = key_ref[:, : 2 * HD]
    folded = q_term[:, :HD]
    for start in range(HD, width, HD):
        folded = folded + q_term[:, start : start + HD]
    gacc_ref[0:1, :] = acc_ref[0:1, :] + jnp.sum(folded.T, axis=0, keepdims=True)
    gacc_ref[1:2, :] = acc_ref[1:2, :] + jnp.sum(d_kr * key_ref[:, :HD], axis=0, keepdims=True)


def one_head(meta, near, far, kept, q_gain, acc):
    rows = kept[2].shape[0]
    total = kept[0].shape[1]
    return pl.pallas_call(
        functools.partial(head_kernel, 2 * HD),
        out_shape=[
            jax.ShapeDtypeStruct(near.shape, BF),
            jax.ShapeDtypeStruct(acc.shape, F32),
            jax.ShapeDtypeStruct((3 * HD + 8 + rows, total), F32),
        ],
        in_specs=[SMEM] + [VMEM] * 7,
        out_specs=[VMEM] * 3,
        compiler_params=params(16),
        cost_estimate=SHORT,
        name="attend_head",
    )(meta, near, far, *kept, q_gain, acc)


def settle_kernel(heads, rows, width, meta, gain_ref, kg_ref, *rest):
    stores = rest[: len(heads)]
    outs, bufs, sems = rest[-9:-5], rest[-5:-1], rest[-1]
    live_len = meta[0]
    q_gain = gain_ref[...]
    k_gain = kg_ref[...]
    base = 3 * HD + 8
    copies = []
    for s, (head, store_ref) in enumerate(zip(heads, stores)):
        a_buf, q_buf, k_buf, v_buf = [buf.at[s] for buf in bufs]
        total = store_ref.shape[1]
        share = total // rows

        def send(j, buf):
            size = buf.shape[1]
            out = outs[j].at[:, head * size : (head + 1) * size]
            copy = pltpu.make_async_copy(buf, out, sems.at[s, j])
            copy.start()
            copies.append(copy)

        att = store_ref[HD : 2 * HD, :].astype(BF).T
        live = lax.broadcasted_iota(jnp.int32, (rows, HD), 0) < live_len
        for i in range(share):
            block = att[i * rows : (i + 1) * rows, :].astype(F32)
            a_buf[:, i * HD : (i + 1) * HD] = jnp.where(live, block, 0.0).astype(BF)
        send(0, a_buf)
        v_buf[...] = store_ref[base:, HD : 2 * HD].astype(BF)
        send(3, v_buf)
        k_unit = store_ref[base:, 2 * HD : 3 * HD]
        k_inv = store_ref[base:, 3 * HD : 4 * HD]
        up_k = store_ref[base:, :HD] * k_gain
        mean_k = jnp.mean(up_k * k_unit, axis=-1, keepdims=True)
        k_buf[...] = (k_inv * (up_k - k_unit * mean_k)).astype(BF)
        send(2, k_buf)
        parts = []
        for start in range(0, total, width):
            cols = slice(start, start + width)
            q_unit = store_ref[2 * HD : 3 * HD, cols]
            up = store_ref[:HD, cols] * q_gain
            mean = jnp.mean(up * q_unit, axis=0, keepdims=True)
            parts.append((store_ref[3 * HD : 3 * HD + 1, cols] * (up - q_unit * mean)).astype(BF))
        d_q = jnp.concatenate(parts, axis=1).T
        for i in range(share):
            q_buf[:, i * HD : (i + 1) * HD] = d_q[i * rows : (i + 1) * rows, :]
        send(1, q_buf)
    for copy in copies:
        copy.wait()


def settle(heads, meta, q_gain, k_gain, stores, buffers, q_width, k_width):
    total = stores[0].shape[1]
    rows = stores[0].shape[0] - 3 * HD - 8
    count = len(heads)
    wide = total // rows * HD
    return pl.pallas_call(
        functools.partial(settle_kernel, heads, rows, 2 * HD),
        out_shape=[jax.ShapeDtypeStruct((rows, w), BF) for w in (q_width, q_width, k_width, k_width)],
        in_specs=[SMEM] + [VMEM] * (2 + count) + [HBM] * len(buffers),
        out_specs=[HBM] * 4,
        scratch_shapes=[pltpu.VMEM((count, rows, w), BF) for w in (wide, wide, HD, HD)]
        + [pltpu.SemaphoreType.DMA((count, 4))],
        input_output_aliases={3 + count + i: i for i in range(len(buffers))},
        compiler_params=params(16),
        cost_estimate=SHORT,
        name="settle_heads",
    )(meta, q_gain, k_gain, *stores, *buffers)


def join(a, b):
    return (a.astype(F32) + b.astype(F32)).astype(BF)


def place_kernel(meta, *refs):
    ins, out_ref = refs[:-1], refs[-1]
    for i in range(len(ins) // 2):
        near, far = ins[2 * i][...], ins[2 * i + 1][...]
        block = jnp.where(meta[1] > 0, far, near)
        out_ref[:, :, i * HD : (i + 1) * HD] = jnp.where(meta[2] > 0, block, jnp.zeros_like(block))


def place(meta, pairs):
    depth, rows, _ = pairs[0][0].shape
    return pl.pallas_call(
        place_kernel,
        out_shape=jax.ShapeDtypeStruct((depth, rows, HD * len(pairs)), BF),
        in_specs=[SMEM] + [VMEM] * (2 * len(pairs)),
        out_specs=VMEM,
        compiler_params=params(8),
        cost_estimate=SHORT,
        name="place_prompt_grad",
    )(meta, *[x for pair in pairs for x in pair])


def after(x, *others):
    return lax.optimization_barrier((x,) + others)[0]


def pair_sum(value, axis, size):
    step = 1
    while step < size:
        value = value + lax.ppermute(value, axis, [(i, i ^ step) for i in range(size)])
        step *= 2
    return value


def local(
    n_dp, n_group, queries, resp_keys, resp_values, prompt_cache, owners, lengths, q_gain, k_gain, grad_out
):
    q, g = queries[0, 0], grad_out[0, 0]
    k, v = resp_keys[0, 0], resp_values[0, 0]
    cache = prompt_cache[0, 0]
    owner = owners[0]
    live_len = lengths[0, 0]
    me = lax.axis_index("group")
    kv_heads = k.shape[1] // HD
    depth, p_rows, _ = cache.shape
    q, g, k, v = [pltpu.with_memory_space_constraint(x, pltpu.HBM) for x in (q, g, k, v)]
    gain_col = q_gain[:, None]
    gain_row = k_gain[None, :]
    line = n_group == 4
    at_end = (me == 0) | (me == n_group - 1)
    far_flag = (at_end & (me != owner) if line else jnp.zeros((), bool)).astype(jnp.int32)
    meta = jnp.stack([live_len, far_flag])
    half = max(kv_heads // 2, 1)

    def prepared(low, high, order):
        return prepare(tuple(range(low, high)), order, q, g, k, v, gain_col, gain_row)

    kept = prepared(0, half, meta)

    def inward(x):
        return lax.ppermute(x, "group", [(0, 1), (3, 2)])

    def across(x):
        return lax.ppermute(x, "group", [(1, 2), (2, 1)])

    def outward(x):
        return lax.ppermute(x, "group", [(1, 0), (2, 3)])

    acc = jnp.zeros((2, HD), F32)
    mine_flag = (me == owner).astype(jnp.int32)
    heads = range(kv_heads)

    def attend(s, near, far, acc):
        return one_head(meta, near, far, kept[s], gain_col, acc)

    def settled(low, high, stores, buffers):
        return settle(
            tuple(range(low, high)), meta, gain_col, gain_row, stores[low:high], buffers, q.shape[1], k.shape[1]
        )

    if line:
        last = kv_heads - 1
        blocks = cut(pltpu.with_memory_space_constraint(cache, pltpu.HBM), kv_heads)
        from_end = ((me == 1) & (owner == 0)) | ((me == 2) & (owner == 3))
        from_side = ((me == 1) & (owner >= 2)) | ((me == 2) & (owner <= 1))
        sent = [inward(b) for b in blocks]
        sides, nears, mark = [], [], [kept[0][1]]

        def take_side(s, *waits):
            got = after(sent[s], *mark, *waits)
            sides.append(jnp.where(from_end, got, blocks[s]))
            mark[:] = sides[-1:]

        def take_near(s):
            got = after(across(sides[s]), *mark)
            nears.append(jnp.where(from_side, got, sides[s]))
            mark[:] = nears[-1:]

        for s in heads:
            if s == half:
                kept += prepared(half, kv_heads, after(meta, *mark))
            take_side(s, *([kept[half][1]] if s == half else []))
            if s >= 2:
                take_near(s - 2)
        for s in heads[len(nears) :]:
            take_near(s)
        fars = [outward(y) for y in nears]
        fars[0] = after(fars[0], nears[last])
        for s in range(1, last):
            fars[s] = after(fars[s], fars[s + 1])
        parts, stores, firsts = [], [], []
        for s in heads:
            near = nears[s]
            if s >= 2:
                firsts.append(join(parts[s - 2], inward(parts[s - 2])))
                near = after(near, firsts[s - 2])
            part, acc, store = attend(s, near, fars[s], acc)
            parts.append(part)
            stores.append(store)
        totals, lasts = [], []

        def take_total(s, *waits):
            totals.append(join(firsts[s], after(across(firsts[s]), *totals[-1:], *waits)))
            lasts.append(outward(totals[s]))

        for s in heads[len(firsts) :]:
            take_total(s - 2)
            firsts.append(join(parts[s], after(inward(parts[s]), firsts[-1], totals[-1])))
        gains = after(acc, firsts[last - 1])
        gains = gains + lax.ppermute(gains, "group", [(i, i ^ 1) for i in range(n_group)])
        gains = after(gains, firsts[last])
        gains = gains + lax.ppermute(gains, "group", [(i, i ^ 2) for i in range(n_group)])
        half_stores = [after(x, firsts[last]) for x in stores[:half]]
        buffers = settled(0, half, half_stores, ())
        take_total(last - 1, buffers[2])
        take_total(last, gains, *lasts[: last - 1])
        rest_stores = [after(x, totals[last]) for x in stores[half:]]
        buffers = settled(half, kv_heads, stores[:half] + rest_stores, buffers)
        lasts[last] = after(lasts[last], buffers[2])
        placed = place(
            jnp.stack([live_len, at_end.astype(jnp.int32), mine_flag]), list(zip(totals, lasts))
        )
        gains = pair_sum(after(gains, totals[last]), "dp", n_dp)
    else:
        kept += prepared(half, kv_heads, meta)
        cache = lax.psum(jnp.where(me == owner, cache, jnp.zeros_like(cache)), "group")
        prompts = cut(cache, kv_heads)
        parts, stores = [], []
        for s in heads:
            part, acc, store = attend(s, prompts[s], prompts[s], acc)
            parts.append(part)
            stores.append(store)
        buffers = settled(0, kv_heads, stores, ())
        total = lax.psum(jnp.concatenate(parts, axis=-1).astype(F32), "group").astype(BF)
        placed = jnp.where(mine_flag > 0, total, jnp.zeros((), BF))
        gains = pair_sum(pair_sum(acc, "group", n_group), "dp", n_dp)
    attended, d_query, d_key, d_value = buffers
    return (
        attended[None, None],
        d_query[None, None],
        d_key[None, None],
        d_value[None, None],
        placed[None, None],
        gains,
    )


def solution(mesh):
    in_specs = (
        P("dp", "group", None, None),
        P("dp", "group", None, None),
        P("dp", "group", None, None),
        P("dp", "group", None, None, None),
        P("dp"),
        P("dp", "group"),
        P(),
        P(),
        P("dp", "group", None, None),
    )
    out_specs = (
        P("dp", "group", None, None),
        P("dp", "group", None, None),
        P("dp", "group", None, None),
        P("dp", "group", None, None),
        P("dp", "group", None, None, None),
        P(),
    )
    body = functools.partial(local, mesh.shape["dp"], mesh.shape["group"])
    return jax.shard_map(body, mesh=mesh, in_specs=in_specs, out_specs=out_specs, check_vma=False)
```

```python
import functools

import jax
import jax.numpy as jnp
from jax import lax
from jax.experimental import pallas as pl
from jax.experimental.pallas import tpu as pltpu
from jax.sharding import PartitionSpec as P

HD = 128
EPS = 1e-06
LOG2E = 1.4426950408889634
BF = jnp.bfloat16
F32 = jnp.float32


def dot_nn(a, b):
    return lax.dot_general(a, b, (((1,), (0,)), ((), ())), preferred_element_type=F32)


def dot_nt(a, b):
    return lax.dot_general(a, b, (((1,), (1,)), ((), ())), preferred_element_type=F32)


VMEM = pl.BlockSpec(memory_space=pltpu.VMEM)
SMEM = pl.BlockSpec(memory_space=pltpu.SMEM)
HBM = pl.BlockSpec(memory_space=pltpu.HBM)


def params(mib):
    return pltpu.CompilerParams(vmem_limit_bytes=mib * 2**20)


def cut_kernel(order, cache_ref, *rest):
    outs, sems = rest[:-1], rest[-1]
    copies = []
    for i, out in enumerate(outs):
        at = pl.multiple_of(order[i] * HD, HD)
        copy = pltpu.make_async_copy(cache_ref.at[:, :, pl.ds(at, HD)], out, sems.at[i])
        copy.start()
        copies.append(copy)
    for copy in copies:
        copy.wait()


def cut(order, cache, count):
    depth, rows, _ = cache.shape
    return pl.pallas_call(
        cut_kernel,
        out_shape=[jax.ShapeDtypeStruct((depth, rows, HD), BF)] * count,
        in_specs=[SMEM, HBM],
        out_specs=[VMEM] * count,
        scratch_shapes=[pltpu.SemaphoreType.DMA((count,))],
        compiler_params=params(4),
        name="cut_prompt",
    )(order, cache)


def pick_kernel(which, *refs):
    picked = refs[0][...]
    for i in range(1, len(refs) - 1):
        picked = jnp.where(which[0] == i, refs[i][...], picked)
    refs[-1][...] = picked


def pick(which, blocks):
    return pl.pallas_call(
        pick_kernel,
        out_shape=jax.ShapeDtypeStruct(blocks[0].shape, BF),
        in_specs=[SMEM] + [VMEM] * len(blocks),
        out_specs=VMEM,
        compiler_params=params(4),
        name="pick_owner",
    )(which, *blocks)


KEPT = 8


def prepare_kernel(count, share, rows, width, meta, q_in, g_in, k_in, v_in, gain_ref, kg_ref, *rest):
    outs, (q_buf, g_buf, k_buf, v_buf, sems) = rest[:-5], rest[-5:]
    live_len = meta[count]
    scale = HD ** (-0.5)
    wide = share * HD
    copies = []
    for s in range(count):
        group = []
        for j, (src, buf, size) in enumerate(
            ((q_in, q_buf, wide), (k_in, k_buf, HD), (g_in, g_buf, wide), (v_in, v_buf, HD))
        ):
            at = pl.multiple_of(meta[s] * size, size)
            copy = pltpu.make_async_copy(src.at[:, pl.ds(at, size)], buf.at[s], sems.at[s, j])
            copy.start()
            group.append(copy)
        copies.append(group)
    q_gain = gain_ref[...]
    k_gain = kg_ref[...]
    for s in range(count):
        qt_ref, gt_ref, row_ref, er_ref, ot_ref, dp_ref, kh_ref, ku_ref = outs[s * KEPT : (s + 1) * KEPT]
        for copy in copies[s]:
            copy.wait()
        q_t = jnp.concatenate([q_buf[s, :, i * HD : (i + 1) * HD] for i in range(share)], axis=0).T
        g_t = jnp.concatenate([g_buf[s, :, i * HD : (i + 1) * HD] for i in range(share)], axis=0).T
        qt_ref[...] = q_t
        raw_k = k_buf[s].astype(F32)
        k_inv = lax.rsqrt(jnp.mean(raw_k * raw_k, axis=-1, keepdims=True) + EPS)
        k_unit = raw_k * k_inv
        k_hat = (k_unit * k_gain).astype(BF)
        kh_ref[...] = k_hat
        ku_ref[:, :HD] = k_unit
        ku_ref[:, HD:] = jnp.broadcast_to(k_inv, (rows, HD))
        r_val = v_buf[s]
        r_val_t = r_val.T
        for start in range(0, share * rows, width):
            cols = slice(start, start + width)
            token = (lax.broadcasted_iota(jnp.int32, (1, width), 1) + start) % rows
            raw_q = q_t[:, cols].astype(F32)
            q_inv = lax.rsqrt(jnp.mean(raw_q * raw_q, axis=0, keepdims=True) + EPS)
            q_hat = (raw_q * q_inv * q_gain).astype(BF)
            d_o = jnp.where(token < live_len, g_t[:, cols].astype(F32), 0.0).astype(BF)
            gt_ref[:, cols] = d_o
            causal = lax.broadcasted_iota(jnp.int32, (rows, width), 0) <= token
            e_r = jnp.where(causal, jnp.exp2(dot_nn(k_hat, q_hat) * (scale * LOG2E)), 0.0)
            eb_r = e_r.astype(BF)
            er_ref[:, cols] = eb_r
            ot_ref[:, cols] = dot_nn(r_val_t, eb_r)
            dp_ref[:, cols] = dot_nn(r_val, d_o)
            row_ref[0:1, cols] = q_inv
            row_ref[1:2, cols] = jnp.sum(e_r, axis=0, keepdims=True)


def prepare(meta, q, g, k, v, q_gain, k_gain, count):
    rows, q_width = q.shape
    share = q_width // k.shape[1]
    total = share * rows
    each = [
        jax.ShapeDtypeStruct((HD, total), BF),
        jax.ShapeDtypeStruct((HD, total), BF),
        jax.ShapeDtypeStruct((8, total), F32),
        jax.ShapeDtypeStruct((rows, total), BF),
        jax.ShapeDtypeStruct((HD, total), F32),
        jax.ShapeDtypeStruct((rows, total), F32),
        jax.ShapeDtypeStruct((rows, HD), BF),
        jax.ShapeDtypeStruct((rows, 2 * HD), F32),
    ]
    outs = pl.pallas_call(
        functools.partial(prepare_kernel, count, share, rows, 2 * HD),
        out_shape=each * count,
        in_specs=[SMEM] + [HBM] * 4 + [VMEM] * 2,
        out_specs=[VMEM] * (KEPT * count),
        scratch_shapes=[
            pltpu.VMEM((count, rows, share * HD), BF),
            pltpu.VMEM((count, rows, share * HD), BF),
            pltpu.VMEM((count, rows, HD), BF),
            pltpu.VMEM((count, rows, HD), BF),
            pltpu.SemaphoreType.DMA((count, 4)),
        ],
        compiler_params=params(16),
        cost_estimate=pl.CostEstimate(
            flops=6 * count * total * rows * HD,
            bytes_accessed=5 * rows * q_width * 2,
            transcendentals=count * total * rows,
        ),
        name="prepare_response",
    )(meta, q, g, k, v, q_gain, k_gain)
    return [list(outs[s * KEPT : (s + 1) * KEPT]) for s in range(count)]


def attend(width, pr_ref, kept, q_gain, acc_ref, part_ref, at_ref, dq_ref, gacc_ref):
    qt_ref, gt_ref, row_ref, er_ref, ot_ref, dp_ref, kh_ref, ku_ref = kept
    scale = HD ** (-0.5)
    p_key = pr_ref[0]
    p_val = pr_ref[1]
    k_hat_t = kh_ref[...].T
    p_key_t = p_key.T
    p_val_t = p_val.T
    sums = None
    for start in range(0, qt_ref.shape[1], width):
        cols = slice(start, start + width)
        q_unit = qt_ref[:, cols].astype(F32) * row_ref[0:1, cols]
        q_hat = (q_unit * q_gain).astype(BF)
        d_ob = gt_ref[:, cols]
        d_o = d_ob.astype(F32)
        e_p = jnp.exp2(dot_nn(p_key, q_hat) * (scale * LOG2E))
        inv_sum = 1.0 / (jnp.sum(e_p, axis=0, keepdims=True) + row_ref[1:2, cols])
        eb_p = e_p.astype(BF)
        eb_r = er_ref[:, cols]
        out = (dot_nn(p_val_t, eb_p) + ot_ref[:, cols]) * inv_sum
        at_ref[:, cols] = out.astype(BF)
        delta = jnp.sum(d_o * out, axis=0, keepdims=True)
        ds_p = (e_p * (dot_nn(p_val, d_ob) - delta)).astype(BF)
        ds_r = (eb_r.astype(F32) * (dp_ref[:, cols] - delta)).astype(BF)
        weight = inv_sum * scale
        q_w = (q_hat.astype(F32) * weight).astype(BF)
        d_ow = (d_o * inv_sum).astype(BF)
        d_qhat = (dot_nn(p_key_t, ds_p) + dot_nn(k_hat_t, ds_r)) * weight
        dq_ref[:, cols] = d_qhat
        terms = (
            dot_nt(ds_p, q_w),
            dot_nt(eb_p, d_ow),
            dot_nt(ds_r, q_w),
            dot_nt(eb_r, d_ow),
            d_qhat * q_unit,
        )
        sums = terms if sums is None else [a + b for a, b in zip(sums, terms)]
    d_kp, d_vp, d_kr, d_vr, q_term = sums
    part_ref[0] = d_kp.astype(BF)
    part_ref[1] = d_vp.astype(BF)
    folded = q_term[:, :HD]
    for start in range(HD, width, HD):
        folded = folded + q_term[:, start : start + HD]
    gacc_ref[0:1, :] = acc_ref[0:1, :] + jnp.sum(folded.T, axis=0, keepdims=True)
    gacc_ref[1:2, :] = acc_ref[1:2, :] + jnp.sum(d_kr * ku_ref[:, :HD], axis=0, keepdims=True)
    return d_kr, d_vr


def settle(width, head, live_len, kept, q_gain, k_gain, at_ref, dq_ref, d_kr, d_vr, outs, bufs, sems):
    qt_ref, row_ref, ku_ref = kept[0], kept[2], kept[7]
    a_buf, q_buf, k_buf, v_buf = bufs
    rows, wide = a_buf.shape
    share = wide // HD
    copies = []

    def send(j, buf):
        size = buf.shape[1]
        at = pl.multiple_of(head * size, size)
        copy = pltpu.make_async_copy(buf, outs[j].at[:, pl.ds(at, size)], sems.at[j])
        copy.start()
        copies.append(copy)

    att = at_ref[...].T
    live = lax.broadcasted_iota(jnp.int32, (rows, HD), 0) < live_len
    for i in range(share):
        block = att[i * rows : (i + 1) * rows, :].astype(F32)
        a_buf[:, i * HD : (i + 1) * HD] = jnp.where(live, block, 0.0).astype(BF)
    send(0, a_buf)
    v_buf[...] = d_vr.astype(BF)
    send(3, v_buf)
    k_unit = ku_ref[:, :HD]
    up_k = d_kr * k_gain
    mean_k = jnp.mean(up_k * k_unit, axis=-1, keepdims=True)
    k_buf[...] = (ku_ref[:, HD:] * (up_k - k_unit * mean_k)).astype(BF)
    send(2, k_buf)
    parts = []
    for start in range(0, share * rows, width):
        cols = slice(start, start + width)
        q_inv = row_ref[0:1, cols]
        q_unit = qt_ref[:, cols].astype(F32) * q_inv
        up = dq_ref[:, cols] * q_gain
        mean = jnp.mean(up * q_unit, axis=0, keepdims=True)
        parts.append((q_inv * (up - q_unit * mean)).astype(BF))
    d_q = jnp.concatenate(parts, axis=1).T
    for i in range(share):
        q_buf[:, i * HD : (i + 1) * HD] = d_q[i * rows : (i + 1) * rows, :]
    send(1, q_buf)
    for copy in copies:
        copy.wait()


def whole_kernel(s, width, meta, pr_ref, *rest):
    kept, (gain_ref, kg_ref, acc_ref) = rest[:KEPT], rest[KEPT : KEPT + 3]
    part_ref, gacc_ref, *rest = rest[-13:]
    outs, (at_ref, dq_ref), bufs, sems = rest[:4], rest[4:6], rest[6:10], rest[10]
    q_gain = gain_ref[...]
    d_kr, d_vr = attend(width, pr_ref, kept, q_gain, acc_ref, part_ref, at_ref, dq_ref, gacc_ref)
    live_len = meta[meta.shape[0] - 1]
    settle(width, meta[s], live_len, kept, q_gain, kg_ref[...], at_ref, dq_ref, d_kr, d_vr, outs, bufs, sems)


def first_kernel(width, pr_ref, *rest):
    kept, (gain_ref, acc_ref) = rest[:KEPT], rest[KEPT : KEPT + 2]
    part_ref, gacc_ref, at_ref, dq_ref, dkr_ref, dvr_ref = rest[-6:]
    d_kr, d_vr = attend(width, pr_ref, kept, gain_ref[...], acc_ref, part_ref, at_ref, dq_ref, gacc_ref)
    dkr_ref[...] = d_kr
    dvr_ref[...] = d_vr


def second_kernel(s, width, meta, *rest):
    kept, (gain_ref, kg_ref, at_ref, dq_ref, dkr_ref, dvr_ref) = rest[:KEPT], rest[KEPT : KEPT + 6]
    outs, bufs, sems = rest[-9:-5], rest[-5:-1], rest[-1]
    live_len = meta[meta.shape[0] - 1]
    settle(
        width, meta[s], live_len, kept, gain_ref[...], kg_ref[...], at_ref, dq_ref,
        dkr_ref[...], dvr_ref[...], outs, bufs, sems,
    )


def out_shapes(rows, q_width, k_width):
    widths = (q_width, q_width, k_width, k_width)
    return [jax.ShapeDtypeStruct((rows, w), BF) for w in widths]


def out_scratch(rows, share):
    widths = (share * HD, share * HD, HD, HD)
    return [pltpu.VMEM((rows, w), BF) for w in widths] + [pltpu.SemaphoreType.DMA((4,))]


def cost(prompt_rows, rows, total):
    return pl.CostEstimate(
        flops=(8 * prompt_rows + 4 * rows) * total * HD,
        bytes_accessed=2**20,
        transcendentals=total * prompt_rows,
    )


def whole_head(s, meta, prompt, kept, q_gain, k_gain, acc, buffers, q_width, k_width):
    total = kept[0].shape[1]
    rows = kept[3].shape[0]
    outs = pl.pallas_call(
        functools.partial(whole_kernel, s, 2 * HD),
        out_shape=[
            jax.ShapeDtypeStruct(prompt.shape, BF),
            jax.ShapeDtypeStruct(acc.shape, F32),
        ]
        + out_shapes(rows, q_width, k_width),
        in_specs=[SMEM] + [VMEM] * (4 + KEPT) + [HBM] * len(buffers),
        out_specs=[VMEM] * 2 + [HBM] * 4,
        scratch_shapes=[pltpu.VMEM((HD, total), BF), pltpu.VMEM((HD, total), F32)]
        + out_scratch(rows, total // rows),
        input_output_aliases={5 + KEPT + i: 2 + i for i in range(len(buffers))},
        compiler_params=params(16),
        cost_estimate=cost(prompt.shape[1], rows, total),
        name="attend_head",
    )(meta, prompt, *kept, q_gain, k_gain, acc, *buffers)
    return outs[0], outs[1], outs[2:]


def first_half(prompt, kept, q_gain, acc):
    total = kept[0].shape[1]
    rows = kept[3].shape[0]
    return pl.pallas_call(
        functools.partial(first_kernel, 2 * HD),
        out_shape=[
            jax.ShapeDtypeStruct(prompt.shape, BF),
            jax.ShapeDtypeStruct(acc.shape, F32),
            jax.ShapeDtypeStruct((HD, total), BF),
            jax.ShapeDtypeStruct((HD, total), F32),
            jax.ShapeDtypeStruct((rows, HD), F32),
            jax.ShapeDtypeStruct((rows, HD), F32),
        ],
        in_specs=[VMEM] * (3 + KEPT),
        out_specs=[VMEM] * 6,
        compiler_params=params(16),
        cost_estimate=cost(prompt.shape[1], rows, total),
        name="attend_last_head",
    )(prompt, *kept, q_gain, acc)


def second_half(s, meta, kept, q_gain, k_gain, results, buffers):
    total = kept[0].shape[1]
    rows = kept[3].shape[0]
    return pl.pallas_call(
        functools.partial(second_kernel, s, 2 * HD),
        out_shape=out_shapes(rows, buffers[0].shape[1], buffers[2].shape[1]),
        in_specs=[SMEM] + [VMEM] * (KEPT + 6) + [HBM] * 4,
        out_specs=[HBM] * 4,
        scratch_shapes=out_scratch(rows, total // rows),
        input_output_aliases={7 + KEPT + i: i for i in range(4)},
        compiler_params=params(16),
        cost_estimate=pl.CostEstimate(flops=0, bytes_accessed=2**20, transcendentals=0),
        name="settle_last_head",
    )(meta, *kept, q_gain, k_gain, *results, *buffers)


def join(a, b):
    return (a.astype(F32) + b.astype(F32)).astype(BF)


def place_kernel(meta, *refs):
    heads, out_ref = refs[:-1], refs[-1]
    mine = meta[0] > 0
    for i, ref in enumerate(heads):
        at = pl.multiple_of(meta[1 + i] * HD, HD)
        out_ref[:, :, pl.ds(at, HD)] = jnp.where(mine, ref[...], jnp.zeros_like(ref[...]))


def place(meta, heads):
    depth, rows, _ = heads[0].shape
    return pl.pallas_call(
        place_kernel,
        out_shape=jax.ShapeDtypeStruct((depth, rows, HD * len(heads)), BF),
        in_specs=[SMEM] + [VMEM] * len(heads),
        out_specs=VMEM,
        compiler_params=params(8),
        name="place_prompt_grad",
    )(meta, *heads)


def after(x, *others):
    return lax.optimization_barrier((x,) + others)[0]


def pair_sum(value, axis, size):
    step = 1
    while step < size:
        value = value + lax.ppermute(value, axis, [(i, i ^ step) for i in range(size)])
        step *= 2
    return value


def local(
    n_dp, n_group, queries, resp_keys, resp_values, prompt_cache, owners, lengths, q_gain, k_gain, grad_out
):
    q, g = queries[0, 0], grad_out[0, 0]
    k, v = resp_keys[0, 0], resp_values[0, 0]
    cache = prompt_cache[0, 0]
    owner = owners[0]
    live_len = lengths[0, 0]
    me = lax.axis_index("group")
    kv_heads = k.shape[1] // HD
    depth, p_rows, _ = cache.shape
    direct = n_group == kv_heads

    def shift(x, s):
        return lax.ppermute(x, "group", [(i, (i + s) % n_group) for i in range(n_group)])

    gain_col = q_gain[:, None]
    gain_row = k_gain[None, :]
    if direct:
        order = jnp.stack([(me - s) % n_group for s in range(n_group)]).astype(jnp.int32)
    else:
        order = jnp.arange(kv_heads, dtype=jnp.int32)
    meta = jnp.concatenate([order, live_len[None]])
    q, g, k, v = [pltpu.with_memory_space_constraint(x, pltpu.HBM) for x in (q, g, k, v)]
    kept = prepare(meta, q, g, k, v, gain_col, gain_row, kv_heads)
    if direct:
        blocks = cut(order, pltpu.with_memory_space_constraint(cache, pltpu.HBM), kv_heads)
        got = [blocks[0]] + [shift(blocks[s], -s) for s in range(1, n_group)]
        got[1], kept[0][2] = lax.optimization_barrier((got[1], kept[0][2]))
        mine = pick(jnp.reshape((owner - me) % n_group, (1,)).astype(jnp.int32), got)
        prompts = [mine]
        for s in range(1, n_group):
            prompts.append(shift(prompts[-1], 1))
    else:
        cache = lax.psum(jnp.where(me == owner, cache, jnp.zeros_like(cache)), "group")
        prompts = cut(order, cache, kv_heads)

    acc = jnp.zeros((2, HD), F32)
    parts, buffers, ring = [], (), None
    for s, prompt in enumerate(prompts):
        last = s == kv_heads - 1
        if last and ring is not None:
            prompt = after(prompt, ring)
        if last:
            part, acc, *results = first_half(prompt, kept[s], gain_col, acc)
        else:
            part, acc, buffers = whole_head(
                s, meta, prompt, kept[s], gain_col, gain_row, acc, buffers, q.shape[1], k.shape[1]
            )
        parts.append(part)
        if direct and s > 0:
            ring = part if s == 1 else join(part, shift(ring, 1))
    buffers = list(second_half(kv_heads - 1, meta, kept[-1], gain_col, gain_row, results, buffers))

    mine_flag = (me == owner).astype(jnp.int32)
    if direct:
        total = join(parts[0], after(shift(ring, 1), buffers[2]))
        gains = pair_sum(after(acc, ring), "group", n_group)
        total, gains = lax.optimization_barrier((total, gains))
        heads = [total] + [shift(total, s) for s in range(1, n_group)]
        placed = place(jnp.concatenate([mine_flag[None], order]), heads)
    else:
        total = lax.psum(jnp.concatenate(parts, axis=-1).astype(F32), "group").astype(BF)
        placed = jnp.where(mine_flag > 0, total, jnp.zeros((), BF))
        gains = pair_sum(acc, "group", n_group)
    gains = pair_sum(gains, "dp", n_dp)
    attended, d_query, d_key, d_value = buffers
    return (
        attended[None, None],
        d_query[None, None],
        d_key[None, None],
        d_value[None, None],
        placed[None, None],
        gains,
    )


def solution(mesh):
    in_specs = (
        P("dp", "group", None, None),
        P("dp", "group", None, None),
        P("dp", "group", None, None),
        P("dp", "group", None, None, None),
        P("dp"),
        P("dp", "group"),
        P(),
        P(),
        P("dp", "group", None, None),
    )
    out_specs = (
        P("dp", "group", None, None),
        P("dp", "group", None, None),
        P("dp", "group", None, None),
        P("dp", "group", None, None),
        P("dp", "group", None, None, None),
        P(),
    )
    body = functools.partial(local, mesh.shape["dp"], mesh.shape["group"])
    return jax.shard_map(body, mesh=mesh, in_specs=in_specs, out_specs=out_specs, check_vma=False)
```

```python
import functools

import jax
import jax.numpy as jnp
from jax import lax
from jax.experimental import pallas as pl
from jax.experimental.pallas import tpu as pltpu
from jax.sharding import PartitionSpec as P

HD = 128
EPS = 1e-06
LOG2E = 1.4426950408889634
BF = jnp.bfloat16
F32 = jnp.float32


def dot_nn(a, b):
    return lax.dot_general(a, b, (((1,), (0,)), ((), ())), preferred_element_type=F32)


def dot_nt(a, b):
    return lax.dot_general(a, b, (((1,), (1,)), ((), ())), preferred_element_type=F32)


VMEM = pl.BlockSpec(memory_space=pltpu.VMEM)
SMEM = pl.BlockSpec(memory_space=pltpu.SMEM)
HBM = pl.BlockSpec(memory_space=pltpu.HBM)


def params(mib):
    return pltpu.CompilerParams(vmem_limit_bytes=mib * 2**20)


def cut_kernel(order, cache_ref, *rest):
    outs, sems = rest[:-1], rest[-1]
    copies = []
    for i, out in enumerate(outs):
        at = pl.multiple_of(order[i] * HD, HD)
        copy = pltpu.make_async_copy(cache_ref.at[:, :, pl.ds(at, HD)], out, sems.at[i])
        copy.start()
        copies.append(copy)
    for copy in copies:
        copy.wait()


def cut(order, cache, count):
    depth, rows, _ = cache.shape
    return pl.pallas_call(
        cut_kernel,
        out_shape=[jax.ShapeDtypeStruct((depth, rows, HD), BF)] * count,
        in_specs=[SMEM, HBM],
        out_specs=[VMEM] * count,
        scratch_shapes=[pltpu.SemaphoreType.DMA((count,))],
        compiler_params=params(4),
        name="cut_prompt",
    )(order, cache)


def pick_kernel(which, *refs):
    picked = refs[0][...]
    for i in range(1, len(refs) - 1):
        picked = jnp.where(which[0] == i, refs[i][...], picked)
    refs[-1][...] = picked


def pick(which, blocks):
    return pl.pallas_call(
        pick_kernel,
        out_shape=jax.ShapeDtypeStruct(blocks[0].shape, BF),
        in_specs=[SMEM] + [VMEM] * len(blocks),
        out_specs=VMEM,
        compiler_params=params(4),
        name="pick_owner",
    )(which, *blocks)


KEPT = 8


def prepare_kernel(count, share, rows, width, meta, q_in, g_in, k_in, v_in, gain_ref, kg_ref, *rest):
    outs, (q_buf, g_buf, k_buf, v_buf, sems) = rest[:-5], rest[-5:]
    live_len = meta[count]
    scale = HD ** (-0.5)
    wide = share * HD
    copies = []
    for s in range(count):
        group = []
        for j, (src, buf, size) in enumerate(
            ((q_in, q_buf, wide), (k_in, k_buf, HD), (g_in, g_buf, wide), (v_in, v_buf, HD))
        ):
            at = pl.multiple_of(meta[s] * size, size)
            copy = pltpu.make_async_copy(src.at[:, pl.ds(at, size)], buf.at[s], sems.at[s, j])
            copy.start()
            group.append(copy)
        copies.append(group)
    q_gain = gain_ref[...]
    k_gain = kg_ref[...]
    for s in range(count):
        qt_ref, gt_ref, row_ref, er_ref, ot_ref, dp_ref, kh_ref, ku_ref = outs[s * KEPT : (s + 1) * KEPT]
        for copy in copies[s]:
            copy.wait()
        q_t = jnp.concatenate([q_buf[s, :, i * HD : (i + 1) * HD] for i in range(share)], axis=0).T
        g_t = jnp.concatenate([g_buf[s, :, i * HD : (i + 1) * HD] for i in range(share)], axis=0).T
        qt_ref[...] = q_t
        raw_k = k_buf[s].astype(F32)
        k_inv = lax.rsqrt(jnp.mean(raw_k * raw_k, axis=-1, keepdims=True) + EPS)
        k_unit = raw_k * k_inv
        k_hat = (k_unit * k_gain).astype(BF)
        kh_ref[...] = k_hat
        ku_ref[:, :HD] = k_unit
        ku_ref[:, HD:] = jnp.broadcast_to(k_inv, (rows, HD))
        r_val = v_buf[s]
        r_val_t = r_val.T
        for start in range(0, share * rows, width):
            cols = slice(start, start + width)
            token = (lax.broadcasted_iota(jnp.int32, (1, width), 1) + start) % rows
            raw_q = q_t[:, cols].astype(F32)
            q_inv = lax.rsqrt(jnp.mean(raw_q * raw_q, axis=0, keepdims=True) + EPS)
            q_hat = (raw_q * q_inv * q_gain).astype(BF)
            d_o = jnp.where(token < live_len, g_t[:, cols].astype(F32), 0.0).astype(BF)
            gt_ref[:, cols] = d_o
            causal = lax.broadcasted_iota(jnp.int32, (rows, width), 0) <= token
            e_r = jnp.where(causal, jnp.exp2(dot_nn(k_hat, q_hat) * (scale * LOG2E)), 0.0)
            eb_r = e_r.astype(BF)
            er_ref[:, cols] = eb_r
            ot_ref[:, cols] = dot_nn(r_val_t, eb_r)
            dp_ref[:, cols] = dot_nn(r_val, d_o)
            row_ref[0:1, cols] = q_inv
            row_ref[1:2, cols] = jnp.sum(e_r, axis=0, keepdims=True)


def prepare(meta, q, g, k, v, q_gain, k_gain, count):
    rows, q_width = q.shape
    share = q_width // k.shape[1]
    total = share * rows
    each = [
        jax.ShapeDtypeStruct((HD, total), BF),
        jax.ShapeDtypeStruct((HD, total), BF),
        jax.ShapeDtypeStruct((8, total), F32),
        jax.ShapeDtypeStruct((rows, total), BF),
        jax.ShapeDtypeStruct((HD, total), F32),
        jax.ShapeDtypeStruct((rows, total), F32),
        jax.ShapeDtypeStruct((rows, HD), BF),
        jax.ShapeDtypeStruct((rows, 2 * HD), F32),
    ]
    outs = pl.pallas_call(
        functools.partial(prepare_kernel, count, share, rows, 2 * HD),
        out_shape=each * count,
        in_specs=[SMEM] + [HBM] * 4 + [VMEM] * 2,
        out_specs=[VMEM] * (KEPT * count),
        scratch_shapes=[
            pltpu.VMEM((count, rows, share * HD), BF),
            pltpu.VMEM((count, rows, share * HD), BF),
            pltpu.VMEM((count, rows, HD), BF),
            pltpu.VMEM((count, rows, HD), BF),
            pltpu.SemaphoreType.DMA((count, 4)),
        ],
        compiler_params=params(16),
        cost_estimate=pl.CostEstimate(
            flops=6 * count * total * rows * HD,
            bytes_accessed=5 * rows * q_width * 2,
            transcendentals=count * total * rows,
        ),
        name="prepare_response",
    )(meta, q, g, k, v, q_gain, k_gain)
    return [list(outs[s * KEPT : (s + 1) * KEPT]) for s in range(count)]


def attend(width, pr_ref, kept, q_gain, acc_ref, part_ref, at_ref, dq_ref, gacc_ref):
    qt_ref, gt_ref, row_ref, er_ref, ot_ref, dp_ref, kh_ref, ku_ref = kept
    scale = HD ** (-0.5)
    p_key = pr_ref[0]
    p_val = pr_ref[1]
    k_hat_t = kh_ref[...].T
    p_key_t = p_key.T
    p_val_t = p_val.T
    sums = None
    for start in range(0, qt_ref.shape[1], width):
        cols = slice(start, start + width)
        q_unit = qt_ref[:, cols].astype(F32) * row_ref[0:1, cols]
        q_hat = (q_unit * q_gain).astype(BF)
        d_ob = gt_ref[:, cols]
        d_o = d_ob.astype(F32)
        e_p = jnp.exp2(dot_nn(p_key, q_hat) * (scale * LOG2E))
        inv_sum = 1.0 / (jnp.sum(e_p, axis=0, keepdims=True) + row_ref[1:2, cols])
        eb_p = e_p.astype(BF)
        eb_r = er_ref[:, cols]
        out = (dot_nn(p_val_t, eb_p) + ot_ref[:, cols]) * inv_sum
        at_ref[:, cols] = out.astype(BF)
        delta = jnp.sum(d_o * out, axis=0, keepdims=True)
        ds_p = (e_p * (dot_nn(p_val, d_ob) - delta)).astype(BF)
        ds_r = (eb_r.astype(F32) * (dp_ref[:, cols] - delta)).astype(BF)
        weight = inv_sum * scale
        q_w = (q_hat.astype(F32) * weight).astype(BF)
        d_ow = (d_o * inv_sum).astype(BF)
        d_qhat = (dot_nn(p_key_t, ds_p) + dot_nn(k_hat_t, ds_r)) * weight
        dq_ref[:, cols] = d_qhat
        terms = (
            dot_nt(ds_p, q_w),
            dot_nt(eb_p, d_ow),
            dot_nt(ds_r, q_w),
            dot_nt(eb_r, d_ow),
            d_qhat * q_unit,
        )
        sums = terms if sums is None else [a + b for a, b in zip(sums, terms)]
    d_kp, d_vp, d_kr, d_vr, q_term = sums
    part_ref[0] = d_kp.astype(BF)
    part_ref[1] = d_vp.astype(BF)
    folded = q_term[:, :HD]
    for start in range(HD, width, HD):
        folded = folded + q_term[:, start : start + HD]
    gacc_ref[0:1, :] = acc_ref[0:1, :] + jnp.sum(folded.T, axis=0, keepdims=True)
    gacc_ref[1:2, :] = acc_ref[1:2, :] + jnp.sum(d_kr * ku_ref[:, :HD], axis=0, keepdims=True)
    return d_kr, d_vr


def settle(width, head, live_len, kept, q_gain, k_gain, at_ref, dq_ref, d_kr, d_vr, outs, bufs, sems):
    qt_ref, row_ref, ku_ref = kept[0], kept[2], kept[7]
    a_buf, q_buf, k_buf, v_buf = bufs
    rows, wide = a_buf.shape
    share = wide // HD
    copies = []

    def send(j, buf):
        size = buf.shape[1]
        at = pl.multiple_of(head * size, size)
        copy = pltpu.make_async_copy(buf, outs[j].at[:, pl.ds(at, size)], sems.at[j])
        copy.start()
        copies.append(copy)

    att = at_ref[...].T
    live = lax.broadcasted_iota(jnp.int32, (rows, HD), 0) < live_len
    for i in range(share):
        block = att[i * rows : (i + 1) * rows, :].astype(F32)
        a_buf[:, i * HD : (i + 1) * HD] = jnp.where(live, block, 0.0).astype(BF)
    send(0, a_buf)
    v_buf[...] = d_vr.astype(BF)
    send(3, v_buf)
    k_unit = ku_ref[:, :HD]
    up_k = d_kr * k_gain
    mean_k = jnp.mean(up_k * k_unit, axis=-1, keepdims=True)
    k_buf[...] = (ku_ref[:, HD:] * (up_k - k_unit * mean_k)).astype(BF)
    send(2, k_buf)
    parts = []
    for start in range(0, share * rows, width):
        cols = slice(start, start + width)
        q_inv = row_ref[0:1, cols]
        q_unit = qt_ref[:, cols].astype(F32) * q_inv
        up = dq_ref[:, cols] * q_gain
        mean = jnp.mean(up * q_unit, axis=0, keepdims=True)
        parts.append((q_inv * (up - q_unit * mean)).astype(BF))
    d_q = jnp.concatenate(parts, axis=1).T
    for i in range(share):
        q_buf[:, i * HD : (i + 1) * HD] = d_q[i * rows : (i + 1) * rows, :]
    send(1, q_buf)
    for copy in copies:
        copy.wait()


def whole_kernel(s, width, meta, pr_ref, *rest):
    kept, (gain_ref, kg_ref, acc_ref) = rest[:KEPT], rest[KEPT : KEPT + 3]
    part_ref, gacc_ref, *rest = rest[-13:]
    outs, (at_ref, dq_ref), bufs, sems = rest[:4], rest[4:6], rest[6:10], rest[10]
    q_gain = gain_ref[...]
    d_kr, d_vr = attend(width, pr_ref, kept, q_gain, acc_ref, part_ref, at_ref, dq_ref, gacc_ref)
    live_len = meta[meta.shape[0] - 1]
    settle(width, meta[s], live_len, kept, q_gain, kg_ref[...], at_ref, dq_ref, d_kr, d_vr, outs, bufs, sems)


def first_kernel(width, pr_ref, *rest):
    kept, (gain_ref, acc_ref) = rest[:KEPT], rest[KEPT : KEPT + 2]
    part_ref, gacc_ref, at_ref, dq_ref, dkr_ref, dvr_ref = rest[-6:]
    d_kr, d_vr = attend(width, pr_ref, kept, gain_ref[...], acc_ref, part_ref, at_ref, dq_ref, gacc_ref)
    dkr_ref[...] = d_kr
    dvr_ref[...] = d_vr


def second_kernel(s, width, meta, *rest):
    kept, (gain_ref, kg_ref, at_ref, dq_ref, dkr_ref, dvr_ref) = rest[:KEPT], rest[KEPT : KEPT + 6]
    outs, bufs, sems = rest[-9:-5], rest[-5:-1], rest[-1]
    live_len = meta[meta.shape[0] - 1]
    settle(
        width, meta[s], live_len, kept, gain_ref[...], kg_ref[...], at_ref, dq_ref,
        dkr_ref[...], dvr_ref[...], outs, bufs, sems,
    )


def out_shapes(rows, q_width, k_width):
    widths = (q_width, q_width, k_width, k_width)
    return [jax.ShapeDtypeStruct((rows, w), BF) for w in widths]


def out_scratch(rows, share):
    widths = (share * HD, share * HD, HD, HD)
    return [pltpu.VMEM((rows, w), BF) for w in widths] + [pltpu.SemaphoreType.DMA((4,))]


def cost(prompt_rows, rows, total):
    return pl.CostEstimate(
        flops=(8 * prompt_rows + 4 * rows) * total * HD,
        bytes_accessed=2**20,
        transcendentals=total * prompt_rows,
    )


def whole_head(s, meta, prompt, kept, q_gain, k_gain, acc, buffers, q_width, k_width):
    total = kept[0].shape[1]
    rows = kept[3].shape[0]
    outs = pl.pallas_call(
        functools.partial(whole_kernel, s, 2 * HD),
        out_shape=[
            jax.ShapeDtypeStruct(prompt.shape, BF),
            jax.ShapeDtypeStruct(acc.shape, F32),
        ]
        + out_shapes(rows, q_width, k_width),
        in_specs=[SMEM] + [VMEM] * (4 + KEPT) + [HBM] * len(buffers),
        out_specs=[VMEM] * 2 + [HBM] * 4,
        scratch_shapes=[pltpu.VMEM((HD, total), BF), pltpu.VMEM((HD, total), F32)]
        + out_scratch(rows, total // rows),
        input_output_aliases={5 + KEPT + i: 2 + i for i in range(len(buffers))},
        compiler_params=params(16),
        cost_estimate=cost(prompt.shape[1], rows, total),
        name="attend_head",
    )(meta, prompt, *kept, q_gain, k_gain, acc, *buffers)
    return outs[0], outs[1], outs[2:]


def first_half(prompt, kept, q_gain, acc):
    total = kept[0].shape[1]
    rows = kept[3].shape[0]
    return pl.pallas_call(
        functools.partial(first_kernel, 2 * HD),
        out_shape=[
            jax.ShapeDtypeStruct(prompt.shape, BF),
            jax.ShapeDtypeStruct(acc.shape, F32),
            jax.ShapeDtypeStruct((HD, total), BF),
            jax.ShapeDtypeStruct((HD, total), F32),
            jax.ShapeDtypeStruct((rows, HD), F32),
            jax.ShapeDtypeStruct((rows, HD), F32),
        ],
        in_specs=[VMEM] * (3 + KEPT),
        out_specs=[VMEM] * 6,
        compiler_params=params(16),
        cost_estimate=cost(prompt.shape[1], rows, total),
        name="attend_last_head",
    )(prompt, *kept, q_gain, acc)


def second_half(s, meta, kept, q_gain, k_gain, results, buffers):
    total = kept[0].shape[1]
    rows = kept[3].shape[0]
    return pl.pallas_call(
        functools.partial(second_kernel, s, 2 * HD),
        out_shape=out_shapes(rows, buffers[0].shape[1], buffers[2].shape[1]),
        in_specs=[SMEM] + [VMEM] * (KEPT + 6) + [HBM] * 4,
        out_specs=[HBM] * 4,
        scratch_shapes=out_scratch(rows, total // rows),
        input_output_aliases={7 + KEPT + i: i for i in range(4)},
        compiler_params=params(16),
        cost_estimate=pl.CostEstimate(flops=0, bytes_accessed=2**20, transcendentals=0),
        name="settle_last_head",
    )(meta, *kept, q_gain, k_gain, *results, *buffers)


TAIL = 16


def join_kernel(own_ref, *rest):
    backs, gains_ref, out_ref = rest[:-2], rest[-2], rest[-1]
    depth, rows, _ = own_ref.shape
    for d in range(depth):
        total = own_ref[d].astype(F32)
        for back in backs:
            total = total + back[d].astype(F32)
        out_ref[d * rows : (d + 1) * rows, :] = total.astype(BF)
    gains = gains_ref[...]
    high = gains.astype(BF)
    gains = gains - high.astype(F32)
    middle = gains.astype(BF)
    low = (gains - middle.astype(F32)).astype(BF)
    pieces = jnp.concatenate([p[0:2].astype(F32) for p in (high, middle, low)], axis=0)
    pad = jnp.zeros((TAIL - pieces.shape[0], HD), F32)
    out_ref[depth * rows :, :] = jnp.concatenate([pieces, pad], axis=0).astype(BF)


def join(own, backs, gains):
    depth, rows, _ = own.shape
    return pl.pallas_call(
        join_kernel,
        out_shape=jax.ShapeDtypeStruct((depth * rows + TAIL, HD), BF),
        in_specs=[VMEM] * (2 + len(backs)),
        out_specs=VMEM,
        compiler_params=params(8),
        name="join_parts",
    )(own, *backs, gains)


def place_kernel(meta, *refs):
    payloads, out_ref, gain_ref, stage = refs[:-3], refs[-3], refs[-2], refs[-1]
    mine = meta[0] > 0
    depth, rows, _ = out_ref.shape
    for i, ref in enumerate(payloads):
        at = pl.multiple_of(meta[1 + i] * HD, HD)
        for d in range(depth):
            block = ref[d * rows : (d + 1) * rows, :]
            out_ref[d, :, pl.ds(at, HD)] = jnp.where(mine, block, jnp.zeros_like(block))
        tail = ref[depth * rows :, :].astype(F32)
        stage[meta[1 + i]] = tail[0:2] + tail[2:4] + tail[4:6]
    total = stage[0]
    for i in range(1, len(payloads)):
        total = total + stage[i]
    gain_ref[...] = total


def place(meta, payloads, depth, rows):
    count = len(payloads)
    return pl.pallas_call(
        place_kernel,
        out_shape=[
            jax.ShapeDtypeStruct((depth, rows, HD * count), BF),
            jax.ShapeDtypeStruct((2, HD), F32),
        ],
        in_specs=[SMEM] + [VMEM] * count,
        out_specs=[VMEM, VMEM],
        scratch_shapes=[pltpu.VMEM((count, 2, HD), F32)],
        compiler_params=params(8),
        name="place_prompt_grad",
    )(meta, *payloads)


def after(x, *others):
    return lax.optimization_barrier((x,) + others)[0]


def pair_sum(value, axis, size):
    step = 1
    while step < size:
        value = value + lax.ppermute(value, axis, [(i, i ^ step) for i in range(size)])
        step *= 2
    return value


def local(
    n_dp, n_group, queries, resp_keys, resp_values, prompt_cache, owners, lengths, q_gain, k_gain, grad_out
):
    q, g = queries[0, 0], grad_out[0, 0]
    k, v = resp_keys[0, 0], resp_values[0, 0]
    cache = prompt_cache[0, 0]
    owner = owners[0]
    live_len = lengths[0, 0]
    me = lax.axis_index("group")
    kv_heads = k.shape[1] // HD
    depth, p_rows, _ = cache.shape
    direct = n_group == kv_heads

    def shift(x, s):
        return lax.ppermute(x, "group", [(i, (i + s) % n_group) for i in range(n_group)])

    gain_col = q_gain[:, None]
    gain_row = k_gain[None, :]
    if direct:
        order = jnp.stack([(me - s) % n_group for s in range(n_group)]).astype(jnp.int32)
    else:
        order = jnp.arange(kv_heads, dtype=jnp.int32)
    meta = jnp.concatenate([order, live_len[None]])
    q, g, k, v = [pltpu.with_memory_space_constraint(x, pltpu.HBM) for x in (q, g, k, v)]
    kept = prepare(meta, q, g, k, v, gain_col, gain_row, kv_heads)
    if direct:
        blocks = cut(order, pltpu.with_memory_space_constraint(cache, pltpu.HBM), kv_heads)
        got = [blocks[0]] + [shift(blocks[s], -s) for s in range(1, n_group)]
        got[1], kept[0][2] = lax.optimization_barrier((got[1], kept[0][2]))
        mine = pick(jnp.reshape((owner - me) % n_group, (1,)).astype(jnp.int32), got)
        prompts = [mine] + [shift(mine, s) for s in range(1, n_group)]
    else:
        cache = lax.psum(jnp.where(me == owner, cache, jnp.zeros_like(cache)), "group")
        prompts = cut(order, cache, kv_heads)

    acc = jnp.zeros((2, HD), F32)
    parts, backs, buffers = [], [], ()
    for s, prompt in enumerate(prompts):
        last = s == kv_heads - 1
        if last:
            part, acc, *results = first_half(prompt, kept[s], gain_col, acc)
        else:
            part, acc, buffers = whole_head(
                s, meta, prompt, kept[s], gain_col, gain_row, acc, buffers, q.shape[1], k.shape[1]
            )
        parts.append(part)
        if direct and s > 0:
            backs.append(shift(part, -s))
    mine_flag = (me == owner).astype(jnp.int32)
    if direct:
        results[0] = after(results[0], *backs[:-1])
    buffers = list(second_half(kv_heads - 1, meta, kept[-1], gain_col, gain_row, results, buffers))
    gains = pair_sum(acc, "dp", n_dp)
    if direct:
        backs[-1] = after(backs[-1], buffers[2])
        payload = join(parts[0], backs, gains)
        payloads = [payload] + [shift(payload, s) for s in range(1, n_group)]
        placed, gains = place(jnp.concatenate([mine_flag[None], order]), payloads, depth, p_rows)
    else:
        total = lax.psum(jnp.concatenate(parts, axis=-1).astype(F32), "group").astype(BF)
        placed = jnp.where(mine_flag > 0, total, jnp.zeros((), BF))
        gains = pair_sum(gains, "group", n_group)
    attended, d_query, d_key, d_value = buffers
    return (
        attended[None, None],
        d_query[None, None],
        d_key[None, None],
        d_value[None, None],
        placed[None, None],
        gains,
    )


def solution(mesh):
    in_specs = (
        P("dp", "group", None, None),
        P("dp", "group", None, None),
        P("dp", "group", None, None),
        P("dp", "group", None, None, None),
        P("dp"),
        P("dp", "group"),
        P(),
        P(),
        P("dp", "group", None, None),
    )
    out_specs = (
        P("dp", "group", None, None),
        P("dp", "group", None, None),
        P("dp", "group", None, None),
        P("dp", "group", None, None),
        P("dp", "group", None, None, None),
        P(),
    )
    body = functools.partial(local, mesh.shape["dp"], mesh.shape["group"])
    return jax.shard_map(body, mesh=mesh, in_specs=in_specs, out_specs=out_specs, check_vma=False)
```

```python
import functools

import jax
import jax.numpy as jnp
from jax import lax
from jax.experimental import pallas as pl
from jax.experimental.pallas import tpu as pltpu
from jax.sharding import PartitionSpec as P

HD = 128
EPS = 1e-06
LOG2E = 1.4426950408889634
BF = jnp.bfloat16
F32 = jnp.float32


def dot_nn(a, b):
    return lax.dot_general(a, b, (((1,), (0,)), ((), ())), preferred_element_type=F32)


def dot_nt(a, b):
    return lax.dot_general(a, b, (((1,), (1,)), ((), ())), preferred_element_type=F32)


VMEM = pl.BlockSpec(memory_space=pltpu.VMEM)
SMEM = pl.BlockSpec(memory_space=pltpu.SMEM)
HBM = pl.BlockSpec(memory_space=pltpu.HBM)


SHORT = pl.CostEstimate(flops=0, bytes_accessed=0, transcendentals=0)


def params(mib):
    return pltpu.CompilerParams(vmem_limit_bytes=mib * 2**20)


def cut_kernel(cache_ref, out_ref, sems):
    copies = []
    for i in range(out_ref.shape[0]):
        src = cache_ref.at[:, :, i * HD : (i + 1) * HD]
        copy = pltpu.make_async_copy(src, out_ref.at[i], sems.at[i])
        copy.start()
        copies.append(copy)
    for copy in copies:
        copy.wait()


def cut(cache, count):
    depth, rows, _ = cache.shape
    return pl.pallas_call(
        cut_kernel,
        out_shape=jax.ShapeDtypeStruct((count, depth, rows, HD), BF),
        in_specs=[HBM],
        out_specs=VMEM,
        scratch_shapes=[pltpu.SemaphoreType.DMA((count,))],
        compiler_params=params(4),
        name="cut_prompt",
    )(cache)


def prepare_kernel(count, share, rows, width, meta, q_in, g_in, k_in, v_in, gain_ref, kg_ref, *rest):
    outs, (q_buf, g_buf, k_buf, v_buf, sems) = rest[:-5], rest[-5:]
    live_len = meta[count]
    scale = HD ** (-0.5)
    wide = share * HD
    copies = []
    for s in range(count):
        group = []
        for j, (src, buf, size) in enumerate(
            ((q_in, q_buf, wide), (k_in, k_buf, HD), (g_in, g_buf, wide), (v_in, v_buf, HD))
        ):
            src = src.at[:, pl.ds(pl.multiple_of(meta[s] * size, size), size)]
            copy = pltpu.make_async_copy(src, buf.at[s], sems.at[s, j])
            copy.start()
            group.append(copy)
        copies.append(group)
    q_gain = gain_ref[...]
    k_gain = kg_ref[...]
    for s in range(count):
        low_ref, high_ref, key_ref = outs[s * 3 : (s + 1) * 3]
        for copy in copies[s]:
            copy.wait()
        q_t = jnp.concatenate([q_buf[s, :, i * HD : (i + 1) * HD] for i in range(share)], axis=0).T
        g_t = jnp.concatenate([g_buf[s, :, i * HD : (i + 1) * HD] for i in range(share)], axis=0).T
        low_ref[:HD, :] = q_t
        raw_k = k_buf[s].astype(F32)
        k_inv = lax.rsqrt(jnp.mean(raw_k * raw_k, axis=-1, keepdims=True) + EPS)
        k_unit = raw_k * k_inv
        k_hat = (k_unit * k_gain).astype(BF)
        key_ref[:, :HD] = k_unit
        key_ref[:, HD : 2 * HD] = jnp.broadcast_to(k_inv, (rows, HD))
        key_ref[:, 2 * HD :] = k_hat.astype(F32)
        r_val = v_buf[s]
        r_val_t = r_val.T
        for start in range(0, share * rows, width):
            cols = slice(start, start + width)
            token = (lax.broadcasted_iota(jnp.int32, (1, width), 1) + start) % rows
            raw_q = q_t[:, cols].astype(F32)
            q_inv = lax.rsqrt(jnp.mean(raw_q * raw_q, axis=0, keepdims=True) + EPS)
            q_hat = (raw_q * q_inv * q_gain).astype(BF)
            d_o = jnp.where(token < live_len, g_t[:, cols].astype(F32), 0.0).astype(BF)
            low_ref[HD : 2 * HD, cols] = d_o
            causal = lax.broadcasted_iota(jnp.int32, (rows, width), 0) <= token
            e_r = jnp.where(causal, jnp.exp2(dot_nn(k_hat, q_hat) * (scale * LOG2E)), 0.0)
            eb_r = e_r.astype(BF)
            low_ref[2 * HD :, cols] = eb_r
            high_ref[:HD, cols] = dot_nn(r_val_t, eb_r)
            high_ref[HD : HD + rows, cols] = dot_nn(r_val, d_o)
            high_ref[HD + rows : HD + rows + 1, cols] = q_inv
            high_ref[HD + rows + 1 : HD + rows + 2, cols] = jnp.sum(e_r, axis=0, keepdims=True)


def prepare(count, meta, q, g, k, v, q_gain, k_gain):
    rows, q_width = q.shape
    share = q_width // k.shape[1]
    total = share * rows
    each = [
        jax.ShapeDtypeStruct((2 * HD + rows, total), BF),
        jax.ShapeDtypeStruct((HD + rows + 8, total), F32),
        jax.ShapeDtypeStruct((rows, 3 * HD), F32),
    ]
    outs = pl.pallas_call(
        functools.partial(prepare_kernel, count, share, rows, 2 * HD),
        out_shape=each * count,
        in_specs=[SMEM] + [HBM] * 4 + [VMEM] * 2,
        out_specs=[VMEM] * (3 * count),
        scratch_shapes=[
            pltpu.VMEM((count, rows, share * HD), BF),
            pltpu.VMEM((count, rows, share * HD), BF),
            pltpu.VMEM((count, rows, HD), BF),
            pltpu.VMEM((count, rows, HD), BF),
            pltpu.SemaphoreType.DMA((count, 4)),
        ],
        compiler_params=params(16),
        cost_estimate=SHORT,
        name="prepare_response",
    )(meta, q, g, k, v, q_gain, k_gain)
    return [list(outs[s * 3 : (s + 1) * 3]) for s in range(count)]


def attend(width, prompt, low_ref, high_ref, key_ref, q_gain, part_ref, store_ref):
    rows = key_ref.shape[0]
    scale = HD ** (-0.5)
    p_key, p_val = prompt
    k_hat_t = key_ref[:, 2 * HD :].astype(BF).T
    p_key_t = p_key.T
    p_val_t = p_val.T
    sums = None
    for start in range(0, low_ref.shape[1], width):
        cols = slice(start, start + width)
        q_inv = high_ref[HD + rows : HD + rows + 1, cols]
        q_unit = low_ref[:HD, cols].astype(F32) * q_inv
        q_hat = (q_unit * q_gain).astype(BF)
        d_ob = low_ref[HD : 2 * HD, cols]
        d_o = d_ob.astype(F32)
        e_p = jnp.exp2(dot_nn(p_key, q_hat) * (scale * LOG2E))
        row_sum = jnp.sum(e_p, axis=0, keepdims=True) + high_ref[HD + rows + 1 : HD + rows + 2, cols]
        inv_sum = 1.0 / row_sum
        eb_p = e_p.astype(BF)
        eb_r = low_ref[2 * HD :, cols]
        out = (dot_nn(p_val_t, eb_p) + high_ref[:HD, cols]) * inv_sum
        delta = jnp.sum(d_o * out, axis=0, keepdims=True)
        ds_p = (e_p * (dot_nn(p_val, d_ob) - delta)).astype(BF)
        ds_r = (eb_r.astype(F32) * (high_ref[HD : HD + rows, cols] - delta)).astype(BF)
        weight = inv_sum * scale
        q_w = (q_hat.astype(F32) * weight).astype(BF)
        d_ow = (d_o * inv_sum).astype(BF)
        d_qhat = (dot_nn(p_key_t, ds_p) + dot_nn(k_hat_t, ds_r)) * weight
        store_ref[:HD, cols] = d_qhat
        store_ref[HD : 2 * HD, cols] = out
        store_ref[2 * HD : 3 * HD, cols] = q_unit
        store_ref[3 * HD : 3 * HD + 1, cols] = q_inv
        terms = (
            dot_nt(ds_p, q_w),
            dot_nt(eb_p, d_ow),
            dot_nt(ds_r, q_w),
            dot_nt(eb_r, d_ow),
            d_qhat * q_unit,
        )
        sums = terms if sums is None else [a + b for a, b in zip(sums, terms)]
    d_kp, d_vp, d_kr, d_vr, q_term = sums
    part_ref[0] = d_kp.astype(BF)
    part_ref[1] = d_vp.astype(BF)
    base = 3 * HD + 8
    store_ref[base:, :HD] = d_kr
    store_ref[base:, HD : 2 * HD] = d_vr
    store_ref[base:, 2 * HD : 4 * HD] = key_ref[:, : 2 * HD]
    folded = q_term[:, :HD]
    for start in range(HD, width, HD):
        folded = folded + q_term[:, start : start + HD]
    return (
        jnp.sum(folded.T, axis=0, keepdims=True),
        jnp.sum(d_kr * key_ref[:, :HD], axis=0, keepdims=True),
    )


def own_kernel(width, prompt_ref, low_ref, high_ref, key_ref, gain_ref, part_ref, gacc_ref, store_ref):
    prompt = (prompt_ref[0], prompt_ref[1])
    q_term, k_term = attend(width, prompt, low_ref, high_ref, key_ref, gain_ref[...], part_ref, store_ref)
    gacc_ref[0:1, :] = q_term
    gacc_ref[1:2, :] = k_term


def others_kernel(slots, width, meta, prompts_ref, own_ref, gain_ref, acc_ref, *rest):
    count = len(slots)
    kept, (parts_ref, gacc_ref), stores = rest[: 3 * count], rest[3 * count : 3 * count + 2], rest[3 * count + 2 :]
    if len(slots) < parts_ref.shape[0]:
        parts_ref[meta[0]] = own_ref[...]
    q_gain = gain_ref[...]
    q_sum, k_sum = acc_ref[0:1, :], acc_ref[1:2, :]
    for i, s in enumerate(slots):
        head = meta[s]
        prompt = (prompts_ref[head, 0], prompts_ref[head, 1])
        low_ref, high_ref, key_ref = kept[3 * i : 3 * i + 3]
        q_term, k_term = attend(
            width, prompt, low_ref, high_ref, key_ref, q_gain, parts_ref.at[head], stores[i]
        )
        q_sum, k_sum = q_sum + q_term, k_sum + k_term
    gacc_ref[0:1, :] = q_sum
    gacc_ref[1:2, :] = k_sum


def store_shape(kept):
    return jax.ShapeDtypeStruct((3 * HD + 8 + kept[2].shape[0], kept[0].shape[1]), F32)


def own_head(prompt, kept, q_gain):
    return pl.pallas_call(
        functools.partial(own_kernel, 2 * HD),
        out_shape=[
            jax.ShapeDtypeStruct(prompt.shape, BF),
            jax.ShapeDtypeStruct((2, HD), F32),
            store_shape(kept),
        ],
        in_specs=[VMEM] * 5,
        out_specs=[VMEM] * 3,
        compiler_params=params(16),
        name="attend_own_head",
    )(prompt, *kept, q_gain)


def other_heads(slots, meta, prompts, own, kept, q_gain, acc):
    outs = pl.pallas_call(
        functools.partial(others_kernel, slots, 2 * HD),
        out_shape=[jax.ShapeDtypeStruct(prompts.shape, BF), jax.ShapeDtypeStruct((2, HD), F32)]
        + [store_shape(kept[s]) for s in slots],
        in_specs=[SMEM] + [VMEM] * (4 + 3 * len(slots)),
        out_specs=[VMEM] * (2 + len(slots)),
        compiler_params=params(16),
        name="attend_other_heads",
    )(meta, prompts, own, q_gain, acc, *[x for s in slots for x in kept[s]])
    return outs[0], outs[1], list(outs[2:])


def settle_kernel(count, rows, width, meta, gain_ref, kg_ref, *rest):
    stores = rest[:count]
    outs, bufs, sems = rest[-9:-5], rest[-5:-1], rest[-1]
    live_len = meta[count]
    q_gain = gain_ref[...]
    k_gain = kg_ref[...]
    base = 3 * HD + 8
    copies = []
    for s, store_ref in enumerate(stores):
        head = meta[s]
        a_buf, q_buf, k_buf, v_buf = [buf.at[s] for buf in bufs]
        total = store_ref.shape[1]
        share = total // rows

        def send(j, buf):
            size = buf.shape[1]
            out = outs[j].at[:, pl.ds(pl.multiple_of(head * size, size), size)]
            copy = pltpu.make_async_copy(buf, out, sems.at[s, j])
            copy.start()
            copies.append(copy)

        att = store_ref[HD : 2 * HD, :].astype(BF).T
        live = lax.broadcasted_iota(jnp.int32, (rows, HD), 0) < live_len
        for i in range(share):
            block = att[i * rows : (i + 1) * rows, :].astype(F32)
            a_buf[:, i * HD : (i + 1) * HD] = jnp.where(live, block, 0.0).astype(BF)
        send(0, a_buf)
        v_buf[...] = store_ref[base:, HD : 2 * HD].astype(BF)
        send(3, v_buf)
        k_unit = store_ref[base:, 2 * HD : 3 * HD]
        k_inv = store_ref[base:, 3 * HD : 4 * HD]
        up_k = store_ref[base:, :HD] * k_gain
        mean_k = jnp.mean(up_k * k_unit, axis=-1, keepdims=True)
        k_buf[...] = (k_inv * (up_k - k_unit * mean_k)).astype(BF)
        send(2, k_buf)
        parts = []
        for start in range(0, total, width):
            cols = slice(start, start + width)
            q_unit = store_ref[2 * HD : 3 * HD, cols]
            up = store_ref[:HD, cols] * q_gain
            mean = jnp.mean(up * q_unit, axis=0, keepdims=True)
            parts.append((store_ref[3 * HD : 3 * HD + 1, cols] * (up - q_unit * mean)).astype(BF))
        d_q = jnp.concatenate(parts, axis=1).T
        for i in range(share):
            q_buf[:, i * HD : (i + 1) * HD] = d_q[i * rows : (i + 1) * rows, :]
        send(1, q_buf)
    for copy in copies:
        copy.wait()


def settle(meta, q_gain, k_gain, stores, q_width, k_width):
    total = stores[0].shape[1]
    rows = stores[0].shape[0] - 3 * HD - 8
    count = len(stores)
    wide = total // rows * HD
    return pl.pallas_call(
        functools.partial(settle_kernel, count, rows, 2 * HD),
        out_shape=[jax.ShapeDtypeStruct((rows, w), BF) for w in (q_width, q_width, k_width, k_width)],
        in_specs=[SMEM] + [VMEM] * (2 + count),
        out_specs=[HBM] * 4,
        scratch_shapes=[pltpu.VMEM((count, rows, w), BF) for w in (wide, wide, HD, HD)]
        + [pltpu.SemaphoreType.DMA((count, 4))],
        compiler_params=params(16),
        name="settle_heads",
    )(meta, q_gain, k_gain, *stores)


TAIL = 16


def join_kernel(got_ref, gains_ref, out_ref):
    count, depth, rows, _ = got_ref.shape
    for d in range(depth):
        total = got_ref[0, d].astype(F32)
        for j in range(1, count):
            total = total + got_ref[j, d].astype(F32)
        total = total.astype(BF)
        for j in range(count):
            out_ref[j, d * rows : (d + 1) * rows, :] = total
    gains = gains_ref[...]
    high = gains.astype(BF)
    gains = gains - high.astype(F32)
    middle = gains.astype(BF)
    low = (gains - middle.astype(F32)).astype(BF)
    pieces = jnp.concatenate([p.astype(F32) for p in (high, middle, low)], axis=0)
    pad = jnp.zeros((TAIL - pieces.shape[0], HD), F32)
    tail = jnp.concatenate([pieces, pad], axis=0).astype(BF)
    for j in range(count):
        out_ref[j, depth * rows :, :] = tail


def join(got, gains):
    count, depth, rows, _ = got.shape
    return pl.pallas_call(
        join_kernel,
        out_shape=jax.ShapeDtypeStruct((count, depth * rows + TAIL, HD), BF),
        in_specs=[VMEM] * 2,
        out_specs=VMEM,
        compiler_params=params(8),
        name="join_parts",
    )(got, gains)


def place_kernel(mine, in_ref, out_ref, gain_ref):
    depth, rows, _ = out_ref.shape
    total = jnp.zeros(gain_ref.shape, F32)
    for i in range(in_ref.shape[0]):
        for d in range(depth):
            block = in_ref[i, d * rows : (d + 1) * rows, :]
            out_ref[d, :, i * HD : (i + 1) * HD] = jnp.where(mine[0] > 0, block, jnp.zeros_like(block))
        tail = in_ref[i, depth * rows :, :].astype(F32)
        total = total + (tail[0:2] + tail[2:4] + tail[4:6])
    gain_ref[...] = total


def place(mine, payloads, depth, rows):
    count = payloads.shape[0]
    return pl.pallas_call(
        place_kernel,
        out_shape=[
            jax.ShapeDtypeStruct((depth, rows, HD * count), BF),
            jax.ShapeDtypeStruct((2, HD), F32),
        ],
        in_specs=[SMEM, VMEM],
        out_specs=[VMEM, VMEM],
        compiler_params=params(8),
        name="place_prompt_grad",
    )(mine, payloads)


def after(x, *others):
    return lax.optimization_barrier((x,) + others)[0]


def pair_sum(value, axis, size):
    step = 1
    while step < size:
        value = value + lax.ppermute(value, axis, [(i, i ^ step) for i in range(size)])
        step *= 2
    return value


def local(
    n_dp, n_group, queries, resp_keys, resp_values, prompt_cache, owners, lengths, q_gain, k_gain, grad_out
):
    q, g = queries[0, 0], grad_out[0, 0]
    k, v = resp_keys[0, 0], resp_values[0, 0]
    cache = prompt_cache[0, 0]
    owner = owners[0]
    live_len = lengths[0, 0]
    me = lax.axis_index("group")
    kv_heads = k.shape[1] // HD
    depth, p_rows, _ = cache.shape
    q, g, k, v = [pltpu.with_memory_space_constraint(x, pltpu.HBM) for x in (q, g, k, v)]
    gain_col = q_gain[:, None]
    gain_row = k_gain[None, :]
    direct = n_group == kv_heads
    mine_flag = (me == owner).astype(jnp.int32)
    slots = tuple(range(kv_heads))
    order = jnp.arange(kv_heads, dtype=jnp.int32)
    if direct:
        order = (order + me) % kv_heads
    meta = jnp.concatenate([order, live_len[None]])
    kept = prepare(kv_heads, meta, q, g, k, v, gain_col, gain_row)

    def exchange(blocks):
        return lax.all_to_all(blocks, "group", 0, 0)

    if direct:
        blocks = cut(pltpu.with_memory_space_constraint(cache, pltpu.HBM), kv_heads)
        got = exchange(blocks)
        got = after(got, kept[0][1])
        mine = lax.dynamic_index_in_dim(got, owner, 0, keepdims=False)
        prompts = exchange(jnp.broadcast_to(mine[None], got.shape))
        own, acc, store = own_head(mine, kept[0], gain_col)
        prompts = after(prompts, own)
        parts, acc, stores = other_heads(slots[1:], meta, prompts, own, kept, gain_col, acc)
        attended, d_query, d_key, d_value = settle(
            meta, gain_col, gain_row, [store] + stores, q.shape[1], k.shape[1]
        )
        gains = pair_sum(acc, "dp", n_dp)
        back = after(exchange(parts), d_key)
        payloads = exchange(join(back, gains))
        placed, gains = place(mine_flag[None], payloads, depth, p_rows)
    else:
        cache = lax.psum(jnp.where(me == owner, cache, jnp.zeros_like(cache)), "group")
        prompts = cut(cache, kv_heads)
        acc = jnp.zeros((2, HD), F32)
        parts, acc, stores = other_heads(slots, meta, prompts, prompts[0], kept, gain_col, acc)
        attended, d_query, d_key, d_value = settle(
            meta, gain_col, gain_row, stores, q.shape[1], k.shape[1]
        )
        total = jnp.transpose(parts, (1, 2, 0, 3)).reshape(depth, p_rows, kv_heads * HD)
        total = lax.psum(total.astype(F32), "group").astype(BF)
        placed = jnp.where(mine_flag > 0, total, jnp.zeros((), BF))
        gains = pair_sum(pair_sum(acc, "group", n_group), "dp", n_dp)
    return (
        attended[None, None],
        d_query[None, None],
        d_key[None, None],
        d_value[None, None],
        placed[None, None],
        gains,
    )


def solution(mesh):
    in_specs = (
        P("dp", "group", None, None),
        P("dp", "group", None, None),
        P("dp", "group", None, None),
        P("dp", "group", None, None, None),
        P("dp"),
        P("dp", "group"),
        P(),
        P(),
        P("dp", "group", None, None),
    )
    out_specs = (
        P("dp", "group", None, None),
        P("dp", "group", None, None),
        P("dp", "group", None, None),
        P("dp", "group", None, None),
        P("dp", "group", None, None, None),
        P(),
    )
    body = functools.partial(local, mesh.shape["dp"], mesh.shape["group"])
    return jax.shard_map(body, mesh=mesh, in_specs=in_specs, out_specs=out_specs, check_vma=False)
```

```python
import functools

import jax
import jax.numpy as jnp
from jax import lax
from jax.experimental import pallas as pl
from jax.experimental.pallas import tpu as pltpu
from jax.sharding import PartitionSpec as P

HD = 128
EPS = 1e-06
LOG2E = 1.4426950408889634
BF = jnp.bfloat16
F32 = jnp.float32


def dot_nn(a, b):
    return lax.dot_general(a, b, (((1,), (0,)), ((), ())), preferred_element_type=F32)


def dot_nt(a, b):
    return lax.dot_general(a, b, (((1,), (1,)), ((), ())), preferred_element_type=F32)


VMEM = pl.BlockSpec(memory_space=pltpu.VMEM)
SMEM = pl.BlockSpec(memory_space=pltpu.SMEM)
HBM = pl.BlockSpec(memory_space=pltpu.HBM)


def params(mib):
    return pltpu.CompilerParams(vmem_limit_bytes=mib * 2**20)


def cut_kernel(per, order, cache_ref, *rest):
    outs, sems = rest[:-1], rest[-1]
    copies = []
    for i, out in enumerate(outs):
        for j in range(per):
            s = i * per + j
            at = pl.ds(pl.multiple_of(order[s] * HD, HD), HD)
            copy = pltpu.make_async_copy(cache_ref.at[:, :, at], out.at[j], sems.at[s])
            copy.start()
            copies.append(copy)
    for copy in copies:
        copy.wait()


def cut(order, cache, halves, per):
    depth, rows, _ = cache.shape
    return pl.pallas_call(
        functools.partial(cut_kernel, per),
        out_shape=[jax.ShapeDtypeStruct((per, depth, rows, HD), BF)] * halves,
        in_specs=[SMEM, HBM],
        out_specs=[VMEM] * halves,
        scratch_shapes=[pltpu.SemaphoreType.DMA((halves * per,))],
        compiler_params=params(4),
        name="cut_prompt",
    )(order, cache)


KEPT = 8


def prepare_kernel(count, share, rows, width, meta, q_in, g_in, k_in, v_in, gain_ref, kg_ref, *rest):
    outs, (q_buf, g_buf, k_buf, v_buf, sems) = rest[:-5], rest[-5:]
    live_len = meta[count]
    scale = HD ** (-0.5)
    wide = share * HD
    copies = []
    for s in range(count):
        group = []
        for j, (src, buf, size) in enumerate(
            ((q_in, q_buf, wide), (k_in, k_buf, HD), (g_in, g_buf, wide), (v_in, v_buf, HD))
        ):
            at = pl.multiple_of(meta[s] * size, size)
            copy = pltpu.make_async_copy(src.at[:, pl.ds(at, size)], buf.at[s], sems.at[s, j])
            copy.start()
            group.append(copy)
        copies.append(group)
    q_gain = gain_ref[...]
    k_gain = kg_ref[...]
    for s in range(count):
        qt_ref, gt_ref, row_ref, er_ref, ot_ref, dp_ref, kh_ref, ku_ref = outs[s * KEPT : (s + 1) * KEPT]
        for copy in copies[s]:
            copy.wait()
        q_t = jnp.concatenate([q_buf[s, :, i * HD : (i + 1) * HD] for i in range(share)], axis=0).T
        g_t = jnp.concatenate([g_buf[s, :, i * HD : (i + 1) * HD] for i in range(share)], axis=0).T
        qt_ref[...] = q_t
        raw_k = k_buf[s].astype(F32)
        k_inv = lax.rsqrt(jnp.mean(raw_k * raw_k, axis=-1, keepdims=True) + EPS)
        k_unit = raw_k * k_inv
        k_hat = (k_unit * k_gain).astype(BF)
        kh_ref[...] = k_hat
        ku_ref[:, :HD] = k_unit
        ku_ref[:, HD:] = jnp.broadcast_to(k_inv, (rows, HD))
        r_val = v_buf[s]
        r_val_t = r_val.T
        for start in range(0, share * rows, width):
            cols = slice(start, start + width)
            token = (lax.broadcasted_iota(jnp.int32, (1, width), 1) + start) % rows
            raw_q = q_t[:, cols].astype(F32)
            q_inv = lax.rsqrt(jnp.mean(raw_q * raw_q, axis=0, keepdims=True) + EPS)
            q_hat = (raw_q * q_inv * q_gain).astype(BF)
            d_o = jnp.where(token < live_len, g_t[:, cols].astype(F32), 0.0).astype(BF)
            gt_ref[:, cols] = d_o
            causal = lax.broadcasted_iota(jnp.int32, (rows, width), 0) <= token
            e_r = jnp.where(causal, jnp.exp2(dot_nn(k_hat, q_hat) * (scale * LOG2E)), 0.0)
            eb_r = e_r.astype(BF)
            er_ref[:, cols] = eb_r
            ot_ref[:, cols] = dot_nn(r_val_t, eb_r)
            dp_ref[:, cols] = dot_nn(r_val, d_o)
            row_ref[0:1, cols] = q_inv
            row_ref[1:2, cols] = jnp.sum(e_r, axis=0, keepdims=True)


def prepare(meta, q, g, k, v, q_gain, k_gain, count):
    rows, q_width = q.shape
    share = q_width // k.shape[1]
    total = share * rows
    each = [
        jax.ShapeDtypeStruct((HD, total), BF),
        jax.ShapeDtypeStruct((HD, total), BF),
        jax.ShapeDtypeStruct((8, total), F32),
        jax.ShapeDtypeStruct((rows, total), BF),
        jax.ShapeDtypeStruct((HD, total), F32),
        jax.ShapeDtypeStruct((rows, total), F32),
        jax.ShapeDtypeStruct((rows, HD), BF),
        jax.ShapeDtypeStruct((rows, 2 * HD), F32),
    ]
    outs = pl.pallas_call(
        functools.partial(prepare_kernel, count, share, rows, 2 * HD),
        out_shape=each * count,
        in_specs=[SMEM] + [HBM] * 4 + [VMEM] * 2,
        out_specs=[VMEM] * (KEPT * count),
        scratch_shapes=[
            pltpu.VMEM((count, rows, share * HD), BF),
            pltpu.VMEM((count, rows, share * HD), BF),
            pltpu.VMEM((count, rows, HD), BF),
            pltpu.VMEM((count, rows, HD), BF),
            pltpu.SemaphoreType.DMA((count, 4)),
        ],
        compiler_params=params(16),
        cost_estimate=pl.CostEstimate(
            flops=6 * count * total * rows * HD,
            bytes_accessed=5 * rows * q_width * 2,
            transcendentals=count * total * rows,
        ),
        name="prepare_response",
    )(meta, q, g, k, v, q_gain, k_gain)
    return [list(outs[s * KEPT : (s + 1) * KEPT]) for s in range(count)]


def attend(width, pr_ref, kept, q_gain, part_ref, at_ref, dq_ref):
    qt_ref, gt_ref, row_ref, er_ref, ot_ref, dp_ref, kh_ref, ku_ref = kept
    scale = HD ** (-0.5)
    p_key = pr_ref[0]
    p_val = pr_ref[1]
    k_hat_t = kh_ref[...].T
    p_key_t = p_key.T
    p_val_t = p_val.T
    sums = None
    for start in range(0, qt_ref.shape[1], width):
        cols = slice(start, start + width)
        q_unit = qt_ref[:, cols].astype(F32) * row_ref[0:1, cols]
        q_hat = (q_unit * q_gain).astype(BF)
        d_ob = gt_ref[:, cols]
        d_o = d_ob.astype(F32)
        e_p = jnp.exp2(dot_nn(p_key, q_hat) * (scale * LOG2E))
        inv_sum = 1.0 / (jnp.sum(e_p, axis=0, keepdims=True) + row_ref[1:2, cols])
        eb_p = e_p.astype(BF)
        eb_r = er_ref[:, cols]
        out = (dot_nn(p_val_t, eb_p) + ot_ref[:, cols]) * inv_sum
        at_ref[:, cols] = out.astype(BF)
        delta = jnp.sum(d_o * out, axis=0, keepdims=True)
        ds_p = (e_p * (dot_nn(p_val, d_ob) - delta)).astype(BF)
        ds_r = (eb_r.astype(F32) * (dp_ref[:, cols] - delta)).astype(BF)
        weight = inv_sum * scale
        q_w = (q_hat.astype(F32) * weight).astype(BF)
        d_ow = (d_o * inv_sum).astype(BF)
        d_qhat = (dot_nn(p_key_t, ds_p) + dot_nn(k_hat_t, ds_r)) * weight
        dq_ref[:, cols] = d_qhat
        terms = (
            dot_nt(ds_p, q_w),
            dot_nt(eb_p, d_ow),
            dot_nt(ds_r, q_w),
            dot_nt(eb_r, d_ow),
            d_qhat * q_unit,
        )
        sums = terms if sums is None else [a + b for a, b in zip(sums, terms)]
    d_kp, d_vp, d_kr, d_vr, q_term = sums
    part_ref[0] = d_kp.astype(BF)
    part_ref[1] = d_vp.astype(BF)
    folded = q_term[:, :HD]
    for start in range(HD, width, HD):
        folded = folded + q_term[:, start : start + HD]
    q_term = jnp.sum(folded.T, axis=0, keepdims=True)
    k_term = jnp.sum(d_kr * ku_ref[:, :HD], axis=0, keepdims=True)
    return d_kr, d_vr, q_term, k_term


def settle(width, head, live_len, kept, q_gain, k_gain, at_ref, dq_ref, d_kr, d_vr, outs, bufs, sems):
    qt_ref, row_ref, ku_ref = kept[0], kept[2], kept[7]
    a_buf, q_buf, k_buf, v_buf = bufs
    rows, wide = a_buf.shape
    share = wide // HD
    copies = []

    def send(j, buf):
        size = buf.shape[1]
        at = pl.multiple_of(head * size, size)
        copy = pltpu.make_async_copy(buf, outs[j].at[:, pl.ds(at, size)], sems.at[j])
        copy.start()
        copies.append(copy)

    att = at_ref[...].T
    live = lax.broadcasted_iota(jnp.int32, (rows, HD), 0) < live_len
    for i in range(share):
        block = att[i * rows : (i + 1) * rows, :].astype(F32)
        a_buf[:, i * HD : (i + 1) * HD] = jnp.where(live, block, 0.0).astype(BF)
    send(0, a_buf)
    v_buf[...] = d_vr.astype(BF)
    send(3, v_buf)
    k_unit = ku_ref[:, :HD]
    up_k = d_kr * k_gain
    mean_k = jnp.mean(up_k * k_unit, axis=-1, keepdims=True)
    k_buf[...] = (ku_ref[:, HD:] * (up_k - k_unit * mean_k)).astype(BF)
    send(2, k_buf)
    parts = []
    for start in range(0, share * rows, width):
        cols = slice(start, start + width)
        q_inv = row_ref[0:1, cols]
        q_unit = qt_ref[:, cols].astype(F32) * q_inv
        up = dq_ref[:, cols] * q_gain
        mean = jnp.mean(up * q_unit, axis=0, keepdims=True)
        parts.append((q_inv * (up - q_unit * mean)).astype(BF))
    d_q = jnp.concatenate(parts, axis=1).T
    for i in range(share):
        q_buf[:, i * HD : (i + 1) * HD] = d_q[i * rows : (i + 1) * rows, :]
    send(1, q_buf)
    return copies


def whole_kernel(slots, width, meta, pr_ref, gain_ref, kg_ref, acc_ref, *rest):
    count = len(slots)
    kept, rest = rest[: KEPT * count], rest[-13:]
    part_ref, gacc_ref, *rest = rest
    outs, (at_ref, dq_ref), bufs, sems = rest[:4], rest[4:6], rest[6:10], rest[10]
    q_gain = gain_ref[...]
    k_gain = kg_ref[...]
    q_sum, k_sum = acc_ref[0:1, :], acc_ref[1:2, :]
    copies = []
    for i, s in enumerate(slots):
        mine = kept[i * KEPT : (i + 1) * KEPT]
        d_kr, d_vr, q_term, k_term = attend(
            width, pr_ref.at[i], mine, q_gain, part_ref.at[i], at_ref.at[i], dq_ref.at[i]
        )
        q_sum, k_sum = q_sum + q_term, k_sum + k_term
        copies += settle(
            width, meta[s], meta[meta.shape[0] - 1], mine, q_gain, k_gain, at_ref.at[i], dq_ref.at[i],
            d_kr, d_vr, outs, [buf.at[i] for buf in bufs], sems.at[i],
        )
    gacc_ref[0:1, :] = q_sum
    gacc_ref[1:2, :] = k_sum
    for copy in copies:
        copy.wait()


def first_kernel(slots, width, pr_ref, gain_ref, acc_ref, *rest):
    count = len(slots)
    kept, (part_ref, gacc_ref, *results) = rest[: KEPT * count], rest[KEPT * count :]
    q_gain = gain_ref[...]
    q_sum, k_sum = acc_ref[0:1, :], acc_ref[1:2, :]
    for i in range(count):
        at_ref, dq_ref, dkr_ref, dvr_ref = results[4 * i : 4 * i + 4]
        d_kr, d_vr, q_term, k_term = attend(
            width, pr_ref.at[i], kept[i * KEPT : (i + 1) * KEPT], q_gain, part_ref.at[i], at_ref, dq_ref
        )
        q_sum, k_sum = q_sum + q_term, k_sum + k_term
        dkr_ref[...] = d_kr
        dvr_ref[...] = d_vr
    gacc_ref[0:1, :] = q_sum
    gacc_ref[1:2, :] = k_sum


def second_kernel(slots, width, meta, gain_ref, kg_ref, *rest):
    count = len(slots)
    kept, results = rest[: KEPT * count], rest[KEPT * count : (KEPT + 4) * count]
    outs, bufs, sems = rest[-9:-5], rest[-5:-1], rest[-1]
    copies = []
    for i, s in enumerate(slots):
        at_ref, dq_ref, dkr_ref, dvr_ref = results[4 * i : 4 * i + 4]
        copies += settle(
            width, meta[s], meta[meta.shape[0] - 1], kept[i * KEPT : (i + 1) * KEPT], gain_ref[...],
            kg_ref[...], at_ref, dq_ref, dkr_ref[...], dvr_ref[...], outs,
            [buf.at[i] for buf in bufs], sems.at[i],
        )
    for copy in copies:
        copy.wait()


def out_shapes(rows, q_width, k_width):
    widths = (q_width, q_width, k_width, k_width)
    return [jax.ShapeDtypeStruct((rows, w), BF) for w in widths]


def out_scratch(count, rows, share):
    widths = (share * HD, share * HD, HD, HD)
    return [pltpu.VMEM((count, rows, w), BF) for w in widths] + [pltpu.SemaphoreType.DMA((count, 4))]


def whole_heads(slots, meta, prompt, kept, q_gain, k_gain, acc, buffers, q_width, k_width):
    count = len(slots)
    total = kept[0][0].shape[1]
    rows = kept[0][3].shape[0]
    flat = [x for s in slots for x in kept[s]]
    outs = pl.pallas_call(
        functools.partial(whole_kernel, slots, 2 * HD),
        out_shape=[
            jax.ShapeDtypeStruct(prompt.shape, BF),
            jax.ShapeDtypeStruct(acc.shape, F32),
        ]
        + out_shapes(rows, q_width, k_width),
        in_specs=[SMEM] + [VMEM] * (4 + len(flat)) + [HBM] * len(buffers),
        out_specs=[VMEM] * 2 + [HBM] * 4,
        scratch_shapes=[pltpu.VMEM((count, HD, total), BF), pltpu.VMEM((count, HD, total), F32)]
        + out_scratch(count, rows, total // rows),
        input_output_aliases={5 + len(flat) + i: 2 + i for i in range(len(buffers))},
        compiler_params=params(16),
        name="attend_own_half",
    )(meta, prompt, q_gain, k_gain, acc, *flat, *buffers)
    return outs[0], outs[1], list(outs[2:])


def first_part(slots, prompt, kept, q_gain, acc):
    total = kept[0][0].shape[1]
    rows = kept[0][3].shape[0]
    flat = [x for s in slots for x in kept[s]]
    each = [
        jax.ShapeDtypeStruct((HD, total), BF),
        jax.ShapeDtypeStruct((HD, total), F32),
        jax.ShapeDtypeStruct((rows, HD), F32),
        jax.ShapeDtypeStruct((rows, HD), F32),
    ]
    outs = pl.pallas_call(
        functools.partial(first_kernel, slots, 2 * HD),
        out_shape=[
            jax.ShapeDtypeStruct(prompt.shape, BF),
            jax.ShapeDtypeStruct(acc.shape, F32),
        ]
        + each * len(slots),
        in_specs=[VMEM] * (3 + len(flat)),
        out_specs=[VMEM] * (2 + 4 * len(slots)),
        compiler_params=params(16),
        name="attend_other_half",
    )(prompt, q_gain, acc, *flat)
    return outs[0], outs[1], list(outs[2:])


def second_part(slots, meta, kept, q_gain, k_gain, results, buffers):
    count = len(slots)
    total = kept[0][0].shape[1]
    rows = kept[0][3].shape[0]
    flat = [x for s in slots for x in kept[s]]
    return pl.pallas_call(
        functools.partial(second_kernel, slots, 2 * HD),
        out_shape=out_shapes(rows, buffers[0].shape[1], buffers[2].shape[1]),
        in_specs=[SMEM] + [VMEM] * (2 + len(flat) + len(results)) + [HBM] * 4,
        out_specs=[HBM] * 4,
        scratch_shapes=out_scratch(count, rows, total // rows),
        input_output_aliases={3 + len(flat) + len(results) + i: i for i in range(4)},
        compiler_params=params(16),
        name="settle_other_half",
    )(meta, q_gain, k_gain, *flat, *results, *buffers)


def place_kernel(meta, *refs):
    halves, out_ref = refs[:-1], refs[-1]
    mine = meta[0] > 0
    s = 1
    for ref in halves:
        for j in range(ref.shape[0]):
            at = pl.ds(pl.multiple_of(meta[s] * HD, HD), HD)
            out_ref[:, :, at] = jnp.where(mine, ref[j], jnp.zeros_like(ref[j]))
            s += 1


def place(meta, halves):
    per, depth, rows, _ = halves[0].shape
    return pl.pallas_call(
        place_kernel,
        out_shape=jax.ShapeDtypeStruct((depth, rows, HD * per * len(halves)), BF),
        in_specs=[SMEM] + [VMEM] * len(halves),
        out_specs=VMEM,
        compiler_params=params(8),
        name="place_prompt_grad",
    )(meta, *halves)


def after(x, *others):
    return lax.optimization_barrier((x,) + others)[0]


def pair_sum(value, axis, size):
    step = 1
    while step < size:
        value = value + lax.ppermute(value, axis, [(i, i ^ step) for i in range(size)])
        step *= 2
    return value


def local(
    n_dp, n_group, queries, resp_keys, resp_values, prompt_cache, owners, lengths, q_gain, k_gain, grad_out
):
    q, g = queries[0, 0], grad_out[0, 0]
    k, v = resp_keys[0, 0], resp_values[0, 0]
    cache = prompt_cache[0, 0]
    owner = owners[0]
    live_len = lengths[0, 0]
    me = lax.axis_index("group")
    kv_heads = k.shape[1] // HD
    depth, p_rows, _ = cache.shape
    pairs = n_group == 4 and kv_heads % 2 == 0
    per = kv_heads // 2 if pairs else kv_heads
    mine_flag = (me == owner).astype(jnp.int32)
    gain_col = q_gain[:, None]
    gain_row = k_gain[None, :]
    order = jnp.arange(kv_heads, dtype=jnp.int32)
    if pairs:
        order = (order + (me % 2) * per) % kv_heads
    meta = jnp.concatenate([order, live_len[None]])
    q, g, k, v = [pltpu.with_memory_space_constraint(x, pltpu.HBM) for x in (q, g, k, v)]
    kept = prepare(meta, q, g, k, v, gain_col, gain_row, kv_heads)
    acc = jnp.zeros((2, HD), F32)

    def swap(x, step, axis="group", size=n_group):
        return lax.ppermute(x, axis, [(i, i ^ step) for i in range(size)])

    def join(a, b):
        return (a.astype(F32) + b.astype(F32)).astype(BF)

    if pairs:
        own, other = tuple(range(per)), tuple(range(per, kv_heads))
        mine, theirs = cut(order, pltpu.with_memory_space_constraint(cache, pltpu.HBM), 2, per)
        got = after(swap(theirs, 1), kept[0][2])
        mine = jnp.where(owner == me ^ 1, got, mine)
        got = swap(mine, 2)
        mine = jnp.where(owner // 2 == me // 2, mine, got)
        theirs = swap(mine, 1)
        part, acc, buffers = whole_heads(
            own, meta, mine, kept, gain_col, gain_row, acc, (), q.shape[1], k.shape[1]
        )
        sent, acc, results = first_part(other, after(theirs, part), kept, gain_col, acc)
        buffers = list(second_part(other, meta, kept, gain_col, gain_row, results, buffers))
        gains = acc + swap(acc, 1)
        part = join(part, after(swap(sent, 1), gains, buffers[2]))
        gains = after(gains, part)
        gains = gains + swap(gains, 2)
        gains = pair_sum(gains, "dp", n_dp)
        part = join(part, after(swap(part, 2), gains))
        placed = place(jnp.concatenate([mine_flag[None], order]), [part, swap(part, 1)])
    else:
        cache = lax.psum(jnp.where(me == owner, cache, jnp.zeros_like(cache)), "group")
        (prompt,) = cut(order, cache, 1, kv_heads)
        part, acc, buffers = whole_heads(
            tuple(range(kv_heads)), meta, prompt, kept, gain_col, gain_row, acc, (), q.shape[1], k.shape[1]
        )
        total = jnp.transpose(part, (1, 2, 0, 3)).reshape(depth, p_rows, kv_heads * HD)
        total = lax.psum(total.astype(F32), "group").astype(BF)
        placed = jnp.where(mine_flag > 0, total, jnp.zeros((), BF))
        gains = pair_sum(pair_sum(acc, "group", n_group), "dp", n_dp)
    attended, d_query, d_key, d_value = buffers
    return (
        attended[None, None],
        d_query[None, None],
        d_key[None, None],
        d_value[None, None],
        placed[None, None],
        gains,
    )


def solution(mesh):
    in_specs = (
        P("dp", "group", None, None),
        P("dp", "group", None, None),
        P("dp", "group", None, None),
        P("dp", "group", None, None, None),
        P("dp"),
        P("dp", "group"),
        P(),
        P(),
        P("dp", "group", None, None),
    )
    out_specs = (
        P("dp", "group", None, None),
        P("dp", "group", None, None),
        P("dp", "group", None, None),
        P("dp", "group", None, None),
        P("dp", "group", None, None, None),
        P(),
    )
    body = functools.partial(local, mesh.shape["dp"], mesh.shape["group"])
    return jax.shard_map(body, mesh=mesh, in_specs=in_specs, out_specs=out_specs, check_vma=False)
```

```python
import functools

import jax
import jax.numpy as jnp
from jax import lax
from jax.experimental import pallas as pl
from jax.experimental.pallas import tpu as pltpu
from jax.sharding import PartitionSpec as P

HD = 128
EPS = 1e-06
LOG2E = 1.4426950408889634
BF = jnp.bfloat16
F32 = jnp.float32


def dot_nn(a, b):
    return lax.dot_general(a, b, (((1,), (0,)), ((), ())), preferred_element_type=F32)


def dot_nt(a, b):
    return lax.dot_general(a, b, (((1,), (1,)), ((), ())), preferred_element_type=F32)


VMEM = pl.BlockSpec(memory_space=pltpu.VMEM)
SMEM = pl.BlockSpec(memory_space=pltpu.SMEM)
HBM = pl.BlockSpec(memory_space=pltpu.HBM)


def params(mib):
    return pltpu.CompilerParams(vmem_limit_bytes=mib * 2**20)


def cut_kernel(per, order, cache_ref, *rest):
    outs, sems = rest[:-1], rest[-1]
    copies = []
    for i, out in enumerate(outs):
        for j in range(per):
            s = i * per + j
            at = pl.ds(pl.multiple_of(order[s] * HD, HD), HD)
            copy = pltpu.make_async_copy(cache_ref.at[:, :, at], out.at[j], sems.at[s])
            copy.start()
            copies.append(copy)
    for copy in copies:
        copy.wait()


def cut(order, cache, halves, per):
    depth, rows, _ = cache.shape
    return pl.pallas_call(
        functools.partial(cut_kernel, per),
        out_shape=[jax.ShapeDtypeStruct((per, depth, rows, HD), BF)] * halves,
        in_specs=[SMEM, HBM],
        out_specs=[VMEM] * halves,
        scratch_shapes=[pltpu.SemaphoreType.DMA((halves * per,))],
        compiler_params=params(4),
        name="cut_prompt",
    )(order, cache)


def views(low, high, key):
    rows = key.shape[0]
    return (
        low.at[0:HD, :],
        low.at[HD : 2 * HD, :],
        high.at[HD + rows : HD + rows + 8, :],
        low.at[2 * HD : 2 * HD + rows, :],
        high.at[0:HD, :],
        high.at[HD : HD + rows, :],
        key.at[:, 2 * HD : 3 * HD],
        key.at[:, 0 : 2 * HD],
    )


def kept_shapes(count, rows, total):
    return [
        ((count, 2 * HD + rows, total), BF),
        ((count, HD + rows + 8, total), F32),
        ((count, rows, 3 * HD), F32),
    ]


def prepare_kernel(count, share, rows, width, turn, meta, q_in, g_in, k_in, v_in, gain_ref, kg_ref, *rest):
    kept, (low, high, key, q_buf, g_buf, k_buf, v_buf, sems, out_sems) = rest[-12:-9], rest[-9:]

    @pl.when(meta[count + 1] == turn)
    def _():
        live_len = meta[count]
        scale = HD ** (-0.5)
        wide = share * HD
        copies = []
        for s in range(count):
            group = []
            for j, (src, buf, size) in enumerate(
                ((q_in, q_buf, wide), (k_in, k_buf, HD), (g_in, g_buf, wide), (v_in, v_buf, HD))
            ):
                at = pl.multiple_of(meta[s] * size, size)
                copy = pltpu.make_async_copy(src.at[:, pl.ds(at, size)], buf.at[s], sems.at[s, j])
                copy.start()
                group.append(copy)
            copies.append(group)
        q_gain = gain_ref[...]
        k_gain = kg_ref[...]
        sent = []
        for s in range(count):
            qt_ref, gt_ref, row_ref, er_ref, ot_ref, dp_ref, kh_ref, ku_ref = views(
                low.at[s], high.at[s], key.at[s]
            )
            for copy in copies[s]:
                copy.wait()
            q_t = jnp.concatenate([q_buf[s, :, i * HD : (i + 1) * HD] for i in range(share)], axis=0).T
            g_t = jnp.concatenate([g_buf[s, :, i * HD : (i + 1) * HD] for i in range(share)], axis=0).T
            qt_ref[...] = q_t
            raw_k = k_buf[s].astype(F32)
            k_inv = lax.rsqrt(jnp.mean(raw_k * raw_k, axis=-1, keepdims=True) + EPS)
            k_unit = raw_k * k_inv
            k_hat = (k_unit * k_gain).astype(BF)
            kh_ref[...] = k_hat.astype(F32)
            ku_ref[:, :HD] = k_unit
            ku_ref[:, HD:] = jnp.broadcast_to(k_inv, (rows, HD))
            r_val = v_buf[s]
            r_val_t = r_val.T
            for start in range(0, share * rows, width):
                cols = slice(start, start + width)
                token = (lax.broadcasted_iota(jnp.int32, (1, width), 1) + start) % rows
                raw_q = q_t[:, cols].astype(F32)
                q_inv = lax.rsqrt(jnp.mean(raw_q * raw_q, axis=0, keepdims=True) + EPS)
                q_hat = (raw_q * q_inv * q_gain).astype(BF)
                d_o = jnp.where(token < live_len, g_t[:, cols].astype(F32), 0.0).astype(BF)
                gt_ref[:, cols] = d_o
                causal = lax.broadcasted_iota(jnp.int32, (rows, width), 0) <= token
                e_r = jnp.where(causal, jnp.exp2(dot_nn(k_hat, q_hat) * (scale * LOG2E)), 0.0)
                eb_r = e_r.astype(BF)
                er_ref[:, cols] = eb_r
                ot_ref[:, cols] = dot_nn(r_val_t, eb_r)
                dp_ref[:, cols] = dot_nn(r_val, d_o)
                row_ref[0:1, cols] = q_inv
                row_ref[1:2, cols] = jnp.sum(e_r, axis=0, keepdims=True)
            for j, buf in enumerate((low, high, key)):
                copy = pltpu.make_async_copy(buf.at[s], kept[j].at[s], out_sems.at[s, j])
                copy.start()
                sent.append(copy)
        for copy in sent:
            copy.wait()


def prepare(turn, meta, q, g, k, v, q_gain, k_gain, count, kept):
    rows, q_width = q.shape
    share = q_width // k.shape[1]
    shapes = kept_shapes(count, rows, share * rows)
    return pl.pallas_call(
        functools.partial(prepare_kernel, count, share, rows, 2 * HD, turn),
        out_shape=[jax.ShapeDtypeStruct(*x) for x in shapes],
        in_specs=[SMEM] + [HBM] * 4 + [VMEM] * 2 + [HBM] * len(kept),
        out_specs=[HBM] * 3,
        scratch_shapes=[pltpu.VMEM(*x) for x in shapes]
        + [
            pltpu.VMEM((count, rows, share * HD), BF),
            pltpu.VMEM((count, rows, share * HD), BF),
            pltpu.VMEM((count, rows, HD), BF),
            pltpu.VMEM((count, rows, HD), BF),
            pltpu.SemaphoreType.DMA((count, 4)),
            pltpu.SemaphoreType.DMA((count, 3)),
        ],
        input_output_aliases={7 + i: i for i in range(len(kept))},
        compiler_params=params(24),
        name="prepare_response",
    )(meta, q, g, k, v, q_gain, k_gain, *kept)


def fetch(slots, kept, bufs, sems):
    copies = []
    for i, s in enumerate(slots):
        group = [
            pltpu.make_async_copy(src.at[s], buf.at[i], sems.at[i, j])
            for j, (src, buf) in enumerate(zip(kept, bufs))
        ]
        for copy in group:
            copy.start()
        copies.append(group)
    return copies


def fetch_scratch(count, kept):
    shapes = [pltpu.VMEM((count,) + x.shape[1:], x.dtype) for x in kept]
    return shapes + [pltpu.SemaphoreType.DMA((count, 3))]


def attend(width, pr_ref, kept, q_gain, part_ref, at_ref, dq_ref):
    qt_ref, gt_ref, row_ref, er_ref, ot_ref, dp_ref, kh_ref, ku_ref = kept
    scale = HD ** (-0.5)
    p_key = pr_ref[0]
    p_val = pr_ref[1]
    k_hat_t = kh_ref[...].astype(BF).T
    p_key_t = p_key.T
    p_val_t = p_val.T
    sums = None
    for start in range(0, qt_ref.shape[1], width):
        cols = slice(start, start + width)
        q_unit = qt_ref[:, cols].astype(F32) * row_ref[0:1, cols]
        q_hat = (q_unit * q_gain).astype(BF)
        d_ob = gt_ref[:, cols]
        d_o = d_ob.astype(F32)
        e_p = jnp.exp2(dot_nn(p_key, q_hat) * (scale * LOG2E))
        inv_sum = 1.0 / (jnp.sum(e_p, axis=0, keepdims=True) + row_ref[1:2, cols])
        eb_p = e_p.astype(BF)
        eb_r = er_ref[:, cols]
        out = (dot_nn(p_val_t, eb_p) + ot_ref[:, cols]) * inv_sum
        at_ref[:, cols] = out.astype(BF)
        delta = jnp.sum(d_o * out, axis=0, keepdims=True)
        ds_p = (e_p * (dot_nn(p_val, d_ob) - delta)).astype(BF)
        ds_r = (eb_r.astype(F32) * (dp_ref[:, cols] - delta)).astype(BF)
        weight = inv_sum * scale
        q_w = (q_hat.astype(F32) * weight).astype(BF)
        d_ow = (d_o * inv_sum).astype(BF)
        d_qhat = (dot_nn(p_key_t, ds_p) + dot_nn(k_hat_t, ds_r)) * weight
        dq_ref[:, cols] = d_qhat
        terms = (
            dot_nt(ds_p, q_w),
            dot_nt(eb_p, d_ow),
            dot_nt(ds_r, q_w),
            dot_nt(eb_r, d_ow),
            d_qhat * q_unit,
        )
        sums = terms if sums is None else [a + b for a, b in zip(sums, terms)]
    d_kp, d_vp, d_kr, d_vr, q_term = sums
    part_ref[0] = d_kp.astype(BF)
    part_ref[1] = d_vp.astype(BF)
    folded = q_term[:, :HD]
    for start in range(HD, width, HD):
        folded = folded + q_term[:, start : start + HD]
    q_term = jnp.sum(folded.T, axis=0, keepdims=True)
    k_term = jnp.sum(d_kr * ku_ref[:, :HD], axis=0, keepdims=True)
    return d_kr, d_vr, q_term, k_term


def settle(width, head, live_len, kept, q_gain, k_gain, at_ref, dq_ref, d_kr, d_vr, outs, bufs, sems):
    qt_ref, row_ref, ku_ref = kept[0], kept[2], kept[7]
    a_buf, q_buf, k_buf, v_buf = bufs
    rows, wide = a_buf.shape
    share = wide // HD
    copies = []

    def send(j, buf):
        size = buf.shape[1]
        at = pl.multiple_of(head * size, size)
        copy = pltpu.make_async_copy(buf, outs[j].at[:, pl.ds(at, size)], sems.at[j])
        copy.start()
        copies.append(copy)

    att = at_ref[...].T
    live = lax.broadcasted_iota(jnp.int32, (rows, HD), 0) < live_len
    for i in range(share):
        block = att[i * rows : (i + 1) * rows, :].astype(F32)
        a_buf[:, i * HD : (i + 1) * HD] = jnp.where(live, block, 0.0).astype(BF)
    send(0, a_buf)
    v_buf[...] = d_vr.astype(BF)
    send(3, v_buf)
    k_unit = ku_ref[:, :HD]
    up_k = d_kr * k_gain
    mean_k = jnp.mean(up_k * k_unit, axis=-1, keepdims=True)
    k_buf[...] = (ku_ref[:, HD:] * (up_k - k_unit * mean_k)).astype(BF)
    send(2, k_buf)
    parts = []
    for start in range(0, share * rows, width):
        cols = slice(start, start + width)
        q_inv = row_ref[0:1, cols]
        q_unit = qt_ref[:, cols].astype(F32) * q_inv
        up = dq_ref[:, cols] * q_gain
        mean = jnp.mean(up * q_unit, axis=0, keepdims=True)
        parts.append((q_inv * (up - q_unit * mean)).astype(BF))
    d_q = jnp.concatenate(parts, axis=1).T
    for i in range(share):
        q_buf[:, i * HD : (i + 1) * HD] = d_q[i * rows : (i + 1) * rows, :]
    send(1, q_buf)
    return copies


def whole_kernel(slots, width, meta, pr_ref, gain_ref, kg_ref, acc_ref, low, high, key, *rest):
    count = len(slots)
    part_ref, gacc_ref, *rest = rest
    outs, (at_ref, dq_ref), bufs, sems, store, got_sems = rest[:4], rest[4:6], rest[6:10], rest[10], rest[11:14], rest[14]
    fetched = fetch(slots, (low, high, key), store, got_sems)
    q_gain = gain_ref[...]
    k_gain = kg_ref[...]
    q_sum, k_sum = acc_ref[0:1, :], acc_ref[1:2, :]
    copies = []
    for i, s in enumerate(slots):
        for copy in fetched[i]:
            copy.wait()
        mine = views(*[x.at[i] for x in store])
        d_kr, d_vr, q_term, k_term = attend(
            width, pr_ref.at[i], mine, q_gain, part_ref.at[i], at_ref.at[i], dq_ref.at[i]
        )
        q_sum, k_sum = q_sum + q_term, k_sum + k_term
        copies += settle(
            width, meta[s], meta[meta.shape[0] - 2], mine, q_gain, k_gain, at_ref.at[i], dq_ref.at[i],
            d_kr, d_vr, outs, [buf.at[i] for buf in bufs], sems.at[i],
        )
    gacc_ref[0:1, :] = q_sum
    gacc_ref[1:2, :] = k_sum
    for copy in copies:
        copy.wait()


def first_kernel(slots, width, pr_ref, gain_ref, acc_ref, low, high, key, part_ref, gacc_ref, *rest):
    count = len(slots)
    results, store, got_sems = rest[: 4 * count], rest[4 * count : 4 * count + 3], rest[-1]
    fetched = fetch(slots, (low, high, key), store, got_sems)
    q_gain = gain_ref[...]
    q_sum, k_sum = acc_ref[0:1, :], acc_ref[1:2, :]
    for i in range(count):
        for copy in fetched[i]:
            copy.wait()
        at_ref, dq_ref, dkr_ref, dvr_ref = results[4 * i : 4 * i + 4]
        mine = views(*[x.at[i] for x in store])
        d_kr, d_vr, q_term, k_term = attend(
            width, pr_ref.at[i], mine, q_gain, part_ref.at[i], at_ref, dq_ref
        )
        q_sum, k_sum = q_sum + q_term, k_sum + k_term
        dkr_ref[...] = d_kr
        dvr_ref[...] = d_vr
    gacc_ref[0:1, :] = q_sum
    gacc_ref[1:2, :] = k_sum


def second_kernel(slots, width, meta, gain_ref, kg_ref, low, high, key, *rest):
    count = len(slots)
    results, rest = rest[: 4 * count], rest[-13:]
    outs, bufs, sems, store, got_sems = rest[:4], rest[4:8], rest[8], rest[9:12], rest[12]
    fetched = fetch(slots, (low, high, key), store, got_sems)
    copies = []
    for i, s in enumerate(slots):
        for copy in fetched[i]:
            copy.wait()
        at_ref, dq_ref, dkr_ref, dvr_ref = results[4 * i : 4 * i + 4]
        copies += settle(
            width, meta[s], meta[meta.shape[0] - 2], views(*[x.at[i] for x in store]), gain_ref[...],
            kg_ref[...], at_ref, dq_ref, dkr_ref[...], dvr_ref[...], outs,
            [buf.at[i] for buf in bufs], sems.at[i],
        )
    for copy in copies:
        copy.wait()


def out_shapes(rows, q_width, k_width):
    widths = (q_width, q_width, k_width, k_width)
    return [jax.ShapeDtypeStruct((rows, w), BF) for w in widths]


def out_scratch(count, rows, share):
    widths = (share * HD, share * HD, HD, HD)
    return [pltpu.VMEM((count, rows, w), BF) for w in widths] + [pltpu.SemaphoreType.DMA((count, 4))]


def whole_heads(slots, meta, prompt, kept, q_gain, k_gain, acc, q_width, k_width):
    count = len(slots)
    total = kept[0].shape[2]
    rows = kept[2].shape[1]
    outs = pl.pallas_call(
        functools.partial(whole_kernel, slots, 2 * HD),
        out_shape=[
            jax.ShapeDtypeStruct(prompt.shape, BF),
            jax.ShapeDtypeStruct(acc.shape, F32),
        ]
        + out_shapes(rows, q_width, k_width),
        in_specs=[SMEM] + [VMEM] * 4 + [HBM] * 3,
        out_specs=[VMEM] * 2 + [HBM] * 4,
        scratch_shapes=[pltpu.VMEM((count, HD, total), BF), pltpu.VMEM((count, HD, total), F32)]
        + out_scratch(count, rows, total // rows)
        + fetch_scratch(count, kept),
        compiler_params=params(24),
        name="attend_own_half",
    )(meta, prompt, q_gain, k_gain, acc, *kept)
    return outs[0], outs[1], list(outs[2:])


def first_part(slots, prompt, kept, q_gain, acc):
    total = kept[0].shape[2]
    rows = kept[2].shape[1]
    each = [
        jax.ShapeDtypeStruct((HD, total), BF),
        jax.ShapeDtypeStruct((HD, total), F32),
        jax.ShapeDtypeStruct((rows, HD), F32),
        jax.ShapeDtypeStruct((rows, HD), F32),
    ]
    outs = pl.pallas_call(
        functools.partial(first_kernel, slots, 2 * HD),
        out_shape=[
            jax.ShapeDtypeStruct(prompt.shape, BF),
            jax.ShapeDtypeStruct(acc.shape, F32),
        ]
        + each * len(slots),
        in_specs=[VMEM] * 3 + [HBM] * 3,
        out_specs=[VMEM] * (2 + 4 * len(slots)),
        scratch_shapes=fetch_scratch(len(slots), kept),
        compiler_params=params(24),
        name="attend_other_half",
    )(prompt, q_gain, acc, *kept)
    return outs[0], outs[1], list(outs[2:])


def second_part(slots, meta, kept, q_gain, k_gain, results, buffers):
    count = len(slots)
    total = kept[0].shape[2]
    rows = kept[2].shape[1]
    return pl.pallas_call(
        functools.partial(second_kernel, slots, 2 * HD),
        out_shape=out_shapes(rows, buffers[0].shape[1], buffers[2].shape[1]),
        in_specs=[SMEM] + [VMEM] * 2 + [HBM] * 3 + [VMEM] * len(results) + [HBM] * 4,
        out_specs=[HBM] * 4,
        scratch_shapes=out_scratch(count, rows, total // rows) + fetch_scratch(count, kept),
        input_output_aliases={6 + len(results) + i: i for i in range(4)},
        compiler_params=params(24),
        name="settle_other_half",
    )(meta, q_gain, k_gain, *kept, *results, *buffers)


def place_kernel(meta, *refs):
    halves, out_ref = refs[:-1], refs[-1]
    mine = meta[0] > 0
    s = 1
    for ref in halves:
        for j in range(ref.shape[0]):
            at = pl.ds(pl.multiple_of(meta[s] * HD, HD), HD)
            out_ref[:, :, at] = jnp.where(mine, ref[j], jnp.zeros_like(ref[j]))
            s += 1


def place(meta, halves):
    per, depth, rows, _ = halves[0].shape
    return pl.pallas_call(
        place_kernel,
        out_shape=jax.ShapeDtypeStruct((depth, rows, HD * per * len(halves)), BF),
        in_specs=[SMEM] + [VMEM] * len(halves),
        out_specs=VMEM,
        compiler_params=params(8),
        name="place_prompt_grad",
    )(meta, *halves)


def after(x, *others):
    return lax.optimization_barrier((x,) + others)[0]


def pair_sum(value, axis, size):
    step = 1
    while step < size:
        value = value + lax.ppermute(value, axis, [(i, i ^ step) for i in range(size)])
        step *= 2
    return value


def local(
    n_dp, n_group, queries, resp_keys, resp_values, prompt_cache, owners, lengths, q_gain, k_gain, grad_out
):
    q, g = queries[0, 0], grad_out[0, 0]
    k, v = resp_keys[0, 0], resp_values[0, 0]
    cache = prompt_cache[0, 0]
    owner = owners[0]
    live_len = lengths[0, 0]
    me = lax.axis_index("group")
    kv_heads = k.shape[1] // HD
    depth, p_rows, _ = cache.shape
    pairs = n_group == 4 and kv_heads % 2 == 0
    per = kv_heads // 2 if pairs else kv_heads
    mine_flag = (me == owner).astype(jnp.int32)
    gain_col = q_gain[:, None]
    gain_row = k_gain[None, :]
    order = jnp.arange(kv_heads, dtype=jnp.int32)
    if pairs:
        order = (order + (me % 2) * per) % kv_heads
    turn = lax.axis_index("dp") % 2 if pairs else jnp.int32(0)
    meta = jnp.concatenate([order, jnp.stack([live_len, turn.astype(jnp.int32)])])
    q, g, k, v = [pltpu.with_memory_space_constraint(x, pltpu.HBM) for x in (q, g, k, v)]
    kept = prepare(0, meta, q, g, k, v, gain_col, gain_row, kv_heads, ())
    acc = jnp.zeros((2, HD), F32)

    def swap(x, step, axis="group", size=n_group):
        return lax.ppermute(x, axis, [(i, i ^ step) for i in range(size)])

    def join(a, b):
        return (a.astype(F32) + b.astype(F32)).astype(BF)

    if pairs:
        own, other = tuple(range(per)), tuple(range(per, kv_heads))
        mine, theirs = cut(order, pltpu.with_memory_space_constraint(cache, pltpu.HBM), 2, per)
        got = swap(after(theirs, kept[2]), 1)
        kept = prepare(1, meta, q, g, k, v, gain_col, gain_row, kv_heads, kept)
        got = after(got, kept[2])
        mine = jnp.where(owner == me ^ 1, got, mine)
        got = swap(mine, 2)
        mine = jnp.where(owner // 2 == me // 2, mine, got)
        theirs = swap(mine, 1)
        part, acc, buffers = whole_heads(
            own, meta, mine, kept, gain_col, gain_row, acc, q.shape[1], k.shape[1]
        )
        sent, acc, results = first_part(other, after(theirs, part), kept, gain_col, acc)
        gains = acc + swap(acc, 1)
        gains = gains + swap(gains, 2)
        part = join(part, after(swap(sent, 1), gains))
        results[0] = after(results[0], part)
        buffers = list(second_part(other, meta, kept, gain_col, gain_row, results, buffers))
        gains = after(gains, part)
        step = 1
        while 2 * step < n_dp:
            gains = gains + swap(gains, step, "dp", n_dp)
            step *= 2
        part = join(part, after(swap(part, 2), gains, buffers[2]))
        back = swap(part, 1)
        gains = after(gains, part)
        gains = gains + swap(gains, step, "dp", n_dp)
        placed = place(jnp.concatenate([mine_flag[None], order]), [part, back])
    else:
        cache = lax.psum(jnp.where(me == owner, cache, jnp.zeros_like(cache)), "group")
        (prompt,) = cut(order, cache, 1, kv_heads)
        part, acc, buffers = whole_heads(
            tuple(range(kv_heads)), meta, prompt, kept, gain_col, gain_row, acc, q.shape[1], k.shape[1]
        )
        total = jnp.transpose(part, (1, 2, 0, 3)).reshape(depth, p_rows, kv_heads * HD)
        total = lax.psum(total.astype(F32), "group").astype(BF)
        placed = jnp.where(mine_flag > 0, total, jnp.zeros((), BF))
        gains = pair_sum(pair_sum(acc, "group", n_group), "dp", n_dp)
    attended, d_query, d_key, d_value = buffers
    return (
        attended[None, None],
        d_query[None, None],
        d_key[None, None],
        d_value[None, None],
        placed[None, None],
        gains,
    )


def solution(mesh):
    in_specs = (
        P("dp", "group", None, None),
        P("dp", "group", None, None),
        P("dp", "group", None, None),
        P("dp", "group", None, None, None),
        P("dp"),
        P("dp", "group"),
        P(),
        P(),
        P("dp", "group", None, None),
    )
    out_specs = (
        P("dp", "group", None, None),
        P("dp", "group", None, None),
        P("dp", "group", None, None),
        P("dp", "group", None, None),
        P("dp", "group", None, None, None),
        P(),
    )
    body = functools.partial(local, mesh.shape["dp"], mesh.shape["group"])
    return jax.shard_map(body, mesh=mesh, in_specs=in_specs, out_specs=out_specs, check_vma=False)
```

```python
import functools

import jax
import jax.numpy as jnp
from jax import lax
from jax.experimental import pallas as pl
from jax.experimental.pallas import tpu as pltpu
from jax.sharding import PartitionSpec as P

HD = 128
EPS = 1e-06
LOG2E = 1.4426950408889634
BF = jnp.bfloat16
F32 = jnp.float32


def dot_nn(a, b):
    return lax.dot_general(a, b, (((1,), (0,)), ((), ())), preferred_element_type=F32)


def dot_nt(a, b):
    return lax.dot_general(a, b, (((1,), (1,)), ((), ())), preferred_element_type=F32)


VMEM = pl.BlockSpec(memory_space=pltpu.VMEM)
SMEM = pl.BlockSpec(memory_space=pltpu.SMEM)
HBM = pl.BlockSpec(memory_space=pltpu.HBM)


def params(mib):
    return pltpu.CompilerParams(vmem_limit_bytes=mib * 2**20)


def cut_kernel(order, cache_ref, *rest):
    outs, sems = rest[:-1], rest[-1]
    copies = []
    for i, out in enumerate(outs):
        at = pl.multiple_of(order[i] * HD, HD)
        copy = pltpu.make_async_copy(cache_ref.at[:, :, pl.ds(at, HD)], out, sems.at[i])
        copy.start()
        copies.append(copy)
    for copy in copies:
        copy.wait()


def cut(order, cache, count):
    depth, rows, _ = cache.shape
    return pl.pallas_call(
        cut_kernel,
        out_shape=[jax.ShapeDtypeStruct((depth, rows, HD), BF)] * count,
        in_specs=[SMEM, HBM],
        out_specs=[VMEM] * count,
        scratch_shapes=[pltpu.SemaphoreType.DMA((count,))],
        compiler_params=params(4),
        name="cut_prompt",
    )(order, cache)


def pick_kernel(which, *refs):
    picked = refs[0][...]
    for i in range(1, len(refs) - 1):
        picked = jnp.where(which[0] == i, refs[i][...], picked)
    refs[-1][...] = picked


def pick(which, blocks):
    return pl.pallas_call(
        pick_kernel,
        out_shape=jax.ShapeDtypeStruct(blocks[0].shape, BF),
        in_specs=[SMEM] + [VMEM] * len(blocks),
        out_specs=VMEM,
        compiler_params=params(4),
        name="pick_owner",
    )(which, *blocks)


KEPT = 8


def prepare_kernel(turn, count, share, rows, width, meta, q_in, g_in, k_in, v_in, gain_ref, kg_ref, *rest):
    tail = count * KEPT + 6

    @pl.when(meta[count + 1] == turn)
    def _():
        prepare_body(
            count, share, rows, width, meta, q_in, g_in, k_in, v_in, gain_ref, kg_ref, *rest[-tail:]
        )

    if len(rest) > tail:

        @pl.when(meta[count + 1] != turn)
        def _():
            for old, new in zip(rest[:-tail], rest[-tail:-6]):
                new[...] = old[...]


def prepare_body(count, share, rows, width, meta, q_in, g_in, k_in, v_in, gain_ref, kg_ref, *rest):
    outs, (q_buf, g_buf, k_buf, v_buf, gain_buf, sems) = rest[:-6], rest[-6:]
    live_len = meta[count]
    scale = HD ** (-0.5)
    wide = share * HD
    copies = []
    for s in range(count):
        group = []
        for j, (src, buf, size) in enumerate(
            ((q_in, q_buf, wide), (k_in, k_buf, HD), (g_in, g_buf, wide), (v_in, v_buf, HD))
        ):
            at = pl.multiple_of(meta[s] * size, size)
            copy = pltpu.make_async_copy(src.at[:, pl.ds(at, size)], buf.at[s], sems.at[s, j])
            copy.start()
            group.append(copy)
        copies.append(group)
    gains = []
    for j, src in enumerate((gain_ref, kg_ref)):
        copy = pltpu.make_async_copy(src, gain_buf.at[j], sems.at[count, j])
        copy.start()
        gains.append(copy)
    for copy in gains:
        copy.wait()
    q_gain = jnp.broadcast_to(gain_buf[0].reshape(1, HD), (8, HD)).T[:, 0:1]
    k_gain = gain_buf[1].reshape(1, HD)
    for s in range(count):
        qt_ref, gt_ref, row_ref, er_ref, ot_ref, dp_ref, kh_ref, ku_ref = outs[s * KEPT : (s + 1) * KEPT]
        for copy in copies[s]:
            copy.wait()
        q_t = jnp.concatenate([q_buf[s, :, i * HD : (i + 1) * HD] for i in range(share)], axis=0).T
        g_t = jnp.concatenate([g_buf[s, :, i * HD : (i + 1) * HD] for i in range(share)], axis=0).T
        qt_ref[...] = q_t
        raw_k = k_buf[s].astype(F32)
        k_inv = lax.rsqrt(jnp.mean(raw_k * raw_k, axis=-1, keepdims=True) + EPS)
        k_unit = raw_k * k_inv
        k_hat = (k_unit * k_gain).astype(BF)
        kh_ref[...] = k_hat
        ku_ref[:, :HD] = k_unit
        ku_ref[:, HD:] = jnp.broadcast_to(k_inv, (rows, HD))
        r_val = v_buf[s]
        r_val_t = r_val.T
        for start in range(0, share * rows, width):
            cols = slice(start, start + width)
            token = (lax.broadcasted_iota(jnp.int32, (1, width), 1) + start) % rows
            raw_q = q_t[:, cols].astype(F32)
            q_inv = lax.rsqrt(jnp.mean(raw_q * raw_q, axis=0, keepdims=True) + EPS)
            q_hat = (raw_q * q_inv * q_gain).astype(BF)
            d_o = jnp.where(token < live_len, g_t[:, cols].astype(F32), 0.0).astype(BF)
            gt_ref[:, cols] = d_o
            causal = lax.broadcasted_iota(jnp.int32, (rows, width), 0) <= token
            e_r = jnp.where(causal, jnp.exp2(dot_nn(k_hat, q_hat) * (scale * LOG2E)), 0.0)
            eb_r = e_r.astype(BF)
            er_ref[:, cols] = eb_r
            ot_ref[:, cols] = dot_nn(r_val_t, eb_r)
            dp_ref[:, cols] = dot_nn(r_val, d_o)
            row_ref[0:1, cols] = q_inv
            row_ref[1:2, cols] = jnp.sum(e_r, axis=0, keepdims=True)


def prepare(turn, meta, q, g, k, v, q_gain, k_gain, count, before):
    rows, q_width = q.shape
    share = q_width // k.shape[1]
    total = share * rows
    each = [
        jax.ShapeDtypeStruct((HD, total), BF),
        jax.ShapeDtypeStruct((HD, total), BF),
        jax.ShapeDtypeStruct((8, total), F32),
        jax.ShapeDtypeStruct((rows, total), BF),
        jax.ShapeDtypeStruct((HD, total), F32),
        jax.ShapeDtypeStruct((rows, total), F32),
        jax.ShapeDtypeStruct((rows, HD), BF),
        jax.ShapeDtypeStruct((rows, 2 * HD), F32),
    ]
    outs = pl.pallas_call(
        functools.partial(prepare_kernel, turn, count, share, rows, 2 * HD),
        out_shape=each * count,
        in_specs=[SMEM] + [HBM] * 6 + [VMEM] * (KEPT * len(before)),
        out_specs=[VMEM] * (KEPT * count),
        scratch_shapes=[
            pltpu.VMEM((count, rows, share * HD), BF),
            pltpu.VMEM((count, rows, share * HD), BF),
            pltpu.VMEM((count, rows, HD), BF),
            pltpu.VMEM((count, rows, HD), BF),
            pltpu.VMEM((2, HD), F32),
            pltpu.SemaphoreType.DMA((count + 1, 4)),
        ],
        compiler_params=params(16),
        cost_estimate=pl.CostEstimate(
            flops=6 * count * total * rows * HD,
            bytes_accessed=5 * rows * q_width * 2,
            transcendentals=count * total * rows,
        ),
        name="prepare_response",
    )(meta, q, g, k, v, q_gain, k_gain, *[x for group in before for x in group])
    return [list(outs[s * KEPT : (s + 1) * KEPT]) for s in range(count)]


def attend(width, pr_ref, kept, q_gain, acc_ref, part_ref, at_ref, dq_ref, gacc_ref):
    qt_ref, gt_ref, row_ref, er_ref, ot_ref, dp_ref, kh_ref, ku_ref = kept
    scale = HD ** (-0.5)
    p_key = pr_ref[0]
    p_val = pr_ref[1]
    k_hat_t = kh_ref[...].T
    p_key_t = p_key.T
    p_val_t = p_val.T
    sums = None
    for start in range(0, qt_ref.shape[1], width):
        cols = slice(start, start + width)
        q_unit = qt_ref[:, cols].astype(F32) * row_ref[0:1, cols]
        q_hat = (q_unit * q_gain).astype(BF)
        d_ob = gt_ref[:, cols]
        d_o = d_ob.astype(F32)
        e_p = jnp.exp2(dot_nn(p_key, q_hat) * (scale * LOG2E))
        inv_sum = 1.0 / (jnp.sum(e_p, axis=0, keepdims=True) + row_ref[1:2, cols])
        eb_p = e_p.astype(BF)
        eb_r = er_ref[:, cols]
        out = (dot_nn(p_val_t, eb_p) + ot_ref[:, cols]) * inv_sum
        at_ref[:, cols] = out.astype(BF)
        delta = jnp.sum(d_o * out, axis=0, keepdims=True)
        ds_p = (e_p * (dot_nn(p_val, d_ob) - delta)).astype(BF)
        ds_r = (eb_r.astype(F32) * (dp_ref[:, cols] - delta)).astype(BF)
        weight = inv_sum * scale
        q_w = (q_hat.astype(F32) * weight).astype(BF)
        d_ow = (d_o * inv_sum).astype(BF)
        d_qhat = (dot_nn(p_key_t, ds_p) + dot_nn(k_hat_t, ds_r)) * weight
        dq_ref[:, cols] = d_qhat
        terms = (
            dot_nt(ds_p, q_w),
            dot_nt(eb_p, d_ow),
            dot_nt(ds_r, q_w),
            dot_nt(eb_r, d_ow),
            d_qhat * q_unit,
        )
        sums = terms if sums is None else [a + b for a, b in zip(sums, terms)]
    d_kp, d_vp, d_kr, d_vr, q_term = sums
    part_ref[0] = d_kp.astype(BF)
    part_ref[1] = d_vp.astype(BF)
    folded = q_term[:, :HD]
    for start in range(HD, width, HD):
        folded = folded + q_term[:, start : start + HD]
    gacc_ref[0:1, :] = acc_ref[0:1, :] + jnp.sum(folded.T, axis=0, keepdims=True)
    gacc_ref[1:2, :] = acc_ref[1:2, :] + jnp.sum(d_kr * ku_ref[:, :HD], axis=0, keepdims=True)
    return d_kr, d_vr


def settle(width, head, live_len, kept, q_gain, k_gain, at_ref, dq_ref, d_kr, d_vr, outs, bufs, sems):
    qt_ref, row_ref, ku_ref = kept[0], kept[2], kept[7]
    a_buf, q_buf, k_buf, v_buf = bufs
    rows, wide = a_buf.shape
    share = wide // HD
    copies = []

    def send(j, buf):
        size = buf.shape[1]
        at = pl.multiple_of(head * size, size)
        copy = pltpu.make_async_copy(buf, outs[j].at[:, pl.ds(at, size)], sems.at[j])
        copy.start()
        copies.append(copy)

    att = at_ref[...].T
    live = lax.broadcasted_iota(jnp.int32, (rows, HD), 0) < live_len
    for i in range(share):
        block = att[i * rows : (i + 1) * rows, :].astype(F32)
        a_buf[:, i * HD : (i + 1) * HD] = jnp.where(live, block, 0.0).astype(BF)
    send(0, a_buf)
    v_buf[...] = d_vr.astype(BF)
    send(3, v_buf)
    k_unit = ku_ref[:, :HD]
    up_k = d_kr * k_gain
    mean_k = jnp.mean(up_k * k_unit, axis=-1, keepdims=True)
    k_buf[...] = (ku_ref[:, HD:] * (up_k - k_unit * mean_k)).astype(BF)
    send(2, k_buf)
    parts = []
    for start in range(0, share * rows, width):
        cols = slice(start, start + width)
        q_inv = row_ref[0:1, cols]
        q_unit = qt_ref[:, cols].astype(F32) * q_inv
        up = dq_ref[:, cols] * q_gain
        mean = jnp.mean(up * q_unit, axis=0, keepdims=True)
        parts.append((q_inv * (up - q_unit * mean)).astype(BF))
    d_q = jnp.concatenate(parts, axis=1).T
    for i in range(share):
        q_buf[:, i * HD : (i + 1) * HD] = d_q[i * rows : (i + 1) * rows, :]
    send(1, q_buf)
    for copy in copies:
        copy.wait()


def whole_kernel(s, width, meta, pr_ref, *rest):
    kept, (gain_ref, kg_ref, acc_ref) = rest[:KEPT], rest[KEPT : KEPT + 3]
    part_ref, gacc_ref, *rest = rest[-13:]
    outs, (at_ref, dq_ref), bufs, sems = rest[:4], rest[4:6], rest[6:10], rest[10]
    q_gain = gain_ref[...]
    d_kr, d_vr = attend(width, pr_ref, kept, q_gain, acc_ref, part_ref, at_ref, dq_ref, gacc_ref)
    live_len = meta[meta.shape[0] - 2]
    settle(width, meta[s], live_len, kept, q_gain, kg_ref[...], at_ref, dq_ref, d_kr, d_vr, outs, bufs, sems)


def first_kernel(width, pr_ref, *rest):
    kept, (gain_ref, acc_ref) = rest[:KEPT], rest[KEPT : KEPT + 2]
    part_ref, gacc_ref, at_ref, dq_ref, dkr_ref, dvr_ref = rest[-6:]
    d_kr, d_vr = attend(width, pr_ref, kept, gain_ref[...], acc_ref, part_ref, at_ref, dq_ref, gacc_ref)
    dkr_ref[...] = d_kr
    dvr_ref[...] = d_vr


def second_kernel(s, width, meta, *rest):
    kept, (gain_ref, kg_ref, at_ref, dq_ref, dkr_ref, dvr_ref) = rest[:KEPT], rest[KEPT : KEPT + 6]
    outs, bufs, sems = rest[-9:-5], rest[-5:-1], rest[-1]
    live_len = meta[meta.shape[0] - 2]
    settle(
        width, meta[s], live_len, kept, gain_ref[...], kg_ref[...], at_ref, dq_ref,
        dkr_ref[...], dvr_ref[...], outs, bufs, sems,
    )


def out_shapes(rows, q_width, k_width):
    widths = (q_width, q_width, k_width, k_width)
    return [jax.ShapeDtypeStruct((rows, w), BF) for w in widths]


def out_scratch(rows, share):
    widths = (share * HD, share * HD, HD, HD)
    return [pltpu.VMEM((rows, w), BF) for w in widths] + [pltpu.SemaphoreType.DMA((4,))]


def cost(prompt_rows, rows, total):
    return pl.CostEstimate(
        flops=(8 * prompt_rows + 4 * rows) * total * HD,
        bytes_accessed=2**20,
        transcendentals=total * prompt_rows,
    )


def whole_head(s, meta, prompt, kept, q_gain, k_gain, acc, buffers, q_width, k_width):
    total = kept[0].shape[1]
    rows = kept[3].shape[0]
    outs = pl.pallas_call(
        functools.partial(whole_kernel, s, 2 * HD),
        out_shape=[
            jax.ShapeDtypeStruct(prompt.shape, BF),
            jax.ShapeDtypeStruct(acc.shape, F32),
        ]
        + out_shapes(rows, q_width, k_width),
        in_specs=[SMEM] + [VMEM] * (4 + KEPT) + [HBM] * len(buffers),
        out_specs=[VMEM] * 2 + [HBM] * 4,
        scratch_shapes=[pltpu.VMEM((HD, total), BF), pltpu.VMEM((HD, total), F32)]
        + out_scratch(rows, total // rows),
        input_output_aliases={5 + KEPT + i: 2 + i for i in range(len(buffers))},
        compiler_params=params(16),
        cost_estimate=cost(prompt.shape[1], rows, total),
        name="attend_head",
    )(meta, prompt, *kept, q_gain, k_gain, acc, *buffers)
    return outs[0], outs[1], outs[2:]


def first_half(prompt, kept, q_gain, acc):
    total = kept[0].shape[1]
    rows = kept[3].shape[0]
    return pl.pallas_call(
        functools.partial(first_kernel, 2 * HD),
        out_shape=[
            jax.ShapeDtypeStruct(prompt.shape, BF),
            jax.ShapeDtypeStruct(acc.shape, F32),
            jax.ShapeDtypeStruct((HD, total), BF),
            jax.ShapeDtypeStruct((HD, total), F32),
            jax.ShapeDtypeStruct((rows, HD), F32),
            jax.ShapeDtypeStruct((rows, HD), F32),
        ],
        in_specs=[VMEM] * (3 + KEPT),
        out_specs=[VMEM] * 6,
        compiler_params=params(16),
        cost_estimate=cost(prompt.shape[1], rows, total),
        name="attend_last_head",
    )(prompt, *kept, q_gain, acc)


def second_half(s, meta, kept, q_gain, k_gain, results, buffers):
    total = kept[0].shape[1]
    rows = kept[3].shape[0]
    return pl.pallas_call(
        functools.partial(second_kernel, s, 2 * HD),
        out_shape=out_shapes(rows, buffers[0].shape[1], buffers[2].shape[1]),
        in_specs=[SMEM] + [VMEM] * (KEPT + 6) + [HBM] * 4,
        out_specs=[HBM] * 4,
        scratch_shapes=out_scratch(rows, total // rows),
        input_output_aliases={7 + KEPT + i: i for i in range(4)},
        compiler_params=params(16),
        cost_estimate=pl.CostEstimate(flops=0, bytes_accessed=2**20, transcendentals=0),
        name="settle_last_head",
    )(meta, *kept, q_gain, k_gain, *results, *buffers)


TAIL = 16


def join_kernel(own_ref, *rest):
    backs, gains_ref, out_ref = rest[:-2], rest[-2], rest[-1]
    depth, rows, _ = own_ref.shape
    for d in range(depth):
        total = own_ref[d].astype(F32)
        for back in backs:
            total = total + back[d].astype(F32)
        out_ref[d * rows : (d + 1) * rows, :] = total.astype(BF)
    gains = gains_ref[...]
    high = gains.astype(BF)
    gains = gains - high.astype(F32)
    middle = gains.astype(BF)
    low = (gains - middle.astype(F32)).astype(BF)
    pieces = jnp.concatenate([p[0:2].astype(F32) for p in (high, middle, low)], axis=0)
    pad = jnp.zeros((TAIL - pieces.shape[0], HD), F32)
    out_ref[depth * rows :, :] = jnp.concatenate([pieces, pad], axis=0).astype(BF)


def join(own, backs, gains):
    depth, rows, _ = own.shape
    return pl.pallas_call(
        join_kernel,
        out_shape=jax.ShapeDtypeStruct((depth * rows + TAIL, HD), BF),
        in_specs=[VMEM] * (2 + len(backs)),
        out_specs=VMEM,
        compiler_params=params(8),
        name="join_parts",
    )(own, *backs, gains)


def place_kernel(meta, *refs):
    payloads, out_ref, gain_ref, stage = refs[:-3], refs[-3], refs[-2], refs[-1]
    mine = meta[0] > 0
    depth, rows, _ = out_ref.shape
    for i, ref in enumerate(payloads):
        at = pl.multiple_of(meta[1 + i] * HD, HD)
        for d in range(depth):
            block = ref[d * rows : (d + 1) * rows, :]
            out_ref[d, :, pl.ds(at, HD)] = jnp.where(mine, block, jnp.zeros_like(block))
        tail = ref[depth * rows :, :].astype(F32)
        stage[meta[1 + i]] = tail[0:2] + tail[2:4] + tail[4:6]
    total = stage[0]
    for i in range(1, len(payloads)):
        total = total + stage[i]
    gain_ref[...] = total


def place(meta, payloads, depth, rows):
    count = len(payloads)
    return pl.pallas_call(
        place_kernel,
        out_shape=[
            jax.ShapeDtypeStruct((depth, rows, HD * count), BF),
            jax.ShapeDtypeStruct((2, HD), F32),
        ],
        in_specs=[SMEM] + [VMEM] * count,
        out_specs=[VMEM, VMEM],
        scratch_shapes=[pltpu.VMEM((count, 2, HD), F32)],
        compiler_params=params(8),
        name="place_prompt_grad",
    )(meta, *payloads)


def after(x, *others):
    return lax.optimization_barrier((x,) + others)[0]


def pair_sum(value, axis, size):
    step = 1
    while step < size:
        value = value + lax.ppermute(value, axis, [(i, i ^ step) for i in range(size)])
        step *= 2
    return value


def local(
    n_dp, n_group, queries, resp_keys, resp_values, prompt_cache, owners, lengths, q_gain, k_gain, grad_out
):
    q, g = queries[0, 0], grad_out[0, 0]
    k, v = resp_keys[0, 0], resp_values[0, 0]
    cache = prompt_cache[0, 0]
    owner = owners[0]
    live_len = lengths[0, 0]
    me = lax.axis_index("group")
    kv_heads = k.shape[1] // HD
    depth, p_rows, _ = cache.shape
    direct = n_group == kv_heads

    gain_col = q_gain[:, None]
    gain_row = k_gain[None, :]
    order = jnp.arange(kv_heads, dtype=jnp.int32)
    if direct:
        order = order ^ me
    turn = lax.axis_index("dp") % 2 if direct else jnp.int32(0)
    meta = jnp.concatenate([order, jnp.stack([live_len, turn.astype(jnp.int32)])])
    q, g, k, v, *gains_in = [
        pltpu.with_memory_space_constraint(x, pltpu.HBM) for x in (q, g, k, v, q_gain, k_gain)
    ]
    kept = prepare(0, meta, q, g, k, v, *gains_in, kv_heads, ())

    def swap(x, step):
        return lax.ppermute(x, "group", [(i, i ^ step) for i in range(n_group)])

    if direct:
        blocks = list(cut(order, pltpu.with_memory_space_constraint(cache, pltpu.HBM), kv_heads))
        blocks[1:] = [after(x, kept[0][2]) for x in blocks[1:]]
        got = [blocks[0]] + [swap(blocks[s], s) for s in range(1, n_group)]
        kept = prepare(1, meta, q, g, k, v, *gains_in, kv_heads, kept)
        for s in range(1, n_group):
            got[s] = after(got[s], kept[0][2])
        mine = pick(jnp.reshape(owner ^ me, (1,)).astype(jnp.int32), got)
        prompts = [mine] + [swap(mine, s) for s in range(1, n_group)]
    else:
        cache = lax.psum(jnp.where(me == owner, cache, jnp.zeros_like(cache)), "group")
        prompts = cut(order, cache, kv_heads)

    acc = jnp.zeros((2, HD), F32)
    parts, backs, buffers = [], [], ()
    for s, prompt in enumerate(prompts):
        last = s == kv_heads - 1
        if last:
            part, acc, *results = first_half(prompt, kept[s], gain_col, acc)
        else:
            part, acc, buffers = whole_head(
                s, meta, prompt, kept[s], gain_col, gain_row, acc, buffers, q.shape[1], k.shape[1]
            )
        parts.append(part)
        if direct and s > 0:
            backs.append(swap(part, s))
    mine_flag = (me == owner).astype(jnp.int32)
    def settled(results, buffers):
        return list(second_half(kv_heads - 1, meta, kept[-1], gain_col, gain_row, results, buffers))

    if direct:
        gains = acc + lax.ppermute(acc, "dp", [(i, i ^ 1) for i in range(n_dp)])
        results[0] = after(results[0], gains, *backs[:-1])
        buffers = settled(results, buffers)
        step = 2
        while step < n_dp:
            hop = lax.ppermute(gains, "dp", [(i, i ^ step) for i in range(n_dp)])
            gains = gains + (after(hop, buffers[2]) if step == 2 else hop)
            step *= 2
        payload = join(parts[0], backs, gains)
        payloads = [payload] + [swap(payload, s) for s in range(1, n_group)]
        placed, gains = place(jnp.concatenate([mine_flag[None], order]), payloads, depth, p_rows)
    else:
        total = lax.psum(jnp.concatenate(parts, axis=-1).astype(F32), "group").astype(BF)
        placed = jnp.where(mine_flag > 0, total, jnp.zeros((), BF))
        gains = pair_sum(pair_sum(acc, "dp", n_dp), "group", n_group)
        buffers = settled(results, buffers)
    attended, d_query, d_key, d_value = buffers
    return (
        attended[None, None],
        d_query[None, None],
        d_key[None, None],
        d_value[None, None],
        placed[None, None],
        gains,
    )


def solution(mesh):
    in_specs = (
        P("dp", "group", None, None),
        P("dp", "group", None, None),
        P("dp", "group", None, None),
        P("dp", "group", None, None, None),
        P("dp"),
        P("dp", "group"),
        P(),
        P(),
        P("dp", "group", None, None),
    )
    out_specs = (
        P("dp", "group", None, None),
        P("dp", "group", None, None),
        P("dp", "group", None, None),
        P("dp", "group", None, None),
        P("dp", "group", None, None, None),
        P(),
    )
    body = functools.partial(local, mesh.shape["dp"], mesh.shape["group"])
    return jax.shard_map(body, mesh=mesh, in_specs=in_specs, out_specs=out_specs, check_vma=False)
```

```python
import functools

import jax
import jax.numpy as jnp
from jax import lax
from jax.experimental import pallas as pl
from jax.experimental.pallas import tpu as pltpu
from jax.sharding import PartitionSpec as P

HD = 128
EPS = 1e-06
LOG2E = 1.4426950408889634
BF = jnp.bfloat16
F32 = jnp.float32


def dot_nn(a, b):
    return lax.dot_general(a, b, (((1,), (0,)), ((), ())), preferred_element_type=F32)


def dot_nt(a, b):
    return lax.dot_general(a, b, (((1,), (1,)), ((), ())), preferred_element_type=F32)


VMEM = pl.BlockSpec(memory_space=pltpu.VMEM)
SMEM = pl.BlockSpec(memory_space=pltpu.SMEM)
HBM = pl.BlockSpec(memory_space=pltpu.HBM)


def params(mib):
    return pltpu.CompilerParams(vmem_limit_bytes=mib * 2**20)


def cut_kernel(order, cache_ref, *rest):
    outs, sems = rest[:-1], rest[-1]
    copies = []
    for i, out in enumerate(outs):
        at = pl.multiple_of(order[i] * HD, HD)
        copy = pltpu.make_async_copy(cache_ref.at[:, :, pl.ds(at, HD)], out, sems.at[i])
        copy.start()
        copies.append(copy)
    for copy in copies:
        copy.wait()


def cut(order, cache, count):
    depth, rows, _ = cache.shape
    return pl.pallas_call(
        cut_kernel,
        out_shape=[jax.ShapeDtypeStruct((depth, rows, HD), BF)] * count,
        in_specs=[SMEM, HBM],
        out_specs=[VMEM] * count,
        scratch_shapes=[pltpu.SemaphoreType.DMA((count,))],
        compiler_params=params(4),
        name="cut_prompt",
    )(order, cache)


def pick_kernel(meta, *refs):
    picked = refs[0][...]
    for i in range(1, len(refs) - 1):
        picked = jnp.where(meta[meta.shape[0] - 2] == i, refs[i][...], picked)
    refs[-1][...] = picked


def pick(meta, blocks):
    return pl.pallas_call(
        pick_kernel,
        out_shape=jax.ShapeDtypeStruct(blocks[0].shape, BF),
        in_specs=[SMEM] + [VMEM] * len(blocks),
        out_specs=VMEM,
        compiler_params=params(4),
        name="pick_owner",
    )(meta, *blocks)


KEPT = 8


def column(row):
    return jnp.broadcast_to(row, (8, HD)).T[:, 0:1]


def prepare_kernel(turn, count, share, rows, width, meta, q_in, g_in, k_in, v_in, gain_ref, kg_ref, *rest):
    tail = count * KEPT + 6

    @pl.when(meta[count + 1] == turn)
    def _():
        prepare_body(
            count, share, rows, width, meta, q_in, g_in, k_in, v_in, gain_ref, kg_ref, *rest[-tail:]
        )

    if len(rest) > tail:

        @pl.when(meta[count + 1] != turn)
        def _():
            for old, new in zip(rest[:-tail], rest[-tail:-6]):
                new[...] = old[...]


def prepare_body(count, share, rows, width, meta, q_in, g_in, k_in, v_in, gain_ref, kg_ref, *rest):
    outs, (q_buf, g_buf, k_buf, v_buf, gain_buf, sems) = rest[:-6], rest[-6:]
    live_len = meta[count]
    scale = HD ** (-0.5)
    wide = share * HD
    copies = []
    for s in range(count):
        group = []
        for j, (src, buf, size) in enumerate(
            ((q_in, q_buf, wide), (k_in, k_buf, HD), (g_in, g_buf, wide), (v_in, v_buf, HD))
        ):
            at = pl.multiple_of(meta[s] * size, size)
            copy = pltpu.make_async_copy(src.at[:, pl.ds(at, size)], buf.at[s], sems.at[s, j])
            copy.start()
            group.append(copy)
        copies.append(group)
    gains = []
    for j, src in enumerate((gain_ref, kg_ref)):
        copy = pltpu.make_async_copy(src, gain_buf.at[j], sems.at[count, j])
        copy.start()
        gains.append(copy)
    for copy in gains:
        copy.wait()
    q_gain = column(gain_buf[0].reshape(1, HD))
    k_gain = gain_buf[1].reshape(1, HD)
    for s in range(count):
        qt_ref, gt_ref, row_ref, er_ref, ot_ref, dp_ref, kh_ref, ku_ref = outs[s * KEPT : (s + 1) * KEPT]
        for copy in copies[s]:
            copy.wait()
        q_t = jnp.concatenate([q_buf[s, :, i * HD : (i + 1) * HD] for i in range(share)], axis=0).T
        g_t = jnp.concatenate([g_buf[s, :, i * HD : (i + 1) * HD] for i in range(share)], axis=0).T
        qt_ref[...] = q_t
        raw_k = k_buf[s].astype(F32)
        k_inv = lax.rsqrt(jnp.mean(raw_k * raw_k, axis=-1, keepdims=True) + EPS)
        k_unit = raw_k * k_inv
        k_hat = (k_unit * k_gain).astype(BF)
        kh_ref[...] = k_hat
        ku_ref[:, :HD] = k_unit
        ku_ref[:, HD:] = jnp.broadcast_to(k_inv, (rows, HD))
        r_val = v_buf[s]
        r_val_t = r_val.T
        for start in range(0, share * rows, width):
            cols = slice(start, start + width)
            token = (lax.broadcasted_iota(jnp.int32, (1, width), 1) + start) % rows
            raw_q = q_t[:, cols].astype(F32)
            q_inv = lax.rsqrt(jnp.mean(raw_q * raw_q, axis=0, keepdims=True) + EPS)
            q_hat = (raw_q * q_inv * q_gain).astype(BF)
            d_o = jnp.where(token < live_len, g_t[:, cols].astype(F32), 0.0).astype(BF)
            gt_ref[:, cols] = d_o
            causal = lax.broadcasted_iota(jnp.int32, (rows, width), 0) <= token
            e_r = jnp.where(causal, jnp.exp2(dot_nn(k_hat, q_hat) * (scale * LOG2E)), 0.0)
            eb_r = e_r.astype(BF)
            er_ref[:, cols] = eb_r
            ot_ref[:, cols] = dot_nn(r_val_t, eb_r)
            dp_ref[:, cols] = dot_nn(r_val, d_o)
            row_ref[0:1, cols] = q_inv
            row_ref[1:2, cols] = jnp.sum(e_r, axis=0, keepdims=True)


def prepare(turn, meta, q, g, k, v, q_gain, k_gain, count, before):
    rows, q_width = q.shape
    share = q_width // k.shape[1]
    total = share * rows
    each = [
        jax.ShapeDtypeStruct((HD, total), BF),
        jax.ShapeDtypeStruct((HD, total), BF),
        jax.ShapeDtypeStruct((8, total), F32),
        jax.ShapeDtypeStruct((rows, total), BF),
        jax.ShapeDtypeStruct((HD, total), F32),
        jax.ShapeDtypeStruct((rows, total), F32),
        jax.ShapeDtypeStruct((rows, HD), BF),
        jax.ShapeDtypeStruct((rows, 2 * HD), F32),
    ]
    outs = pl.pallas_call(
        functools.partial(prepare_kernel, turn, count, share, rows, 2 * HD),
        out_shape=each * count,
        in_specs=[SMEM] + [HBM] * 6 + [VMEM] * (KEPT * len(before)),
        out_specs=[VMEM] * (KEPT * count),
        scratch_shapes=[
            pltpu.VMEM((count, rows, share * HD), BF),
            pltpu.VMEM((count, rows, share * HD), BF),
            pltpu.VMEM((count, rows, HD), BF),
            pltpu.VMEM((count, rows, HD), BF),
            pltpu.VMEM((2, HD), F32),
            pltpu.SemaphoreType.DMA((count + 1, 4)),
        ],
        compiler_params=params(16),
        cost_estimate=pl.CostEstimate(
            flops=6 * count * total * rows * HD,
            bytes_accessed=5 * rows * q_width * 2,
            transcendentals=count * total * rows,
        ),
        name="prepare_response",
    )(meta, q, g, k, v, q_gain, k_gain, *[x for group in before for x in group])
    return [list(outs[s * KEPT : (s + 1) * KEPT]) for s in range(count)]


def attend(width, pr_ref, kept, q_gain, acc_ref, part_ref, at_ref, dq_ref, gacc_ref):
    qt_ref, gt_ref, row_ref, er_ref, ot_ref, dp_ref, kh_ref, ku_ref = kept
    scale = HD ** (-0.5)
    p_key = pr_ref[0]
    p_val = pr_ref[1]
    k_hat_t = kh_ref[...].T
    p_key_t = p_key.T
    p_val_t = p_val.T
    sums = None
    for start in range(0, qt_ref.shape[1], width):
        cols = slice(start, start + width)
        q_unit = qt_ref[:, cols].astype(F32) * row_ref[0:1, cols]
        q_hat = (q_unit * q_gain).astype(BF)
        d_ob = gt_ref[:, cols]
        d_o = d_ob.astype(F32)
        e_p = jnp.exp2(dot_nn(p_key, q_hat) * (scale * LOG2E))
        inv_sum = 1.0 / (jnp.sum(e_p, axis=0, keepdims=True) + row_ref[1:2, cols])
        eb_p = e_p.astype(BF)
        eb_r = er_ref[:, cols]
        out = (dot_nn(p_val_t, eb_p) + ot_ref[:, cols]) * inv_sum
        at_ref[:, cols] = out.astype(BF)
        delta = jnp.sum(d_o * out, axis=0, keepdims=True)
        ds_p = (e_p * (dot_nn(p_val, d_ob) - delta)).astype(BF)
        ds_r = (eb_r.astype(F32) * (dp_ref[:, cols] - delta)).astype(BF)
        weight = inv_sum * scale
        q_w = (q_hat.astype(F32) * weight).astype(BF)
        d_ow = (d_o * inv_sum).astype(BF)
        d_qhat = (dot_nn(p_key_t, ds_p) + dot_nn(k_hat_t, ds_r)) * weight
        dq_ref[:, cols] = d_qhat
        terms = (
            dot_nt(ds_p, q_w),
            dot_nt(eb_p, d_ow),
            dot_nt(ds_r, q_w),
            dot_nt(eb_r, d_ow),
            d_qhat * q_unit,
        )
        sums = terms if sums is None else [a + b for a, b in zip(sums, terms)]
    d_kp, d_vp, d_kr, d_vr, q_term = sums
    part_ref[0] = d_kp.astype(BF)
    part_ref[1] = d_vp.astype(BF)
    folded = q_term[:, :HD]
    for start in range(HD, width, HD):
        folded = folded + q_term[:, start : start + HD]
    gacc_ref[0:1, :] = acc_ref[0:1, :] + jnp.sum(folded.T, axis=0, keepdims=True)
    gacc_ref[1:2, :] = acc_ref[1:2, :] + jnp.sum(d_kr * ku_ref[:, :HD], axis=0, keepdims=True)
    return d_kr, d_vr


def settle(width, head, live_len, kept, q_gain, k_gain, at_ref, dq_ref, d_kr, d_vr, outs, bufs, sems):
    qt_ref, row_ref, ku_ref = kept[0], kept[2], kept[7]
    a_buf, q_buf, k_buf, v_buf = bufs
    rows, wide = a_buf.shape
    share = wide // HD
    copies = []

    def send(j, buf):
        size = buf.shape[1]
        at = pl.multiple_of(head * size, size)
        copy = pltpu.make_async_copy(buf, outs[j].at[:, pl.ds(at, size)], sems.at[j])
        copy.start()
        copies.append(copy)

    att = at_ref[...].T
    live = lax.broadcasted_iota(jnp.int32, (rows, HD), 0) < live_len
    for i in range(share):
        block = att[i * rows : (i + 1) * rows, :].astype(F32)
        a_buf[:, i * HD : (i + 1) * HD] = jnp.where(live, block, 0.0).astype(BF)
    send(0, a_buf)
    v_buf[...] = d_vr.astype(BF)
    send(3, v_buf)
    k_unit = ku_ref[:, :HD]
    up_k = d_kr * k_gain
    mean_k = jnp.mean(up_k * k_unit, axis=-1, keepdims=True)
    k_buf[...] = (ku_ref[:, HD:] * (up_k - k_unit * mean_k)).astype(BF)
    send(2, k_buf)
    parts = []
    for start in range(0, share * rows, width):
        cols = slice(start, start + width)
        q_inv = row_ref[0:1, cols]
        q_unit = qt_ref[:, cols].astype(F32) * q_inv
        up = dq_ref[:, cols] * q_gain
        mean = jnp.mean(up * q_unit, axis=0, keepdims=True)
        parts.append((q_inv * (up - q_unit * mean)).astype(BF))
    d_q = jnp.concatenate(parts, axis=1).T
    for i in range(share):
        q_buf[:, i * HD : (i + 1) * HD] = d_q[i * rows : (i + 1) * rows, :]
    send(1, q_buf)
    for copy in copies:
        copy.wait()


def whole_kernel(s, width, meta, pr_ref, *rest):
    kept, (gain_ref, kg_ref, acc_ref) = rest[:KEPT], rest[KEPT : KEPT + 3]
    part_ref, gacc_ref, *rest = rest[-13:]
    outs, (at_ref, dq_ref), bufs, sems = rest[:4], rest[4:6], rest[6:10], rest[10]
    q_gain = column(gain_ref[...])
    d_kr, d_vr = attend(width, pr_ref, kept, q_gain, acc_ref, part_ref, at_ref, dq_ref, gacc_ref)
    live_len = meta[meta.shape[0] - 4]
    settle(width, meta[s], live_len, kept, q_gain, kg_ref[...], at_ref, dq_ref, d_kr, d_vr, outs, bufs, sems)


def first_kernel(width, pr_ref, *rest):
    kept, (gain_ref, acc_ref) = rest[:KEPT], rest[KEPT : KEPT + 2]
    part_ref, gacc_ref, at_ref, dq_ref, dkr_ref, dvr_ref = rest[-6:]
    d_kr, d_vr = attend(width, pr_ref, kept, column(gain_ref[...]), acc_ref, part_ref, at_ref, dq_ref, gacc_ref)
    dkr_ref[...] = d_kr
    dvr_ref[...] = d_vr


def second_kernel(s, width, meta, *rest):
    kept, (gain_ref, kg_ref, at_ref, dq_ref, dkr_ref, dvr_ref) = rest[:KEPT], rest[KEPT : KEPT + 6]
    outs, bufs, sems = rest[-9:-5], rest[-5:-1], rest[-1]
    live_len = meta[meta.shape[0] - 4]
    settle(
        width, meta[s], live_len, kept, column(gain_ref[...]), kg_ref[...], at_ref, dq_ref,
        dkr_ref[...], dvr_ref[...], outs, bufs, sems,
    )


def out_shapes(rows, q_width, k_width):
    widths = (q_width, q_width, k_width, k_width)
    return [jax.ShapeDtypeStruct((rows, w), BF) for w in widths]


def out_scratch(rows, share):
    widths = (share * HD, share * HD, HD, HD)
    return [pltpu.VMEM((rows, w), BF) for w in widths] + [pltpu.SemaphoreType.DMA((4,))]


def cost(prompt_rows, rows, total):
    return pl.CostEstimate(
        flops=(8 * prompt_rows + 4 * rows) * total * HD,
        bytes_accessed=2**20,
        transcendentals=total * prompt_rows,
    )


def whole_head(s, meta, prompt, kept, q_gain, k_gain, acc, buffers, q_width, k_width):
    total = kept[0].shape[1]
    rows = kept[3].shape[0]
    outs = pl.pallas_call(
        functools.partial(whole_kernel, s, 2 * HD),
        out_shape=[
            jax.ShapeDtypeStruct(prompt.shape, BF),
            jax.ShapeDtypeStruct(acc.shape, F32),
        ]
        + out_shapes(rows, q_width, k_width),
        in_specs=[SMEM] + [VMEM] * (4 + KEPT) + [HBM] * len(buffers),
        out_specs=[VMEM] * 2 + [HBM] * 4,
        scratch_shapes=[pltpu.VMEM((HD, total), BF), pltpu.VMEM((HD, total), F32)]
        + out_scratch(rows, total // rows),
        input_output_aliases={5 + KEPT + i: 2 + i for i in range(len(buffers))},
        compiler_params=params(16),
        cost_estimate=cost(prompt.shape[1], rows, total),
        name="attend_head",
    )(meta, prompt, *kept, q_gain, k_gain, acc, *buffers)
    return outs[0], outs[1], outs[2:]


def first_half(prompt, kept, q_gain, acc):
    total = kept[0].shape[1]
    rows = kept[3].shape[0]
    return pl.pallas_call(
        functools.partial(first_kernel, 2 * HD),
        out_shape=[
            jax.ShapeDtypeStruct(prompt.shape, BF),
            jax.ShapeDtypeStruct(acc.shape, F32),
            jax.ShapeDtypeStruct((HD, total), BF),
            jax.ShapeDtypeStruct((HD, total), F32),
            jax.ShapeDtypeStruct((rows, HD), F32),
            jax.ShapeDtypeStruct((rows, HD), F32),
        ],
        in_specs=[VMEM] * (3 + KEPT),
        out_specs=[VMEM] * 6,
        compiler_params=params(16),
        cost_estimate=cost(prompt.shape[1], rows, total),
        name="attend_last_head",
    )(prompt, *kept, q_gain, acc)


def second_half(s, meta, kept, q_gain, k_gain, results, buffers):
    total = kept[0].shape[1]
    rows = kept[3].shape[0]
    return pl.pallas_call(
        functools.partial(second_kernel, s, 2 * HD),
        out_shape=out_shapes(rows, buffers[0].shape[1], buffers[2].shape[1]),
        in_specs=[SMEM] + [VMEM] * (KEPT + 6) + [HBM] * 4,
        out_specs=[HBM] * 4,
        scratch_shapes=out_scratch(rows, total // rows),
        input_output_aliases={7 + KEPT + i: i for i in range(4)},
        compiler_params=params(16),
        cost_estimate=pl.CostEstimate(flops=0, bytes_accessed=2**20, transcendentals=0),
        name="settle_last_head",
    )(meta, *kept, q_gain, k_gain, *results, *buffers)


TAIL = 16


def join_kernel(own_ref, *rest):
    backs, gains_ref, out_ref = rest[:-2], rest[-2], rest[-1]
    depth, rows, _ = own_ref.shape
    for d in range(depth):
        total = own_ref[d].astype(F32)
        for back in backs:
            total = total + back[d].astype(F32)
        out_ref[d * rows : (d + 1) * rows, :] = total.astype(BF)
    gains = gains_ref[...]
    high = gains.astype(BF)
    gains = gains - high.astype(F32)
    middle = gains.astype(BF)
    low = (gains - middle.astype(F32)).astype(BF)
    pieces = jnp.concatenate([p[0:2].astype(F32) for p in (high, middle, low)], axis=0)
    pad = jnp.zeros((TAIL - pieces.shape[0], HD), F32)
    out_ref[depth * rows :, :] = jnp.concatenate([pieces, pad], axis=0).astype(BF)


def join(own, backs, gains):
    depth, rows, _ = own.shape
    return pl.pallas_call(
        join_kernel,
        out_shape=jax.ShapeDtypeStruct((depth * rows + TAIL, HD), BF),
        in_specs=[VMEM] * (2 + len(backs)),
        out_specs=VMEM,
        compiler_params=params(8),
        name="join_parts",
    )(own, *backs, gains)


def place_kernel(meta, *refs):
    payloads, out_ref, gain_ref, stage = refs[:-3], refs[-3], refs[-2], refs[-1]
    mine = meta[meta.shape[0] - 1] > 0
    depth, rows, _ = out_ref.shape
    for i, ref in enumerate(payloads):
        at = pl.multiple_of(meta[i] * HD, HD)
        for d in range(depth):
            block = ref[d * rows : (d + 1) * rows, :]
            out_ref[d, :, pl.ds(at, HD)] = jnp.where(mine, block, jnp.zeros_like(block))
        tail = ref[depth * rows :, :].astype(F32)
        stage[meta[i]] = tail[0:2] + tail[2:4] + tail[4:6]
    total = stage[0]
    for i in range(1, len(payloads)):
        total = total + stage[i]
    gain_ref[...] = total


def place(meta, payloads, depth, rows):
    count = len(payloads)
    return pl.pallas_call(
        place_kernel,
        out_shape=[
            jax.ShapeDtypeStruct((depth, rows, HD * count), BF),
            jax.ShapeDtypeStruct((2, HD), F32),
        ],
        in_specs=[SMEM] + [VMEM] * count,
        out_specs=[VMEM, VMEM],
        scratch_shapes=[pltpu.VMEM((count, 2, HD), F32)],
        compiler_params=params(8),
        name="place_prompt_grad",
    )(meta, *payloads)


def after(x, *others):
    return lax.optimization_barrier((x,) + others)[0]


def pair_sum(value, axis, size):
    step = 1
    while step < size:
        value = value + lax.ppermute(value, axis, [(i, i ^ step) for i in range(size)])
        step *= 2
    return value


def local(
    n_dp, n_group, queries, resp_keys, resp_values, prompt_cache, owners, lengths, q_gain, k_gain, grad_out
):
    q, g = queries[0, 0], grad_out[0, 0]
    k, v = resp_keys[0, 0], resp_values[0, 0]
    cache = prompt_cache[0, 0]
    owner = owners[0]
    live_len = lengths[0, 0]
    me = lax.axis_index("group")
    kv_heads = k.shape[1] // HD
    depth, p_rows, _ = cache.shape
    direct = n_group == kv_heads

    q_row = q_gain[None, :]
    k_row = k_gain[None, :]
    order = jnp.arange(kv_heads, dtype=jnp.int32)
    if direct:
        order = order ^ me
    turn = lax.axis_index("dp") % 2 if direct else jnp.int32(0)
    mine_flag = (me == owner).astype(jnp.int32)
    meta = jnp.concatenate([order, jnp.stack([live_len, turn.astype(jnp.int32), owner ^ me, mine_flag])])
    q, g, k, v, *gains_in = [
        pltpu.with_memory_space_constraint(x, pltpu.HBM) for x in (q, g, k, v, q_gain, k_gain)
    ]
    kept = prepare(0, meta, q, g, k, v, *gains_in, kv_heads, ())

    def swap(x, step):
        return lax.ppermute(x, "group", [(i, i ^ step) for i in range(n_group)])

    if direct:
        blocks = list(cut(order, pltpu.with_memory_space_constraint(cache, pltpu.HBM), kv_heads))
        blocks[1:] = [after(x, kept[0][2]) for x in blocks[1:]]
        got = [blocks[0]] + [swap(blocks[s], s) for s in range(1, n_group)]
        kept = prepare(1, meta, q, g, k, v, *gains_in, kv_heads, kept)
        for s in range(1, n_group):
            got[s] = after(got[s], kept[0][2])
        mine = pick(meta, got)
        prompts = [mine] + [swap(mine, s) for s in range(1, n_group)]
    else:
        cache = lax.psum(jnp.where(me == owner, cache, jnp.zeros_like(cache)), "group")
        prompts = cut(order, cache, kv_heads)

    acc = jnp.zeros((2, HD), F32)
    parts, backs, buffers = [], [], ()
    for s, prompt in enumerate(prompts):
        last = s == kv_heads - 1
        if last:
            part, acc, *results = first_half(prompt, kept[s], q_row, acc)
        else:
            part, acc, buffers = whole_head(
                s, meta, prompt, kept[s], q_row, k_row, acc, buffers, q.shape[1], k.shape[1]
            )
        parts.append(part)
        if direct and s > 0:
            backs.append(swap(part, s))
    def settled(results, buffers):
        return list(second_half(kv_heads - 1, meta, kept[-1], q_row, k_row, results, buffers))

    if direct:
        gains = acc + lax.ppermute(acc, "dp", [(i, i ^ 1) for i in range(n_dp)])
        results[0] = after(results[0], gains, *backs[:-1])
        buffers = settled(results, buffers)
        step = 2
        while step < n_dp:
            hop = lax.ppermute(gains, "dp", [(i, i ^ step) for i in range(n_dp)])
            gains = gains + (after(hop, buffers[2]) if step == 2 else hop)
            step *= 2
        payload = join(parts[0], backs, gains)
        payloads = [payload] + [swap(payload, s) for s in range(1, n_group)]
        placed, gains = place(meta, payloads, depth, p_rows)
    else:
        total = lax.psum(jnp.concatenate(parts, axis=-1).astype(F32), "group").astype(BF)
        placed = jnp.where(mine_flag > 0, total, jnp.zeros((), BF))
        gains = pair_sum(pair_sum(acc, "dp", n_dp), "group", n_group)
        buffers = settled(results, buffers)
    attended, d_query, d_key, d_value = buffers
    return (
        attended[None, None],
        d_query[None, None],
        d_key[None, None],
        d_value[None, None],
        placed[None, None],
        gains,
    )


def solution(mesh):
    in_specs = (
        P("dp", "group", None, None),
        P("dp", "group", None, None),
        P("dp", "group", None, None),
        P("dp", "group", None, None, None),
        P("dp"),
        P("dp", "group"),
        P(),
        P(),
        P("dp", "group", None, None),
    )
    out_specs = (
        P("dp", "group", None, None),
        P("dp", "group", None, None),
        P("dp", "group", None, None),
        P("dp", "group", None, None),
        P("dp", "group", None, None, None),
        P(),
    )
    body = functools.partial(local, mesh.shape["dp"], mesh.shape["group"])
    return jax.shard_map(body, mesh=mesh, in_specs=in_specs, out_specs=out_specs, check_vma=False)
```

```python
import functools

import jax
import jax.numpy as jnp
from jax import lax
from jax.experimental import pallas as pl
from jax.experimental.pallas import tpu as pltpu
from jax.sharding import PartitionSpec as P

HD = 128
EPS = 1e-06
LOG2E = 1.4426950408889634
BF = jnp.bfloat16
F32 = jnp.float32


def dot_nn(a, b):
    return lax.dot_general(a, b, (((1,), (0,)), ((), ())), preferred_element_type=F32)


def dot_nt(a, b):
    return lax.dot_general(a, b, (((1,), (1,)), ((), ())), preferred_element_type=F32)


VMEM = pl.BlockSpec(memory_space=pltpu.VMEM)
SMEM = pl.BlockSpec(memory_space=pltpu.SMEM)
HBM = pl.BlockSpec(memory_space=pltpu.HBM)


def params(mib):
    return pltpu.CompilerParams(vmem_limit_bytes=mib * 2**20)


def cut_kernel(order, cache_ref, *rest):
    outs, sems = rest[:-1], rest[-1]
    copies = []
    for i, out in enumerate(outs):
        at = pl.multiple_of(order[i] * HD, HD)
        copy = pltpu.make_async_copy(cache_ref.at[:, :, pl.ds(at, HD)], out, sems.at[i])
        copy.start()
        copies.append(copy)
    for copy in copies:
        copy.wait()


def cut(order, cache, count):
    depth, rows, _ = cache.shape
    return pl.pallas_call(
        cut_kernel,
        out_shape=[jax.ShapeDtypeStruct((depth, rows, HD), BF)] * count,
        in_specs=[SMEM, HBM],
        out_specs=[VMEM] * count,
        scratch_shapes=[pltpu.SemaphoreType.DMA((count,))],
        compiler_params=params(4),
        name="cut_prompt",
    )(order, cache)


def pick_kernel(meta, *refs):
    picked = refs[0][...]
    for i in range(1, len(refs) - 1):
        picked = jnp.where(meta[meta.shape[0] - 2] == i, refs[i][...], picked)
    refs[-1][...] = picked


def pick(meta, blocks):
    return pl.pallas_call(
        pick_kernel,
        out_shape=jax.ShapeDtypeStruct(blocks[0].shape, BF),
        in_specs=[SMEM] + [VMEM] * len(blocks),
        out_specs=VMEM,
        compiler_params=params(4),
        name="pick_owner",
    )(meta, *blocks)


KEPT = 8


def column(row):
    return jnp.broadcast_to(row, (8, HD)).T[:, 0:1]


def prepare_kernel(turn, slots, share, rows, width, meta, *refs):
    tail = len(slots) * KEPT + 6
    before = len(refs) - 6 - tail
    run = functools.partial(prepare_body, slots, share, rows, width, meta, *refs[:6], *refs[6 + before :])
    if turn is None:
        run()
        return
    mine = meta[meta.shape[0] - 3] == turn
    pl.when(mine)(run)
    if before > 0:

        @pl.when(jnp.logical_not(mine))
        def _():
            for old, new in zip(refs[6 : 6 + before], refs[6 + before : -6]):
                new[...] = old[...]


def prepare_body(slots, share, rows, width, meta, q_in, g_in, k_in, v_in, gain_ref, kg_ref, *rest):
    outs, (q_buf, g_buf, k_buf, v_buf, gain_buf, sems) = rest[:-6], rest[-6:]
    live_len = meta[meta.shape[0] - 4]
    count = len(slots)
    scale = HD ** (-0.5)
    wide = share * HD
    copies = []
    for s, slot in enumerate(slots):
        group = []
        for j, (src, buf, size) in enumerate(
            ((q_in, q_buf, wide), (k_in, k_buf, HD), (g_in, g_buf, wide), (v_in, v_buf, HD))
        ):
            at = pl.multiple_of(meta[slot] * size, size)
            copy = pltpu.make_async_copy(src.at[:, pl.ds(at, size)], buf.at[s], sems.at[s, j])
            copy.start()
            group.append(copy)
        copies.append(group)
    gains = []
    for j, src in enumerate((gain_ref, kg_ref)):
        copy = pltpu.make_async_copy(src, gain_buf.at[j], sems.at[count, j])
        copy.start()
        gains.append(copy)
    for copy in gains:
        copy.wait()
    q_gain = column(gain_buf[0].reshape(1, HD))
    k_gain = gain_buf[1].reshape(1, HD)
    for s in range(count):
        qt_ref, gt_ref, row_ref, er_ref, ot_ref, dp_ref, kh_ref, ku_ref = outs[s * KEPT : (s + 1) * KEPT]
        for copy in copies[s]:
            copy.wait()
        q_t = jnp.concatenate([q_buf[s, :, i * HD : (i + 1) * HD] for i in range(share)], axis=0).T
        g_t = jnp.concatenate([g_buf[s, :, i * HD : (i + 1) * HD] for i in range(share)], axis=0).T
        qt_ref[...] = q_t
        raw_k = k_buf[s].astype(F32)
        k_inv = lax.rsqrt(jnp.mean(raw_k * raw_k, axis=-1, keepdims=True) + EPS)
        k_unit = raw_k * k_inv
        k_hat = (k_unit * k_gain).astype(BF)
        kh_ref[...] = k_hat
        ku_ref[:, :HD] = k_unit
        ku_ref[:, HD:] = jnp.broadcast_to(k_inv, (rows, HD))
        r_val = v_buf[s]
        r_val_t = r_val.T
        for start in range(0, share * rows, width):
            cols = slice(start, start + width)
            token = (lax.broadcasted_iota(jnp.int32, (1, width), 1) + start) % rows
            raw_q = q_t[:, cols].astype(F32)
            q_inv = lax.rsqrt(jnp.mean(raw_q * raw_q, axis=0, keepdims=True) + EPS)
            q_hat = (raw_q * q_inv * q_gain).astype(BF)
            d_o = jnp.where(token < live_len, g_t[:, cols].astype(F32), 0.0).astype(BF)
            gt_ref[:, cols] = d_o
            causal = lax.broadcasted_iota(jnp.int32, (rows, width), 0) <= token
            e_r = jnp.where(causal, jnp.exp2(dot_nn(k_hat, q_hat) * (scale * LOG2E)), 0.0)
            eb_r = e_r.astype(BF)
            er_ref[:, cols] = eb_r
            ot_ref[:, cols] = dot_nn(r_val_t, eb_r)
            dp_ref[:, cols] = dot_nn(r_val, d_o)
            row_ref[0:1, cols] = q_inv
            row_ref[1:2, cols] = jnp.sum(e_r, axis=0, keepdims=True)


def prepare(turn, slots, meta, q, g, k, v, q_gain, k_gain, before=()):
    count = len(slots)
    rows, q_width = q.shape
    share = q_width // k.shape[1]
    total = share * rows
    each = [
        jax.ShapeDtypeStruct((HD, total), BF),
        jax.ShapeDtypeStruct((HD, total), BF),
        jax.ShapeDtypeStruct((8, total), F32),
        jax.ShapeDtypeStruct((rows, total), BF),
        jax.ShapeDtypeStruct((HD, total), F32),
        jax.ShapeDtypeStruct((rows, total), F32),
        jax.ShapeDtypeStruct((rows, HD), BF),
        jax.ShapeDtypeStruct((rows, 2 * HD), F32),
    ]
    outs = pl.pallas_call(
        functools.partial(prepare_kernel, turn, slots, share, rows, 2 * HD),
        out_shape=each * count,
        in_specs=[SMEM] + [HBM] * 6 + [VMEM] * (KEPT * len(before)),
        out_specs=[VMEM] * (KEPT * count),
        scratch_shapes=[
            pltpu.VMEM((count, rows, share * HD), BF),
            pltpu.VMEM((count, rows, share * HD), BF),
            pltpu.VMEM((count, rows, HD), BF),
            pltpu.VMEM((count, rows, HD), BF),
            pltpu.VMEM((2, HD), F32),
            pltpu.SemaphoreType.DMA((count + 1, 4)),
        ],
        compiler_params=params(16),
        cost_estimate=pl.CostEstimate(
            flops=6 * count * total * rows * HD,
            bytes_accessed=5 * rows * q_width * 2,
            transcendentals=count * total * rows,
        ),
        name="prepare_response",
    )(meta, q, g, k, v, q_gain, k_gain, *[x for group in before for x in group])
    return [list(outs[s * KEPT : (s + 1) * KEPT]) for s in range(count)]


def attend(width, pr_ref, kept, q_gain, acc_ref, part_ref, at_ref, dq_ref, gacc_ref):
    qt_ref, gt_ref, row_ref, er_ref, ot_ref, dp_ref, kh_ref, ku_ref = kept
    scale = HD ** (-0.5)
    p_key = pr_ref[0]
    p_val = pr_ref[1]
    k_hat_t = kh_ref[...].T
    p_key_t = p_key.T
    p_val_t = p_val.T
    sums = None
    for start in range(0, qt_ref.shape[1], width):
        cols = slice(start, start + width)
        q_unit = qt_ref[:, cols].astype(F32) * row_ref[0:1, cols]
        q_hat = (q_unit * q_gain).astype(BF)
        d_ob = gt_ref[:, cols]
        d_o = d_ob.astype(F32)
        e_p = jnp.exp2(dot_nn(p_key, q_hat) * (scale * LOG2E))
        inv_sum = 1.0 / (jnp.sum(e_p, axis=0, keepdims=True) + row_ref[1:2, cols])
        eb_p = e_p.astype(BF)
        eb_r = er_ref[:, cols]
        out = (dot_nn(p_val_t, eb_p) + ot_ref[:, cols]) * inv_sum
        at_ref[:, cols] = out.astype(BF)
        delta = jnp.sum(d_o * out, axis=0, keepdims=True)
        ds_p = (e_p * (dot_nn(p_val, d_ob) - delta)).astype(BF)
        ds_r = (eb_r.astype(F32) * (dp_ref[:, cols] - delta)).astype(BF)
        weight = inv_sum * scale
        q_w = (q_hat.astype(F32) * weight).astype(BF)
        d_ow = (d_o * inv_sum).astype(BF)
        d_qhat = (dot_nn(p_key_t, ds_p) + dot_nn(k_hat_t, ds_r)) * weight
        dq_ref[:, cols] = d_qhat
        terms = (
            dot_nt(ds_p, q_w),
            dot_nt(eb_p, d_ow),
            dot_nt(ds_r, q_w),
            dot_nt(eb_r, d_ow),
            d_qhat * q_unit,
        )
        sums = terms if sums is None else [a + b for a, b in zip(sums, terms)]
    d_kp, d_vp, d_kr, d_vr, q_term = sums
    part_ref[0] = d_kp.astype(BF)
    part_ref[1] = d_vp.astype(BF)
    folded = q_term[:, :HD]
    for start in range(HD, width, HD):
        folded = folded + q_term[:, start : start + HD]
    gacc_ref[0:1, :] = acc_ref[0:1, :] + jnp.sum(folded.T, axis=0, keepdims=True)
    gacc_ref[1:2, :] = acc_ref[1:2, :] + jnp.sum(d_kr * ku_ref[:, :HD], axis=0, keepdims=True)
    return d_kr, d_vr


def settle(width, head, live_len, kept, q_gain, k_gain, at_ref, dq_ref, d_kr, d_vr, outs, bufs, sems):
    qt_ref, row_ref, ku_ref = kept
    a_buf, q_buf, k_buf, v_buf = bufs
    rows, wide = a_buf.shape
    share = wide // HD
    copies = []

    def send(j, buf):
        size = buf.shape[1]
        at = pl.multiple_of(head * size, size)
        copy = pltpu.make_async_copy(buf, outs[j].at[:, pl.ds(at, size)], sems.at[j])
        copy.start()
        copies.append(copy)

    att = at_ref[...].T
    live = lax.broadcasted_iota(jnp.int32, (rows, HD), 0) < live_len
    for i in range(share):
        block = att[i * rows : (i + 1) * rows, :].astype(F32)
        a_buf[:, i * HD : (i + 1) * HD] = jnp.where(live, block, 0.0).astype(BF)
    send(0, a_buf)
    v_buf[...] = d_vr.astype(BF)
    send(3, v_buf)
    k_unit = ku_ref[:, :HD]
    up_k = d_kr * k_gain
    mean_k = jnp.mean(up_k * k_unit, axis=-1, keepdims=True)
    k_buf[...] = (ku_ref[:, HD:] * (up_k - k_unit * mean_k)).astype(BF)
    send(2, k_buf)
    parts = []
    for start in range(0, share * rows, width):
        cols = slice(start, start + width)
        q_inv = row_ref[0:1, cols]
        q_unit = qt_ref[:, cols].astype(F32) * q_inv
        up = dq_ref[:, cols] * q_gain
        mean = jnp.mean(up * q_unit, axis=0, keepdims=True)
        parts.append((q_inv * (up - q_unit * mean)).astype(BF))
    d_q = jnp.concatenate(parts, axis=1).T
    for i in range(share):
        q_buf[:, i * HD : (i + 1) * HD] = d_q[i * rows : (i + 1) * rows, :]
    send(1, q_buf)
    return copies


def first_kernel(width, pr_ref, *rest):
    kept, (gain_ref, acc_ref) = rest[:KEPT], rest[KEPT : KEPT + 2]
    part_ref, gacc_ref, at_ref, dq_ref, dkr_ref, dvr_ref = rest[-6:]
    d_kr, d_vr = attend(width, pr_ref, kept, column(gain_ref[...]), acc_ref, part_ref, at_ref, dq_ref, gacc_ref)
    dkr_ref[...] = d_kr
    dvr_ref[...] = d_vr


def settle_kernel(width, meta, gain_ref, kg_ref, *rest):
    outs, bufs, sems = rest[-9:-5], rest[-5:-1], rest[-1]
    q_gain = column(gain_ref[...])
    copies = []
    for i in range(sems.shape[0]):
        kept, results = rest[i * 7 : i * 7 + 3], rest[i * 7 + 3 : i * 7 + 7]
        at_ref, dq_ref, dkr_ref, dvr_ref = results
        copies += settle(
            width, meta[i], meta[meta.shape[0] - 4], kept, q_gain, kg_ref[...], at_ref, dq_ref,
            dkr_ref[...], dvr_ref[...], outs, [buf.at[i] for buf in bufs], sems.at[i],
        )
    for copy in copies:
        copy.wait()


def out_shapes(rows, q_width, k_width):
    widths = (q_width, q_width, k_width, k_width)
    return [jax.ShapeDtypeStruct((rows, w), BF) for w in widths]


def out_scratch(count, rows, share):
    widths = (share * HD, share * HD, HD, HD)
    return [pltpu.VMEM((count, rows, w), BF) for w in widths] + [pltpu.SemaphoreType.DMA((count, 4))]


def cost(prompt_rows, rows, total):
    return pl.CostEstimate(
        flops=(8 * prompt_rows + 4 * rows) * total * HD,
        bytes_accessed=2**20,
        transcendentals=total * prompt_rows,
    )


def first_half(prompt, kept, q_gain, acc):
    total = kept[0].shape[1]
    rows = kept[3].shape[0]
    return pl.pallas_call(
        functools.partial(first_kernel, 2 * HD),
        out_shape=[
            jax.ShapeDtypeStruct(prompt.shape, BF),
            jax.ShapeDtypeStruct(acc.shape, F32),
            jax.ShapeDtypeStruct((HD, total), BF),
            jax.ShapeDtypeStruct((HD, total), F32),
            jax.ShapeDtypeStruct((rows, HD), F32),
            jax.ShapeDtypeStruct((rows, HD), F32),
        ],
        in_specs=[VMEM] * (3 + KEPT),
        out_specs=[VMEM] * 6,
        compiler_params=params(16),
        cost_estimate=cost(prompt.shape[1], rows, total),
        name="attend_head",
    )(prompt, *kept, q_gain, acc)


def settle_heads(meta, q_gain, k_gain, per_head, q_width, k_width):
    count = len(per_head)
    total = per_head[0][0].shape[1]
    rows = per_head[0][5].shape[0]
    flat = [x for group in per_head for x in group]
    return pl.pallas_call(
        functools.partial(settle_kernel, 2 * HD),
        out_shape=out_shapes(rows, q_width, k_width),
        in_specs=[SMEM] + [VMEM] * (2 + len(flat)),
        out_specs=[HBM] * 4,
        scratch_shapes=out_scratch(count, rows, total // rows),
        compiler_params=params(16),
        name="settle_heads",
    )(meta, q_gain, k_gain, *flat)


TAIL = 16


def join_kernel(own_ref, *rest):
    backs, gains_ref, out_ref = rest[:-2], rest[-2], rest[-1]
    depth, rows, _ = own_ref.shape
    for d in range(depth):
        total = own_ref[d].astype(F32)
        for back in backs:
            total = total + back[d].astype(F32)
        out_ref[d * rows : (d + 1) * rows, :] = total.astype(BF)
    gains = gains_ref[...]
    high = gains.astype(BF)
    gains = gains - high.astype(F32)
    middle = gains.astype(BF)
    low = (gains - middle.astype(F32)).astype(BF)
    pieces = jnp.concatenate([p[0:2].astype(F32) for p in (high, middle, low)], axis=0)
    pad = jnp.zeros((TAIL - pieces.shape[0], HD), F32)
    out_ref[depth * rows :, :] = jnp.concatenate([pieces, pad], axis=0).astype(BF)


def join(own, backs, gains):
    depth, rows, _ = own.shape
    return pl.pallas_call(
        join_kernel,
        out_shape=jax.ShapeDtypeStruct((depth * rows + TAIL, HD), BF),
        in_specs=[VMEM] * (2 + len(backs)),
        out_specs=VMEM,
        compiler_params=params(8),
        name="join_parts",
    )(own, *backs, gains)


def place_kernel(meta, *refs):
    payloads, out_ref, gain_ref, stage = refs[:-3], refs[-3], refs[-2], refs[-1]
    mine = meta[meta.shape[0] - 1] > 0
    depth, rows, _ = out_ref.shape
    for i, ref in enumerate(payloads):
        at = pl.multiple_of(meta[i] * HD, HD)
        for d in range(depth):
            block = ref[d * rows : (d + 1) * rows, :]
            out_ref[d, :, pl.ds(at, HD)] = jnp.where(mine, block, jnp.zeros_like(block))
        tail = ref[depth * rows :, :].astype(F32)
        stage[meta[i]] = tail[0:2] + tail[2:4] + tail[4:6]
    total = stage[0]
    for i in range(1, len(payloads)):
        total = total + stage[i]
    gain_ref[...] = total


def place(meta, payloads, depth, rows):
    count = len(payloads)
    return pl.pallas_call(
        place_kernel,
        out_shape=[
            jax.ShapeDtypeStruct((depth, rows, HD * count), BF),
            jax.ShapeDtypeStruct((2, HD), F32),
        ],
        in_specs=[SMEM] + [VMEM] * count,
        out_specs=[VMEM, VMEM],
        scratch_shapes=[pltpu.VMEM((count, 2, HD), F32)],
        compiler_params=params(8),
        name="place_prompt_grad",
    )(meta, *payloads)


def after(x, *others):
    return lax.optimization_barrier((x,) + others)[0]


def pair_sum(value, axis, size):
    step = 1
    while step < size:
        value = value + lax.ppermute(value, axis, [(i, i ^ step) for i in range(size)])
        step *= 2
    return value


def local(
    n_dp, n_group, queries, resp_keys, resp_values, prompt_cache, owners, lengths, q_gain, k_gain, grad_out
):
    q, g = queries[0, 0], grad_out[0, 0]
    k, v = resp_keys[0, 0], resp_values[0, 0]
    cache = prompt_cache[0, 0]
    owner = owners[0]
    live_len = lengths[0, 0]
    me = lax.axis_index("group")
    kv_heads = k.shape[1] // HD
    depth, p_rows, _ = cache.shape
    direct = n_group == kv_heads

    q_row = q_gain[None, :]
    k_row = k_gain[None, :]
    order = jnp.arange(kv_heads, dtype=jnp.int32)
    if direct:
        order = order ^ me
    turn = lax.axis_index("dp") % 2 if direct else jnp.int32(0)
    mine_flag = (me == owner).astype(jnp.int32)
    meta = jnp.concatenate([order, jnp.stack([live_len, turn.astype(jnp.int32), owner ^ me, mine_flag])])
    q, g, k, v, *gains_in = [
        pltpu.with_memory_space_constraint(x, pltpu.HBM) for x in (q, g, k, v, q_gain, k_gain)
    ]
    half = kv_heads // 2 if direct else kv_heads
    ahead, beside = tuple(range(half)), tuple(range(half, kv_heads))
    acc = jnp.zeros((2, HD), F32)
    kept = prepare(0 if direct else None, ahead, meta, q, g, k, v, *gains_in)

    def swap(x, step):
        return lax.ppermute(x, "group", [(i, i ^ step) for i in range(n_group)])

    if direct:
        blocks = list(cut(order, pltpu.with_memory_space_constraint(cache, pltpu.HBM), kv_heads))
        blocks[1:] = [after(x, kept[0][2]) for x in blocks[1:]]
        got = [blocks[0]] + [swap(blocks[s], s) for s in range(1, n_group)]
        kept = prepare(1, ahead, meta, q, g, k, v, *gains_in, kept)
        kept += prepare(None, beside, meta, q, g, k, v, *gains_in)
        for s in range(1, n_group):
            got[s] = after(got[s], kept[0][2], kept[-1][2])
        mine = pick(meta, got)
        prompts = [mine] + [swap(mine, s) for s in range(1, n_group)]
    else:
        cache = lax.psum(jnp.where(me == owner, cache, jnp.zeros_like(cache)), "group")
        prompts = cut(order, cache, kv_heads)

    parts, backs, per_head = [], [], []
    for s, prompt in enumerate(prompts):
        part, acc, *results = first_half(prompt, kept[s], q_row, acc)
        per_head.append([kept[s][0], kept[s][2], kept[s][7], *results])
        parts.append(part)
        if direct and s > 0:
            backs.append(swap(part, s))

    def hop(x, step):
        return lax.ppermute(x, "dp", [(i, i ^ step) for i in range(n_dp)])

    gains = acc + hop(acc, 1)
    if direct:
        gains = after(gains, *backs[:-1])
    step = 2
    while step < n_dp:
        if 2 * step < n_dp:
            near, far, both = hop(gains, step), hop(gains, 2 * step), hop(gains, 3 * step)
            if direct:
                near = after(near, *backs)
            gains = (gains + near) + (far + both)
            step *= 4
        else:
            gains = gains + hop(gains, step)
            step *= 2
    if direct:
        payload = join(parts[0], backs, gains)
        payloads = [payload] + [swap(payload, s) for s in range(1, n_group)]
        per_head[0][3] = after(per_head[0][3], payload)
        buffers = settle_heads(meta, q_row, k_row, per_head, q.shape[1], k.shape[1])
        payloads[1] = after(payloads[1], buffers[2])
        placed, gains = place(meta, payloads, depth, p_rows)
    else:
        total = lax.psum(jnp.concatenate(parts, axis=-1).astype(F32), "group").astype(BF)
        placed = jnp.where(mine_flag > 0, total, jnp.zeros((), BF))
        gains = pair_sum(gains, "group", n_group)
        buffers = settle_heads(meta, q_row, k_row, per_head, q.shape[1], k.shape[1])
    attended, d_query, d_key, d_value = buffers
    return (
        attended[None, None],
        d_query[None, None],
        d_key[None, None],
        d_value[None, None],
        placed[None, None],
        gains,
    )


def solution(mesh):
    in_specs = (
        P("dp", "group", None, None),
        P("dp", "group", None, None),
        P("dp", "group", None, None),
        P("dp", "group", None, None, None),
        P("dp"),
        P("dp", "group"),
        P(),
        P(),
        P("dp", "group", None, None),
    )
    out_specs = (
        P("dp", "group", None, None),
        P("dp", "group", None, None),
        P("dp", "group", None, None),
        P("dp", "group", None, None),
        P("dp", "group", None, None, None),
        P(),
    )
    body = functools.partial(local, mesh.shape["dp"], mesh.shape["group"])
    return jax.shard_map(body, mesh=mesh, in_specs=in_specs, out_specs=out_specs, check_vma=False)
```

```python
import functools

import jax
import jax.numpy as jnp
from jax import lax
from jax.experimental import pallas as pl
from jax.experimental.pallas import tpu as pltpu
from jax.sharding import PartitionSpec as P

HD = 128
EPS = 1e-06
LOG2E = 1.4426950408889634
BF = jnp.bfloat16
F32 = jnp.float32


def dot_nn(a, b):
    return lax.dot_general(a, b, (((1,), (0,)), ((), ())), preferred_element_type=F32)


def dot_nt(a, b):
    return lax.dot_general(a, b, (((1,), (1,)), ((), ())), preferred_element_type=F32)


VMEM = pl.BlockSpec(memory_space=pltpu.VMEM)
SMEM = pl.BlockSpec(memory_space=pltpu.SMEM)
HBM = pl.BlockSpec(memory_space=pltpu.HBM)


def params(mib):
    return pltpu.CompilerParams(vmem_limit_bytes=mib * 2**20)


def cut_kernel(order, cache_ref, *rest):
    outs, sems = rest[:-1], rest[-1]
    copies = []
    for i, out in enumerate(outs):
        at = pl.multiple_of(order[i] * HD, HD)
        copy = pltpu.make_async_copy(cache_ref.at[:, :, pl.ds(at, HD)], out, sems.at[i])
        copy.start()
        copies.append(copy)
    for copy in copies:
        copy.wait()


def cut(order, cache, count):
    depth, rows, _ = cache.shape
    return pl.pallas_call(
        cut_kernel,
        out_shape=[jax.ShapeDtypeStruct((depth, rows, HD), BF)] * count,
        in_specs=[SMEM, HBM],
        out_specs=[VMEM] * count,
        scratch_shapes=[pltpu.SemaphoreType.DMA((count,))],
        compiler_params=params(4),
        name="cut_prompt",
    )(order, cache)


def pick_kernel(meta, *refs):
    picked = refs[0][...]
    for i in range(1, len(refs) - 1):
        picked = jnp.where(meta[meta.shape[0] - 2] == i, refs[i][...], picked)
    refs[-1][...] = picked


def pick(meta, blocks):
    return pl.pallas_call(
        pick_kernel,
        out_shape=jax.ShapeDtypeStruct(blocks[0].shape, BF),
        in_specs=[SMEM] + [VMEM] * len(blocks),
        out_specs=VMEM,
        compiler_params=params(4),
        name="pick_owner",
    )(meta, *blocks)


KEPT = 8


def column(row):
    return jnp.broadcast_to(row, (8, HD)).T[:, 0:1]


def prepare_kernel(slots, share, rows, width, meta, q_in, g_in, k_in, v_in, gain_ref, kg_ref, *rest):
    outs, (q_buf, g_buf, k_buf, v_buf, gain_buf, sems) = rest[:-6], rest[-6:]
    live_len = meta[meta.shape[0] - 3]
    count = len(slots)
    scale = HD ** (-0.5)
    wide = share * HD
    copies = []
    for s, slot in enumerate(slots):
        group = []
        for j, (src, buf, size) in enumerate(
            ((q_in, q_buf, wide), (k_in, k_buf, HD), (g_in, g_buf, wide), (v_in, v_buf, HD))
        ):
            at = pl.multiple_of(meta[slot] * size, size)
            copy = pltpu.make_async_copy(src.at[:, pl.ds(at, size)], buf.at[s], sems.at[s, j])
            copy.start()
            group.append(copy)
        copies.append(group)
    gains = []
    for j, src in enumerate((gain_ref, kg_ref)):
        copy = pltpu.make_async_copy(src, gain_buf.at[j], sems.at[count, j])
        copy.start()
        gains.append(copy)
    for copy in gains:
        copy.wait()
    q_row = gain_buf[0].reshape(1, HD)
    q_gain = column(q_row)
    k_gain = gain_buf[1].reshape(1, HD)
    for s in range(count):
        qt_ref, gt_ref, row_ref, er_ref, ot_ref, dp_ref, kh_ref, ku_ref = outs[s * KEPT : (s + 1) * KEPT]
        for copy in copies[s]:
            copy.wait()
        q_t = jnp.concatenate([q_buf[s, :, i * HD : (i + 1) * HD] for i in range(share)], axis=0).T
        g_t = jnp.concatenate([g_buf[s, :, i * HD : (i + 1) * HD] for i in range(share)], axis=0).T
        qt_ref[...] = q_t
        row_ref[2:3, :HD] = q_row
        row_ref[3:4, :HD] = k_gain
        raw_k = k_buf[s].astype(F32)
        k_inv = lax.rsqrt(jnp.mean(raw_k * raw_k, axis=-1, keepdims=True) + EPS)
        k_unit = raw_k * k_inv
        k_hat = (k_unit * k_gain).astype(BF)
        kh_ref[...] = k_hat
        ku_ref[:, :HD] = k_unit
        ku_ref[:, HD:] = jnp.broadcast_to(k_inv, (rows, HD))
        r_val = v_buf[s]
        r_val_t = r_val.T
        for start in range(0, share * rows, width):
            cols = slice(start, start + width)
            token = (lax.broadcasted_iota(jnp.int32, (1, width), 1) + start) % rows
            raw_q = q_t[:, cols].astype(F32)
            q_inv = lax.rsqrt(jnp.mean(raw_q * raw_q, axis=0, keepdims=True) + EPS)
            q_hat = (raw_q * q_inv * q_gain).astype(BF)
            d_o = jnp.where(token < live_len, g_t[:, cols].astype(F32), 0.0).astype(BF)
            gt_ref[:, cols] = d_o
            causal = lax.broadcasted_iota(jnp.int32, (rows, width), 0) <= token
            e_r = jnp.where(causal, jnp.exp2(dot_nn(k_hat, q_hat) * (scale * LOG2E)), 0.0)
            eb_r = e_r.astype(BF)
            er_ref[:, cols] = eb_r
            ot_ref[:, cols] = dot_nn(r_val_t, eb_r)
            dp_ref[:, cols] = dot_nn(r_val, d_o)
            row_ref[0:1, cols] = q_inv
            row_ref[1:2, cols] = jnp.sum(e_r, axis=0, keepdims=True)


def prepare(slots, meta, q, g, k, v, q_gain, k_gain):
    count = len(slots)
    rows, q_width = q.shape
    share = q_width // k.shape[1]
    total = share * rows
    each = [
        jax.ShapeDtypeStruct((HD, total), BF),
        jax.ShapeDtypeStruct((HD, total), BF),
        jax.ShapeDtypeStruct((8, total), F32),
        jax.ShapeDtypeStruct((rows, total), BF),
        jax.ShapeDtypeStruct((HD, total), F32),
        jax.ShapeDtypeStruct((rows, total), F32),
        jax.ShapeDtypeStruct((rows, HD), BF),
        jax.ShapeDtypeStruct((rows, 2 * HD), F32),
    ]
    outs = pl.pallas_call(
        functools.partial(prepare_kernel, slots, share, rows, 2 * HD),
        out_shape=each * count,
        in_specs=[SMEM] + [HBM] * 6,
        out_specs=[VMEM] * (KEPT * count),
        scratch_shapes=[
            pltpu.VMEM((count, rows, share * HD), BF),
            pltpu.VMEM((count, rows, share * HD), BF),
            pltpu.VMEM((count, rows, HD), BF),
            pltpu.VMEM((count, rows, HD), BF),
            pltpu.VMEM((2, HD), F32),
            pltpu.SemaphoreType.DMA((count + 1, 4)),
        ],
        compiler_params=params(16),
        cost_estimate=pl.CostEstimate(
            flops=6 * count * total * rows * HD,
            bytes_accessed=5 * rows * q_width * 2,
            transcendentals=count * total * rows,
        ),
        name="prepare_response",
    )(meta, q, g, k, v, q_gain, k_gain)
    return [list(outs[s * KEPT : (s + 1) * KEPT]) for s in range(count)]


def attend(width, pr_ref, kept, acc_ref, part_ref, at_ref, dq_ref, gacc_ref):
    qt_ref, gt_ref, row_ref, er_ref, ot_ref, dp_ref, kh_ref, ku_ref = kept
    scale = HD ** (-0.5)
    q_gain = column(row_ref[2:3, :HD])
    p_key = pr_ref[0]
    p_val = pr_ref[1]
    k_hat_t = kh_ref[...].T
    p_key_t = p_key.T
    p_val_t = p_val.T
    sums = None
    for start in range(0, qt_ref.shape[1], width):
        cols = slice(start, start + width)
        q_unit = qt_ref[:, cols].astype(F32) * row_ref[0:1, cols]
        q_hat = (q_unit * q_gain).astype(BF)
        d_ob = gt_ref[:, cols]
        d_o = d_ob.astype(F32)
        e_p = jnp.exp2(dot_nn(p_key, q_hat) * (scale * LOG2E))
        inv_sum = 1.0 / (jnp.sum(e_p, axis=0, keepdims=True) + row_ref[1:2, cols])
        eb_p = e_p.astype(BF)
        eb_r = er_ref[:, cols]
        out = (dot_nn(p_val_t, eb_p) + ot_ref[:, cols]) * inv_sum
        at_ref[:, cols] = out.astype(BF)
        delta = jnp.sum(d_o * out, axis=0, keepdims=True)
        ds_p = (e_p * (dot_nn(p_val, d_ob) - delta)).astype(BF)
        ds_r = (eb_r.astype(F32) * (dp_ref[:, cols] - delta)).astype(BF)
        weight = inv_sum * scale
        q_w = (q_hat.astype(F32) * weight).astype(BF)
        d_ow = (d_o * inv_sum).astype(BF)
        d_qhat = (dot_nn(p_key_t, ds_p) + dot_nn(k_hat_t, ds_r)) * weight
        dq_ref[:, cols] = d_qhat
        terms = (
            dot_nt(ds_p, q_w),
            dot_nt(eb_p, d_ow),
            dot_nt(ds_r, q_w),
            dot_nt(eb_r, d_ow),
            d_qhat * q_unit,
        )
        sums = terms if sums is None else [a + b for a, b in zip(sums, terms)]
    d_kp, d_vp, d_kr, d_vr, q_term = sums
    part_ref[0] = d_kp.astype(BF)
    part_ref[1] = d_vp.astype(BF)
    folded = q_term[:, :HD]
    for start in range(HD, width, HD):
        folded = folded + q_term[:, start : start + HD]
    gacc_ref[0:1, :] = acc_ref[0:1, :] + jnp.sum(folded.T, axis=0, keepdims=True)
    gacc_ref[1:2, :] = acc_ref[1:2, :] + jnp.sum(d_kr * ku_ref[:, :HD], axis=0, keepdims=True)
    return d_kr, d_vr


def settle(width, head, live_len, kept, at_ref, dq_ref, d_kr, d_vr, outs, bufs, sems):
    qt_ref, row_ref, ku_ref = kept
    q_gain = column(row_ref[2:3, :HD])
    k_gain = row_ref[3:4, :HD]
    a_buf, q_buf, k_buf, v_buf = bufs
    rows, wide = a_buf.shape
    share = wide // HD
    copies = []

    def send(j, buf):
        size = buf.shape[1]
        at = pl.multiple_of(head * size, size)
        copy = pltpu.make_async_copy(buf, outs[j].at[:, pl.ds(at, size)], sems.at[j])
        copy.start()
        copies.append(copy)

    att = at_ref[...].T
    live = lax.broadcasted_iota(jnp.int32, (rows, HD), 0) < live_len
    for i in range(share):
        block = att[i * rows : (i + 1) * rows, :].astype(F32)
        a_buf[:, i * HD : (i + 1) * HD] = jnp.where(live, block, 0.0).astype(BF)
    send(0, a_buf)
    v_buf[...] = d_vr.astype(BF)
    send(3, v_buf)
    k_unit = ku_ref[:, :HD]
    up_k = d_kr * k_gain
    mean_k = jnp.mean(up_k * k_unit, axis=-1, keepdims=True)
    k_buf[...] = (ku_ref[:, HD:] * (up_k - k_unit * mean_k)).astype(BF)
    send(2, k_buf)
    parts = []
    for start in range(0, share * rows, width):
        cols = slice(start, start + width)
        q_inv = row_ref[0:1, cols]
        q_unit = qt_ref[:, cols].astype(F32) * q_inv
        up = dq_ref[:, cols] * q_gain
        mean = jnp.mean(up * q_unit, axis=0, keepdims=True)
        parts.append((q_inv * (up - q_unit * mean)).astype(BF))
    d_q = jnp.concatenate(parts, axis=1).T
    for i in range(share):
        q_buf[:, i * HD : (i + 1) * HD] = d_q[i * rows : (i + 1) * rows, :]
    send(1, q_buf)
    return copies


def first_kernel(width, pr_ref, *rest):
    kept, acc_ref = rest[:KEPT], rest[KEPT]
    part_ref, gacc_ref, at_ref, dq_ref, dkr_ref, dvr_ref = rest[-6:]
    d_kr, d_vr = attend(width, pr_ref, kept, acc_ref, part_ref, at_ref, dq_ref, gacc_ref)
    dkr_ref[...] = d_kr
    dvr_ref[...] = d_vr


def settle_kernel(width, meta, *rest):
    outs, bufs, sems = rest[-9:-5], rest[-5:-1], rest[-1]
    copies = []
    for i in range(sems.shape[0]):
        kept, results = rest[i * 7 : i * 7 + 3], rest[i * 7 + 3 : i * 7 + 7]
        at_ref, dq_ref, dkr_ref, dvr_ref = results
        copies += settle(
            width, meta[i], meta[meta.shape[0] - 3], kept, at_ref, dq_ref,
            dkr_ref[...], dvr_ref[...], outs, [buf.at[i] for buf in bufs], sems.at[i],
        )
    for copy in copies:
        copy.wait()


def out_shapes(rows, q_width, k_width):
    widths = (q_width, q_width, k_width, k_width)
    return [jax.ShapeDtypeStruct((rows, w), BF) for w in widths]


def out_scratch(count, rows, share):
    widths = (share * HD, share * HD, HD, HD)
    return [pltpu.VMEM((count, rows, w), BF) for w in widths] + [pltpu.SemaphoreType.DMA((count, 4))]


def cost(prompt_rows, rows, total):
    return pl.CostEstimate(
        flops=(8 * prompt_rows + 4 * rows) * total * HD,
        bytes_accessed=2**20,
        transcendentals=total * prompt_rows,
    )


def first_half(prompt, kept, acc):
    total = kept[0].shape[1]
    rows = kept[3].shape[0]
    return pl.pallas_call(
        functools.partial(first_kernel, 2 * HD),
        out_shape=[
            jax.ShapeDtypeStruct(prompt.shape, BF),
            jax.ShapeDtypeStruct(acc.shape, F32),
            jax.ShapeDtypeStruct((HD, total), BF),
            jax.ShapeDtypeStruct((HD, total), F32),
            jax.ShapeDtypeStruct((rows, HD), F32),
            jax.ShapeDtypeStruct((rows, HD), F32),
        ],
        in_specs=[VMEM] * (2 + KEPT),
        out_specs=[VMEM] * 6,
        compiler_params=params(16),
        cost_estimate=cost(prompt.shape[1], rows, total),
        name="attend_head",
    )(prompt, *kept, acc)


def settle_heads(meta, per_head, q_width, k_width):
    count = len(per_head)
    total = per_head[0][0].shape[1]
    rows = per_head[0][5].shape[0]
    flat = [x for group in per_head for x in group]
    return pl.pallas_call(
        functools.partial(settle_kernel, 2 * HD),
        out_shape=out_shapes(rows, q_width, k_width),
        in_specs=[SMEM] + [VMEM] * len(flat),
        out_specs=[HBM] * 4,
        scratch_shapes=out_scratch(count, rows, total // rows),
        compiler_params=params(16),
        name="settle_heads",
    )(meta, *flat)


TAIL = 16


def join_kernel(own_ref, *rest):
    backs, gains_ref, out_ref = rest[:-2], rest[-2], rest[-1]
    depth, rows, _ = own_ref.shape
    for d in range(depth):
        total = own_ref[d].astype(F32)
        for back in backs:
            total = total + back[d].astype(F32)
        out_ref[d * rows : (d + 1) * rows, :] = total.astype(BF)
    gains = gains_ref[...]
    high = gains.astype(BF)
    gains = gains - high.astype(F32)
    middle = gains.astype(BF)
    low = (gains - middle.astype(F32)).astype(BF)
    pieces = jnp.concatenate([p[0:2].astype(F32) for p in (high, middle, low)], axis=0)
    pad = jnp.zeros((TAIL - pieces.shape[0], HD), F32)
    out_ref[depth * rows :, :] = jnp.concatenate([pieces, pad], axis=0).astype(BF)


def join(own, backs, gains):
    depth, rows, _ = own.shape
    return pl.pallas_call(
        join_kernel,
        out_shape=jax.ShapeDtypeStruct((depth * rows + TAIL, HD), BF),
        in_specs=[VMEM] * (2 + len(backs)),
        out_specs=VMEM,
        compiler_params=params(8),
        name="join_parts",
    )(own, *backs, gains)


def place_kernel(meta, *refs):
    payloads, out_ref, gain_ref, stage = refs[:-3], refs[-3], refs[-2], refs[-1]
    mine = meta[meta.shape[0] - 1] > 0
    depth, rows, _ = out_ref.shape
    for i, ref in enumerate(payloads):
        at = pl.multiple_of(meta[i] * HD, HD)
        for d in range(depth):
            block = ref[d * rows : (d + 1) * rows, :]
            out_ref[d, :, pl.ds(at, HD)] = jnp.where(mine, block, jnp.zeros_like(block))
        tail = ref[depth * rows :, :].astype(F32)
        stage[meta[i]] = tail[0:2] + tail[2:4] + tail[4:6]
    total = stage[0]
    for i in range(1, len(payloads)):
        total = total + stage[i]
    gain_ref[...] = total


def place(meta, payloads, depth, rows):
    count = len(payloads)
    return pl.pallas_call(
        place_kernel,
        out_shape=[
            jax.ShapeDtypeStruct((depth, rows, HD * count), BF),
            jax.ShapeDtypeStruct((2, HD), F32),
        ],
        in_specs=[SMEM] + [VMEM] * count,
        out_specs=[VMEM, VMEM],
        scratch_shapes=[pltpu.VMEM((count, 2, HD), F32)],
        compiler_params=params(8),
        name="place_prompt_grad",
    )(meta, *payloads)


def after(x, *others):
    return lax.optimization_barrier((x,) + others)[0]


def pair_sum(value, axis, size):
    step = 1
    while step < size:
        value = value + lax.ppermute(value, axis, [(i, i ^ step) for i in range(size)])
        step *= 2
    return value


def local(
    n_dp, n_group, queries, resp_keys, resp_values, prompt_cache, owners, lengths, q_gain, k_gain, grad_out
):
    q, g = queries[0, 0], grad_out[0, 0]
    k, v = resp_keys[0, 0], resp_values[0, 0]
    cache = prompt_cache[0, 0]
    owner = owners[0]
    live_len = lengths[0, 0]
    me = lax.axis_index("group")
    kv_heads = k.shape[1] // HD
    depth, p_rows, _ = cache.shape
    direct = n_group == kv_heads

    order = jnp.arange(kv_heads, dtype=jnp.int32)
    if direct:
        order = order ^ me
    mine_flag = (me == owner).astype(jnp.int32)
    meta = jnp.concatenate([order, jnp.stack([live_len, owner ^ me, mine_flag])])
    q, g, k, v, *gains_in = [
        pltpu.with_memory_space_constraint(x, pltpu.HBM) for x in (q, g, k, v, q_gain, k_gain)
    ]
    acc = jnp.zeros((2, HD), F32)
    kept = prepare(tuple(range(kv_heads)), meta, q, g, k, v, *gains_in)

    def swap(x, step):
        return lax.ppermute(x, "group", [(i, i ^ step) for i in range(n_group)])

    if direct:
        blocks = list(cut(order, pltpu.with_memory_space_constraint(cache, pltpu.HBM), kv_heads))
        got = [blocks[0]] + [swap(blocks[s], s) for s in range(1, n_group)]
        for s in range(1, n_group):
            got[s] = after(got[s], kept[0][2])
        mine = pick(meta, got)
        prompts = [mine] + [swap(mine, s) for s in range(1, n_group)]
    else:
        cache = lax.psum(jnp.where(me == owner, cache, jnp.zeros_like(cache)), "group")
        prompts = cut(order, cache, kv_heads)

    parts, backs, per_head = [], [], []
    for s, prompt in enumerate(prompts):
        part, acc, *results = first_half(prompt, kept[s], acc)
        per_head.append([kept[s][0], kept[s][2], kept[s][7], *results])
        parts.append(part)
        if direct and s > 0:
            backs.append(swap(part, s))

    def hop(x, step):
        return lax.ppermute(x, "dp", [(i, i ^ step) for i in range(n_dp)])

    gains = acc + hop(acc, 1)
    if direct:
        gains = after(gains, *backs[:-1])
    step = 2
    while step < n_dp:
        gains = gains + hop(gains, step)
        step *= 2
    if direct:
        payload = join(parts[0], backs, gains)
        payloads = [payload] + [swap(payload, s) for s in range(1, n_group)]
        per_head[0][3] = after(per_head[0][3], payload)
        buffers = settle_heads(meta, per_head, q.shape[1], k.shape[1])
        payloads[1] = after(payloads[1], buffers[2])
        placed, gains = place(meta, payloads, depth, p_rows)
    else:
        total = lax.psum(jnp.concatenate(parts, axis=-1).astype(F32), "group").astype(BF)
        placed = jnp.where(mine_flag > 0, total, jnp.zeros((), BF))
        gains = pair_sum(gains, "group", n_group)
        buffers = settle_heads(meta, per_head, q.shape[1], k.shape[1])
    attended, d_query, d_key, d_value = buffers
    return (
        attended[None, None],
        d_query[None, None],
        d_key[None, None],
        d_value[None, None],
        placed[None, None],
        gains,
    )


def solution(mesh):
    in_specs = (
        P("dp", "group", None, None),
        P("dp", "group", None, None),
        P("dp", "group", None, None),
        P("dp", "group", None, None, None),
        P("dp"),
        P("dp", "group"),
        P(),
        P(),
        P("dp", "group", None, None),
    )
    out_specs = (
        P("dp", "group", None, None),
        P("dp", "group", None, None),
        P("dp", "group", None, None),
        P("dp", "group", None, None),
        P("dp", "group", None, None, None),
        P(),
    )
    body = functools.partial(local, mesh.shape["dp"], mesh.shape["group"])
    return jax.shard_map(body, mesh=mesh, in_specs=in_specs, out_specs=out_specs, check_vma=False)
```

```python
import functools

import jax
import jax.numpy as jnp
from jax import lax
from jax.experimental import pallas as pl
from jax.experimental.pallas import tpu as pltpu
from jax.sharding import PartitionSpec as P

HD = 128
EPS = 1e-06
LOG2E = 1.4426950408889634
BF = jnp.bfloat16
F32 = jnp.float32


def dot_nn(a, b):
    return lax.dot_general(a, b, (((1,), (0,)), ((), ())), preferred_element_type=F32)


def dot_nt(a, b):
    return lax.dot_general(a, b, (((1,), (1,)), ((), ())), preferred_element_type=F32)


VMEM = pl.BlockSpec(memory_space=pltpu.VMEM)
SMEM = pl.BlockSpec(memory_space=pltpu.SMEM)
HBM = pl.BlockSpec(memory_space=pltpu.HBM)


def params(mib):
    return pltpu.CompilerParams(vmem_limit_bytes=mib * 2**20)


def cut_kernel(order, cache_ref, *rest):
    outs, sems = rest[:-1], rest[-1]
    copies = []
    for i, out in enumerate(outs):
        at = pl.multiple_of(order[i] * HD, HD)
        copy = pltpu.make_async_copy(cache_ref.at[:, :, pl.ds(at, HD)], out, sems.at[i])
        copy.start()
        copies.append(copy)
    for copy in copies:
        copy.wait()


def cut(order, cache, count):
    depth, rows, _ = cache.shape
    return pl.pallas_call(
        cut_kernel,
        out_shape=[jax.ShapeDtypeStruct((depth, rows, HD), BF)] * count,
        in_specs=[SMEM, HBM],
        out_specs=[VMEM] * count,
        scratch_shapes=[pltpu.SemaphoreType.DMA((count,))],
        compiler_params=params(4),
        name="cut_prompt",
    )(order, cache)


def pick_kernel(meta, *refs):
    picked = refs[0][...]
    for i in range(1, len(refs) - 1):
        picked = jnp.where(meta[meta.shape[0] - 2] == i, refs[i][...], picked)
    refs[-1][...] = picked


def pick(meta, blocks):
    return pl.pallas_call(
        pick_kernel,
        out_shape=jax.ShapeDtypeStruct(blocks[0].shape, BF),
        in_specs=[SMEM] + [VMEM] * len(blocks),
        out_specs=VMEM,
        compiler_params=params(4),
        name="pick_owner",
    )(meta, *blocks)


KEPT = 8


def column(row):
    return jnp.broadcast_to(row, (8, HD)).T[:, 0:1]


def prepare_kernel(slots, share, rows, width, meta, q_in, g_in, k_in, v_in, gain_ref, kg_ref, *rest):
    outs, (q_buf, g_buf, k_buf, v_buf, gain_buf, sems) = rest[:-6], rest[-6:]
    live_len = meta[meta.shape[0] - 3]
    count = len(slots)
    scale = HD ** (-0.5)
    wide = share * HD
    copies = []
    for s, slot in enumerate(slots):
        group = []
        for j, (src, buf, size) in enumerate(
            ((q_in, q_buf, wide), (k_in, k_buf, HD), (g_in, g_buf, wide), (v_in, v_buf, HD))
        ):
            at = pl.multiple_of(meta[slot] * size, size)
            copy = pltpu.make_async_copy(src.at[:, pl.ds(at, size)], buf.at[s], sems.at[s, j])
            copy.start()
            group.append(copy)
        copies.append(group)
    gains = []
    for j, src in enumerate((gain_ref, kg_ref)):
        copy = pltpu.make_async_copy(src, gain_buf.at[j], sems.at[count, j])
        copy.start()
        gains.append(copy)
    for copy in gains:
        copy.wait()
    q_row = gain_buf[0].reshape(1, HD)
    q_gain = column(q_row)
    k_gain = gain_buf[1].reshape(1, HD)
    for s in range(count):
        qt_ref, gt_ref, row_ref, er_ref, ot_ref, dp_ref, kh_ref, ku_ref = outs[s * KEPT : (s + 1) * KEPT]
        for copy in copies[s]:
            copy.wait()
        q_t = jnp.concatenate([q_buf[s, :, i * HD : (i + 1) * HD] for i in range(share)], axis=0).T
        g_t = jnp.concatenate([g_buf[s, :, i * HD : (i + 1) * HD] for i in range(share)], axis=0).T
        qt_ref[...] = q_t
        row_ref[2:3, :HD] = q_row
        row_ref[3:4, :HD] = k_gain
        raw_k = k_buf[s].astype(F32)
        k_inv = lax.rsqrt(jnp.mean(raw_k * raw_k, axis=-1, keepdims=True) + EPS)
        k_unit = raw_k * k_inv
        k_hat = (k_unit * k_gain).astype(BF)
        kh_ref[...] = k_hat
        ku_ref[:, :HD] = k_unit
        ku_ref[:, HD:] = jnp.broadcast_to(k_inv, (rows, HD))
        r_val = v_buf[s]
        r_val_t = r_val.T
        for start in range(0, share * rows, width):
            cols = slice(start, start + width)
            token = (lax.broadcasted_iota(jnp.int32, (1, width), 1) + start) % rows
            raw_q = q_t[:, cols].astype(F32)
            q_inv = lax.rsqrt(jnp.mean(raw_q * raw_q, axis=0, keepdims=True) + EPS)
            q_hat = (raw_q * q_inv * q_gain).astype(BF)
            d_o = jnp.where(token < live_len, g_t[:, cols].astype(F32), 0.0).astype(BF)
            gt_ref[:, cols] = d_o
            causal = lax.broadcasted_iota(jnp.int32, (rows, width), 0) <= token
            e_r = jnp.where(causal, jnp.exp2(dot_nn(k_hat, q_hat) * (scale * LOG2E)), 0.0)
            eb_r = e_r.astype(BF)
            er_ref[:, cols] = eb_r
            ot_ref[:, cols] = dot_nn(r_val_t, eb_r)
            dp_ref[:, cols] = dot_nn(r_val, d_o)
            row_ref[0:1, cols] = q_inv
            row_ref[1:2, cols] = jnp.sum(e_r, axis=0, keepdims=True)


def prepare(slots, meta, q, g, k, v, q_gain, k_gain):
    count = len(slots)
    rows, q_width = q.shape
    share = q_width // k.shape[1]
    total = share * rows
    each = [
        jax.ShapeDtypeStruct((HD, total), BF),
        jax.ShapeDtypeStruct((HD, total), BF),
        jax.ShapeDtypeStruct((8, total), F32),
        jax.ShapeDtypeStruct((rows, total), BF),
        jax.ShapeDtypeStruct((HD, total), F32),
        jax.ShapeDtypeStruct((rows, total), F32),
        jax.ShapeDtypeStruct((rows, HD), BF),
        jax.ShapeDtypeStruct((rows, 2 * HD), F32),
    ]
    outs = pl.pallas_call(
        functools.partial(prepare_kernel, slots, share, rows, 2 * HD),
        out_shape=each * count,
        in_specs=[SMEM] + [HBM] * 6,
        out_specs=[VMEM] * (KEPT * count),
        scratch_shapes=[
            pltpu.VMEM((count, rows, share * HD), BF),
            pltpu.VMEM((count, rows, share * HD), BF),
            pltpu.VMEM((count, rows, HD), BF),
            pltpu.VMEM((count, rows, HD), BF),
            pltpu.VMEM((2, HD), F32),
            pltpu.SemaphoreType.DMA((count + 1, 4)),
        ],
        compiler_params=params(16),
        cost_estimate=pl.CostEstimate(
            flops=6 * count * total * rows * HD,
            bytes_accessed=5 * rows * q_width * 2,
            transcendentals=count * total * rows,
        ),
        name="prepare_response",
    )(meta, q, g, k, v, q_gain, k_gain)
    return [list(outs[s * KEPT : (s + 1) * KEPT]) for s in range(count)]


def attend(width, pr_ref, kept, acc_ref, part_ref, at_ref, dq_ref, gacc_ref):
    qt_ref, gt_ref, row_ref, er_ref, ot_ref, dp_ref, kh_ref, ku_ref = kept
    scale = HD ** (-0.5)
    q_gain = column(row_ref[2:3, :HD])
    p_key = pr_ref[0]
    p_val = pr_ref[1]
    k_hat_t = kh_ref[...].T
    p_key_t = p_key.T
    p_val_t = p_val.T
    sums = None
    for start in range(0, qt_ref.shape[1], width):
        cols = slice(start, start + width)
        q_unit = qt_ref[:, cols].astype(F32) * row_ref[0:1, cols]
        q_hat = (q_unit * q_gain).astype(BF)
        d_ob = gt_ref[:, cols]
        d_o = d_ob.astype(F32)
        e_p = jnp.exp2(dot_nn(p_key, q_hat) * (scale * LOG2E))
        inv_sum = 1.0 / (jnp.sum(e_p, axis=0, keepdims=True) + row_ref[1:2, cols])
        eb_p = e_p.astype(BF)
        eb_r = er_ref[:, cols]
        out = (dot_nn(p_val_t, eb_p) + ot_ref[:, cols]) * inv_sum
        at_ref[:, cols] = out.astype(BF)
        delta = jnp.sum(d_o * out, axis=0, keepdims=True)
        ds_p = (e_p * (dot_nn(p_val, d_ob) - delta)).astype(BF)
        ds_r = (eb_r.astype(F32) * (dp_ref[:, cols] - delta)).astype(BF)
        weight = inv_sum * scale
        q_w = (q_hat.astype(F32) * weight).astype(BF)
        d_ow = (d_o * inv_sum).astype(BF)
        d_qhat = (dot_nn(p_key_t, ds_p) + dot_nn(k_hat_t, ds_r)) * weight
        dq_ref[:, cols] = d_qhat
        terms = (
            dot_nt(ds_p, q_w),
            dot_nt(eb_p, d_ow),
            dot_nt(ds_r, q_w),
            dot_nt(eb_r, d_ow),
            d_qhat * q_unit,
        )
        sums = terms if sums is None else [a + b for a, b in zip(sums, terms)]
    d_kp, d_vp, d_kr, d_vr, q_term = sums
    part_ref[0] = d_kp.astype(BF)
    part_ref[1] = d_vp.astype(BF)
    folded = q_term[:, :HD]
    for start in range(HD, width, HD):
        folded = folded + q_term[:, start : start + HD]
    gacc_ref[0:1, :] = acc_ref[0:1, :] + jnp.sum(folded.T, axis=0, keepdims=True)
    gacc_ref[1:2, :] = acc_ref[1:2, :] + jnp.sum(d_kr * ku_ref[:, :HD], axis=0, keepdims=True)
    return d_kr, d_vr


def settle(width, head, live_len, kept, at_ref, dq_ref, d_kr, d_vr, outs, bufs, sems):
    qt_ref, row_ref, ku_ref = kept
    q_gain = column(row_ref[2:3, :HD])
    k_gain = row_ref[3:4, :HD]
    a_buf, q_buf, k_buf, v_buf = bufs
    rows, wide = a_buf.shape
    share = wide // HD
    copies = []

    def send(j, buf):
        size = buf.shape[1]
        at = pl.multiple_of(head * size, size)
        copy = pltpu.make_async_copy(buf, outs[j].at[:, pl.ds(at, size)], sems.at[j])
        copy.start()
        copies.append(copy)

    att = at_ref[...].T
    live = lax.broadcasted_iota(jnp.int32, (rows, HD), 0) < live_len
    for i in range(share):
        block = att[i * rows : (i + 1) * rows, :].astype(F32)
        a_buf[:, i * HD : (i + 1) * HD] = jnp.where(live, block, 0.0).astype(BF)
    send(0, a_buf)
    v_buf[...] = d_vr.astype(BF)
    send(3, v_buf)
    k_unit = ku_ref[:, :HD]
    up_k = d_kr * k_gain
    mean_k = jnp.mean(up_k * k_unit, axis=-1, keepdims=True)
    k_buf[...] = (ku_ref[:, HD:] * (up_k - k_unit * mean_k)).astype(BF)
    send(2, k_buf)
    parts = []
    for start in range(0, share * rows, width):
        cols = slice(start, start + width)
        q_inv = row_ref[0:1, cols]
        q_unit = qt_ref[:, cols].astype(F32) * q_inv
        up = dq_ref[:, cols] * q_gain
        mean = jnp.mean(up * q_unit, axis=0, keepdims=True)
        parts.append((q_inv * (up - q_unit * mean)).astype(BF))
    d_q = jnp.concatenate(parts, axis=1).T
    for i in range(share):
        q_buf[:, i * HD : (i + 1) * HD] = d_q[i * rows : (i + 1) * rows, :]
    send(1, q_buf)
    return copies


def first_kernel(width, pr_ref, *rest):
    kept, acc_ref = rest[:KEPT], rest[KEPT]
    part_ref, gacc_ref, at_ref, dq_ref, dkr_ref, dvr_ref = rest[-6:]
    d_kr, d_vr = attend(width, pr_ref, kept, acc_ref, part_ref, at_ref, dq_ref, gacc_ref)
    dkr_ref[...] = d_kr
    dvr_ref[...] = d_vr


def settle_kernel(width, meta, *rest):
    outs, bufs, sems = rest[-9:-5], rest[-5:-1], rest[-1]
    copies = []
    for i in range(sems.shape[0]):
        kept, results = rest[i * 7 : i * 7 + 3], rest[i * 7 + 3 : i * 7 + 7]
        at_ref, dq_ref, dkr_ref, dvr_ref = results
        copies += settle(
            width, meta[i], meta[meta.shape[0] - 3], kept, at_ref, dq_ref,
            dkr_ref[...], dvr_ref[...], outs, [buf.at[i] for buf in bufs], sems.at[i],
        )
    for copy in copies:
        copy.wait()


def out_shapes(rows, q_width, k_width):
    widths = (q_width, q_width, k_width, k_width)
    return [jax.ShapeDtypeStruct((rows, w), BF) for w in widths]


def out_scratch(count, rows, share):
    widths = (share * HD, share * HD, HD, HD)
    return [pltpu.VMEM((count, rows, w), BF) for w in widths] + [pltpu.SemaphoreType.DMA((count, 4))]


def cost(prompt_rows, rows, total):
    return pl.CostEstimate(
        flops=(8 * prompt_rows + 4 * rows) * total * HD,
        bytes_accessed=2**20,
        transcendentals=total * prompt_rows,
    )


def first_half(prompt, kept, acc):
    total = kept[0].shape[1]
    rows = kept[3].shape[0]
    return pl.pallas_call(
        functools.partial(first_kernel, 2 * HD),
        out_shape=[
            jax.ShapeDtypeStruct(prompt.shape, BF),
            jax.ShapeDtypeStruct(acc.shape, F32),
            jax.ShapeDtypeStruct((HD, total), BF),
            jax.ShapeDtypeStruct((HD, total), F32),
            jax.ShapeDtypeStruct((rows, HD), F32),
            jax.ShapeDtypeStruct((rows, HD), F32),
        ],
        in_specs=[VMEM] * (2 + KEPT),
        out_specs=[VMEM] * 6,
        compiler_params=params(16),
        cost_estimate=cost(prompt.shape[1], rows, total),
        name="attend_head",
    )(prompt, *kept, acc)


def settle_heads(meta, per_head, q_width, k_width):
    count = len(per_head)
    total = per_head[0][0].shape[1]
    rows = per_head[0][5].shape[0]
    flat = [x for group in per_head for x in group]
    return pl.pallas_call(
        functools.partial(settle_kernel, 2 * HD),
        out_shape=out_shapes(rows, q_width, k_width),
        in_specs=[SMEM] + [VMEM] * len(flat),
        out_specs=[HBM] * 4,
        scratch_shapes=out_scratch(count, rows, total // rows),
        compiler_params=params(16),
        name="settle_heads",
    )(meta, *flat)


TAIL = 16


def join_kernel(own_ref, *rest):
    backs, gains_ref, out_ref = rest[:-2], rest[-2], rest[-1]
    depth, rows, _ = own_ref.shape
    for d in range(depth):
        total = own_ref[d].astype(F32)
        for back in backs:
            total = total + back[d].astype(F32)
        out_ref[d * rows : (d + 1) * rows, :] = total.astype(BF)
    gains = gains_ref[...]
    high = gains.astype(BF)
    gains = gains - high.astype(F32)
    middle = gains.astype(BF)
    low = (gains - middle.astype(F32)).astype(BF)
    pieces = jnp.concatenate([p[0:2].astype(F32) for p in (high, middle, low)], axis=0)
    pad = jnp.zeros((TAIL - pieces.shape[0], HD), F32)
    out_ref[depth * rows :, :] = jnp.concatenate([pieces, pad], axis=0).astype(BF)


def join(own, backs, gains):
    depth, rows, _ = own.shape
    return pl.pallas_call(
        join_kernel,
        out_shape=jax.ShapeDtypeStruct((depth * rows + TAIL, HD), BF),
        in_specs=[VMEM] * (2 + len(backs)),
        out_specs=VMEM,
        compiler_params=params(8),
        name="join_parts",
    )(own, *backs, gains)


def place_kernel(meta, *refs):
    payloads, out_ref, gain_ref, stage = refs[:-3], refs[-3], refs[-2], refs[-1]
    mine = meta[meta.shape[0] - 1] > 0
    depth, rows, _ = out_ref.shape
    for i, ref in enumerate(payloads):
        at = pl.multiple_of(meta[i] * HD, HD)
        for d in range(depth):
            block = ref[d * rows : (d + 1) * rows, :]
            out_ref[d, :, pl.ds(at, HD)] = jnp.where(mine, block, jnp.zeros_like(block))
        tail = ref[depth * rows :, :].astype(F32)
        stage[meta[i]] = tail[0:2] + tail[2:4] + tail[4:6]
    total = stage[0]
    for i in range(1, len(payloads)):
        total = total + stage[i]
    gain_ref[...] = total


def place(meta, payloads, depth, rows):
    count = len(payloads)
    return pl.pallas_call(
        place_kernel,
        out_shape=[
            jax.ShapeDtypeStruct((depth, rows, HD * count), BF),
            jax.ShapeDtypeStruct((2, HD), F32),
        ],
        in_specs=[SMEM] + [VMEM] * count,
        out_specs=[VMEM, VMEM],
        scratch_shapes=[pltpu.VMEM((count, 2, HD), F32)],
        compiler_params=params(8),
        name="place_prompt_grad",
    )(meta, *payloads)


def after(x, *others):
    return lax.optimization_barrier((x,) + others)[0]


def pair_sum(value, axis, size):
    step = 1
    while step < size:
        value = value + lax.ppermute(value, axis, [(i, i ^ step) for i in range(size)])
        step *= 2
    return value


def local(
    n_dp, n_group, queries, resp_keys, resp_values, prompt_cache, owners, lengths, q_gain, k_gain, grad_out
):
    q, g = queries[0, 0], grad_out[0, 0]
    k, v = resp_keys[0, 0], resp_values[0, 0]
    cache = prompt_cache[0, 0]
    owner = owners[0]
    live_len = lengths[0, 0]
    me = lax.axis_index("group")
    kv_heads = k.shape[1] // HD
    depth, p_rows, _ = cache.shape
    direct = n_group == kv_heads and n_group <= 4
    steps = [s ^ (s >> 1) for s in range(kv_heads)]

    order = jnp.arange(kv_heads, dtype=jnp.int32)
    if direct:
        order = order ^ (order >> 1) ^ me
    mine_flag = (me == owner).astype(jnp.int32)
    away = owner ^ me
    meta = jnp.concatenate([order, jnp.stack([live_len, away ^ (away >> 1), mine_flag])])
    q, g, k, v, *gains_in = [
        pltpu.with_memory_space_constraint(x, pltpu.HBM) for x in (q, g, k, v, q_gain, k_gain)
    ]
    acc = jnp.zeros((2, HD), F32)
    kept = prepare(tuple(range(kv_heads)), meta, q, g, k, v, *gains_in)

    def swap(x, step):
        return lax.ppermute(x, "group", [(i, i ^ step) for i in range(n_group)])

    if direct:
        blocks = list(cut(order, pltpu.with_memory_space_constraint(cache, pltpu.HBM), kv_heads))
        got = [blocks[0]] + [swap(blocks[s], steps[s]) for s in range(1, n_group)]
        for s in range(1, n_group):
            got[s] = after(got[s], kept[0][2])
        mine = pick(meta, got)
        prompts = [mine] + [swap(mine, steps[s]) for s in range(1, n_group)]
    else:
        cache = lax.psum(jnp.where(me == owner, cache, jnp.zeros_like(cache)), "group")
        prompts = cut(order, cache, kv_heads)

    parts, backs, per_head = [], [], []
    for s, prompt in enumerate(prompts):
        part, acc, *results = first_half(prompt, kept[s], acc)
        per_head.append([kept[s][0], kept[s][2], kept[s][7], *results])
        parts.append(part)
        if direct and s > 0:
            backs.append(swap(part, steps[s]))

    def hop(x, step):
        return lax.ppermute(x, "dp", [(i, i ^ step) for i in range(n_dp)])

    gains = acc + hop(acc, 1)
    if direct:
        gains = after(gains, *backs[:-1])
    step = 2
    while step < n_dp:
        gains = gains + hop(gains, step)
        step *= 2
    if direct:
        payload = join(parts[0], backs, gains)
        payloads = [payload] + [swap(payload, steps[s]) for s in range(1, n_group)]
        per_head[0][3] = after(per_head[0][3], payload)
        buffers = settle_heads(meta, per_head, q.shape[1], k.shape[1])
        payloads[1] = after(payloads[1], buffers[2])
        placed, gains = place(meta, payloads, depth, p_rows)
    else:
        total = lax.psum(jnp.concatenate(parts, axis=-1).astype(F32), "group").astype(BF)
        placed = jnp.where(mine_flag > 0, total, jnp.zeros((), BF))
        gains = pair_sum(gains, "group", n_group)
        buffers = settle_heads(meta, per_head, q.shape[1], k.shape[1])
    attended, d_query, d_key, d_value = buffers
    return (
        attended[None, None],
        d_query[None, None],
        d_key[None, None],
        d_value[None, None],
        placed[None, None],
        gains,
    )


def solution(mesh):
    in_specs = (
        P("dp", "group", None, None),
        P("dp", "group", None, None),
        P("dp", "group", None, None),
        P("dp", "group", None, None, None),
        P("dp"),
        P("dp", "group"),
        P(),
        P(),
        P("dp", "group", None, None),
    )
    out_specs = (
        P("dp", "group", None, None),
        P("dp", "group", None, None),
        P("dp", "group", None, None),
        P("dp", "group", None, None),
        P("dp", "group", None, None, None),
        P(),
    )
    body = functools.partial(local, mesh.shape["dp"], mesh.shape["group"])
    return jax.shard_map(body, mesh=mesh, in_specs=in_specs, out_specs=out_specs, check_vma=False)
```

```python
import functools

import jax
import jax.numpy as jnp
from jax import lax
from jax.experimental import pallas as pl
from jax.experimental.pallas import tpu as pltpu
from jax.sharding import PartitionSpec as P

HD = 128
EPS = 1e-06
LOG2E = 1.4426950408889634
BF = jnp.bfloat16
F32 = jnp.float32


def dot_nn(a, b):
    return lax.dot_general(a, b, (((1,), (0,)), ((), ())), preferred_element_type=F32)


def dot_nt(a, b):
    return lax.dot_general(a, b, (((1,), (1,)), ((), ())), preferred_element_type=F32)


VMEM = pl.BlockSpec(memory_space=pltpu.VMEM)
SMEM = pl.BlockSpec(memory_space=pltpu.SMEM)
HBM = pl.BlockSpec(memory_space=pltpu.HBM)


def params(mib):
    return pltpu.CompilerParams(vmem_limit_bytes=mib * 2**20)


def cut_kernel(order, cache_ref, *rest):
    outs, sems = rest[:-1], rest[-1]
    copies = []
    for i, out in enumerate(outs):
        at = pl.multiple_of(order[i] * HD, HD)
        copy = pltpu.make_async_copy(cache_ref.at[:, :, pl.ds(at, HD)], out, sems.at[i])
        copy.start()
        copies.append(copy)
    for copy in copies:
        copy.wait()


def cut(order, cache, count):
    depth, rows, _ = cache.shape
    return pl.pallas_call(
        cut_kernel,
        out_shape=[jax.ShapeDtypeStruct((depth, rows, HD), BF)] * count,
        in_specs=[SMEM, HBM],
        out_specs=[VMEM] * count,
        scratch_shapes=[pltpu.SemaphoreType.DMA((count,))],
        compiler_params=params(4),
        name="cut_prompt",
    )(order, cache)


def pick_kernel(which, *refs):
    picked = refs[0][...]
    for i in range(1, len(refs) - 1):
        picked = jnp.where(which[0] == i, refs[i][...], picked)
    refs[-1][...] = picked


def pick(which, blocks):
    return pl.pallas_call(
        pick_kernel,
        out_shape=jax.ShapeDtypeStruct(blocks[0].shape, BF),
        in_specs=[SMEM] + [VMEM] * len(blocks),
        out_specs=VMEM,
        compiler_params=params(4),
        name="pick_owner",
    )(which, *blocks)


KEPT = 8


def column(row):
    return jnp.broadcast_to(row, (8, HD)).T[:, 0:1]


def prepare_kernel(slots, share, rows, width, meta, q_in, g_in, k_in, v_in, gain_ref, kg_ref, *rest):
    outs, (q_buf, g_buf, k_buf, v_buf, gain_buf, sems) = rest[:-6], rest[-6:]
    live_len = meta[meta.shape[0] - 1]
    count = len(slots)
    scale = HD ** (-0.5)
    wide = share * HD
    copies = []
    for s, slot in enumerate(slots):
        group = []
        for j, (src, buf, size) in enumerate(
            ((q_in, q_buf, wide), (k_in, k_buf, HD), (g_in, g_buf, wide), (v_in, v_buf, HD))
        ):
            at = pl.multiple_of(meta[slot] * size, size)
            copy = pltpu.make_async_copy(src.at[:, pl.ds(at, size)], buf.at[s], sems.at[s, j])
            copy.start()
            group.append(copy)
        copies.append(group)
    gains = []
    for j, src in enumerate((gain_ref, kg_ref)):
        copy = pltpu.make_async_copy(src, gain_buf.at[j], sems.at[count, j])
        copy.start()
        gains.append(copy)
    for copy in gains:
        copy.wait()
    q_row = gain_buf[0].reshape(1, HD)
    q_gain = column(q_row)
    k_gain = gain_buf[1].reshape(1, HD)
    for s in range(count):
        qt_ref, gt_ref, row_ref, er_ref, ot_ref, dp_ref, kh_ref, ku_ref = outs[s * KEPT : (s + 1) * KEPT]
        for copy in copies[s]:
            copy.wait()
        q_t = jnp.concatenate([q_buf[s, :, i * HD : (i + 1) * HD] for i in range(share)], axis=0).T
        g_t = jnp.concatenate([g_buf[s, :, i * HD : (i + 1) * HD] for i in range(share)], axis=0).T
        qt_ref[...] = q_t
        row_ref[2:3, :HD] = q_row
        row_ref[3:4, :HD] = k_gain
        raw_k = k_buf[s].astype(F32)
        k_inv = lax.rsqrt(jnp.mean(raw_k * raw_k, axis=-1, keepdims=True) + EPS)
        k_unit = raw_k * k_inv
        k_hat = (k_unit * k_gain).astype(BF)
        kh_ref[...] = k_hat
        ku_ref[:, :HD] = k_unit
        ku_ref[:, HD:] = jnp.broadcast_to(k_inv, (rows, HD))
        r_val = v_buf[s]
        r_val_t = r_val.T
        for start in range(0, share * rows, width):
            cols = slice(start, start + width)
            token = (lax.broadcasted_iota(jnp.int32, (1, width), 1) + start) % rows
            raw_q = q_t[:, cols].astype(F32)
            q_inv = lax.rsqrt(jnp.mean(raw_q * raw_q, axis=0, keepdims=True) + EPS)
            q_hat = (raw_q * q_inv * q_gain).astype(BF)
            d_o = jnp.where(token < live_len, g_t[:, cols].astype(F32), 0.0).astype(BF)
            gt_ref[:, cols] = d_o
            causal = lax.broadcasted_iota(jnp.int32, (rows, width), 0) <= token
            e_r = jnp.where(causal, jnp.exp2(dot_nn(k_hat, q_hat) * (scale * LOG2E)), 0.0)
            eb_r = e_r.astype(BF)
            er_ref[:, cols] = eb_r
            ot_ref[:, cols] = dot_nn(r_val_t, eb_r)
            dp_ref[:, cols] = dot_nn(r_val, d_o)
            row_ref[0:1, cols] = q_inv
            row_ref[1:2, cols] = jnp.sum(e_r, axis=0, keepdims=True)


def prepare(slots, meta, q, g, k, v, q_gain, k_gain):
    count = len(slots)
    rows, q_width = q.shape
    share = q_width // k.shape[1]
    total = share * rows
    each = [
        jax.ShapeDtypeStruct((HD, total), BF),
        jax.ShapeDtypeStruct((HD, total), BF),
        jax.ShapeDtypeStruct((8, total), F32),
        jax.ShapeDtypeStruct((rows, total), BF),
        jax.ShapeDtypeStruct((HD, total), F32),
        jax.ShapeDtypeStruct((rows, total), F32),
        jax.ShapeDtypeStruct((rows, HD), BF),
        jax.ShapeDtypeStruct((rows, 2 * HD), F32),
    ]
    outs = pl.pallas_call(
        functools.partial(prepare_kernel, slots, share, rows, 2 * HD),
        out_shape=each * count,
        in_specs=[SMEM] + [HBM] * 6,
        out_specs=[VMEM] * (KEPT * count),
        scratch_shapes=[
            pltpu.VMEM((count, rows, share * HD), BF),
            pltpu.VMEM((count, rows, share * HD), BF),
            pltpu.VMEM((count, rows, HD), BF),
            pltpu.VMEM((count, rows, HD), BF),
            pltpu.VMEM((2, HD), F32),
            pltpu.SemaphoreType.DMA((count + 1, 4)),
        ],
        compiler_params=params(16),
        cost_estimate=pl.CostEstimate(
            flops=6 * count * total * rows * HD,
            bytes_accessed=5 * rows * q_width * 2,
            transcendentals=count * total * rows,
        ),
        name="prepare_response",
    )(meta, q, g, k, v, q_gain, k_gain)
    return [list(outs[s * KEPT : (s + 1) * KEPT]) for s in range(count)]


def attend(width, pr_ref, kept, acc_ref, part_ref, at_ref, dq_ref, gacc_ref):
    qt_ref, gt_ref, row_ref, er_ref, ot_ref, dp_ref, kh_ref, ku_ref = kept
    scale = HD ** (-0.5)
    q_gain = column(row_ref[2:3, :HD])
    p_key = pr_ref[0]
    p_val = pr_ref[1]
    k_hat_t = kh_ref[...].T
    p_key_t = p_key.T
    p_val_t = p_val.T
    sums = None
    for start in range(0, qt_ref.shape[1], width):
        cols = slice(start, start + width)
        q_unit = qt_ref[:, cols].astype(F32) * row_ref[0:1, cols]
        q_hat = (q_unit * q_gain).astype(BF)
        d_ob = gt_ref[:, cols]
        d_o = d_ob.astype(F32)
        e_p = jnp.exp2(dot_nn(p_key, q_hat) * (scale * LOG2E))
        inv_sum = 1.0 / (jnp.sum(e_p, axis=0, keepdims=True) + row_ref[1:2, cols])
        eb_p = e_p.astype(BF)
        eb_r = er_ref[:, cols]
        out = (dot_nn(p_val_t, eb_p) + ot_ref[:, cols]) * inv_sum
        at_ref[:, cols] = out.astype(BF)
        delta = jnp.sum(d_o * out, axis=0, keepdims=True)
        ds_p = (e_p * (dot_nn(p_val, d_ob) - delta)).astype(BF)
        ds_r = (eb_r.astype(F32) * (dp_ref[:, cols] - delta)).astype(BF)
        weight = inv_sum * scale
        q_w = (q_hat.astype(F32) * weight).astype(BF)
        d_ow = (d_o * inv_sum).astype(BF)
        d_qhat = (dot_nn(p_key_t, ds_p) + dot_nn(k_hat_t, ds_r)) * weight
        dq_ref[:, cols] = d_qhat
        terms = (
            dot_nt(ds_p, q_w),
            dot_nt(eb_p, d_ow),
            dot_nt(ds_r, q_w),
            dot_nt(eb_r, d_ow),
            d_qhat * q_unit,
        )
        sums = terms if sums is None else [a + b for a, b in zip(sums, terms)]
    d_kp, d_vp, d_kr, d_vr, q_term = sums
    part_ref[0] = d_kp.astype(BF)
    part_ref[1] = d_vp.astype(BF)
    folded = q_term[:, :HD]
    for start in range(HD, width, HD):
        folded = folded + q_term[:, start : start + HD]
    gacc_ref[0:1, :] = acc_ref[0:1, :] + jnp.sum(folded.T, axis=0, keepdims=True)
    gacc_ref[1:2, :] = acc_ref[1:2, :] + jnp.sum(d_kr * ku_ref[:, :HD], axis=0, keepdims=True)
    return d_kr, d_vr


def settle(width, head, live_len, kept, at_ref, dq_ref, d_kr, d_vr, outs, bufs, sems):
    qt_ref, row_ref, ku_ref = kept
    q_gain = column(row_ref[2:3, :HD])
    k_gain = row_ref[3:4, :HD]
    a_buf, q_buf, k_buf, v_buf = bufs
    rows, wide = a_buf.shape
    share = wide // HD
    copies = []

    def send(j, buf):
        size = buf.shape[1]
        at = pl.multiple_of(head * size, size)
        copy = pltpu.make_async_copy(buf, outs[j].at[:, pl.ds(at, size)], sems.at[j])
        copy.start()
        copies.append(copy)

    att = at_ref[...].T
    live = lax.broadcasted_iota(jnp.int32, (rows, HD), 0) < live_len
    for i in range(share):
        block = att[i * rows : (i + 1) * rows, :].astype(F32)
        a_buf[:, i * HD : (i + 1) * HD] = jnp.where(live, block, 0.0).astype(BF)
    send(0, a_buf)
    v_buf[...] = d_vr.astype(BF)
    send(3, v_buf)
    k_unit = ku_ref[:, :HD]
    up_k = d_kr * k_gain
    mean_k = jnp.mean(up_k * k_unit, axis=-1, keepdims=True)
    k_buf[...] = (ku_ref[:, HD:] * (up_k - k_unit * mean_k)).astype(BF)
    send(2, k_buf)
    parts = []
    for start in range(0, share * rows, width):
        cols = slice(start, start + width)
        q_inv = row_ref[0:1, cols]
        q_unit = qt_ref[:, cols].astype(F32) * q_inv
        up = dq_ref[:, cols] * q_gain
        mean = jnp.mean(up * q_unit, axis=0, keepdims=True)
        parts.append((q_inv * (up - q_unit * mean)).astype(BF))
    d_q = jnp.concatenate(parts, axis=1).T
    for i in range(share):
        q_buf[:, i * HD : (i + 1) * HD] = d_q[i * rows : (i + 1) * rows, :]
    send(1, q_buf)
    return copies


def first_kernel(width, pr_ref, *rest):
    kept, acc_ref = rest[:KEPT], rest[KEPT]
    part_ref, gacc_ref, at_ref, dq_ref, dkr_ref, dvr_ref = rest[-6:]
    d_kr, d_vr = attend(width, pr_ref, kept, acc_ref, part_ref, at_ref, dq_ref, gacc_ref)
    dkr_ref[...] = d_kr
    dvr_ref[...] = d_vr


def settle_kernel(width, meta, *rest):
    outs, bufs, sems = rest[-9:-5], rest[-5:-1], rest[-1]
    copies = []
    for i in range(sems.shape[0]):
        kept, results = rest[i * 7 : i * 7 + 3], rest[i * 7 + 3 : i * 7 + 7]
        at_ref, dq_ref, dkr_ref, dvr_ref = results
        copies += settle(
            width, meta[i], meta[meta.shape[0] - 1], kept, at_ref, dq_ref,
            dkr_ref[...], dvr_ref[...], outs, [buf.at[i] for buf in bufs], sems.at[i],
        )
    for copy in copies:
        copy.wait()


def out_shapes(rows, q_width, k_width):
    widths = (q_width, q_width, k_width, k_width)
    return [jax.ShapeDtypeStruct((rows, w), BF) for w in widths]


def out_scratch(count, rows, share):
    widths = (share * HD, share * HD, HD, HD)
    return [pltpu.VMEM((count, rows, w), BF) for w in widths] + [pltpu.SemaphoreType.DMA((count, 4))]


def cost(prompt_rows, rows, total):
    return pl.CostEstimate(
        flops=(8 * prompt_rows + 4 * rows) * total * HD,
        bytes_accessed=2**20,
        transcendentals=total * prompt_rows,
    )


def first_half(prompt, kept, acc):
    total = kept[0].shape[1]
    rows = kept[3].shape[0]
    return pl.pallas_call(
        functools.partial(first_kernel, 2 * HD),
        out_shape=[
            jax.ShapeDtypeStruct(prompt.shape, BF),
            jax.ShapeDtypeStruct(acc.shape, F32),
            jax.ShapeDtypeStruct((HD, total), BF),
            jax.ShapeDtypeStruct((HD, total), F32),
            jax.ShapeDtypeStruct((rows, HD), F32),
            jax.ShapeDtypeStruct((rows, HD), F32),
        ],
        in_specs=[VMEM] * (2 + KEPT),
        out_specs=[VMEM] * 6,
        compiler_params=params(16),
        cost_estimate=cost(prompt.shape[1], rows, total),
        name="attend_head",
    )(prompt, *kept, acc)


def settle_heads(meta, per_head, q_width, k_width):
    count = len(per_head)
    total = per_head[0][0].shape[1]
    rows = per_head[0][5].shape[0]
    flat = [x for group in per_head for x in group]
    return pl.pallas_call(
        functools.partial(settle_kernel, 2 * HD),
        out_shape=out_shapes(rows, q_width, k_width),
        in_specs=[SMEM] + [VMEM] * len(flat),
        out_specs=[HBM] * 4,
        scratch_shapes=out_scratch(count, rows, total // rows),
        compiler_params=params(16),
        name="settle_heads",
    )(meta, *flat)


TAIL = 16


def join_kernel(own_ref, *rest):
    backs, gains_ref, out_ref = rest[:-2], rest[-2], rest[-1]
    depth, rows, _ = own_ref.shape
    for d in range(depth):
        total = own_ref[d].astype(F32)
        for back in backs:
            total = total + back[d].astype(F32)
        out_ref[d * rows : (d + 1) * rows, :] = total.astype(BF)
    gains = gains_ref[...]
    high = gains.astype(BF)
    gains = gains - high.astype(F32)
    middle = gains.astype(BF)
    low = (gains - middle.astype(F32)).astype(BF)
    pieces = jnp.concatenate([p[0:2].astype(F32) for p in (high, middle, low)], axis=0)
    pad = jnp.zeros((TAIL - pieces.shape[0], HD), F32)
    out_ref[depth * rows :, :] = jnp.concatenate([pieces, pad], axis=0).astype(BF)


def join(own, backs, gains):
    depth, rows, _ = own.shape
    return pl.pallas_call(
        join_kernel,
        out_shape=jax.ShapeDtypeStruct((depth * rows + TAIL, HD), BF),
        in_specs=[VMEM] * (2 + len(backs)),
        out_specs=VMEM,
        compiler_params=params(8),
        name="join_parts",
    )(own, *backs, gains)


def place_kernel(steps, flag, me, *refs):
    payloads, (out_ref, gain_ref, stage, zeros, sems) = refs[:-5], refs[-5:]
    depth, rows, width = out_ref.shape

    @pl.when(flag[0] > 0)
    def _():
        copies = []
        for i, ref in enumerate(payloads):
            at = pl.ds(pl.multiple_of((me[0] ^ steps[i]) * HD, HD), HD)
            for d in range(depth):
                src = ref.at[d * rows : (d + 1) * rows, :]
                copy = pltpu.make_async_copy(src, out_ref.at[d, :, at], sems.at[i * depth + d])
                copy.start()
                copies.append(copy)
        for copy in copies:
            copy.wait()

    @pl.when(flag[0] == 0)
    def _():
        zeros[...] = jnp.zeros_like(zeros)
        copies = []
        for d in range(depth):
            copy = pltpu.make_async_copy(zeros, out_ref.at[d], sems.at[d])
            copy.start()
            copies.append(copy)
        for copy in copies:
            copy.wait()

    for i, ref in enumerate(payloads):
        tail = ref[depth * rows :, :].astype(F32)
        stage[me[0] ^ steps[i]] = tail[0:2] + tail[2:4] + tail[4:6]
    total = stage[0]
    for i in range(1, len(payloads)):
        total = total + stage[i]
    gain_ref[...] = total


def place(steps, flag, me, payloads, depth, rows):
    count = len(payloads)
    width = HD * count
    return pl.pallas_call(
        functools.partial(place_kernel, tuple(steps)),
        out_shape=[
            jax.ShapeDtypeStruct((depth, rows, width), BF),
            jax.ShapeDtypeStruct((2, HD), F32),
        ],
        in_specs=[SMEM] * 2 + [VMEM] * count,
        out_specs=[HBM, VMEM],
        scratch_shapes=[
            pltpu.VMEM((count, 2, HD), F32),
            pltpu.VMEM((rows, width), BF),
            pltpu.SemaphoreType.DMA((count * depth,)),
        ],
        compiler_params=params(8),
        name="place_prompt_grad",
    )(flag, me, *payloads)


def after(x, *others):
    return lax.optimization_barrier((x,) + others)[0]


def pair_sum(value, axis, size):
    step = 1
    while step < size:
        value = value + lax.ppermute(value, axis, [(i, i ^ step) for i in range(size)])
        step *= 2
    return value


def local(
    n_dp, n_group, queries, resp_keys, resp_values, prompt_cache, owners, lengths, q_gain, k_gain, grad_out
):
    q, g = queries[0, 0], grad_out[0, 0]
    k, v = resp_keys[0, 0], resp_values[0, 0]
    cache = prompt_cache[0, 0]
    owner = owners[0]
    live_len = lengths[0, 0]
    me = lax.axis_index("group")
    kv_heads = k.shape[1] // HD
    depth, p_rows, _ = cache.shape
    direct = n_group == kv_heads and n_group <= 4
    steps = [s ^ (s >> 1) for s in range(kv_heads)]

    order = jnp.arange(kv_heads, dtype=jnp.int32)
    if direct:
        order = order ^ (order >> 1) ^ me
    mine_flag = (me == owner).astype(jnp.int32)
    away = owner ^ me
    meta = jnp.concatenate([order, live_len[None]])
    which, flag, self_index = [
        jnp.reshape(x, (1,)).astype(jnp.int32) for x in (away ^ (away >> 1), mine_flag, me)
    ]
    meta, which, flag, self_index = lax.optimization_barrier((meta, which, flag, self_index))
    q, g, k, v, *gains_in = [
        pltpu.with_memory_space_constraint(x, pltpu.HBM) for x in (q, g, k, v, q_gain, k_gain)
    ]
    acc = jnp.zeros((2, HD), F32)
    kept = prepare(tuple(range(kv_heads)), meta, q, g, k, v, *gains_in)

    def swap(x, step):
        return lax.ppermute(x, "group", [(i, i ^ step) for i in range(n_group)])

    if direct:
        blocks = list(cut(order, pltpu.with_memory_space_constraint(cache, pltpu.HBM), kv_heads))
        got = [blocks[0]] + [swap(blocks[s], steps[s]) for s in range(1, n_group)]
        for s in range(1, n_group):
            got[s] = after(got[s], kept[0][2])
        mine = pick(which, got)
        prompts = [mine] + [swap(mine, steps[s]) for s in range(1, n_group)]
    else:
        cache = lax.psum(jnp.where(me == owner, cache, jnp.zeros_like(cache)), "group")
        prompts = cut(order, cache, kv_heads)

    parts, backs, per_head = [], [], []
    for s, prompt in enumerate(prompts):
        part, acc, *results = first_half(prompt, kept[s], acc)
        per_head.append([kept[s][0], kept[s][2], kept[s][7], *results])
        parts.append(part)
        if direct and s > 0:
            backs.append(swap(part, steps[s]))

    def hop(x, step):
        return lax.ppermute(x, "dp", [(i, i ^ step) for i in range(n_dp)])

    gains = acc + hop(acc, 1)
    if direct:
        gains = after(gains, *backs[:-1])
    step = 2
    while step < n_dp:
        gains = gains + hop(gains, step)
        step *= 2
    if direct:
        payload = join(parts[0], backs, gains)
        payloads = [payload] + [swap(payload, steps[s]) for s in range(1, n_group)]
        per_head[0][3] = after(per_head[0][3], payload)
        buffers = settle_heads(meta, per_head, q.shape[1], k.shape[1])
        payloads[1] = after(payloads[1], buffers[2])
        placed, gains = place(steps, flag, self_index, payloads, depth, p_rows)
    else:
        total = lax.psum(jnp.concatenate(parts, axis=-1).astype(F32), "group").astype(BF)
        placed = jnp.where(mine_flag > 0, total, jnp.zeros((), BF))
        gains = pair_sum(gains, "group", n_group)
        buffers = settle_heads(meta, per_head, q.shape[1], k.shape[1])
    attended, d_query, d_key, d_value = buffers
    return (
        attended[None, None],
        d_query[None, None],
        d_key[None, None],
        d_value[None, None],
        placed[None, None],
        gains,
    )


def solution(mesh):
    in_specs = (
        P("dp", "group", None, None),
        P("dp", "group", None, None),
        P("dp", "group", None, None),
        P("dp", "group", None, None, None),
        P("dp"),
        P("dp", "group"),
        P(),
        P(),
        P("dp", "group", None, None),
    )
    out_specs = (
        P("dp", "group", None, None),
        P("dp", "group", None, None),
        P("dp", "group", None, None),
        P("dp", "group", None, None),
        P("dp", "group", None, None, None),
        P(),
    )
    body = functools.partial(local, mesh.shape["dp"], mesh.shape["group"])
    return jax.shard_map(body, mesh=mesh, in_specs=in_specs, out_specs=out_specs, check_vma=False)
```

```python
import functools

import jax
import jax.numpy as jnp
from jax import lax
from jax.experimental import pallas as pl
from jax.experimental.pallas import tpu as pltpu
from jax.sharding import PartitionSpec as P

HD = 128
EPS = 1e-06
LOG2E = 1.4426950408889634
BF = jnp.bfloat16
F32 = jnp.float32


def dot_nn(a, b):
    return lax.dot_general(a, b, (((1,), (0,)), ((), ())), preferred_element_type=F32)


def dot_nt(a, b):
    return lax.dot_general(a, b, (((1,), (1,)), ((), ())), preferred_element_type=F32)


VMEM = pl.BlockSpec(memory_space=pltpu.VMEM)
SMEM = pl.BlockSpec(memory_space=pltpu.SMEM)
HBM = pl.BlockSpec(memory_space=pltpu.HBM)


def params(mib):
    return pltpu.CompilerParams(vmem_limit_bytes=mib * 2**20)


def cut_kernel(order, cache_ref, *rest):
    outs, sems = rest[:-1], rest[-1]
    copies = []
    for i, out in enumerate(outs):
        at = pl.multiple_of(order[i] * HD, HD)
        copy = pltpu.make_async_copy(cache_ref.at[:, :, pl.ds(at, HD)], out, sems.at[i])
        copy.start()
        copies.append(copy)
    for copy in copies:
        copy.wait()


def cut(order, cache, count):
    depth, rows, _ = cache.shape
    return pl.pallas_call(
        cut_kernel,
        out_shape=[jax.ShapeDtypeStruct((depth, rows, HD), BF)] * count,
        in_specs=[SMEM, HBM],
        out_specs=[VMEM] * count,
        scratch_shapes=[pltpu.SemaphoreType.DMA((count,))],
        compiler_params=params(4),
        name="cut_prompt",
    )(order, cache)


def pick_kernel(which, *refs):
    picked = refs[0][...]
    for i in range(1, len(refs) - 1):
        picked = jnp.where(which[0] == i, refs[i][...], picked)
    refs[-1][...] = picked


def pick(which, blocks):
    return pl.pallas_call(
        pick_kernel,
        out_shape=jax.ShapeDtypeStruct(blocks[0].shape, BF),
        in_specs=[SMEM] + [VMEM] * len(blocks),
        out_specs=VMEM,
        compiler_params=params(4),
        name="pick_owner",
    )(which, *blocks)


KEPT = 8


def column(row):
    return jnp.broadcast_to(row, (8, HD)).T[:, 0:1]


def prepare_kernel(slots, share, rows, width, meta, q_in, g_in, k_in, v_in, gain_ref, kg_ref, *rest):
    outs, (q_buf, g_buf, k_buf, v_buf, gain_buf, sems) = rest[:-6], rest[-6:]
    live_len = meta[meta.shape[0] - 1]
    count = len(slots)
    scale = HD ** (-0.5)
    wide = share * HD
    copies = []
    for s, slot in enumerate(slots):
        group = []
        for j, (src, buf, size) in enumerate(
            ((q_in, q_buf, wide), (k_in, k_buf, HD), (g_in, g_buf, wide), (v_in, v_buf, HD))
        ):
            at = pl.multiple_of(meta[slot] * size, size)
            copy = pltpu.make_async_copy(src.at[:, pl.ds(at, size)], buf.at[s], sems.at[s, j])
            copy.start()
            group.append(copy)
        copies.append(group)
    gains = []
    for j, src in enumerate((gain_ref, kg_ref)):
        copy = pltpu.make_async_copy(src, gain_buf.at[j], sems.at[count, j])
        copy.start()
        gains.append(copy)
    for copy in gains:
        copy.wait()
    q_row = gain_buf[0].reshape(1, HD)
    q_gain = column(q_row)
    k_gain = gain_buf[1].reshape(1, HD)
    for s in range(count):
        qt_ref, gt_ref, row_ref, er_ref, ot_ref, dp_ref, kh_ref, ku_ref = outs[s * KEPT : (s + 1) * KEPT]
        for copy in copies[s]:
            copy.wait()
        q_t = jnp.concatenate([q_buf[s, :, i * HD : (i + 1) * HD] for i in range(share)], axis=0).T
        g_t = jnp.concatenate([g_buf[s, :, i * HD : (i + 1) * HD] for i in range(share)], axis=0).T
        qt_ref[...] = q_t
        row_ref[2:3, :HD] = q_row
        row_ref[3:4, :HD] = k_gain
        raw_k = k_buf[s].astype(F32)
        k_inv = lax.rsqrt(jnp.mean(raw_k * raw_k, axis=-1, keepdims=True) + EPS)
        k_unit = raw_k * k_inv
        k_hat = (k_unit * k_gain).astype(BF)
        kh_ref[...] = k_hat
        ku_ref[:, :HD] = k_unit
        ku_ref[:, HD:] = jnp.broadcast_to(k_inv, (rows, HD))
        r_val = v_buf[s]
        r_val_t = r_val.T
        for start in range(0, share * rows, width):
            cols = slice(start, start + width)
            token = (lax.broadcasted_iota(jnp.int32, (1, width), 1) + start) % rows
            raw_q = q_t[:, cols].astype(F32)
            q_inv = lax.rsqrt(jnp.mean(raw_q * raw_q, axis=0, keepdims=True) + EPS)
            q_hat = (raw_q * q_inv * q_gain).astype(BF)
            d_o = jnp.where(token < live_len, g_t[:, cols].astype(F32), 0.0).astype(BF)
            gt_ref[:, cols] = d_o
            causal = lax.broadcasted_iota(jnp.int32, (rows, width), 0) <= token
            e_r = jnp.where(causal, jnp.exp2(dot_nn(k_hat, q_hat) * (scale * LOG2E)), 0.0)
            eb_r = e_r.astype(BF)
            er_ref[:, cols] = eb_r
            ot_ref[:, cols] = dot_nn(r_val_t, eb_r)
            dp_ref[:, cols] = dot_nn(r_val, d_o)
            row_ref[0:1, cols] = q_inv
            row_ref[1:2, cols] = jnp.sum(e_r, axis=0, keepdims=True)


def prepare(slots, meta, q, g, k, v, q_gain, k_gain):
    count = len(slots)
    rows, q_width = q.shape
    share = q_width // k.shape[1]
    total = share * rows
    each = [
        jax.ShapeDtypeStruct((HD, total), BF),
        jax.ShapeDtypeStruct((HD, total), BF),
        jax.ShapeDtypeStruct((8, total), F32),
        jax.ShapeDtypeStruct((rows, total), BF),
        jax.ShapeDtypeStruct((HD, total), F32),
        jax.ShapeDtypeStruct((rows, total), F32),
        jax.ShapeDtypeStruct((rows, HD), BF),
        jax.ShapeDtypeStruct((rows, 2 * HD), F32),
    ]
    outs = pl.pallas_call(
        functools.partial(prepare_kernel, slots, share, rows, 2 * HD),
        out_shape=each * count,
        in_specs=[SMEM] + [HBM] * 6,
        out_specs=[VMEM] * (KEPT * count),
        scratch_shapes=[
            pltpu.VMEM((count, rows, share * HD), BF),
            pltpu.VMEM((count, rows, share * HD), BF),
            pltpu.VMEM((count, rows, HD), BF),
            pltpu.VMEM((count, rows, HD), BF),
            pltpu.VMEM((2, HD), F32),
            pltpu.SemaphoreType.DMA((count + 1, 4)),
        ],
        compiler_params=params(16),
        cost_estimate=pl.CostEstimate(
            flops=6 * count * total * rows * HD,
            bytes_accessed=5 * rows * q_width * 2,
            transcendentals=count * total * rows,
        ),
        name="prepare_response",
    )(meta, q, g, k, v, q_gain, k_gain)
    return [list(outs[s * KEPT : (s + 1) * KEPT]) for s in range(count)]


def attend(width, pr_ref, kept, acc_ref, part_ref, at_ref, dq_ref, gacc_ref):
    qt_ref, gt_ref, row_ref, er_ref, ot_ref, dp_ref, kh_ref, ku_ref = kept
    scale = HD ** (-0.5)
    q_gain = column(row_ref[2:3, :HD])
    p_key = pr_ref[0]
    p_val = pr_ref[1]
    k_hat_t = kh_ref[...].T
    p_key_t = p_key.T
    p_val_t = p_val.T
    sums = None
    for start in range(0, qt_ref.shape[1], width):
        cols = slice(start, start + width)
        q_unit = qt_ref[:, cols].astype(F32) * row_ref[0:1, cols]
        q_hat = (q_unit * q_gain).astype(BF)
        d_ob = gt_ref[:, cols]
        d_o = d_ob.astype(F32)
        e_p = jnp.exp2(dot_nn(p_key, q_hat) * (scale * LOG2E))
        inv_sum = 1.0 / (jnp.sum(e_p, axis=0, keepdims=True) + row_ref[1:2, cols])
        eb_p = e_p.astype(BF)
        eb_r = er_ref[:, cols]
        out = (dot_nn(p_val_t, eb_p) + ot_ref[:, cols]) * inv_sum
        at_ref[:, cols] = out.astype(BF)
        delta = jnp.sum(d_o * out, axis=0, keepdims=True)
        ds_p = (e_p * (dot_nn(p_val, d_ob) - delta)).astype(BF)
        ds_r = (eb_r.astype(F32) * (dp_ref[:, cols] - delta)).astype(BF)
        weight = inv_sum * scale
        q_w = (q_hat.astype(F32) * weight).astype(BF)
        d_ow = (d_o * inv_sum).astype(BF)
        d_qhat = (dot_nn(p_key_t, ds_p) + dot_nn(k_hat_t, ds_r)) * weight
        dq_ref[:, cols] = d_qhat
        terms = (
            dot_nt(ds_p, q_w),
            dot_nt(eb_p, d_ow),
            dot_nt(ds_r, q_w),
            dot_nt(eb_r, d_ow),
            d_qhat * q_unit,
        )
        sums = terms if sums is None else [a + b for a, b in zip(sums, terms)]
    d_kp, d_vp, d_kr, d_vr, q_term = sums
    part_ref[0] = d_kp.astype(BF)
    part_ref[1] = d_vp.astype(BF)
    folded = q_term[:, :HD]
    for start in range(HD, width, HD):
        folded = folded + q_term[:, start : start + HD]
    gacc_ref[0:1, :] = acc_ref[0:1, :] + jnp.sum(folded.T, axis=0, keepdims=True)
    gacc_ref[1:2, :] = acc_ref[1:2, :] + jnp.sum(d_kr * ku_ref[:, :HD], axis=0, keepdims=True)
    return d_kr, d_vr


def settle(width, head, live_len, kept, at_ref, dq_ref, d_kr, d_vr, outs, bufs, sems):
    qt_ref, row_ref, ku_ref = kept
    q_gain = column(row_ref[2:3, :HD])
    k_gain = row_ref[3:4, :HD]
    a_buf, q_buf, k_buf, v_buf = bufs
    rows, wide = a_buf.shape
    share = wide // HD
    copies = []

    def send(j, buf):
        size = buf.shape[1]
        at = pl.multiple_of(head * size, size)
        copy = pltpu.make_async_copy(buf, outs[j].at[:, pl.ds(at, size)], sems.at[j])
        copy.start()
        copies.append(copy)

    att = at_ref[...].T
    live = lax.broadcasted_iota(jnp.int32, (rows, HD), 0) < live_len
    for i in range(share):
        block = att[i * rows : (i + 1) * rows, :].astype(F32)
        a_buf[:, i * HD : (i + 1) * HD] = jnp.where(live, block, 0.0).astype(BF)
    send(0, a_buf)
    v_buf[...] = d_vr.astype(BF)
    send(3, v_buf)
    k_unit = ku_ref[:, :HD]
    up_k = d_kr * k_gain
    mean_k = jnp.mean(up_k * k_unit, axis=-1, keepdims=True)
    k_buf[...] = (ku_ref[:, HD:] * (up_k - k_unit * mean_k)).astype(BF)
    send(2, k_buf)
    parts = []
    for start in range(0, share * rows, width):
        cols = slice(start, start + width)
        q_inv = row_ref[0:1, cols]
        q_unit = qt_ref[:, cols].astype(F32) * q_inv
        up = dq_ref[:, cols] * q_gain
        mean = jnp.mean(up * q_unit, axis=0, keepdims=True)
        parts.append((q_inv * (up - q_unit * mean)).astype(BF))
    d_q = jnp.concatenate(parts, axis=1).T
    for i in range(share):
        q_buf[:, i * HD : (i + 1) * HD] = d_q[i * rows : (i + 1) * rows, :]
    send(1, q_buf)
    return copies


def first_kernel(width, pr_ref, *rest):
    kept, acc_ref = rest[:KEPT], rest[KEPT]
    part_ref, gacc_ref, at_ref, dq_ref, dkr_ref, dvr_ref = rest[-6:]
    d_kr, d_vr = attend(width, pr_ref, kept, acc_ref, part_ref, at_ref, dq_ref, gacc_ref)
    dkr_ref[...] = d_kr
    dvr_ref[...] = d_vr


def settle_kernel(width, meta, *rest):
    outs, bufs, sems = rest[-9:-5], rest[-5:-1], rest[-1]
    copies = []
    for i in range(sems.shape[0]):
        kept, results = rest[i * 7 : i * 7 + 3], rest[i * 7 + 3 : i * 7 + 7]
        at_ref, dq_ref, dkr_ref, dvr_ref = results
        copies += settle(
            width, meta[i], meta[meta.shape[0] - 1], kept, at_ref, dq_ref,
            dkr_ref[...], dvr_ref[...], outs, [buf.at[i] for buf in bufs], sems.at[i],
        )
    for copy in copies:
        copy.wait()


def out_shapes(rows, q_width, k_width):
    widths = (q_width, q_width, k_width, k_width)
    return [jax.ShapeDtypeStruct((rows, w), BF) for w in widths]


def out_scratch(count, rows, share):
    widths = (share * HD, share * HD, HD, HD)
    return [pltpu.VMEM((count, rows, w), BF) for w in widths] + [pltpu.SemaphoreType.DMA((count, 4))]


def cost(prompt_rows, rows, total):
    return pl.CostEstimate(
        flops=(8 * prompt_rows + 4 * rows) * total * HD,
        bytes_accessed=2**20,
        transcendentals=total * prompt_rows,
    )


def first_half(prompt, kept, acc):
    total = kept[0].shape[1]
    rows = kept[3].shape[0]
    return pl.pallas_call(
        functools.partial(first_kernel, 2 * HD),
        out_shape=[
            jax.ShapeDtypeStruct(prompt.shape, BF),
            jax.ShapeDtypeStruct(acc.shape, F32),
            jax.ShapeDtypeStruct((HD, total), BF),
            jax.ShapeDtypeStruct((HD, total), F32),
            jax.ShapeDtypeStruct((rows, HD), F32),
            jax.ShapeDtypeStruct((rows, HD), F32),
        ],
        in_specs=[VMEM] * (2 + KEPT),
        out_specs=[VMEM] * 6,
        compiler_params=params(16),
        cost_estimate=cost(prompt.shape[1], rows, total),
        name="attend_head",
    )(prompt, *kept, acc)


def settle_heads(meta, per_head, q_width, k_width):
    count = len(per_head)
    total = per_head[0][0].shape[1]
    rows = per_head[0][5].shape[0]
    flat = [x for group in per_head for x in group]
    return pl.pallas_call(
        functools.partial(settle_kernel, 2 * HD),
        out_shape=out_shapes(rows, q_width, k_width),
        in_specs=[SMEM] + [VMEM] * len(flat),
        out_specs=[HBM] * 4,
        scratch_shapes=out_scratch(count, rows, total // rows),
        compiler_params=params(16),
        name="settle_heads",
    )(meta, *flat)


TAIL = 16


def join_kernel(own_ref, *rest):
    backs, gains_ref, out_ref = rest[:-2], rest[-2], rest[-1]
    depth, rows, _ = own_ref.shape
    for d in range(depth):
        total = own_ref[d].astype(F32)
        for back in backs:
            total = total + back[d].astype(F32)
        out_ref[d * rows : (d + 1) * rows, :] = total.astype(BF)
    gains = gains_ref[...]
    high = gains.astype(BF)
    gains = gains - high.astype(F32)
    middle = gains.astype(BF)
    low = (gains - middle.astype(F32)).astype(BF)
    pieces = jnp.concatenate([p[0:2].astype(F32) for p in (high, middle, low)], axis=0)
    pad = jnp.zeros((TAIL - pieces.shape[0], HD), F32)
    out_ref[depth * rows :, :] = jnp.concatenate([pieces, pad], axis=0).astype(BF)


def join(own, backs, gains):
    depth, rows, _ = own.shape
    return pl.pallas_call(
        join_kernel,
        out_shape=jax.ShapeDtypeStruct((depth * rows + TAIL, HD), BF),
        in_specs=[VMEM] * (2 + len(backs)),
        out_specs=VMEM,
        compiler_params=params(8),
        name="join_parts",
    )(own, *backs, gains)


def place_kernel(steps, flag, me, *refs):
    payloads, (out_ref, gain_ref, stage, zeros, sems) = refs[:-5], refs[-5:]
    depth, rows, width = out_ref.shape

    @pl.when(flag[0] > 0)
    def _():
        copies = []
        for i, ref in enumerate(payloads):
            at = pl.ds(pl.multiple_of((me[0] ^ steps[i]) * HD, HD), HD)
            for d in range(depth):
                src = ref.at[d * rows : (d + 1) * rows, :]
                copy = pltpu.make_async_copy(src, out_ref.at[d, :, at], sems.at[i * depth + d])
                copy.start()
                copies.append(copy)
        for copy in copies:
            copy.wait()

    @pl.when(flag[0] == 0)
    def _():
        zeros[...] = jnp.zeros_like(zeros)
        copies = []
        for d in range(depth):
            copy = pltpu.make_async_copy(zeros, out_ref.at[d], sems.at[d])
            copy.start()
            copies.append(copy)
        for copy in copies:
            copy.wait()

    for i, ref in enumerate(payloads):
        tail = ref[depth * rows :, :].astype(F32)
        stage[me[0] ^ steps[i]] = tail[0:2] + tail[2:4] + tail[4:6]
    total = stage[0]
    for i in range(1, len(payloads)):
        total = total + stage[i]
    gain_ref[...] = total


def place(steps, flag, me, payloads, depth, rows):
    count = len(payloads)
    width = HD * count
    return pl.pallas_call(
        functools.partial(place_kernel, tuple(steps)),
        out_shape=[
            jax.ShapeDtypeStruct((depth, rows, width), BF),
            jax.ShapeDtypeStruct((2, HD), F32),
        ],
        in_specs=[SMEM] * 2 + [VMEM] * count,
        out_specs=[HBM, VMEM],
        scratch_shapes=[
            pltpu.VMEM((count, 2, HD), F32),
            pltpu.VMEM((rows, width), BF),
            pltpu.SemaphoreType.DMA((count * depth,)),
        ],
        compiler_params=params(8),
        name="place_prompt_grad",
    )(flag, me, *payloads)


def after(x, *others):
    return lax.optimization_barrier((x,) + others)[0]


def pair_sum(value, axis, size):
    step = 1
    while step < size:
        value = value + lax.ppermute(value, axis, [(i, i ^ step) for i in range(size)])
        step *= 2
    return value


def local(
    n_dp, n_group, queries, resp_keys, resp_values, prompt_cache, owners, lengths, q_gain, k_gain, grad_out
):
    q, g = queries[0, 0], grad_out[0, 0]
    k, v = resp_keys[0, 0], resp_values[0, 0]
    cache = prompt_cache[0, 0]
    owner = owners[0]
    live_len = lengths[0, 0]
    me = lax.axis_index("group")
    kv_heads = k.shape[1] // HD
    depth, p_rows, _ = cache.shape
    direct = n_group == kv_heads and n_group <= 4
    steps = [s ^ (s >> 1) for s in range(kv_heads)]

    order = jnp.arange(kv_heads, dtype=jnp.int32)
    if direct:
        order = order ^ (order >> 1) ^ me
    mine_flag = (me == owner).astype(jnp.int32)
    away = owner ^ me
    meta = jnp.concatenate([order, live_len[None]])
    which, flag, self_index = [
        jnp.reshape(x, (1,)).astype(jnp.int32) for x in (away ^ (away >> 1), mine_flag, me)
    ]
    meta, which, flag, self_index = lax.optimization_barrier((meta, which, flag, self_index))
    q, g, k, v, *gains_in = [
        pltpu.with_memory_space_constraint(x, pltpu.HBM) for x in (q, g, k, v, q_gain, k_gain)
    ]
    acc = jnp.zeros((2, HD), F32)
    kept = prepare(tuple(range(kv_heads)), meta, q, g, k, v, *gains_in)

    def swap(x, step):
        return lax.ppermute(x, "group", [(i, i ^ step) for i in range(n_group)])

    if direct:
        blocks = list(cut(order, pltpu.with_memory_space_constraint(cache, pltpu.HBM), kv_heads))
        got = [blocks[0]] + [swap(blocks[s], steps[s]) for s in range(1, n_group)]
        for s in range(1, n_group):
            got[s] = after(got[s], kept[0][2])
        mine = pick(which, got)
        prompts = [mine] + [swap(mine, steps[s]) for s in range(1, n_group)]
    else:
        cache = lax.psum(jnp.where(me == owner, cache, jnp.zeros_like(cache)), "group")
        prompts = cut(order, cache, kv_heads)

    parts, per_head = [], []
    for s, prompt in enumerate(prompts):
        part, acc, *results = first_half(prompt, kept[s], acc)
        per_head.append([kept[s][0], kept[s][2], kept[s][7], *results])
        parts.append(part)

    if direct:
        backs = [swap(after(x, acc), s) for x, s in zip(parts[1:], steps[1:])]

    def hop(x, step):
        return lax.ppermute(x, "dp", [(i, i ^ step) for i in range(n_dp)])

    gains = acc + hop(acc, 1)
    step = 2
    while step < n_dp:
        arrived = hop(gains, step)
        if direct and step == 2:
            arrived = after(arrived, *backs[:-1])
        elif direct:
            arrived = after(arrived, *backs)
        gains = gains + arrived
        step *= 2
    if direct:
        payload = join(parts[0], backs, gains)
        payloads = [payload] + [swap(payload, steps[s]) for s in range(1, n_group)]
        per_head[0][3] = after(per_head[0][3], payload)
        buffers = settle_heads(meta, per_head, q.shape[1], k.shape[1])
        payloads[1] = after(payloads[1], buffers[2])
        placed, gains = place(steps, flag, self_index, payloads, depth, p_rows)
    else:
        total = lax.psum(jnp.concatenate(parts, axis=-1).astype(F32), "group").astype(BF)
        placed = jnp.where(mine_flag > 0, total, jnp.zeros((), BF))
        gains = pair_sum(gains, "group", n_group)
        buffers = settle_heads(meta, per_head, q.shape[1], k.shape[1])
    attended, d_query, d_key, d_value = buffers
    return (
        attended[None, None],
        d_query[None, None],
        d_key[None, None],
        d_value[None, None],
        placed[None, None],
        gains,
    )


def solution(mesh):
    in_specs = (
        P("dp", "group", None, None),
        P("dp", "group", None, None),
        P("dp", "group", None, None),
        P("dp", "group", None, None, None),
        P("dp"),
        P("dp", "group"),
        P(),
        P(),
        P("dp", "group", None, None),
    )
    out_specs = (
        P("dp", "group", None, None),
        P("dp", "group", None, None),
        P("dp", "group", None, None),
        P("dp", "group", None, None),
        P("dp", "group", None, None, None),
        P(),
    )
    body = functools.partial(local, mesh.shape["dp"], mesh.shape["group"])
    return jax.shard_map(body, mesh=mesh, in_specs=in_specs, out_specs=out_specs, check_vma=False)
```

```python
import functools

import jax
import jax.numpy as jnp
from jax import lax
from jax.experimental import pallas as pl
from jax.experimental.pallas import tpu as pltpu
from jax.sharding import PartitionSpec as P

HD = 128
EPS = 1e-06
LOG2E = 1.4426950408889634
BF = jnp.bfloat16
F32 = jnp.float32


def dot_nn(a, b):
    return lax.dot_general(a, b, (((1,), (0,)), ((), ())), preferred_element_type=F32)


def dot_nt(a, b):
    return lax.dot_general(a, b, (((1,), (1,)), ((), ())), preferred_element_type=F32)


VMEM = pl.BlockSpec(memory_space=pltpu.VMEM)
SMEM = pl.BlockSpec(memory_space=pltpu.SMEM)
HBM = pl.BlockSpec(memory_space=pltpu.HBM)


def params(mib):
    return pltpu.CompilerParams(vmem_limit_bytes=mib * 2**20)


def cut_kernel(order, cache_ref, *rest):
    outs, sems = rest[:-1], rest[-1]
    copies = []
    for i, out in enumerate(outs):
        at = pl.multiple_of(order[i] * HD, HD)
        copy = pltpu.make_async_copy(cache_ref.at[:, :, pl.ds(at, HD)], out, sems.at[i])
        copy.start()
        copies.append(copy)
    for copy in copies:
        copy.wait()


def cut(order, cache, count):
    depth, rows, _ = cache.shape
    return pl.pallas_call(
        cut_kernel,
        out_shape=[jax.ShapeDtypeStruct((depth, rows, HD), BF)] * count,
        in_specs=[SMEM, HBM],
        out_specs=[VMEM] * count,
        scratch_shapes=[pltpu.SemaphoreType.DMA((count,))],
        compiler_params=params(4),
        name="cut_prompt",
    )(order, cache)


def pick_kernel(which, *refs):
    picked = refs[0][...]
    for i in range(1, len(refs) - 1):
        picked = jnp.where(which[0] == i, refs[i][...], picked)
    refs[-1][...] = picked


def pick(which, blocks):
    return pl.pallas_call(
        pick_kernel,
        out_shape=jax.ShapeDtypeStruct(blocks[0].shape, BF),
        in_specs=[SMEM] + [VMEM] * len(blocks),
        out_specs=VMEM,
        compiler_params=params(4),
        name="pick_owner",
    )(which, *blocks)


KEPT = 8


def column(row):
    return jnp.broadcast_to(row, (8, HD)).T[:, 0:1]


def prepare_kernel(slots, share, rows, width, meta, q_in, g_in, k_in, v_in, gain_ref, kg_ref, *rest):
    outs, (q_buf, g_buf, k_buf, v_buf, gain_buf, sems) = rest[:-6], rest[-6:]
    live_len = meta[meta.shape[0] - 1]
    count = len(slots)
    scale = HD ** (-0.5)
    wide = share * HD
    copies = []
    for s, slot in enumerate(slots):
        group = []
        for j, (src, buf, size) in enumerate(
            ((q_in, q_buf, wide), (k_in, k_buf, HD), (g_in, g_buf, wide), (v_in, v_buf, HD))
        ):
            at = pl.multiple_of(meta[slot] * size, size)
            copy = pltpu.make_async_copy(src.at[:, pl.ds(at, size)], buf.at[s], sems.at[s, j])
            copy.start()
            group.append(copy)
        copies.append(group)
    gains = []
    for j, src in enumerate((gain_ref, kg_ref)):
        copy = pltpu.make_async_copy(src, gain_buf.at[j], sems.at[count, j])
        copy.start()
        gains.append(copy)
    for copy in gains:
        copy.wait()
    q_row = gain_buf[0].reshape(1, HD)
    q_gain = column(q_row)
    k_gain = gain_buf[1].reshape(1, HD)
    for s in range(count):
        qt_ref, gt_ref, row_ref, er_ref, ot_ref, dp_ref, kh_ref, ku_ref = outs[s * KEPT : (s + 1) * KEPT]
        for copy in copies[s]:
            copy.wait()
        q_t = jnp.concatenate([q_buf[s, :, i * HD : (i + 1) * HD] for i in range(share)], axis=0).T
        g_t = jnp.concatenate([g_buf[s, :, i * HD : (i + 1) * HD] for i in range(share)], axis=0).T
        qt_ref[...] = q_t
        row_ref[2:3, :HD] = q_row
        row_ref[3:4, :HD] = k_gain
        raw_k = k_buf[s].astype(F32)
        k_inv = lax.rsqrt(jnp.mean(raw_k * raw_k, axis=-1, keepdims=True) + EPS)
        k_unit = raw_k * k_inv
        k_hat = (k_unit * k_gain).astype(BF)
        kh_ref[...] = k_hat
        ku_ref[:, :HD] = k_unit
        ku_ref[:, HD:] = jnp.broadcast_to(k_inv, (rows, HD))
        r_val = v_buf[s]
        r_val_t = r_val.T
        for start in range(0, share * rows, width):
            cols = slice(start, start + width)
            token = (lax.broadcasted_iota(jnp.int32, (1, width), 1) + start) % rows
            raw_q = q_t[:, cols].astype(F32)
            q_inv = lax.rsqrt(jnp.mean(raw_q * raw_q, axis=0, keepdims=True) + EPS)
            q_hat = (raw_q * q_inv * q_gain).astype(BF)
            d_o = jnp.where(token < live_len, g_t[:, cols].astype(F32), 0.0).astype(BF)
            gt_ref[:, cols] = d_o
            causal = lax.broadcasted_iota(jnp.int32, (rows, width), 0) <= token
            e_r = jnp.where(causal, jnp.exp2(dot_nn(k_hat, q_hat) * (scale * LOG2E)), 0.0)
            eb_r = e_r.astype(BF)
            er_ref[:, cols] = eb_r
            ot_ref[:, cols] = dot_nn(r_val_t, eb_r)
            dp_ref[:, cols] = dot_nn(r_val, d_o)
            row_ref[0:1, cols] = q_inv
            row_ref[1:2, cols] = jnp.sum(e_r, axis=0, keepdims=True)


def prepare(slots, meta, q, g, k, v, q_gain, k_gain):
    count = len(slots)
    rows, q_width = q.shape
    share = q_width // k.shape[1]
    total = share * rows
    each = [
        jax.ShapeDtypeStruct((HD, total), BF),
        jax.ShapeDtypeStruct((HD, total), BF),
        jax.ShapeDtypeStruct((8, total), F32),
        jax.ShapeDtypeStruct((rows, total), BF),
        jax.ShapeDtypeStruct((HD, total), F32),
        jax.ShapeDtypeStruct((rows, total), F32),
        jax.ShapeDtypeStruct((rows, HD), BF),
        jax.ShapeDtypeStruct((rows, 2 * HD), F32),
    ]
    outs = pl.pallas_call(
        functools.partial(prepare_kernel, slots, share, rows, 2 * HD),
        out_shape=each * count,
        in_specs=[SMEM] + [HBM] * 6,
        out_specs=[VMEM] * (KEPT * count),
        scratch_shapes=[
            pltpu.VMEM((count, rows, share * HD), BF),
            pltpu.VMEM((count, rows, share * HD), BF),
            pltpu.VMEM((count, rows, HD), BF),
            pltpu.VMEM((count, rows, HD), BF),
            pltpu.VMEM((2, HD), F32),
            pltpu.SemaphoreType.DMA((count + 1, 4)),
        ],
        compiler_params=params(16),
        cost_estimate=pl.CostEstimate(
            flops=6 * count * total * rows * HD,
            bytes_accessed=5 * rows * q_width * 2,
            transcendentals=count * total * rows,
        ),
        name="prepare_response",
    )(meta, q, g, k, v, q_gain, k_gain)
    return [list(outs[s * KEPT : (s + 1) * KEPT]) for s in range(count)]


def attend(width, pr_ref, kept, acc_ref, part_ref, at_ref, dq_ref, gacc_ref):
    qt_ref, gt_ref, row_ref, er_ref, ot_ref, dp_ref, kh_ref, ku_ref = kept
    scale = HD ** (-0.5)
    q_gain = column(row_ref[2:3, :HD])
    p_key = pr_ref[0]
    p_val = pr_ref[1]
    k_hat_t = kh_ref[...].T
    p_key_t = p_key.T
    p_val_t = p_val.T
    sums = None
    for start in range(0, qt_ref.shape[1], width):
        cols = slice(start, start + width)
        q_unit = qt_ref[:, cols].astype(F32) * row_ref[0:1, cols]
        q_hat = (q_unit * q_gain).astype(BF)
        d_ob = gt_ref[:, cols]
        d_o = d_ob.astype(F32)
        e_p = jnp.exp2(dot_nn(p_key, q_hat) * (scale * LOG2E))
        inv_sum = 1.0 / (jnp.sum(e_p, axis=0, keepdims=True) + row_ref[1:2, cols])
        eb_p = e_p.astype(BF)
        eb_r = er_ref[:, cols]
        out = (dot_nn(p_val_t, eb_p) + ot_ref[:, cols]) * inv_sum
        at_ref[:, cols] = out.astype(BF)
        delta = jnp.sum(d_o * out, axis=0, keepdims=True)
        ds_p = (e_p * (dot_nn(p_val, d_ob) - delta)).astype(BF)
        ds_r = (eb_r.astype(F32) * (dp_ref[:, cols] - delta)).astype(BF)
        weight = inv_sum * scale
        q_w = (q_hat.astype(F32) * weight).astype(BF)
        d_ow = (d_o * inv_sum).astype(BF)
        d_qhat = (dot_nn(p_key_t, ds_p) + dot_nn(k_hat_t, ds_r)) * weight
        dq_ref[:, cols] = d_qhat
        terms = (
            dot_nt(ds_p, q_w),
            dot_nt(eb_p, d_ow),
            dot_nt(ds_r, q_w),
            dot_nt(eb_r, d_ow),
            d_qhat * q_unit,
        )
        sums = terms if sums is None else [a + b for a, b in zip(sums, terms)]
    d_kp, d_vp, d_kr, d_vr, q_term = sums
    part_ref[0] = d_kp.astype(BF)
    part_ref[1] = d_vp.astype(BF)
    folded = q_term[:, :HD]
    for start in range(HD, width, HD):
        folded = folded + q_term[:, start : start + HD]
    gacc_ref[0:1, :] = acc_ref[0:1, :] + jnp.sum(folded.T, axis=0, keepdims=True)
    gacc_ref[1:2, :] = acc_ref[1:2, :] + jnp.sum(d_kr * ku_ref[:, :HD], axis=0, keepdims=True)
    return d_kr, d_vr


def settle(width, head, live_len, kept, at_ref, dq_ref, d_kr, d_vr, outs, bufs, sems):
    qt_ref, row_ref, ku_ref = kept
    q_gain = column(row_ref[2:3, :HD])
    k_gain = row_ref[3:4, :HD]
    a_buf, q_buf, k_buf, v_buf = bufs
    rows, wide = a_buf.shape
    share = wide // HD
    copies = []

    def send(j, buf):
        size = buf.shape[1]
        at = pl.multiple_of(head * size, size)
        copy = pltpu.make_async_copy(buf, outs[j].at[:, pl.ds(at, size)], sems.at[j])
        copy.start()
        copies.append(copy)

    att = at_ref[...].T
    live = lax.broadcasted_iota(jnp.int32, (rows, HD), 0) < live_len
    for i in range(share):
        block = att[i * rows : (i + 1) * rows, :].astype(F32)
        a_buf[:, i * HD : (i + 1) * HD] = jnp.where(live, block, 0.0).astype(BF)
    send(0, a_buf)
    v_buf[...] = d_vr.astype(BF)
    send(3, v_buf)
    k_unit = ku_ref[:, :HD]
    up_k = d_kr * k_gain
    mean_k = jnp.mean(up_k * k_unit, axis=-1, keepdims=True)
    k_buf[...] = (ku_ref[:, HD:] * (up_k - k_unit * mean_k)).astype(BF)
    send(2, k_buf)
    parts = []
    for start in range(0, share * rows, width):
        cols = slice(start, start + width)
        q_inv = row_ref[0:1, cols]
        q_unit = qt_ref[:, cols].astype(F32) * q_inv
        up = dq_ref[:, cols] * q_gain
        mean = jnp.mean(up * q_unit, axis=0, keepdims=True)
        parts.append((q_inv * (up - q_unit * mean)).astype(BF))
    d_q = jnp.concatenate(parts, axis=1).T
    for i in range(share):
        q_buf[:, i * HD : (i + 1) * HD] = d_q[i * rows : (i + 1) * rows, :]
    send(1, q_buf)
    return copies


def first_kernel(width, pr_ref, *rest):
    kept, acc_ref = rest[:KEPT], rest[KEPT]
    part_ref, gacc_ref, at_ref, dq_ref, dkr_ref, dvr_ref = rest[-6:]
    d_kr, d_vr = attend(width, pr_ref, kept, acc_ref, part_ref, at_ref, dq_ref, gacc_ref)
    dkr_ref[...] = d_kr
    dvr_ref[...] = d_vr


def settle_kernel(width, meta, *rest):
    outs, bufs, sems = rest[-9:-5], rest[-5:-1], rest[-1]
    copies = []
    for i in range(sems.shape[0]):
        kept, results = rest[i * 7 : i * 7 + 3], rest[i * 7 + 3 : i * 7 + 7]
        at_ref, dq_ref, dkr_ref, dvr_ref = results
        copies += settle(
            width, meta[i], meta[meta.shape[0] - 1], kept, at_ref, dq_ref,
            dkr_ref[...], dvr_ref[...], outs, [buf.at[i] for buf in bufs], sems.at[i],
        )
    for copy in copies:
        copy.wait()


def out_shapes(rows, q_width, k_width):
    widths = (q_width, q_width, k_width, k_width)
    return [jax.ShapeDtypeStruct((rows, w), BF) for w in widths]


def out_scratch(count, rows, share):
    widths = (share * HD, share * HD, HD, HD)
    return [pltpu.VMEM((count, rows, w), BF) for w in widths] + [pltpu.SemaphoreType.DMA((count, 4))]


def cost(prompt_rows, rows, total):
    return pl.CostEstimate(
        flops=(8 * prompt_rows + 4 * rows) * total * HD,
        bytes_accessed=2**20,
        transcendentals=total * prompt_rows,
    )


def first_half(prompt, kept, acc):
    total = kept[0].shape[1]
    rows = kept[3].shape[0]
    return pl.pallas_call(
        functools.partial(first_kernel, 2 * HD),
        out_shape=[
            jax.ShapeDtypeStruct(prompt.shape, BF),
            jax.ShapeDtypeStruct(acc.shape, F32),
            jax.ShapeDtypeStruct((HD, total), BF),
            jax.ShapeDtypeStruct((HD, total), F32),
            jax.ShapeDtypeStruct((rows, HD), F32),
            jax.ShapeDtypeStruct((rows, HD), F32),
        ],
        in_specs=[VMEM] * (2 + KEPT),
        out_specs=[VMEM] * 6,
        compiler_params=params(16),
        cost_estimate=cost(prompt.shape[1], rows, total),
        name="attend_head",
    )(prompt, *kept, acc)


def settle_heads(meta, per_head, q_width, k_width):
    count = len(per_head)
    total = per_head[0][0].shape[1]
    rows = per_head[0][5].shape[0]
    flat = [x for group in per_head for x in group]
    return pl.pallas_call(
        functools.partial(settle_kernel, 2 * HD),
        out_shape=out_shapes(rows, q_width, k_width),
        in_specs=[SMEM] + [VMEM] * len(flat),
        out_specs=[HBM] * 4,
        scratch_shapes=out_scratch(count, rows, total // rows),
        compiler_params=params(16),
        name="settle_heads",
    )(meta, *flat)


TAIL = 16


def join_kernel(own_ref, *rest):
    backs, gains_ref, out_ref = rest[:-2], rest[-2], rest[-1]
    depth, rows, _ = own_ref.shape
    for d in range(depth):
        total = own_ref[d].astype(F32)
        for back in backs:
            total = total + back[d].astype(F32)
        out_ref[d * rows : (d + 1) * rows, :] = total.astype(BF)
    gains = gains_ref[...]
    high = gains.astype(BF)
    gains = gains - high.astype(F32)
    middle = gains.astype(BF)
    low = (gains - middle.astype(F32)).astype(BF)
    pieces = jnp.concatenate([p[0:2].astype(F32) for p in (high, middle, low)], axis=0)
    pad = jnp.zeros((TAIL - pieces.shape[0], HD), F32)
    out_ref[depth * rows :, :] = jnp.concatenate([pieces, pad], axis=0).astype(BF)


def join(own, backs, gains):
    depth, rows, _ = own.shape
    return pl.pallas_call(
        join_kernel,
        out_shape=jax.ShapeDtypeStruct((depth * rows + TAIL, HD), BF),
        in_specs=[VMEM] * (2 + len(backs)),
        out_specs=VMEM,
        compiler_params=params(8),
        name="join_parts",
    )(own, *backs, gains)


def place_kernel(steps, flag, me, *refs):
    payloads, (out_ref, gain_ref, stage, zeros, sems) = refs[:-5], refs[-5:]
    depth, rows, width = out_ref.shape

    @pl.when(flag[0] > 0)
    def _():
        copies = []
        for i, ref in enumerate(payloads):
            at = pl.ds(pl.multiple_of((me[0] ^ steps[i]) * HD, HD), HD)
            for d in range(depth):
                src = ref.at[d * rows : (d + 1) * rows, :]
                copy = pltpu.make_async_copy(src, out_ref.at[d, :, at], sems.at[i * depth + d])
                copy.start()
                copies.append(copy)
        for copy in copies:
            copy.wait()

    @pl.when(flag[0] == 0)
    def _():
        zeros[...] = jnp.zeros_like(zeros)
        copies = []
        for d in range(depth):
            copy = pltpu.make_async_copy(zeros, out_ref.at[d], sems.at[d])
            copy.start()
            copies.append(copy)
        for copy in copies:
            copy.wait()

    for i, ref in enumerate(payloads):
        tail = ref[depth * rows :, :].astype(F32)
        stage[me[0] ^ steps[i]] = tail[0:2] + tail[2:4] + tail[4:6]
    total = stage[0]
    for i in range(1, len(payloads)):
        total = total + stage[i]
    gain_ref[...] = total


def place(steps, flag, me, payloads, depth, rows):
    count = len(payloads)
    width = HD * count
    return pl.pallas_call(
        functools.partial(place_kernel, tuple(steps)),
        out_shape=[
            jax.ShapeDtypeStruct((depth, rows, width), BF),
            jax.ShapeDtypeStruct((2, HD), F32),
        ],
        in_specs=[SMEM] * 2 + [VMEM] * count,
        out_specs=[HBM, VMEM],
        scratch_shapes=[
            pltpu.VMEM((count, 2, HD), F32),
            pltpu.VMEM((rows, width), BF),
            pltpu.SemaphoreType.DMA((count * depth,)),
        ],
        compiler_params=params(8),
        name="place_prompt_grad",
    )(flag, me, *payloads)


def after(x, *others):
    return lax.optimization_barrier((x,) + others)[0]


def pair_sum(value, axis, size):
    step = 1
    while step < size:
        value = value + lax.ppermute(value, axis, [(i, i ^ step) for i in range(size)])
        step *= 2
    return value


def local(
    n_dp, n_group, queries, resp_keys, resp_values, prompt_cache, owners, lengths, q_gain, k_gain, grad_out
):
    q, g = queries[0, 0], grad_out[0, 0]
    k, v = resp_keys[0, 0], resp_values[0, 0]
    cache = prompt_cache[0, 0]
    owner = owners[0]
    live_len = lengths[0, 0]
    me = lax.axis_index("group")
    kv_heads = k.shape[1] // HD
    depth, p_rows, _ = cache.shape
    direct = n_group == kv_heads and n_group <= 4
    steps = [s ^ (s >> 1) for s in range(kv_heads)]

    order = jnp.arange(kv_heads, dtype=jnp.int32)
    if direct:
        order = order ^ (order >> 1) ^ me
    mine_flag = (me == owner).astype(jnp.int32)
    away = owner ^ me
    meta = jnp.concatenate([order, live_len[None]])
    which, flag, self_index = [
        jnp.reshape(x, (1,)).astype(jnp.int32) for x in (away ^ (away >> 1), mine_flag, me)
    ]
    meta, which, flag, self_index = lax.optimization_barrier((meta, which, flag, self_index))
    q, g, k, v, *gains_in = [
        pltpu.with_memory_space_constraint(x, pltpu.HBM) for x in (q, g, k, v, q_gain, k_gain)
    ]
    acc = jnp.zeros((2, HD), F32)
    kept = prepare(tuple(range(kv_heads)), meta, q, g, k, v, *gains_in)

    def swap(x, step):
        return lax.ppermute(x, "group", [(i, i ^ step) for i in range(n_group)])

    if direct:
        blocks = list(cut(order, pltpu.with_memory_space_constraint(cache, pltpu.HBM), kv_heads))
        got = [blocks[0]] + [swap(blocks[s], steps[s]) for s in range(1, n_group)]
        for s in range(1, n_group):
            got[s] = after(got[s], kept[0][2])
        mine = pick(which, got)
        prompts = [mine] + [swap(mine, steps[s]) for s in range(1, n_group)]
    else:
        cache = lax.psum(jnp.where(me == owner, cache, jnp.zeros_like(cache)), "group")
        prompts = cut(order, cache, kv_heads)

    parts, per_head = [], []
    for s, prompt in enumerate(prompts):
        part, acc, *results = first_half(prompt, kept[s], acc)
        per_head.append([kept[s][0], kept[s][2], kept[s][7], *results])
        parts.append(part)

    if direct:
        last_crossing = kv_heads - 2
        sent = [x if s == last_crossing else after(x, acc) for s, x in enumerate(parts)]
        backs = [swap(x, s) for x, s in zip(sent[1:], steps[1:])]

    def hop(x, step):
        return lax.ppermute(x, "dp", [(i, i ^ step) for i in range(n_dp)])

    gains = acc + hop(acc, 1)
    if direct:
        gains = after(gains, backs[last_crossing - 1])
    step = 2
    while step < n_dp:
        arrived = hop(gains, step)
        if direct and step == 2:
            arrived = after(arrived, *backs[:-1])
        elif direct:
            arrived = after(arrived, *backs)
        gains = gains + arrived
        step *= 2
    if direct:
        payload = join(parts[0], backs, gains)
        payloads = [payload] + [swap(payload, steps[s]) for s in range(1, n_group)]
        per_head[0][3] = after(per_head[0][3], payload)
        buffers = settle_heads(meta, per_head, q.shape[1], k.shape[1])
        payloads[1] = after(payloads[1], buffers[2])
        placed, gains = place(steps, flag, self_index, payloads, depth, p_rows)
    else:
        total = lax.psum(jnp.concatenate(parts, axis=-1).astype(F32), "group").astype(BF)
        placed = jnp.where(mine_flag > 0, total, jnp.zeros((), BF))
        gains = pair_sum(gains, "group", n_group)
        buffers = settle_heads(meta, per_head, q.shape[1], k.shape[1])
    attended, d_query, d_key, d_value = buffers
    return (
        attended[None, None],
        d_query[None, None],
        d_key[None, None],
        d_value[None, None],
        placed[None, None],
        gains,
    )


def solution(mesh):
    in_specs = (
        P("dp", "group", None, None),
        P("dp", "group", None, None),
        P("dp", "group", None, None),
        P("dp", "group", None, None, None),
        P("dp"),
        P("dp", "group"),
        P(),
        P(),
        P("dp", "group", None, None),
    )
    out_specs = (
        P("dp", "group", None, None),
        P("dp", "group", None, None),
        P("dp", "group", None, None),
        P("dp", "group", None, None),
        P("dp", "group", None, None, None),
        P(),
    )
    body = functools.partial(local, mesh.shape["dp"], mesh.shape["group"])
    return jax.shard_map(body, mesh=mesh, in_specs=in_specs, out_specs=out_specs, check_vma=False)
```

```python
import functools

import jax
import jax.numpy as jnp
from jax import lax
from jax.experimental import pallas as pl
from jax.experimental.pallas import tpu as pltpu
from jax.sharding import PartitionSpec as P

HD = 128
EPS = 1e-06
LOG2E = 1.4426950408889634
BF = jnp.bfloat16
F32 = jnp.float32


def dot_nn(a, b):
    return lax.dot_general(a, b, (((1,), (0,)), ((), ())), preferred_element_type=F32)


def dot_nt(a, b):
    return lax.dot_general(a, b, (((1,), (1,)), ((), ())), preferred_element_type=F32)


VMEM = pl.BlockSpec(memory_space=pltpu.VMEM)
SMEM = pl.BlockSpec(memory_space=pltpu.SMEM)
HBM = pl.BlockSpec(memory_space=pltpu.HBM)


def params(mib):
    return pltpu.CompilerParams(vmem_limit_bytes=mib * 2**20)


def cut_kernel(steps, me, cache_ref, *rest):
    outs, sems = rest[:-1], rest[-1]
    copies = []
    for i, out in enumerate(outs):
        at = pl.multiple_of((me[0] ^ steps[i]) * HD, HD)
        copy = pltpu.make_async_copy(cache_ref.at[:, :, pl.ds(at, HD)], out, sems.at[i])
        copy.start()
        copies.append(copy)
    for copy in copies:
        copy.wait()


def cut(steps, me, cache, count):
    depth, rows, _ = cache.shape
    return pl.pallas_call(
        functools.partial(cut_kernel, tuple(steps)),
        out_shape=[jax.ShapeDtypeStruct((depth, rows, HD), BF)] * count,
        in_specs=[SMEM, HBM],
        out_specs=[VMEM] * count,
        scratch_shapes=[pltpu.SemaphoreType.DMA((count,))],
        compiler_params=params(4),
        name="cut_prompt",
    )(me, cache)


def pick_kernel(which, *refs):
    picked = refs[0][...]
    for i in range(1, len(refs) - 1):
        picked = jnp.where(which[0] == i, refs[i][...], picked)
    refs[-1][...] = picked


def pick(which, blocks):
    return pl.pallas_call(
        pick_kernel,
        out_shape=jax.ShapeDtypeStruct(blocks[0].shape, BF),
        in_specs=[SMEM] + [VMEM] * len(blocks),
        out_specs=VMEM,
        compiler_params=params(4),
        name="pick_owner",
    )(which, *blocks)


KEPT = 8


def column(row):
    return jnp.broadcast_to(row, (8, HD)).T[:, 0:1]


def prepare_kernel(slots, share, rows, width, meta, q_in, g_in, k_in, v_in, gain_ref, kg_ref, *rest):
    outs, (q_buf, g_buf, k_buf, v_buf, gain_buf, sems) = rest[:-6], rest[-6:]
    live_len = meta[meta.shape[0] - 1]
    count = len(slots)
    scale = HD ** (-0.5)
    wide = share * HD
    copies = []
    for s, slot in enumerate(slots):
        group = []
        for j, (src, buf, size) in enumerate(
            ((q_in, q_buf, wide), (k_in, k_buf, HD), (g_in, g_buf, wide), (v_in, v_buf, HD))
        ):
            at = pl.multiple_of(meta[slot] * size, size)
            copy = pltpu.make_async_copy(src.at[:, pl.ds(at, size)], buf.at[s], sems.at[s, j])
            copy.start()
            group.append(copy)
        copies.append(group)
    gains = []
    for j, src in enumerate((gain_ref, kg_ref)):
        copy = pltpu.make_async_copy(src, gain_buf.at[j], sems.at[count, j])
        copy.start()
        gains.append(copy)
    for copy in gains:
        copy.wait()
    q_row = gain_buf[0].reshape(1, HD)
    q_gain = column(q_row)
    k_gain = gain_buf[1].reshape(1, HD)
    for s in range(count):
        qt_ref, gt_ref, row_ref, er_ref, ot_ref, dp_ref, kh_ref, ku_ref = outs[s * KEPT : (s + 1) * KEPT]
        for copy in copies[s]:
            copy.wait()
        q_t = jnp.concatenate([q_buf[s, :, i * HD : (i + 1) * HD] for i in range(share)], axis=0).T
        g_t = jnp.concatenate([g_buf[s, :, i * HD : (i + 1) * HD] for i in range(share)], axis=0).T
        qt_ref[...] = q_t
        row_ref[2:3, :HD] = q_row
        row_ref[3:4, :HD] = k_gain
        raw_k = k_buf[s].astype(F32)
        k_inv = lax.rsqrt(jnp.mean(raw_k * raw_k, axis=-1, keepdims=True) + EPS)
        k_unit = raw_k * k_inv
        k_hat = (k_unit * k_gain).astype(BF)
        kh_ref[...] = k_hat
        ku_ref[:, :HD] = k_unit
        ku_ref[:, HD:] = jnp.broadcast_to(k_inv, (rows, HD))
        r_val = v_buf[s]
        r_val_t = r_val.T
        for start in range(0, share * rows, width):
            cols = slice(start, start + width)
            token = (lax.broadcasted_iota(jnp.int32, (1, width), 1) + start) % rows
            raw_q = q_t[:, cols].astype(F32)
            q_inv = lax.rsqrt(jnp.mean(raw_q * raw_q, axis=0, keepdims=True) + EPS)
            q_hat = (raw_q * q_inv * q_gain).astype(BF)
            d_o = jnp.where(token < live_len, g_t[:, cols].astype(F32), 0.0).astype(BF)
            gt_ref[:, cols] = d_o
            causal = lax.broadcasted_iota(jnp.int32, (rows, width), 0) <= token
            e_r = jnp.where(causal, jnp.exp2(dot_nn(k_hat, q_hat) * (scale * LOG2E)), 0.0)
            eb_r = e_r.astype(BF)
            er_ref[:, cols] = eb_r
            ot_ref[:, cols] = dot_nn(r_val_t, eb_r)
            dp_ref[:, cols] = dot_nn(r_val, d_o)
            row_ref[0:1, cols] = q_inv
            row_ref[1:2, cols] = jnp.sum(e_r, axis=0, keepdims=True)


def prepare(slots, meta, q, g, k, v, q_gain, k_gain):
    count = len(slots)
    rows, q_width = q.shape
    share = q_width // k.shape[1]
    total = share * rows
    each = [
        jax.ShapeDtypeStruct((HD, total), BF),
        jax.ShapeDtypeStruct((HD, total), BF),
        jax.ShapeDtypeStruct((8, total), F32),
        jax.ShapeDtypeStruct((rows, total), BF),
        jax.ShapeDtypeStruct((HD, total), F32),
        jax.ShapeDtypeStruct((rows, total), F32),
        jax.ShapeDtypeStruct((rows, HD), BF),
        jax.ShapeDtypeStruct((rows, 2 * HD), F32),
    ]
    outs = pl.pallas_call(
        functools.partial(prepare_kernel, slots, share, rows, 2 * HD),
        out_shape=each * count,
        in_specs=[SMEM] + [HBM] * 6,
        out_specs=[VMEM] * (KEPT * count),
        scratch_shapes=[
            pltpu.VMEM((count, rows, share * HD), BF),
            pltpu.VMEM((count, rows, share * HD), BF),
            pltpu.VMEM((count, rows, HD), BF),
            pltpu.VMEM((count, rows, HD), BF),
            pltpu.VMEM((2, HD), F32),
            pltpu.SemaphoreType.DMA((count + 1, 4)),
        ],
        compiler_params=params(16),
        cost_estimate=pl.CostEstimate(
            flops=6 * count * total * rows * HD,
            bytes_accessed=5 * rows * q_width * 2,
            transcendentals=count * total * rows,
        ),
        name="prepare_response",
    )(meta, q, g, k, v, q_gain, k_gain)
    return [list(outs[s * KEPT : (s + 1) * KEPT]) for s in range(count)]


def attend(width, pr_ref, kept, acc_ref, part_ref, at_ref, dq_ref, gacc_ref):
    qt_ref, gt_ref, row_ref, er_ref, ot_ref, dp_ref, kh_ref, ku_ref = kept
    scale = HD ** (-0.5)
    q_gain = column(row_ref[2:3, :HD])
    p_key = pr_ref[0]
    p_val = pr_ref[1]
    k_hat_t = kh_ref[...].T
    p_key_t = p_key.T
    p_val_t = p_val.T
    sums = None
    for start in range(0, qt_ref.shape[1], width):
        cols = slice(start, start + width)
        q_unit = qt_ref[:, cols].astype(F32) * row_ref[0:1, cols]
        q_hat = (q_unit * q_gain).astype(BF)
        d_ob = gt_ref[:, cols]
        d_o = d_ob.astype(F32)
        e_p = jnp.exp2(dot_nn(p_key, q_hat) * (scale * LOG2E))
        inv_sum = 1.0 / (jnp.sum(e_p, axis=0, keepdims=True) + row_ref[1:2, cols])
        eb_p = e_p.astype(BF)
        eb_r = er_ref[:, cols]
        out = (dot_nn(p_val_t, eb_p) + ot_ref[:, cols]) * inv_sum
        at_ref[:, cols] = out.astype(BF)
        delta = jnp.sum(d_o * out, axis=0, keepdims=True)
        ds_p = (e_p * (dot_nn(p_val, d_ob) - delta)).astype(BF)
        ds_r = (eb_r.astype(F32) * (dp_ref[:, cols] - delta)).astype(BF)
        weight = inv_sum * scale
        q_w = (q_hat.astype(F32) * weight).astype(BF)
        d_ow = (d_o * inv_sum).astype(BF)
        d_qhat = (dot_nn(p_key_t, ds_p) + dot_nn(k_hat_t, ds_r)) * weight
        dq_ref[:, cols] = d_qhat
        terms = (
            dot_nt(ds_p, q_w),
            dot_nt(eb_p, d_ow),
            dot_nt(ds_r, q_w),
            dot_nt(eb_r, d_ow),
            d_qhat * q_unit,
        )
        sums = terms if sums is None else [a + b for a, b in zip(sums, terms)]
    d_kp, d_vp, d_kr, d_vr, q_term = sums
    part_ref[0] = d_kp.astype(BF)
    part_ref[1] = d_vp.astype(BF)
    folded = q_term[:, :HD]
    for start in range(HD, width, HD):
        folded = folded + q_term[:, start : start + HD]
    gacc_ref[0:1, :] = acc_ref[0:1, :] + jnp.sum(folded.T, axis=0, keepdims=True)
    gacc_ref[1:2, :] = acc_ref[1:2, :] + jnp.sum(d_kr * ku_ref[:, :HD], axis=0, keepdims=True)
    return d_kr, d_vr


def settle(width, head, live_len, kept, at_ref, dq_ref, d_kr, d_vr, outs, bufs, sems):
    qt_ref, row_ref, ku_ref = kept
    q_gain = column(row_ref[2:3, :HD])
    k_gain = row_ref[3:4, :HD]
    a_buf, q_buf, k_buf, v_buf = bufs
    rows, wide = a_buf.shape
    share = wide // HD
    copies = []

    def send(j, buf):
        size = buf.shape[1]
        at = pl.multiple_of(head * size, size)
        copy = pltpu.make_async_copy(buf, outs[j].at[:, pl.ds(at, size)], sems.at[j])
        copy.start()
        copies.append(copy)

    att = at_ref[...].T
    live = lax.broadcasted_iota(jnp.int32, (rows, HD), 0) < live_len
    for i in range(share):
        block = att[i * rows : (i + 1) * rows, :].astype(F32)
        a_buf[:, i * HD : (i + 1) * HD] = jnp.where(live, block, 0.0).astype(BF)
    send(0, a_buf)
    v_buf[...] = d_vr.astype(BF)
    send(3, v_buf)
    k_unit = ku_ref[:, :HD]
    up_k = d_kr * k_gain
    mean_k = jnp.mean(up_k * k_unit, axis=-1, keepdims=True)
    k_buf[...] = (ku_ref[:, HD:] * (up_k - k_unit * mean_k)).astype(BF)
    send(2, k_buf)
    parts = []
    for start in range(0, share * rows, width):
        cols = slice(start, start + width)
        q_inv = row_ref[0:1, cols]
        q_unit = qt_ref[:, cols].astype(F32) * q_inv
        up = dq_ref[:, cols] * q_gain
        mean = jnp.mean(up * q_unit, axis=0, keepdims=True)
        parts.append((q_inv * (up - q_unit * mean)).astype(BF))
    d_q = jnp.concatenate(parts, axis=1).T
    for i in range(share):
        q_buf[:, i * HD : (i + 1) * HD] = d_q[i * rows : (i + 1) * rows, :]
    send(1, q_buf)
    return copies


def first_kernel(width, pr_ref, *rest):
    kept, acc_ref = rest[:KEPT], rest[KEPT]
    part_ref, gacc_ref, at_ref, dq_ref, dkr_ref, dvr_ref = rest[-6:]
    d_kr, d_vr = attend(width, pr_ref, kept, acc_ref, part_ref, at_ref, dq_ref, gacc_ref)
    dkr_ref[...] = d_kr
    dvr_ref[...] = d_vr


def settle_kernel(width, meta, *rest):
    outs, bufs, sems = rest[-9:-5], rest[-5:-1], rest[-1]
    copies = []
    for i in range(sems.shape[0]):
        kept, results = rest[i * 7 : i * 7 + 3], rest[i * 7 + 3 : i * 7 + 7]
        at_ref, dq_ref, dkr_ref, dvr_ref = results
        copies += settle(
            width, meta[i], meta[meta.shape[0] - 1], kept, at_ref, dq_ref,
            dkr_ref[...], dvr_ref[...], outs, [buf.at[i] for buf in bufs], sems.at[i],
        )
    for copy in copies:
        copy.wait()


def out_shapes(rows, q_width, k_width):
    widths = (q_width, q_width, k_width, k_width)
    return [jax.ShapeDtypeStruct((rows, w), BF) for w in widths]


def out_scratch(count, rows, share):
    widths = (share * HD, share * HD, HD, HD)
    return [pltpu.VMEM((count, rows, w), BF) for w in widths] + [pltpu.SemaphoreType.DMA((count, 4))]


def cost(prompt_rows, rows, total):
    return pl.CostEstimate(
        flops=(8 * prompt_rows + 4 * rows) * total * HD,
        bytes_accessed=2**20,
        transcendentals=total * prompt_rows,
    )


def first_half(prompt, kept, acc):
    total = kept[0].shape[1]
    rows = kept[3].shape[0]
    return pl.pallas_call(
        functools.partial(first_kernel, 2 * HD),
        out_shape=[
            jax.ShapeDtypeStruct(prompt.shape, BF),
            jax.ShapeDtypeStruct(acc.shape, F32),
            jax.ShapeDtypeStruct((HD, total), BF),
            jax.ShapeDtypeStruct((HD, total), F32),
            jax.ShapeDtypeStruct((rows, HD), F32),
            jax.ShapeDtypeStruct((rows, HD), F32),
        ],
        in_specs=[VMEM] * (2 + KEPT),
        out_specs=[VMEM] * 6,
        compiler_params=params(16),
        cost_estimate=cost(prompt.shape[1], rows, total),
        name="attend_head",
    )(prompt, *kept, acc)


def settle_heads(meta, per_head, q_width, k_width):
    count = len(per_head)
    total = per_head[0][0].shape[1]
    rows = per_head[0][5].shape[0]
    flat = [x for group in per_head for x in group]
    return pl.pallas_call(
        functools.partial(settle_kernel, 2 * HD),
        out_shape=out_shapes(rows, q_width, k_width),
        in_specs=[SMEM] + [VMEM] * len(flat),
        out_specs=[HBM] * 4,
        scratch_shapes=out_scratch(count, rows, total // rows),
        compiler_params=params(16),
        name="settle_heads",
    )(meta, *flat)


TAIL = 16


def join_kernel(own_ref, *rest):
    backs, gains_ref, out_ref = rest[:-2], rest[-2], rest[-1]
    depth, rows, _ = own_ref.shape
    for d in range(depth):
        total = own_ref[d].astype(F32)
        for back in backs:
            total = total + back[d].astype(F32)
        out_ref[d * rows : (d + 1) * rows, :] = total.astype(BF)
    gains = gains_ref[...]
    high = gains.astype(BF)
    gains = gains - high.astype(F32)
    middle = gains.astype(BF)
    low = (gains - middle.astype(F32)).astype(BF)
    pieces = jnp.concatenate([p[0:2].astype(F32) for p in (high, middle, low)], axis=0)
    pad = jnp.zeros((TAIL - pieces.shape[0], HD), F32)
    out_ref[depth * rows :, :] = jnp.concatenate([pieces, pad], axis=0).astype(BF)


def join(own, backs, gains):
    depth, rows, _ = own.shape
    return pl.pallas_call(
        join_kernel,
        out_shape=jax.ShapeDtypeStruct((depth * rows + TAIL, HD), BF),
        in_specs=[VMEM] * (2 + len(backs)),
        out_specs=VMEM,
        compiler_params=params(8),
        name="join_parts",
    )(own, *backs, gains)


def place_kernel(steps, flag, me, *refs):
    payloads, (out_ref, gain_ref, stage, zeros, sems) = refs[:-5], refs[-5:]
    depth, rows, width = out_ref.shape

    @pl.when(flag[0] > 0)
    def _():
        copies = []
        for i, ref in enumerate(payloads):
            at = pl.ds(pl.multiple_of((me[0] ^ steps[i]) * HD, HD), HD)
            for d in range(depth):
                src = ref.at[d * rows : (d + 1) * rows, :]
                copy = pltpu.make_async_copy(src, out_ref.at[d, :, at], sems.at[i * depth + d])
                copy.start()
                copies.append(copy)
        for copy in copies:
            copy.wait()

    @pl.when(flag[0] == 0)
    def _():
        zeros[...] = jnp.zeros_like(zeros)
        copies = []
        for d in range(depth):
            copy = pltpu.make_async_copy(zeros, out_ref.at[d], sems.at[d])
            copy.start()
            copies.append(copy)
        for copy in copies:
            copy.wait()

    for i, ref in enumerate(payloads):
        tail = ref[depth * rows :, :].astype(F32)
        stage[me[0] ^ steps[i]] = tail[0:2] + tail[2:4] + tail[4:6]
    total = stage[0]
    for i in range(1, len(payloads)):
        total = total + stage[i]
    gain_ref[...] = total


def place(steps, flag, me, payloads, depth, rows):
    count = len(payloads)
    width = HD * count
    return pl.pallas_call(
        functools.partial(place_kernel, tuple(steps)),
        out_shape=[
            jax.ShapeDtypeStruct((depth, rows, width), BF),
            jax.ShapeDtypeStruct((2, HD), F32),
        ],
        in_specs=[SMEM] * 2 + [VMEM] * count,
        out_specs=[HBM, VMEM],
        scratch_shapes=[
            pltpu.VMEM((count, 2, HD), F32),
            pltpu.VMEM((rows, width), BF),
            pltpu.SemaphoreType.DMA((count * depth,)),
        ],
        compiler_params=params(8),
        name="place_prompt_grad",
    )(flag, me, *payloads)


def after(x, *others):
    return lax.optimization_barrier((x,) + others)[0]


def pair_sum(value, axis, size):
    step = 1
    while step < size:
        value = value + lax.ppermute(value, axis, [(i, i ^ step) for i in range(size)])
        step *= 2
    return value


def local(
    n_dp, n_group, queries, resp_keys, resp_values, prompt_cache, owners, lengths, q_gain, k_gain, grad_out
):
    q, g = queries[0, 0], grad_out[0, 0]
    k, v = resp_keys[0, 0], resp_values[0, 0]
    cache = prompt_cache[0, 0]
    owner = owners[0]
    live_len = lengths[0, 0]
    me = lax.axis_index("group")
    kv_heads = k.shape[1] // HD
    depth, p_rows, _ = cache.shape
    direct = n_group == kv_heads and n_group <= 4
    steps = [s ^ (s >> 1) for s in range(kv_heads)]

    order = jnp.arange(kv_heads, dtype=jnp.int32)
    if direct:
        order = order ^ (order >> 1) ^ me
    mine_flag = (me == owner).astype(jnp.int32)
    away = owner ^ me
    meta = jnp.concatenate([order, live_len[None]])
    which, flag, self_index = [
        jnp.reshape(x, (1,)).astype(jnp.int32) for x in (away ^ (away >> 1), mine_flag, me)
    ]
    meta, which, flag, self_index = lax.optimization_barrier((meta, which, flag, self_index))
    q, g, k, v, *gains_in = [
        pltpu.with_memory_space_constraint(x, pltpu.HBM) for x in (q, g, k, v, q_gain, k_gain)
    ]
    acc = jnp.zeros((2, HD), F32)
    kept = prepare(tuple(range(kv_heads)), meta, q, g, k, v, *gains_in)

    def swap(x, step):
        return lax.ppermute(x, "group", [(i, i ^ step) for i in range(n_group)])

    if direct:
        blocks = list(cut(steps, jnp.reshape(me, (1,)).astype(jnp.int32), pltpu.with_memory_space_constraint(cache, pltpu.HBM), kv_heads))
        got = [blocks[0]] + [swap(blocks[s], steps[s]) for s in range(1, n_group)]
        for s in range(1, n_group):
            got[s] = after(got[s], kept[0][2])
        mine = pick(which, got)
        prompts = [mine] + [swap(mine, steps[s]) for s in range(1, n_group)]
    else:
        cache = lax.psum(jnp.where(me == owner, cache, jnp.zeros_like(cache)), "group")
        prompts = cut(range(kv_heads), jnp.zeros((1,), jnp.int32), cache, kv_heads)

    parts, backs, per_head = [], [], []
    for s, prompt in enumerate(prompts):
        part, acc, *results = first_half(prompt, kept[s], acc)
        per_head.append([kept[s][0], kept[s][2], kept[s][7], *results])
        parts.append(part)
        if direct and s > 0:
            backs.append(swap(part, steps[s]))

    def hop(x, step):
        return lax.ppermute(x, "dp", [(i, i ^ step) for i in range(n_dp)])

    gains = acc + hop(acc, 1)
    if direct:
        gains = after(gains, *backs[:-1])
    step = 2
    while step < n_dp:
        gains = gains + hop(gains, step)
        step *= 2
    if direct:
        payload = join(parts[0], backs, gains)
        payloads = [payload] + [swap(payload, steps[s]) for s in range(1, n_group)]
        per_head[0][3] = after(per_head[0][3], payload)
        buffers = settle_heads(meta, per_head, q.shape[1], k.shape[1])
        payloads[1] = after(payloads[1], buffers[2])
        placed, gains = place(steps, flag, self_index, payloads, depth, p_rows)
    else:
        total = lax.psum(jnp.concatenate(parts, axis=-1).astype(F32), "group").astype(BF)
        placed = jnp.where(mine_flag > 0, total, jnp.zeros((), BF))
        gains = pair_sum(gains, "group", n_group)
        buffers = settle_heads(meta, per_head, q.shape[1], k.shape[1])
    attended, d_query, d_key, d_value = buffers
    return (
        attended[None, None],
        d_query[None, None],
        d_key[None, None],
        d_value[None, None],
        placed[None, None],
        gains,
    )


def solution(mesh):
    in_specs = (
        P("dp", "group", None, None),
        P("dp", "group", None, None),
        P("dp", "group", None, None),
        P("dp", "group", None, None, None),
        P("dp"),
        P("dp", "group"),
        P(),
        P(),
        P("dp", "group", None, None),
    )
    out_specs = (
        P("dp", "group", None, None),
        P("dp", "group", None, None),
        P("dp", "group", None, None),
        P("dp", "group", None, None),
        P("dp", "group", None, None, None),
        P(),
    )
    body = functools.partial(local, mesh.shape["dp"], mesh.shape["group"])
    return jax.shard_map(body, mesh=mesh, in_specs=in_specs, out_specs=out_specs, check_vma=False)
```
